32 devices in a mesh: dp: 8 (over z, x), tensor: 4 (over y, core).
Axes of the slice: x: 2, y: 2, z: 4, core: 2. Of those that a mesh axis runs over, the one named last changes fastest.
Arguments:
- inputs: bfloat16 [1024, 16, 1024], P('tensor', 'dp'), may hold values from -6 to 6
- lengths: int32 [16], P('dp'), may hold values from 256 to 1024, as said below
- query_weight: bfloat16 [1024, 1024], P('dp', 'tensor'), may hold values from -0.1875 to 0.1875
- key_value_weight: bfloat16 [1024, 2, 512], P('dp', None, 'tensor'), may hold values from -0.1875 to 0.1875
- output_weight: bfloat16 [1024, 1024], P('tensor', 'dp'), may hold values from -3 to 3
- inner_weight: bfloat16 [1024, 2, 4608], P('dp', None, 'tensor'), may hold values from -0.1875 to 0.1875
- down_weight: bfloat16 [4608, 1024], P('tensor', 'dp'), may hold values from -0.09375 to 0.09375
- mixer_gain: float32 [1024], replicated, may hold values from 0.5 to 1.5
- query_gain: float32 [64], replicated, may hold values from 0.5 to 1.5
- key_gain: float32 [64], replicated, may hold values from 0.5 to 1.5
- dense_gain: float32 [1024], replicated, may hold values from 0.5 to 1.5
- cotangent: bfloat16 [1024, 16, 1024], P('tensor', 'dp'), may hold values from -6 to 6
Outputs:
- block_out: bfloat16 [1024, 16, 1024], P('tensor', 'dp')
- input_gradient: float32 [1024, 16, 1024], P('tensor', 'dp')
- query_gradient: float32 [1024, 1024], P('dp', 'tensor')
- pair_gradient: float32 [1024, 2, 512], P('dp', None, 'tensor')
- output_gradient: float32 [1024, 1024], P('tensor', 'dp')
- inner_gradient: float32 [1024, 2, 4608], P('dp', None, 'tensor')
- down_gradient: float32 [4608, 1024], P('tensor', 'dp')
- mixer_gain_gradient: float32 [1024], replicated
- query_gain_gradient: float32 [64], replicated
- key_gain_gradient: float32 [64], replicated
- dense_gain_gradient: float32 [1024], replicated
The draws below stay inside these ranges and needn't reach their ends.
Inputs may be any that keep to these rules, and one draw needn't show every extreme that they name: `lengths`: among the 2 slots of each index of dp at least one has length 1024.
All inputs are finite; a program needn't handle non-finite values.
Results may differ from the reference program's by a relative error of at most 0.015.
Values may be sent and summed in bfloat16 or wider, within the bound.
A program may use at most 192 MiB of HBM per device.

```python
import jax
import jax.numpy as jnp
from jax import lax

MODEL_WIDTH = 1024
QUERY_HEADS = 16
KEY_VALUE_HEADS = 8
HEAD_SIZE = 64
FF = 4608
SEQ_LEN = 1024
MIN_LEN = 256
GSEQ = 2
SEQS = 16


def draw_lengths(key, part):
    key = jax.random.fold_in(key, 11)
    spread_key, pick_key = jax.random.split(key)
    spans = jax.random.randint(spread_key, (SEQS,), MIN_LEN, SEQ_LEN + 1)
    chosen = jax.random.randint(pick_key, (SEQS // GSEQ,), 0, GSEQ)
    slots = jnp.arange(SEQS)
    full = slots % GSEQ == chosen[slots // GSEQ]
    return jnp.where(full, SEQ_LEN, spans).astype(jnp.int32)


def spiked(values, rng, source, target, shards_of, factor):
    def block_of(axis_at):
        return (jnp.arange(values.shape[axis_at]) // (values.shape[axis_at] // shards_of)).reshape((-1,) + (1,) * (values.ndim - 1 - axis_at))

    near = jax.random.permutation(rng, shards_of)[block_of(target)]
    other_side = (block_of(target) + shards_of // 2) % shards_of
    return jnp.where((block_of(source) == near) | (block_of(source) == other_side), factor * values, values)


def block_levels(key, dims, pieces, least, high):
    factor_of = 1.0
    for axis_at, parts in pieces:
        draws = jax.random.uniform(jax.random.fold_in(jax.random.fold_in(key, 6), axis_at), (parts,), jnp.float32, least / len(pieces), high / len(pieces))
        factor_of = factor_of * jnp.repeat(jnp.exp(draws), dims[axis_at] // parts).reshape((-1,) + (1,) * (len(dims) - 1 - axis_at))
    return factor_of


def bell_draw(rng, extent, width, limit, pieces=(), held_as=jnp.bfloat16):
    entries = width * jax.random.normal(rng, extent, jnp.float32)
    if pieces:
        entries = entries * block_levels(rng, extent, pieces, -0.22, 0.18)
    return jnp.clip(entries, -limit, limit).astype(held_as)


def bell_draw_with(key, dims, deviation, most, cuts, heavy, held_as=jnp.bfloat16):
    drawn = deviation * jax.random.normal(key, dims, jnp.float32)
    if cuts:
        drawn = drawn * block_levels(key, dims, cuts, -0.22, 0.18)
    return jnp.clip(spiked(drawn, jax.random.fold_in(key, 3), *heavy), -most, most).astype(held_as)


def setup_inputs(seed: int = 0) -> dict:
    key_of = jax.random.split(jax.random.key(seed), 13)
    inputs = bell_draw_with(key_of[0], (SEQ_LEN, SEQS, MODEL_WIDTH), 1.0, 6.0, ((0, 4), (1, 8)), (1, 2, 8, 2.0))
    lengths = draw_lengths(jax.random.fold_in(key_of[12], 71), 0)
    query_weight = bell_draw(key_of[2], (MODEL_WIDTH, QUERY_HEADS * HEAD_SIZE), MODEL_WIDTH ** -0.5, 0.1875, ((0, 8), (1, 4)))
    key_value_weight = bell_draw(key_of[3], (MODEL_WIDTH, 2, KEY_VALUE_HEADS * HEAD_SIZE), MODEL_WIDTH ** -0.5, 0.1875, ((0, 8), (2, 4)))
    output_weight = bell_draw(key_of[4], (QUERY_HEADS * HEAD_SIZE, MODEL_WIDTH), (QUERY_HEADS * HEAD_SIZE * 4 // SEQ_LEN) ** -0.5, 3.0, ((0, 4), (1, 8)))
    inner_weight = bell_draw(key_of[5], (MODEL_WIDTH, 2, FF), MODEL_WIDTH ** -0.5, 0.1875, ((0, 8), (2, 4)))
    down_weight = bell_draw(key_of[6], (FF, MODEL_WIDTH), FF ** -0.5, 0.09375, ((0, 4), (1, 8)))
    mixer_gain = jnp.clip(1.0 + 0.1 * jax.random.normal(key_of[7], (MODEL_WIDTH,), jnp.float32), 0.5, 1.5)
    query_gain = jnp.clip(1.0 + 0.1 * jax.random.normal(key_of[8], (HEAD_SIZE,), jnp.float32), 0.5, 1.5)
    key_gain = jnp.clip(1.0 + 0.1 * jax.random.normal(key_of[9], (HEAD_SIZE,), jnp.float32), 0.5, 1.5)
    dense_gain = jnp.clip(1.0 + 0.1 * jax.random.normal(key_of[10], (MODEL_WIDTH,), jnp.float32), 0.5, 1.5)
    cotangent = bell_draw_with(key_of[11], (SEQ_LEN, SEQS, MODEL_WIDTH), 1.0, 6.0, ((0, 4), (1, 8)), (1, 2, 8, 2.0))
    return {"inputs": inputs, "lengths": lengths, "query_weight": query_weight, "key_value_weight": key_value_weight, "output_weight": output_weight, "inner_weight": inner_weight, "down_weight": down_weight, "mixer_gain": mixer_gain, "query_gain": query_gain, "key_gain": key_gain, "dense_gain": dense_gain, "cotangent": cotangent}


EPS = 1e-05
THETA = 1000000.0
HIGH = lax.Precision.HIGHEST

@jax.custom_vjp
def low(v):
    return lax.optimization_barrier(v.astype(jnp.bfloat16)).astype(jnp.float32)

@jax.custom_vjp
def reduced_backward_rows(v):
    return v

def low_keep(v):
    return (low(v), None)

def low_pass(kept, grad):
    return (grad,)

def back_keep(v):
    return (v, None)

def back_low(kept, grad):
    return (low(grad),)
low.defvjp(low_keep, low_pass)
reduced_backward_rows.defvjp(back_keep, back_low)

def matrix_product(left, right):
    return jnp.dot(left, right, precision=HIGH, preferred_element_type=jnp.float32)

def norm_rows(values, gain):
    return values * lax.rsqrt(lax.optimization_barrier(jnp.mean(values * values, axis=-1, keepdims=True)) + EPS) * gain

def rotate(values, cosines, sines):
    half = values.shape[-1] // 2
    first = values[..., :half]
    second = values[..., half:]
    return jnp.concatenate([first * cosines - second * sines, second * cosines + first * sines], axis=-1)

def layer(inputs, length, query_weight, key_value_weight, output_weight, inner_weight, down_weight, mixer_gain, query_gain, key_gain, dense_gain):
    combined_length = inputs.shape[0]
    half = HEAD_SIZE // 2
    freqs = THETA ** (-jnp.arange(half, dtype=jnp.float32) * 2.0 / HEAD_SIZE)
    angles = jnp.arange(combined_length, dtype=jnp.float32)[:, None] * freqs[None, :]
    cosines = jnp.cos(angles)[:, None, :]
    sines = jnp.sin(angles)[:, None, :]
    normalized_rows = low(norm_rows(inputs, mixer_gain))
    queries_raw = reduced_backward_rows(matrix_product(normalized_rows, query_weight)).reshape(combined_length, QUERY_HEADS, HEAD_SIZE)
    unscaled_key_value = reduced_backward_rows(matrix_product(normalized_rows, key_value_weight.reshape(MODEL_WIDTH, 2 * KEY_VALUE_HEADS * HEAD_SIZE))).reshape(combined_length, 2, KEY_VALUE_HEADS, HEAD_SIZE)
    query_rows = low(rotate(norm_rows(queries_raw, query_gain), cosines, sines))
    keys = low(rotate(norm_rows(unscaled_key_value[:, 0], key_gain), cosines, sines))
    values = low(unscaled_key_value[:, 1])
    query_groups = query_rows.reshape(combined_length, KEY_VALUE_HEADS, QUERY_HEADS // KEY_VALUE_HEADS, HEAD_SIZE)
    row_count = min(512, combined_length)
    key_pos = jnp.arange(combined_length, dtype=jnp.int32)
    factor = HEAD_SIZE ** (-0.5)

    def attend(start):
        token_rows = lax.dynamic_slice_in_dim(query_groups, start, row_count, 0)
        scores = reduced_backward_rows(jnp.einsum('qhgd,khd->hgqk', token_rows, keys, precision=HIGH) * factor)
        query_pos = start + jnp.arange(row_count, dtype=jnp.int32)
        allowed = (key_pos[None, :] <= query_pos[:, None]) & (key_pos[None, :] < length)
        scores = jnp.where(allowed, scores, -1e+30)
        weights = jnp.exp(scores - lax.optimization_barrier(jnp.max(scores, axis=-1, keepdims=True)))
        probs = low(weights / lax.optimization_barrier(jnp.sum(weights, axis=-1, keepdims=True)))
        return jnp.einsum('hgqk,khd->qhgd', probs, values, precision=HIGH)
    starts = (jnp.arange(combined_length // row_count) * row_count).astype(jnp.int32)
    attended = lax.map(jax.checkpoint(attend), starts).reshape(combined_length, QUERY_HEADS * HEAD_SIZE)
    attended = reduced_backward_rows(low(attended))
    residual = inputs + reduced_backward_rows(matrix_product(attended, output_weight))
    dense_in = low(norm_rows(residual, dense_gain))
    gate_up = reduced_backward_rows(matrix_product(dense_in, inner_weight.reshape(MODEL_WIDTH, 2 * FF)))
    hidden_state = low(jax.nn.silu(gate_up[:, :FF]) * gate_up[:, FF:])
    result = residual + reduced_backward_rows(matrix_product(hidden_state, down_weight))
    return jnp.where((key_pos < length)[:, None], result, 0.0)

def reference(inputs, lengths, query_weight, key_value_weight, output_weight, inner_weight, down_weight, mixer_gain, query_gain, key_gain, dense_gain, cotangent):
    params = (query_weight.astype(jnp.float32), key_value_weight.astype(jnp.float32), output_weight.astype(jnp.float32), inner_weight.astype(jnp.float32), down_weight.astype(jnp.float32), mixer_gain.astype(jnp.float32), query_gain.astype(jnp.float32), key_gain.astype(jnp.float32), dense_gain.astype(jnp.float32))

    def one(totals, item):
        sequence, length, upstream = item

        def run(sequence, *weights):
            return layer(sequence, length, *weights)
        result, pull = jax.vjp(run, sequence.astype(jnp.float32), *params)
        grads = pull(upstream.astype(jnp.float32))
        totals = tuple((left + right for left, right in zip(totals, grads[1:])))
        return (totals, (result.astype(jnp.bfloat16), grads[0]))
    init = tuple((jnp.zeros_like(weight) for weight in params))
    totals, (results, input_grads) = lax.scan(one, init, (jnp.moveaxis(inputs, 1, 0), lengths, jnp.moveaxis(cotangent, 1, 0)))
    return (jnp.moveaxis(results, 0, 1), jnp.moveaxis(input_grads, 0, 1), totals[0], totals[1], totals[2], totals[3], totals[4], totals[5], totals[6], totals[7], totals[8])
```

```python
import functools

import jax
import jax.numpy as jnp
from jax import lax
from jax.experimental import pallas as pl
from jax.experimental.pallas import tpu as pltpu
from jax.sharding import PartitionSpec as P

EPS = 1e-05
THETA = 1000000.0
LOG2E = 1.4426950408889634
F32 = jnp.float32
BF16 = jnp.bfloat16
HIGH = lax.Precision.HIGHEST
LANES = 128
VMEM_LIMIT = 56 * 1024 * 1024
ANY = pl.BlockSpec(memory_space=pl.ANY)
VMEM = pl.BlockSpec(memory_space=pltpu.VMEM)
SMEM = pl.BlockSpec(memory_space=pltpu.SMEM)


def dot(a, b, **kw):
    return lax.dot_general(
        a, b, (((1,), (0,)), ((), ())), preferred_element_type=F32, **kw
    )


def dot_nt(a, b, **kw):
    return lax.dot_general(
        a, b, (((1,), (1,)), ((), ())), preferred_element_type=F32, **kw
    )


def dot_tn(a, b, **kw):
    return lax.dot_general(
        a, b, (((0,), (0,)), ((), ())), preferred_element_type=F32, **kw
    )


def iota(shape, axis):
    return lax.broadcasted_iota(jnp.int32, shape, axis)


def low_half(shape):
    return iota(shape, 1) % LANES < LANES // 2


def head_blocks(scale):
    shape = (LANES, LANES)
    return jnp.where(iota(shape, 0) // 64 == iota(shape, 1) // 64, scale, 0.0).astype(F32)


def partner(values):
    first = iota(values.shape, 1) % 64 < 32
    return jnp.where(first, pltpu.roll(values, LANES - 32, 1), pltpu.roll(values, 32, 1))


def rows_of(index, size):
    return pl.ds(pl.multiple_of(index * size, size), size)


def load_all(sources, targets, sems, first):
    copies = []
    for number, (source, target) in enumerate(zip(sources, targets)):
        copy = pltpu.make_async_copy(source, target, sems.at[first + number])
        copy.start()
        copies.append(copy)
    return copies


def shard_targets(w_refs, ws, me):
    size = w_refs[0].shape[0]
    if len(w_refs) == 1:
        return [ws]
    return [ws.at[rows_of(me ^ slot, size)] for slot in range(len(w_refs))]


def store_slots(whole, out_refs, me):
    if len(out_refs) == 1:
        out_refs[0][...] = whole[...]
        return
    keep_ref, send_ref = out_refs
    size = keep_ref.shape[1]
    for slot in range(2 * keep_ref.shape[0]):
        (send_ref if slot % 2 else keep_ref)[slot // 2] = whole[rows_of(me ^ slot, size), :]


def attn_fwd_kernel(parts, n_w, scal, cos_ref, sin_ref, gq_ref, gk_ref, *refs):
    x_refs, refs = refs[:parts], refs[parts:]
    w_refs, refs = refs[:n_w], refs[n_w:]
    (raw_ref, q_ref, k_ref, v_ref, att_ref, lse_ref, keep_ref, send_ref, xs, ws, kp, vp, acc, sems) = refs
    size = x_refs[0].shape[0]
    me_t, me_d, length = scal[0], scal[1], scal[2]
    copies = load_all(w_refs, shard_targets(w_refs, ws, me_d), sems, 0)
    copies += load_all(x_refs, [xs.at[rows_of(me_t ^ j, size)] for j in range(parts)], sems, n_w)
    for copy in copies:
        copy.wait()
    mean_of = head_blocks(1.0 / 64)
    low = low_half((size, LANES))
    factor = LOG2E / 8.0

    def project(r, carry):
        rows = rows_of(r, size)
        projected = dot(xs[rows, :], ws[:, :512])
        raw_ref[rows, :] = projected[:, :384]
        cosines, sines = cos_ref[rows, :], sin_ref[rows, :]

        def turned(values, gain):
            mean = dot(values * values, mean_of, precision=HIGH)
            normed = values * lax.rsqrt(mean + EPS) * gain
            return normed * cosines + partner(normed) * sines

        for g in range(2):
            lanes = slice(LANES * g, LANES * (g + 1))
            q_ref[rows, lanes] = turned(projected[:, lanes], gq_ref[...]).astype(BF16)
        keys = turned(projected[:, 256:384], gk_ref[...])
        values = projected[:, 384:512]
        k_ref[rows, :] = keys.astype(BF16)
        v_ref[rows, :] = values.astype(BF16)
        live = r * size + iota((size, LANES), 0) < length
        ones = jnp.where(live, 1.0, 0.0)
        values = jnp.where(live, values, 0.0)
        keys_swap, values_swap = pltpu.roll(keys, 64, 1), pltpu.roll(values, 64, 1)
        for g in range(2):
            for e in range(2):
                here = low if e == 0 else jnp.logical_not(low)
                kp[2 * g + e, rows, :] = jnp.where(here, keys if g == e else keys_swap, 0.0).astype(BF16)
                vp[2 * g + e, rows, :LANES] = jnp.where(here, values if g == e else values_swap, 0.0).astype(BF16)
                vp[2 * g + e, rows, LANES:] = jnp.where(here, ones, 0.0).astype(BF16)
        return carry

    lax.fori_loop(0, parts, project, 0)
    causal = iota((size, size), 1) <= iota((size, size), 0)

    def attend(i, carry):
        rows = rows_of(i, size)
        queries = [q_ref[rows, LANES * g : LANES * (g + 1)] for g in range(2)]

        def block(kb, masked):
            cols = rows_of(kb, size)
            sums = []
            for g in range(2):
                total = None
                for e in range(2):
                    weights = jnp.exp2(dot_nt(queries[g], kp[2 * g + e, cols, :]) * factor)
                    if masked:
                        weights = jnp.where(causal, weights, 0.0)
                    part = dot(weights.astype(BF16), vp[2 * g + e, cols, :])
                    total = part if total is None else total + part
                sums.append(total)
            return sums

        for g, total in enumerate(block(i, True)):
            acc[g] = total

        def more(kb, carry):
            for g, total in enumerate(block(kb, False)):
                acc[g] += total
            return carry

        lax.fori_loop(0, i, more, 0)
        for g in range(2):
            lanes = slice(LANES * g, LANES * (g + 1))
            summed = acc[g, :, LANES:]
            att_ref[rows, lanes] = (acc[g, :, :LANES] / summed).astype(BF16)
            lse_ref[rows, lanes] = jnp.log2(summed)
        return carry

    lax.fori_loop(0, parts, attend, 0)
    for j in range(parts):
        out = dot_nt(att_ref[rows_of(me_t ^ j, size), :], ws[:, 512:])
        (send_ref if j % 2 else keep_ref)[j // 2] = out.astype(BF16)


def attn_fwd(scal, cosines, sines, gq, gk, x_parts, w_parts):
    parts, n_w = len(x_parts), len(w_parts)
    size, width = x_parts[0].shape
    full = parts * size
    cols = w_parts[0].shape[1]
    pair = jax.ShapeDtypeStruct((parts // 2, size, width), BF16)
    return pl.pallas_call(
        functools.partial(attn_fwd_kernel, parts, n_w),
        out_shape=(
            jax.ShapeDtypeStruct((full, 384), F32),
            jax.ShapeDtypeStruct((full, 256), BF16),
            jax.ShapeDtypeStruct((full, 128), BF16),
            jax.ShapeDtypeStruct((full, 128), BF16),
            jax.ShapeDtypeStruct((full, 256), BF16),
            jax.ShapeDtypeStruct((full, 256), F32),
            pair,
            pair,
        ),
        in_specs=[SMEM] + [VMEM] * 4 + [ANY] * (parts + n_w),
        out_specs=(VMEM,) * 8,
        scratch_shapes=[
            pltpu.VMEM((full, width), BF16),
            pltpu.VMEM((width, cols), BF16),
            pltpu.VMEM((4, full, LANES), BF16),
            pltpu.VMEM((4, full, 2 * LANES), BF16),
            pltpu.VMEM((2, size, 2 * LANES), F32),
            pltpu.SemaphoreType.DMA((n_w + parts,)),
        ],
        compiler_params=pltpu.CompilerParams(vmem_limit_bytes=VMEM_LIMIT),
        cost_estimate=pl.CostEstimate(flops=8_000_000_000, bytes_accessed=12_000_000, transcendentals=3_000_000),
        name="attention_forward",
    )(scal, cosines, sines, gq, gk, *x_parts, *w_parts)


def attn_bwd_kernel(parts, n_w, scal, cos_ref, sin_ref, gq_ref, gk_ref, raw_ref, q_ref, k_ref, v_ref, att_ref, lse_ref, *refs):
    x_refs, refs = refs[:parts], refs[parts:]
    r_refs, refs = refs[:parts], refs[parts:]
    w_refs, refs = refs[:n_w], refs[n_w:]
    n_g = 1 if n_w == 1 else 2
    keep_ref, send_ref, gains_ref = refs[:3]
    g_refs, refs = refs[3 : 3 + n_g], refs[3 + n_g :]
    xs, gs, ws, kp, vp, kt, ga, dq, dk, dv, gp, whole, lrow, drow, acc, sems = refs
    size = x_refs[0].shape[0]
    full = parts * size
    me_t, me_d, length = scal[0], scal[1], scal[2]
    copies = load_all(w_refs, shard_targets(w_refs, ws, me_d), sems, 0)
    copies += load_all(r_refs, [gs.at[rows_of(me_t ^ j, size)] for j in range(parts)], sems, n_w)
    copies += load_all(x_refs, [xs.at[rows_of(me_t ^ j, size)] for j in range(parts)], sems, n_w + parts)
    for copy in copies:
        copy.wait()
    mean_of = head_blocks(1.0 / 64)
    low = low_half((size, LANES))
    factor = LOG2E / 8.0
    pick = jnp.where(iota((8, 256), 0) == iota((8, 256), 1) // 64, 1.0, 0.0).astype(F32)

    def prepare(r, carry):
        rows = rows_of(r, size)
        grad = dot(gs[rows, :], ws[:, 512:]).astype(BF16)
        ga[rows, :] = grad
        drow[:, rows] = dot_nt(pick, grad.astype(F32) * att_ref[rows, :].astype(F32), precision=HIGH)
        lrow[:, rows] = dot_nt(pick * (1.0 / 64), lse_ref[rows, :], precision=HIGH)
        live = r * size + iota((size, LANES), 0) < length
        keys = jnp.where(live, k_ref[rows, :].astype(F32), 0.0)
        values = jnp.where(live, v_ref[rows, :].astype(F32), 0.0)
        keys_swap, values_swap = pltpu.roll(keys, 64, 1), pltpu.roll(values, 64, 1)
        for g in range(2):
            for e in range(2):
                here = low if e == 0 else jnp.logical_not(low)
                padded = jnp.where(here, keys if g == e else keys_swap, 0.0)
                kp[2 * g + e, rows, :] = padded.astype(BF16)
                kt[2 * g + e, :, rows] = padded.T.astype(BF16)
                vp[2 * g + e, rows, :] = jnp.where(here, values if g == e else values_swap, 0.0).astype(BF16)
        return carry

    lax.fori_loop(0, parts, prepare, 0)
    dk[...] = jnp.zeros_like(dk)
    dv[...] = jnp.zeros_like(dv)
    causal = iota((size, size), 0) <= iota((size, size), 1)
    low2 = iota((2 * size, LANES), 0) // size == iota((2 * size, LANES), 1) // 64

    def sweep(i, carry):
        rows = rows_of(i, size)
        queries, grads, queries2, grads2 = [], [], [], []
        for g in range(2):
            lanes = slice(LANES * g, LANES * (g + 1))
            queries.append(q_ref[rows, lanes])
            grads.append(ga[rows, lanes])
            for source, target in ((queries, queries2), (grads, grads2)):
                both = jnp.concatenate([source[g], source[g]], axis=0)
                target.append(jnp.where(low2, both, jnp.zeros_like(both)))

        def block(kb, masked):
            cols = rows_of(kb, size)
            parts_t = []
            for g in range(2):
                weights2, scores2, turned = [], [], None
                for e in range(2):
                    h = 2 * g + e
                    weights = jnp.exp2(dot_nt(kp[h, cols, :], queries[g]) * factor - lrow[h : h + 1, rows])
                    if masked:
                        weights = jnp.where(causal, weights, 0.0)
                    grad_weights = dot_nt(vp[h, cols, :], grads[g])
                    grad_scores = (weights * (grad_weights - drow[h : h + 1, rows])).astype(BF16)
                    weights2.append(weights.astype(BF16))
                    scores2.append(grad_scores)
                    part = dot(kt[h, :, cols], grad_scores)
                    turned = part if turned is None else turned + part
                dv[g, cols, :] += dot(jnp.concatenate(weights2, axis=1), grads2[g])
                dk[g, cols, :] += dot(jnp.concatenate(scores2, axis=1), queries2[g])
                parts_t.append(turned)
            return parts_t

        for g, total in enumerate(block(i, True)):
            acc[g] = total

        def more(kb, carry):
            for g, total in enumerate(block(kb, False)):
                acc[g] += total
            return carry

        lax.fori_loop(0, i, more, 0)
        for g in range(2):
            dq[rows, LANES * g : LANES * (g + 1)] = acc[g].T
        return carry

    lax.fori_loop(0, parts, sweep, 0)
    gains_ref[...] = jnp.zeros_like(gains_ref)

    def project(r, carry):
        rows = rows_of(r, size)
        cosines, sines = cos_ref[rows, :], sin_ref[rows, :]
        live = r * size + iota((size, LANES), 0) < length

        def back(grad, lanes, gain, row):
            raw = raw_ref[rows, lanes]
            rms = lax.rsqrt(dot(raw * raw, mean_of, precision=HIGH) + EPS)
            turned = grad * cosines - partner(grad) * sines
            gains_ref[row : row + 1, :] += jnp.sum(turned * raw * rms, axis=0, keepdims=True)
            weighted = turned * gain
            inner = dot(raw * weighted, mean_of, precision=HIGH)
            gp[rows, lanes] = (rms * weighted - raw * (rms * rms * rms) * inner).astype(BF16)

        def folded(ref):
            first, second = ref[0, rows, :], ref[1, rows, :]
            both = jnp.where(low, first + pltpu.roll(first, 64, 1), second + pltpu.roll(second, 64, 1))
            return jnp.where(live, both, 0.0)

        for g in range(2):
            lanes = slice(LANES * g, LANES * (g + 1))
            back(dq[rows, lanes] * 0.125, lanes, gq_ref[...], 0)
        back(folded(dk) * 0.125, slice(256, 384), gk_ref[...], 1)
        gp[rows, 384:512] = folded(dv).astype(BF16)
        return carry

    lax.fori_loop(0, parts, project, 0)
    for j in range(parts):
        out = dot_nt(gp[rows_of(me_t ^ j, size), :], ws[:, :512])
        (send_ref if j % 2 else keep_ref)[j // 2] = out.astype(BF16)

    def weigh(b, carry):
        rows = rows_of(b, 256)
        whole[rows, :512] = dot_tn(xs[:, rows], gp[...]).astype(BF16)
        whole[rows, 512:] = dot_tn(gs[:, rows], att_ref[...]).astype(BF16)
        return carry

    lax.fori_loop(0, whole.shape[0] // 256, weigh, 0)
    store_slots(whole, g_refs, me_d)


def slot_shapes(n_w, width, cols):
    if n_w == 1:
        return (jax.ShapeDtypeStruct((width, cols), BF16),)
    return (jax.ShapeDtypeStruct((n_w // 2, width // n_w, cols), BF16),) * 2


def attn_bwd(scal, cosines, sines, gq, gk, saved, x_parts, r_parts, w_parts):
    parts, n_w = len(x_parts), len(w_parts)
    size, width = x_parts[0].shape
    full = parts * size
    cols = w_parts[0].shape[1]
    pair = jax.ShapeDtypeStruct((parts // 2, size, width), BF16)
    g_shapes = slot_shapes(n_w, width, cols)
    outs = pl.pallas_call(
        functools.partial(attn_bwd_kernel, parts, n_w),
        out_shape=(pair, pair, jax.ShapeDtypeStruct((8, LANES), F32)) + g_shapes,
        in_specs=[SMEM] + [VMEM] * 10 + [ANY] * (2 * parts + n_w),
        out_specs=(VMEM,) * (3 + len(g_shapes)),
        scratch_shapes=[
            pltpu.VMEM((full, width), BF16),
            pltpu.VMEM((full, width), BF16),
            pltpu.VMEM((width, cols), BF16),
            pltpu.VMEM((4, full, LANES), BF16),
            pltpu.VMEM((4, full, LANES), BF16),
            pltpu.VMEM((4, LANES, full), BF16),
            pltpu.VMEM((full, 256), BF16),
            pltpu.VMEM((full, 256), F32),
            pltpu.VMEM((2, full, LANES), F32),
            pltpu.VMEM((2, full, LANES), F32),
            pltpu.VMEM((full, 512), BF16),
            pltpu.VMEM((width, cols), BF16),
            pltpu.VMEM((8, full), F32),
            pltpu.VMEM((8, full), F32),
            pltpu.VMEM((2, LANES, size), F32),
            pltpu.SemaphoreType.DMA((n_w + 2 * parts,)),
        ],
        compiler_params=pltpu.CompilerParams(vmem_limit_bytes=VMEM_LIMIT),
        cost_estimate=pl.CostEstimate(flops=14_000_000_000, bytes_accessed=15_000_000, transcendentals=3_000_000),
        name="attention_backward",
    )(scal, cosines, sines, gq, gk, *saved, *x_parts, *r_parts, *w_parts)
    return outs[0], outs[1], outs[2], outs[3:]


def ff_kernel(n_x, n_w, scal, *refs):
    x_refs, refs = refs[:n_x], refs[n_x:]
    u_refs, refs = refs[:n_x], refs[n_x:]
    w_refs, refs = refs[:n_w], refs[n_w:]
    n_g = 1 if n_w == 1 else 2
    hid_ref, ggu_ref = refs[:2]
    g_refs, refs = refs[2 : 2 + n_g], refs[2 + n_g :]
    xs, us, ws, whole, sems = refs
    size = x_refs[0].shape[0]
    me_d = scal[1]
    cols = ws.shape[1] // 3
    copies = load_all(w_refs, shard_targets(w_refs, ws, me_d), sems, 0)
    x_copies = load_all(x_refs, [xs.at[pl.ds(j * size, size)] for j in range(n_x)], sems, n_w)
    u_copies = load_all(u_refs, [us.at[pl.ds(j * size, size)] for j in range(n_x)], sems, n_w + n_x)
    for copy in copies + x_copies + u_copies:
        copy.wait()

    def tokens(r, carry):
        rows = rows_of(r, size)
        gate_up = dot(xs[rows, :], ws[:, : 2 * cols])
        grad = dot(us[rows, :], ws[:, 2 * cols :])
        gate, up = gate_up[:, :cols], gate_up[:, cols:]
        sig = 1.0 / (1.0 + jnp.exp2(gate * -LOG2E))
        silu = gate * sig
        hid_ref[rows, :] = (silu * up).astype(BF16)
        ggu_ref[rows, :cols] = (grad * up * (sig + silu * (1.0 - sig))).astype(BF16)
        ggu_ref[rows, cols:] = (grad * silu).astype(BF16)
        return carry

    lax.fori_loop(0, n_x, tokens, 0)

    def weigh(b, carry):
        rows = rows_of(b, 256)
        whole[rows, : 2 * cols] = dot_tn(xs[:, rows], ggu_ref[...]).astype(BF16)
        whole[rows, 2 * cols :] = dot_tn(us[:, rows], hid_ref[...]).astype(BF16)
        return carry

    lax.fori_loop(0, whole.shape[0] // 256, weigh, 0)
    store_slots(whole, g_refs, me_d)


def feed_forward(scal, x_parts, u_parts, w_parts):
    n_x, n_w = len(x_parts), len(w_parts)
    size, width = x_parts[0].shape
    full = n_x * size
    wide = w_parts[0].shape[1]
    cols = wide // 3
    g_shapes = slot_shapes(n_w, width, wide)
    outs = pl.pallas_call(
        functools.partial(ff_kernel, n_x, n_w),
        out_shape=(
            jax.ShapeDtypeStruct((full, cols), BF16),
            jax.ShapeDtypeStruct((full, 2 * cols), BF16),
        )
        + g_shapes,
        in_specs=[SMEM] + [ANY] * (2 * n_x + n_w),
        out_specs=(VMEM,) * (2 + len(g_shapes)),
        scratch_shapes=[
            pltpu.VMEM((full, width), BF16),
            pltpu.VMEM((full, width), BF16),
            pltpu.VMEM((width, wide), BF16),
            pltpu.VMEM((width, wide), BF16),
            pltpu.SemaphoreType.DMA((n_w + 2 * n_x,)),
        ],
        compiler_params=pltpu.CompilerParams(vmem_limit_bytes=VMEM_LIMIT),
        cost_estimate=pl.CostEstimate(flops=4 * full * width * wide, bytes_accessed=20_000_000, transcendentals=full * cols),
        name="feed_forward",
    )(scal, *x_parts, *u_parts, *w_parts)
    return outs[0], outs[1], outs[2:]


def ff_out_kernel(parts, n_c, n_w, seq, scal, *refs):
    hid_refs, refs = refs[:n_c], refs[n_c:]
    ggu_refs, refs = refs[:n_c], refs[n_c:]
    w_refs, refs = refs[: n_c * n_w], refs[n_c * n_w :]
    ykeep_ref, ysend_ref, gkeep_ref, gsend_ref, hs, gs, ws, sems = refs
    size = ykeep_ref.shape[1]
    full = parts * size
    me_d = scal[1]
    wide = ws.shape[2]
    cols = wide // 3
    copies = []
    first = 0
    for c in range(n_c):
        targets = shard_targets(w_refs[c * n_w : (c + 1) * n_w], ws.at[c], me_d)
        copies += load_all(w_refs[c * n_w : (c + 1) * n_w], targets, sems, first)
        first += n_w
    mine = pl.ds(seq * full, full)
    copies += load_all([ref.at[mine] for ref in ggu_refs], [gs.at[c] for c in range(n_c)], sems, first)
    copies += load_all([ref.at[mine] for ref in hid_refs], [hs.at[c] for c in range(n_c)], sems, first + n_c)
    for copy in copies:
        copy.wait()
    for j in range(parts):
        rows = pl.ds(j * size, size)
        grad = sum(dot_nt(gs[c, rows, :], ws[c, :, : 2 * cols]) for c in range(n_c))
        (gsend_ref if j % 2 else gkeep_ref)[j // 2] = grad.astype(BF16)
        out = sum(dot_nt(hs[c, rows, :], ws[c, :, 2 * cols :]) for c in range(n_c))
        (ysend_ref if j % 2 else ykeep_ref)[j // 2] = out.astype(BF16)


def ff_out(seq, scal, parts, size, hids, ggus, w_chunks):
    n_c, n_w = len(w_chunks), len(w_chunks[0])
    wide = w_chunks[0][0].shape[1]
    width = w_chunks[0][0].shape[0] * n_w
    full = parts * size
    cols = wide // 3
    pair = jax.ShapeDtypeStruct((parts // 2, size, width), BF16)
    return pl.pallas_call(
        functools.partial(ff_out_kernel, parts, n_c, n_w, seq),
        out_shape=(pair,) * 4,
        in_specs=[SMEM] + [ANY] * (2 * n_c + n_c * n_w),
        out_specs=(VMEM,) * 4,
        scratch_shapes=[
            pltpu.VMEM((n_c, full, cols), BF16),
            pltpu.VMEM((n_c, full, 2 * cols), BF16),
            pltpu.VMEM((n_c, width, wide), BF16),
            pltpu.SemaphoreType.DMA((n_c * n_w + 2 * n_c,)),
        ],
        compiler_params=pltpu.CompilerParams(vmem_limit_bytes=VMEM_LIMIT),
        cost_estimate=pl.CostEstimate(flops=2 * full * width * wide * n_c, bytes_accessed=22_000_000, transcendentals=0),
        name="feed_forward_out",
    )(scal, *hids, *ggus, *[shard for chunk in w_chunks for shard in chunk])


def swap(values, axis, bits):
    return lax.ppermute(values, axis, [(i, i ^ bits) for i in range(lax.axis_size(axis))])


def gather_tokens(block):
    far = swap(block, "tensor", 2)
    return [block, swap(block, "tensor", 1), far, swap(far, "tensor", 1)]


def scatter_tokens(keep, send):
    near = swap(send, "tensor", 1)
    middle = (keep[1].astype(F32) + near[1].astype(F32)).astype(BF16)
    far = swap(middle, "tensor", 2)
    return keep[0].astype(F32) + near[0].astype(F32) + far.astype(F32)


def gather_shards(shard):
    if lax.axis_size("dp") != 8 or shard.shape[0] % LANES:
        return [lax.all_gather(shard, "dp", axis=0, tiled=True)]
    slots = [shard, swap(shard, "dp", 1)]
    for bits in (2, 4, 6):
        there = swap(shard, "dp", bits)
        slots += [there, swap(there, "dp", 1)]
    return slots


def scatter_shards(grads):
    if len(grads) == 1:
        return lax.psum_scatter(grads[0].astype(F32), "dp", scatter_dimension=0, tiled=True)
    keep, send = grads
    near = swap(send, "dp", 1)
    both = keep.astype(F32) + near.astype(F32)
    total = both[0]
    for slot in (1, 2, 3):
        total = total + swap(both[slot].astype(BF16), "dp", 2 * slot).astype(F32)
    return total


def sum_everywhere(values):
    for axis in ("tensor", "dp"):
        bits = 1
        while bits < lax.axis_size(axis):
            values = values + swap(values, axis, bits)
            bits *= 2
    return values


def norm_rows(values, gain):
    factor = lax.rsqrt(jnp.mean(values * values, axis=-1, keepdims=True) + EPS)
    return (values * factor * gain, factor)


def norm_back(values, factor, gain, upstream):
    weighted = upstream * gain
    inner = jnp.mean(values * weighted, axis=-1, keepdims=True)
    return factor * weighted - values * factor * factor * factor * inner


def tables(full, head_width):
    half = head_width // 2
    freqs = THETA ** (-jnp.arange(half, dtype=F32) * 2.0 / head_width)
    angles = jnp.arange(full, dtype=F32)[:, None] * freqs[None, :]
    cosines, sines = jnp.cos(angles), jnp.sin(angles)
    return (jnp.tile(cosines, (1, 4)), jnp.tile(jnp.concatenate([-sines, sines], axis=1), (1, 2)))


def local(
    inputs,
    lengths,
    query_weight,
    key_value_weight,
    output_weight,
    inner_weight,
    down_weight,
    mixer_gain,
    query_gain,
    key_gain,
    dense_gain,
    cotangent,
):
    size, seqs, width = inputs.shape
    parts = lax.axis_size("tensor")
    full = size * parts
    head = query_gain.shape[0]
    query_cols = query_weight.shape[1]
    pair_cols = key_value_weight.shape[2]
    hidden = inner_weight.shape[2]
    shard = query_weight.shape[0]
    me_t, me_d = lax.axis_index("tensor"), lax.axis_index("dp")
    n_c = 3
    cols = hidden // n_c
    cosines, sines = tables(full, head)
    gq = jnp.tile(query_gain, 2)[None, :]
    gk = jnp.tile(key_gain, 2)[None, :]

    down_turned = down_weight.T
    attn_shard = jnp.concatenate(
        [query_weight, key_value_weight.reshape(shard, 2 * pair_cols), output_weight.T], axis=1
    )
    attn_w = gather_shards(attn_shard)
    positions = me_t * size + jnp.arange(size, dtype=jnp.int32)
    scals = [
        jnp.stack([me_t.astype(jnp.int32), me_d.astype(jnp.int32), lengths[s], jnp.int32(0)])
        for s in range(seqs)
    ]
    tokens = [inputs[:, s].astype(F32) for s in range(seqs)]
    valid = [(positions < lengths[s])[:, None] for s in range(seqs)]
    firsts = [norm_rows(tokens[s], mixer_gain) for s in range(seqs)]
    normed = [gather_tokens(firsts[s][0].astype(BF16)) for s in range(seqs)]
    ff_w = []
    for c in range(n_c):
        part = slice(c * cols, (c + 1) * cols)
        ff_w.append(
            gather_shards(
                jnp.concatenate(
                    [inner_weight[:, 0, part], inner_weight[:, 1, part], down_turned[:, part]], axis=1
                )
            )
        )
    upstream = [jnp.where(valid[s], cotangent[:, s].astype(F32), 0.0) for s in range(seqs)]
    up_parts = [gather_tokens(upstream[s].astype(BF16)) for s in range(seqs)]

    saved, residual, seconds, dense = [], [], [], []
    for s in range(seqs):
        outs = attn_fwd(scals[s], cosines, sines, gq, gk, normed[s], attn_w)
        saved.append(outs[:6])
        residual.append(tokens[s] + scatter_tokens(outs[6], outs[7]))
        dense_in, factor = norm_rows(residual[s], dense_gain)
        seconds.append(factor)
        dense.append(gather_tokens(dense_in.astype(BF16)))

    x_parts = [part for s in range(seqs) for part in dense[s]]
    u_parts = [part for s in range(seqs) for part in up_parts[s]]
    hids, ggus, ff_grads = [], [], []
    for c in range(n_c):
        hid, ggu, grads = feed_forward(scals[0], x_parts, u_parts, ff_w[c])
        hids.append(hid)
        ggus.append(ggu)
        ff_grads.append(scatter_shards(grads))

    block_out, input_gradient, attn_grads = [], [], []
    mixer_part = dense_part = gain_part = 0.0
    for s in range(seqs):
        ykeep, ysend, gkeep, gsend = ff_out(s, scals[s], parts, size, hids, ggus, ff_w)
        grad_dense = scatter_tokens(gkeep, gsend)
        dense_part = dense_part + jnp.sum(grad_dense * residual[s] * seconds[s], axis=0)
        grad_residual = upstream[s] + norm_back(residual[s], seconds[s], dense_gain, grad_dense)
        r_parts = gather_tokens(grad_residual.astype(BF16))
        nkeep, nsend, gains, grads = attn_bwd(
            scals[s], cosines, sines, gq, gk, saved[s], normed[s], r_parts, attn_w
        )
        attn_grads.append(grads)
        gain_part = gain_part + gains
        grad_normed = scatter_tokens(nkeep, nsend)
        factor = firsts[s][1]
        mixer_part = mixer_part + jnp.sum(grad_normed * tokens[s] * factor, axis=0)
        input_gradient.append(grad_residual + norm_back(tokens[s], factor, mixer_gain, grad_normed))
        out_sum = scatter_tokens(ykeep, ysend)
        block_out.append(jnp.where(valid[s], residual[s] + out_sum, 0.0).astype(BF16))

    summed = [
        sum(part.astype(F32) for part in parts_of).astype(BF16) for parts_of in zip(*attn_grads)
    ]
    attn_grad = scatter_shards(summed)
    early = sum_everywhere(jnp.concatenate([dense_part.reshape(-1, LANES), gain_part], axis=0))
    mixer = sum_everywhere(mixer_part.reshape(-1, LANES)).reshape(-1)
    dense_rows = width // LANES
    folded = early[dense_rows:, :head] + early[dense_rows:, head:]
    inner_gradient = jnp.stack(
        [
            jnp.concatenate([grad[:, p * cols : (p + 1) * cols] for grad in ff_grads], axis=1)
            for p in range(2)
        ],
        axis=1,
    )
    down_gradient = jnp.concatenate([grad[:, 2 * cols :] for grad in ff_grads], axis=1).T
    return (
        jnp.stack(block_out, axis=1),
        jnp.stack(input_gradient, axis=1),
        attn_grad[:, :query_cols],
        attn_grad[:, query_cols : query_cols + 2 * pair_cols].reshape(shard, 2, pair_cols),
        attn_grad[:, query_cols + 2 * pair_cols :].T,
        inner_gradient,
        down_gradient,
        mixer,
        folded[0],
        folded[1],
        early[:dense_rows].reshape(-1),
    )


def solution(mesh):
    return jax.shard_map(
        local,
        mesh=mesh,
        in_specs=(
            P("tensor", "dp", None),
            P("dp"),
            P("dp", "tensor"),
            P("dp", None, "tensor"),
            P("tensor", "dp"),
            P("dp", None, "tensor"),
            P("tensor", "dp"),
            P(),
            P(),
            P(),
            P(),
            P("tensor", "dp", None),
        ),
        out_specs=(
            P("tensor", "dp", None),
            P("tensor", "dp", None),
            P("dp", "tensor"),
            P("dp", None, "tensor"),
            P("tensor", "dp"),
            P("dp", None, "tensor"),
            P("tensor", "dp"),
            P(),
            P(),
            P(),
            P(),
        ),
        check_vma=False,
    )
```

```python
import functools

import jax
import jax.numpy as jnp
import numpy as np
from jax import lax
from jax.experimental import pallas as pl
from jax.experimental.pallas import tpu as pltpu
from jax.sharding import PartitionSpec as P

EPS = 1e-05
THETA = 1000000.0
LOG2E = 1.4426950408889634
F32 = jnp.float32
BF16 = jnp.bfloat16
HIGH = lax.Precision.HIGHEST
LANES = 128
VMEM_LIMIT = 56 * 1024 * 1024
ANY = pl.BlockSpec(memory_space=pl.ANY)
VMEM = pl.BlockSpec(memory_space=pltpu.VMEM)
SMEM = pl.BlockSpec(memory_space=pltpu.SMEM)


def dot(a, b, **kw):
    return lax.dot_general(
        a, b, (((1,), (0,)), ((), ())), preferred_element_type=F32, **kw
    )


def dot_nt(a, b, **kw):
    return lax.dot_general(
        a, b, (((1,), (1,)), ((), ())), preferred_element_type=F32, **kw
    )


def dot_tn(a, b, **kw):
    return lax.dot_general(
        a, b, (((0,), (0,)), ((), ())), preferred_element_type=F32, **kw
    )


def iota(shape, axis):
    return lax.broadcasted_iota(jnp.int32, shape, axis)


def low_half(shape):
    return iota(shape, 1) % LANES < LANES // 2


def head_blocks(scale):
    shape = (LANES, LANES)
    return jnp.where(iota(shape, 0) // 64 == iota(shape, 1) // 64, scale, 0.0).astype(F32)


def partner(values):
    first = iota(values.shape, 1) % 64 < 32
    return jnp.where(first, pltpu.roll(values, LANES - 32, 1), pltpu.roll(values, 32, 1))


def rows_of(index, size):
    return pl.ds(pl.multiple_of(index * size, size), size)


def load_all(sources, targets, sems, first):
    copies = []
    for number, (source, target) in enumerate(zip(sources, targets)):
        copy = pltpu.make_async_copy(source, target, sems.at[first + number])
        copy.start()
        copies.append(copy)
    return copies


def shard_targets(w_refs, ws, me):
    size = w_refs[0].shape[0]
    if len(w_refs) == 1:
        return [ws]
    return [ws.at[rows_of(me ^ slot, size)] for slot in range(len(w_refs))]


def store_slots(whole, out_refs, me):
    if len(out_refs) == 1:
        out_refs[0][...] = whole[...]
        return
    keep_ref, send_ref = out_refs
    size = keep_ref.shape[1]
    for slot in range(2 * keep_ref.shape[0]):
        (send_ref if slot % 2 else keep_ref)[slot // 2] = whole[rows_of(me ^ slot, size), :]


def padded_heads(first, second, low, g, e):
    here = low if e == 0 else jnp.logical_not(low)
    return jnp.where(here, first if g == e else second, 0.0).astype(BF16)


def project_rows(r, size, length, xs, ws, tabs, gains, raw_ref, q_ref, k_ref, v_ref, kp, vp):
    rows = rows_of(r, size)
    cos_ref, sin_ref = tabs
    gq_ref, gk_ref = gains
    mean_of = head_blocks(1.0 / 64)
    low = low_half((size, LANES))
    projected = dot(xs[rows, :], ws[:, :512])
    raw_ref[rows, :] = projected[:, :384]
    cosines, sines = cos_ref[rows, :], sin_ref[rows, :]

    def turned(values, gain):
        mean = dot(values * values, mean_of, precision=HIGH)
        normed = values * lax.rsqrt(mean + EPS) * gain
        return normed * cosines + partner(normed) * sines

    for g in range(2):
        lanes = slice(LANES * g, LANES * (g + 1))
        q_ref[rows, lanes] = turned(projected[:, lanes], gq_ref[...]).astype(BF16)
    keys = turned(projected[:, 256:384], gk_ref[...])
    values = projected[:, 384:512]
    k_ref[rows, :] = keys.astype(BF16)
    v_ref[rows, :] = values.astype(BF16)
    live = r * size + iota((size, LANES), 0) < length
    ones = jnp.where(live, 1.0, 0.0)
    values = jnp.where(live, values, 0.0)
    keys_swap, values_swap = pltpu.roll(keys, 64, 1), pltpu.roll(values, 64, 1)
    for g in range(2):
        for e in range(2):
            kp[2 * g + e, rows, :] = padded_heads(keys, keys_swap, low, g, e)
            vp[2 * g + e, rows, :LANES] = padded_heads(values, values_swap, low, g, e)
            vp[2 * g + e, rows, LANES:] = padded_heads(ones, ones, low, g, e)


def attend_rows(i, size, q_ref, kp, vp, acc, att_ref, lse_ref):
    rows = rows_of(i, size)
    factor = LOG2E / 8.0
    causal = iota((size, size), 1) <= iota((size, size), 0)
    queries = [q_ref[rows, LANES * g : LANES * (g + 1)] for g in range(2)]

    def block(kb, masked):
        cols = rows_of(kb, size)
        sums = []
        for g in range(2):
            total = None
            for e in range(2):
                weights = jnp.exp2(dot_nt(queries[g], kp[2 * g + e, cols, :]) * factor)
                if masked:
                    weights = jnp.where(causal, weights, 0.0)
                part = dot(weights.astype(BF16), vp[2 * g + e, cols, :])
                total = part if total is None else total + part
            sums.append(total)
        return sums

    for g, total in enumerate(block(i, True)):
        acc[g] = total

    def more(kb, carry):
        for g, total in enumerate(block(kb, False)):
            acc[g] += total
        return carry

    lax.fori_loop(0, i, more, 0)
    for g in range(2):
        lanes = slice(LANES * g, LANES * (g + 1))
        summed = acc[g, :, LANES:]
        att_ref[rows, lanes] = (acc[g, :, :LANES] / summed).astype(BF16)
        lse_ref[rows, lanes] = jnp.log2(summed)


def attn_fwd_kernel(parts, n_w, scal, cos_ref, sin_ref, gq_ref, gk_ref, *refs):
    x_refs, refs = refs[:parts], refs[parts:]
    w_refs, refs = refs[:n_w], refs[n_w:]
    (raw_ref, q_ref, k_ref, v_ref, att_ref, lse_ref, keep_ref, send_ref, xs, ws, kp, vp, acc, sems) = refs
    size = x_refs[0].shape[0]
    me_t, me_d, length = scal[0], scal[1], scal[2]
    copies = load_all(w_refs, shard_targets(w_refs, ws, me_d), sems, 0)
    copies += load_all(x_refs, [xs.at[rows_of(me_t ^ j, size)] for j in range(parts)], sems, n_w)
    for copy in copies:
        copy.wait()

    def project(r, carry):
        project_rows(
            r, size, length, xs, ws, (cos_ref, sin_ref), (gq_ref, gk_ref), raw_ref, q_ref, k_ref, v_ref, kp, vp
        )
        return carry

    def attend(i, carry):
        attend_rows(i, size, q_ref, kp, vp, acc, att_ref, lse_ref)
        return carry

    lax.fori_loop(0, parts, project, 0)
    lax.fori_loop(0, parts, attend, 0)
    for j in range(parts):
        out = dot_nt(att_ref[rows_of(me_t ^ j, size), :], ws[:, 512:])
        (send_ref if j % 2 else keep_ref)[j // 2] = out.astype(BF16)


def attn_fwd(scal, cosines, sines, gq, gk, x_parts, w_parts):
    parts, n_w = len(x_parts), len(w_parts)
    size, width = x_parts[0].shape
    full = parts * size
    cols = w_parts[0].shape[1]
    pair = jax.ShapeDtypeStruct((parts // 2, size, width), BF16)
    return pl.pallas_call(
        functools.partial(attn_fwd_kernel, parts, n_w),
        out_shape=(
            jax.ShapeDtypeStruct((full, 384), F32),
            jax.ShapeDtypeStruct((full, 256), BF16),
            jax.ShapeDtypeStruct((full, 128), BF16),
            jax.ShapeDtypeStruct((full, 128), BF16),
            jax.ShapeDtypeStruct((full, 256), BF16),
            jax.ShapeDtypeStruct((full, 256), F32),
            pair,
            pair,
        ),
        in_specs=[SMEM] + [VMEM] * 4 + [ANY] * (parts + n_w),
        out_specs=(VMEM,) * 8,
        scratch_shapes=[
            pltpu.VMEM((full, width), BF16),
            pltpu.VMEM((width, cols), BF16),
            pltpu.VMEM((4, full, LANES), BF16),
            pltpu.VMEM((4, full, 2 * LANES), BF16),
            pltpu.VMEM((2, size, 2 * LANES), F32),
            pltpu.SemaphoreType.DMA((n_w + parts,)),
        ],
        compiler_params=pltpu.CompilerParams(vmem_limit_bytes=VMEM_LIMIT),
        cost_estimate=pl.CostEstimate(flops=8_000_000_000, bytes_accessed=12_000_000, transcendentals=3_000_000),
        name="attention_forward",
    )(scal, cosines, sines, gq, gk, *x_parts, *w_parts)


def attn_bwd_kernel(parts, n_w, scal, cos_ref, sin_ref, gq_ref, gk_ref, raw_ref, q_ref, k_ref, v_ref, att_ref, lse_ref, *refs):
    x_refs, refs = refs[:parts], refs[parts:]
    r_refs, refs = refs[:parts], refs[parts:]
    w_refs, refs = refs[:n_w], refs[n_w:]
    n_g = 1 if n_w == 1 else 2
    keep_ref, send_ref, gains_ref = refs[:3]
    g_refs, refs = refs[3 : 3 + n_g], refs[3 + n_g :]
    xs, gs, ws, kp, vp, kt, ga, dq, dk, dv, gp, whole, lrow, drow, acc, sems = refs
    size = x_refs[0].shape[0]
    full = parts * size
    me_t, me_d, length = scal[0], scal[1], scal[2]
    copies = load_all(w_refs, shard_targets(w_refs, ws, me_d), sems, 0)
    copies += load_all(r_refs, [gs.at[rows_of(me_t ^ j, size)] for j in range(parts)], sems, n_w)
    copies += load_all(x_refs, [xs.at[rows_of(me_t ^ j, size)] for j in range(parts)], sems, n_w + parts)
    for copy in copies:
        copy.wait()
    mean_of = head_blocks(1.0 / 64)
    low = low_half((size, LANES))
    factor = LOG2E / 8.0
    pick = jnp.where(iota((8, 256), 0) == iota((8, 256), 1) // 64, 1.0, 0.0).astype(F32)

    def prepare(r, carry):
        rows = rows_of(r, size)
        grad = dot(gs[rows, :], ws[:, 512:]).astype(BF16)
        ga[rows, :] = grad
        drow[:, rows] = dot_nt(pick, grad.astype(F32) * att_ref[rows, :].astype(F32), precision=HIGH)
        lrow[:, rows] = dot_nt(pick * (1.0 / 64), lse_ref[rows, :], precision=HIGH)
        live = r * size + iota((size, LANES), 0) < length
        keys = jnp.where(live, k_ref[rows, :].astype(F32), 0.0)
        values = jnp.where(live, v_ref[rows, :].astype(F32), 0.0)
        keys_swap, values_swap = pltpu.roll(keys, 64, 1), pltpu.roll(values, 64, 1)
        for g in range(2):
            for e in range(2):
                here = low if e == 0 else jnp.logical_not(low)
                padded = jnp.where(here, keys if g == e else keys_swap, 0.0)
                kp[2 * g + e, rows, :] = padded.astype(BF16)
                kt[2 * g + e, :, rows] = padded.T.astype(BF16)
                vp[2 * g + e, rows, :] = jnp.where(here, values if g == e else values_swap, 0.0).astype(BF16)
        return carry

    lax.fori_loop(0, parts, prepare, 0)
    dk[...] = jnp.zeros_like(dk)
    dv[...] = jnp.zeros_like(dv)
    causal = iota((size, size), 0) <= iota((size, size), 1)
    low2 = iota((2 * size, LANES), 0) // size == iota((2 * size, LANES), 1) // 64

    def sweep(i, carry):
        rows = rows_of(i, size)
        queries, grads, queries2, grads2 = [], [], [], []
        for g in range(2):
            lanes = slice(LANES * g, LANES * (g + 1))
            queries.append(q_ref[rows, lanes])
            grads.append(ga[rows, lanes])
            for source, target in ((queries, queries2), (grads, grads2)):
                both = jnp.concatenate([source[g], source[g]], axis=0)
                target.append(jnp.where(low2, both, jnp.zeros_like(both)))

        def block(kb, masked):
            cols = rows_of(kb, size)
            parts_t = []
            for g in range(2):
                weights2, scores2, turned = [], [], None
                for e in range(2):
                    h = 2 * g + e
                    weights = jnp.exp2(dot_nt(kp[h, cols, :], queries[g]) * factor - lrow[h : h + 1, rows])
                    if masked:
                        weights = jnp.where(causal, weights, 0.0)
                    grad_weights = dot_nt(vp[h, cols, :], grads[g])
                    grad_scores = (weights * (grad_weights - drow[h : h + 1, rows])).astype(BF16)
                    weights2.append(weights.astype(BF16))
                    scores2.append(grad_scores)
                    part = dot(kt[h, :, cols], grad_scores)
                    turned = part if turned is None else turned + part
                dv[g, cols, :] += dot(jnp.concatenate(weights2, axis=1), grads2[g])
                dk[g, cols, :] += dot(jnp.concatenate(scores2, axis=1), queries2[g])
                parts_t.append(turned)
            return parts_t

        for g, total in enumerate(block(i, True)):
            acc[g] = total

        def more(kb, carry):
            for g, total in enumerate(block(kb, False)):
                acc[g] += total
            return carry

        lax.fori_loop(0, i, more, 0)
        for g in range(2):
            dq[rows, LANES * g : LANES * (g + 1)] = acc[g].T
        return carry

    lax.fori_loop(0, parts, sweep, 0)
    gains_ref[...] = jnp.zeros_like(gains_ref)

    def project(r, carry):
        rows = rows_of(r, size)
        cosines, sines = cos_ref[rows, :], sin_ref[rows, :]
        live = r * size + iota((size, LANES), 0) < length

        def back(grad, lanes, gain, row):
            raw = raw_ref[rows, lanes]
            rms = lax.rsqrt(dot(raw * raw, mean_of, precision=HIGH) + EPS)
            turned = grad * cosines - partner(grad) * sines
            gains_ref[row : row + 1, :] += jnp.sum(turned * raw * rms, axis=0, keepdims=True)
            weighted = turned * gain
            inner = dot(raw * weighted, mean_of, precision=HIGH)
            gp[rows, lanes] = (rms * weighted - raw * (rms * rms * rms) * inner).astype(BF16)

        def folded(ref):
            first, second = ref[0, rows, :], ref[1, rows, :]
            both = jnp.where(low, first + pltpu.roll(first, 64, 1), second + pltpu.roll(second, 64, 1))
            return jnp.where(live, both, 0.0)

        for g in range(2):
            lanes = slice(LANES * g, LANES * (g + 1))
            back(dq[rows, lanes] * 0.125, lanes, gq_ref[...], 0)
        back(folded(dk) * 0.125, slice(256, 384), gk_ref[...], 1)
        gp[rows, 384:512] = folded(dv).astype(BF16)
        return carry

    lax.fori_loop(0, parts, project, 0)
    for j in range(parts):
        out = dot_nt(gp[rows_of(me_t ^ j, size), :], ws[:, :512])
        (send_ref if j % 2 else keep_ref)[j // 2] = out.astype(BF16)

    def weigh(b, carry):
        rows = rows_of(b, 256)
        whole[rows, :512] = dot_tn(xs[:, rows], gp[...]).astype(BF16)
        whole[rows, 512:] = dot_tn(gs[:, rows], att_ref[...]).astype(BF16)
        return carry

    lax.fori_loop(0, whole.shape[0] // 256, weigh, 0)
    store_slots(whole, g_refs, me_d)


def slot_shapes(n_w, width, cols):
    if n_w == 1:
        return (jax.ShapeDtypeStruct((width, cols), BF16),)
    return (jax.ShapeDtypeStruct((n_w // 2, width // n_w, cols), BF16),) * 2


def attn_bwd(scal, cosines, sines, gq, gk, saved, x_parts, r_parts, w_parts):
    parts, n_w = len(x_parts), len(w_parts)
    size, width = x_parts[0].shape
    full = parts * size
    cols = w_parts[0].shape[1]
    pair = jax.ShapeDtypeStruct((parts // 2, size, width), BF16)
    g_shapes = slot_shapes(n_w, width, cols)
    outs = pl.pallas_call(
        functools.partial(attn_bwd_kernel, parts, n_w),
        out_shape=(pair, pair, jax.ShapeDtypeStruct((8, LANES), F32)) + g_shapes,
        in_specs=[SMEM] + [VMEM] * 10 + [ANY] * (2 * parts + n_w),
        out_specs=(VMEM,) * (3 + len(g_shapes)),
        scratch_shapes=[
            pltpu.VMEM((full, width), BF16),
            pltpu.VMEM((full, width), BF16),
            pltpu.VMEM((width, cols), BF16),
            pltpu.VMEM((4, full, LANES), BF16),
            pltpu.VMEM((4, full, LANES), BF16),
            pltpu.VMEM((4, LANES, full), BF16),
            pltpu.VMEM((full, 256), BF16),
            pltpu.VMEM((full, 256), F32),
            pltpu.VMEM((2, full, LANES), F32),
            pltpu.VMEM((2, full, LANES), F32),
            pltpu.VMEM((full, 512), BF16),
            pltpu.VMEM((width, cols), BF16),
            pltpu.VMEM((8, full), F32),
            pltpu.VMEM((8, full), F32),
            pltpu.VMEM((2, LANES, size), F32),
            pltpu.SemaphoreType.DMA((n_w + 2 * parts,)),
        ],
        compiler_params=pltpu.CompilerParams(vmem_limit_bytes=VMEM_LIMIT),
        cost_estimate=pl.CostEstimate(flops=14_000_000_000, bytes_accessed=15_000_000, transcendentals=3_000_000),
        name="attention_backward",
    )(scal, cosines, sines, gq, gk, *saved, *x_parts, *r_parts, *w_parts)
    return outs[0], outs[1], outs[2], outs[3:]


def ff_kernel(n_x, n_w, scal, *refs):
    x_refs, refs = refs[:n_x], refs[n_x:]
    u_refs, refs = refs[:n_x], refs[n_x:]
    w_refs, refs = refs[:n_w], refs[n_w:]
    n_g = 1 if n_w == 1 else 2
    hid_ref, ggu_ref = refs[:2]
    g_refs, refs = refs[2 : 2 + n_g], refs[2 + n_g :]
    xs, us, ws, whole, sems = refs
    size = x_refs[0].shape[0]
    me_d = scal[1]
    cols = ws.shape[1] // 3
    copies = load_all(w_refs, shard_targets(w_refs, ws, me_d), sems, 0)
    x_copies = load_all(x_refs, [xs.at[pl.ds(j * size, size)] for j in range(n_x)], sems, n_w)
    u_copies = load_all(u_refs, [us.at[pl.ds(j * size, size)] for j in range(n_x)], sems, n_w + n_x)
    for copy in copies + x_copies + u_copies:
        copy.wait()

    def tokens(r, carry):
        rows = rows_of(r, size)
        gate_up = dot(xs[rows, :], ws[:, : 2 * cols])
        grad = dot(us[rows, :], ws[:, 2 * cols :])
        gate, up = gate_up[:, :cols], gate_up[:, cols:]
        sig = 1.0 / (1.0 + jnp.exp2(gate * -LOG2E))
        silu = gate * sig
        hid_ref[rows, :] = (silu * up).astype(BF16)
        ggu_ref[rows, :cols] = (grad * up * (sig + silu * (1.0 - sig))).astype(BF16)
        ggu_ref[rows, cols:] = (grad * silu).astype(BF16)
        return carry

    lax.fori_loop(0, n_x, tokens, 0)

    def weigh(b, carry):
        rows = rows_of(b, 256)
        whole[rows, : 2 * cols] = dot_tn(xs[:, rows], ggu_ref[...]).astype(BF16)
        whole[rows, 2 * cols :] = dot_tn(us[:, rows], hid_ref[...]).astype(BF16)
        return carry

    lax.fori_loop(0, whole.shape[0] // 256, weigh, 0)
    store_slots(whole, g_refs, me_d)


def feed_forward(scal, x_parts, u_parts, w_parts):
    n_x, n_w = len(x_parts), len(w_parts)
    size, width = x_parts[0].shape
    full = n_x * size
    wide = w_parts[0].shape[1]
    cols = wide // 3
    g_shapes = slot_shapes(n_w, width, wide)
    outs = pl.pallas_call(
        functools.partial(ff_kernel, n_x, n_w),
        out_shape=(
            jax.ShapeDtypeStruct((full, cols), BF16),
            jax.ShapeDtypeStruct((full, 2 * cols), BF16),
        )
        + g_shapes,
        in_specs=[SMEM] + [ANY] * (2 * n_x + n_w),
        out_specs=(VMEM,) * (2 + len(g_shapes)),
        scratch_shapes=[
            pltpu.VMEM((full, width), BF16),
            pltpu.VMEM((full, width), BF16),
            pltpu.VMEM((width, wide), BF16),
            pltpu.VMEM((width, wide), BF16),
            pltpu.SemaphoreType.DMA((n_w + 2 * n_x,)),
        ],
        compiler_params=pltpu.CompilerParams(vmem_limit_bytes=VMEM_LIMIT),
        cost_estimate=pl.CostEstimate(flops=4 * full * width * wide, bytes_accessed=20_000_000, transcendentals=full * cols),
        name="feed_forward",
    )(scal, *x_parts, *u_parts, *w_parts)
    return outs[0], outs[1], outs[2:]


def ff_out_kernel(parts, n_c, n_w, seq, scal, *refs):
    hid_refs, refs = refs[:n_c], refs[n_c:]
    ggu_refs, refs = refs[:n_c], refs[n_c:]
    w_refs, refs = refs[: n_c * n_w], refs[n_c * n_w :]
    ykeep_ref, ysend_ref, gkeep_ref, gsend_ref, hs, gs, ws, sems = refs
    size = ykeep_ref.shape[1]
    full = parts * size
    me_d = scal[1]
    wide = ws.shape[2]
    cols = wide // 3
    copies = []
    first = 0
    for c in range(n_c):
        targets = shard_targets(w_refs[c * n_w : (c + 1) * n_w], ws.at[c], me_d)
        copies += load_all(w_refs[c * n_w : (c + 1) * n_w], targets, sems, first)
        first += n_w
    mine = pl.ds(seq * full, full)
    copies += load_all([ref.at[mine] for ref in ggu_refs], [gs.at[c] for c in range(n_c)], sems, first)
    copies += load_all([ref.at[mine] for ref in hid_refs], [hs.at[c] for c in range(n_c)], sems, first + n_c)
    for copy in copies:
        copy.wait()
    for j in range(parts):
        rows = pl.ds(j * size, size)
        grad = sum(dot_nt(gs[c, rows, :], ws[c, :, : 2 * cols]) for c in range(n_c))
        (gsend_ref if j % 2 else gkeep_ref)[j // 2] = grad.astype(BF16)
        out = sum(dot_nt(hs[c, rows, :], ws[c, :, 2 * cols :]) for c in range(n_c))
        (ysend_ref if j % 2 else ykeep_ref)[j // 2] = out.astype(BF16)


def ff_out(seq, scal, parts, size, hids, ggus, w_chunks):
    n_c, n_w = len(w_chunks), len(w_chunks[0])
    wide = w_chunks[0][0].shape[1]
    width = w_chunks[0][0].shape[0] * n_w
    full = parts * size
    cols = wide // 3
    pair = jax.ShapeDtypeStruct((parts // 2, size, width), BF16)
    return pl.pallas_call(
        functools.partial(ff_out_kernel, parts, n_c, n_w, seq),
        out_shape=(pair,) * 4,
        in_specs=[SMEM] + [ANY] * (2 * n_c + n_c * n_w),
        out_specs=(VMEM,) * 4,
        scratch_shapes=[
            pltpu.VMEM((n_c, full, cols), BF16),
            pltpu.VMEM((n_c, full, 2 * cols), BF16),
            pltpu.VMEM((n_c, width, wide), BF16),
            pltpu.SemaphoreType.DMA((n_c * n_w + 2 * n_c,)),
        ],
        compiler_params=pltpu.CompilerParams(vmem_limit_bytes=VMEM_LIMIT),
        cost_estimate=pl.CostEstimate(flops=2 * full * width * wide * n_c, bytes_accessed=22_000_000, transcendentals=0),
        name="feed_forward_out",
    )(scal, *hids, *ggus, *[shard for chunk in w_chunks for shard in chunk])


def flip(index, bits):
    for bit in (1, 2, 4):
        if bits & bit:
            index = index + bit - 2 * bit * lax.rem(lax.div(index, bit), 2)
    return index


def enter(me_d, me_t):
    barrier = pltpu.get_barrier_semaphore()
    devices = [{"dp": flip(me_d, bits)} for bits in (1, 2, 4, 6)]
    devices += [{"tensor": flip(me_t, bits)} for bits in (1, 2)]
    for device in devices:
        pl.semaphore_signal(barrier, inc=1, device_id=device, device_id_type=pl.DeviceIdType.MESH)
    return lambda: pl.semaphore_wait(barrier, len(devices))


def remote(source, target, sems, number, device):
    return pltpu.make_async_remote_copy(
        src_ref=source,
        dst_ref=target,
        send_sem=sems.at[0, number],
        recv_sem=sems.at[1, number],
        device_id=device,
        device_id_type=pl.DeviceIdType.MESH,
    )


class ShardGather:
    COPIES = 7

    def __init__(self, shard, whole, sems, first, me_d):
        size = shard.shape[0]
        mine = whole.at[rows_of(me_d, size)]
        beside = {"dp": flip(me_d, 1)}
        self.own = [
            remote(shard, mine, sems, first + n, {"dp": flip(me_d, bits)})
            for n, bits in enumerate((1, 2, 4, 6))
        ]
        self.passed = []
        for n, bits in enumerate((2, 4, 6)):
            there = whole.at[rows_of(flip(me_d, bits), size)]
            self.passed.append(remote(there, there, sems, first + 4 + n, beside))

    def start(self):
        for copy in self.own:
            copy.start()

    def forward(self):
        for come, onward in zip(self.own[1:], self.passed):
            come.wait_recv()
            onward.start()

    def arrive(self):
        self.own[0].wait_recv()
        for copy in self.passed:
            copy.wait_recv()

    def drain(self):
        for copy in self.own + self.passed:
            copy.wait_send()


class TokenGather:
    COPIES = 3

    def __init__(self, block, whole, sems, first, me_t):
        size = block.shape[0]
        mine = whole.at[rows_of(me_t, size)]
        there = whole.at[rows_of(flip(me_t, 2), size)]
        near = {"tensor": flip(me_t, 1)}
        self.near = remote(block, mine, sems, first, near)
        self.far = remote(block, mine, sems, first + 1, {"tensor": flip(me_t, 2)})
        self.passed = remote(there, there, sems, first + 2, near)

    def start(self):
        self.far.start()
        self.near.start()

    def forward(self):
        self.far.wait_recv()
        self.passed.start()

    def arrive(self):
        self.near.wait_recv()
        self.passed.wait_recv()

    def drain(self):
        for copy in (self.near, self.far, self.passed):
            copy.wait_send()


class TokenReduce:
    COPIES = 3

    def __init__(self, blocks, near, far, sems, first, me_t):
        device = {"tensor": flip(me_t, 1)}
        self.blocks, self.near_ref, self.far_ref = blocks, near, far
        self.me = me_t
        self.across = flip(me_t, 2)
        self.near = [
            remote(blocks.at[flip(me_t, 1 + 2 * n)], near.at[n], sems, first + n, device) for n in range(2)
        ]
        self.far = remote(near.at[1], far, sems, first + 2, {"tensor": flip(me_t, 2)})

    def start(self, n):
        self.near[n].start()

    def middle(self):
        self.near[1].wait_recv()

        def step(b, carry):
            rows = rows_of(b, 32)
            total = self.blocks[self.across, rows, :].astype(F32) + self.near_ref[1, rows, :].astype(F32)
            self.near_ref[1, rows, :] = total.astype(BF16)
            return carry

        lax.fori_loop(0, self.near_ref.shape[1] // 32, step, 0)
        self.far.start()

    def arrive(self):
        self.near[0].wait_recv()
        self.far.wait_recv()

    def rows(self, rows):
        total = self.blocks[self.me, rows, :].astype(F32) + self.near_ref[0, rows, :].astype(F32)
        return total + self.far_ref[rows, :].astype(F32)

    def drain(self):
        for copy in self.near + [self.far]:
            copy.wait_send()


def by_rows(count, step, body):
    def run(b, carry):
        body(rows_of(b, step))
        return carry

    lax.fori_loop(0, count // step, run, 0)


def rms_factor(values):
    return lax.rsqrt(jnp.mean(values * values, axis=-1, keepdims=True) + EPS)


def forward_kernel(
    lengths, x_ref, aw_ref, up_ref, fw_ref, cos_ref, sin_ref, gq_ref, gk_ref, mg_ref, dg_ref,
    aw_out, fw_out, normed_out, up_out, dense_out, resid_ref, raw_ref, q_ref, k_ref, v_ref, att_ref, lse_ref,
    xs, ws, kp, vp, acc, outp, near, far, dense, sems, local_sems,
):
    seqs, size, width = resid_ref.shape
    parts = xs.shape[1] // size
    n_c = fw_ref.shape[0]
    me_t, me_d = lax.axis_index("tensor"), lax.axis_index("dp")
    entered = enter(me_d, me_t)
    mine_t, mine_d = rows_of(me_t, size), rows_of(me_d, aw_ref.shape[0])

    first = 0
    attn_w = ShardGather(aw_ref, ws, sems, first, me_d)
    first += ShardGather.COPIES
    ff_w = []
    for c in range(n_c):
        ff_w.append(ShardGather(fw_ref.at[c], fw_out.at[c], sems, first, me_d))
        first += ShardGather.COPIES
    normed, ups, denses, outs = [], [], [], []
    for s in range(seqs):
        normed.append(TokenGather(xs.at[s, mine_t], xs.at[s], sems, first, me_t))
        ups.append(TokenGather(up_ref.at[s], up_out.at[s], sems, first + 3, me_t))
        denses.append(TokenGather(dense.at[s], dense_out.at[s], sems, first + 6, me_t))
        outs.append(TokenReduce(outp.at[s], near.at[s], far.at[s], sems, first + 9, me_t))
        first += 12

    def here(source, target, number):
        copy = pltpu.make_async_copy(source, target, local_sems.at[number])
        copy.start()
        return copy

    mine = here(aw_ref, ws.at[mine_d], 0)
    stays = [here(up_ref.at[s], up_out.at[s, mine_t], 1 + s) for s in range(seqs)]
    stays += [here(fw_ref.at[c], fw_out.at[c, mine_d], 1 + seqs + c) for c in range(n_c)]
    used = 1 + seqs + n_c

    for s in range(seqs):

        def norm(rows):
            values = x_ref[rows, width * s : width * (s + 1)].astype(F32)
            target = pl.ds(pl.multiple_of(me_t * size + rows.start, 32), 32)
            xs[s, target, :] = (values * rms_factor(values) * mg_ref[...]).astype(BF16)

        by_rows(size, 32, norm)
    entered()
    normed[0].start()
    attn_w.start()
    normed[1].start()
    attn_w.forward()
    normed[0].forward()
    normed[0].arrive()
    mine.wait()
    attn_w.arrive()
    ff_w[0].start()
    stays.append(here(ws, aw_out, used))
    used += 1

    def project(s):
        def run(r, carry):
            project_rows(
                r, size, lengths[s], xs.at[s], ws, (cos_ref, sin_ref), (gq_ref, gk_ref),
                raw_ref.at[s], q_ref.at[s], k_ref.at[s], v_ref.at[s], kp, vp,
            )
            return carry

        lax.fori_loop(0, parts, run, 0)

    def attend(s, start, stop):
        def run(i, carry):
            attend_rows(i, size, q_ref.at[s], kp, vp, acc, att_ref.at[s], lse_ref.at[s])
            return carry

        lax.fori_loop(start, stop, run, 0)

    def out(s):
        for n, bits in enumerate((1, 3, 2, 0)):
            block = flip(me_t, bits)
            result = dot_nt(att_ref[s, rows_of(block, size), :], ws[:, 512:])
            outp[s, block] = result.astype(BF16)
            if n < 2:
                outs[s].start(n)

    def after(s):
        outs[s].arrive()

        def norm(rows):
            values = x_ref[rows, width * s : width * (s + 1)].astype(F32) + outs[s].rows(rows)
            resid_ref[s, rows, :] = values
            dense[s, rows, :] = (values * rms_factor(values) * dg_ref[...]).astype(BF16)

        by_rows(size, 32, norm)
        denses[s].start()
        stays.append(here(dense.at[s], dense_out.at[s, mine_t], used + s))

    project(0)
    normed[1].forward()
    for s in range(seqs):
        ups[s].start()
    attend(0, 0, 3)
    ff_w[0].forward()
    if n_c > 1:
        ff_w[1].start()
    attend(0, 3, parts)
    out(0)
    normed[1].arrive()
    for s in range(seqs):
        ups[s].forward()
    outs[0].middle()
    project(1)
    attend(1, 0, 3)
    after(0)
    attend(1, 3, parts)
    out(1)
    outs[1].middle()
    denses[0].forward()
    for c in range(1, n_c):
        ff_w[c].forward()
        if c + 1 < n_c:
            ff_w[c + 1].start()
    after(1)
    denses[1].forward()
    used += seqs
    stays += [here(xs.at[s], normed_out.at[s], used + s) for s in range(seqs)]
    for c in range(n_c):
        ff_w[c].arrive()
    for s in range(seqs):
        ups[s].arrive()
        denses[s].arrive()
    for copy in stays:
        copy.wait()
    attn_w.drain()
    for exchange in ff_w + normed + ups + denses + outs:
        exchange.drain()


def fused_forward(lengths, x, aw, up, fw, tabs, gains):
    seqs, size, width = up.shape
    parts = 4
    full = parts * size
    shard, cols = aw.shape
    n_c, _, wide = fw.shape
    dp = 8

    def shape(dims, kind):
        return jax.ShapeDtypeStruct(dims, kind)

    n_sems = ShardGather.COPIES * (1 + n_c) + 12 * seqs
    return pl.pallas_call(
        forward_kernel,
        out_shape=(
            shape((dp * shard, cols), BF16),
            shape((n_c, dp * shard, wide), BF16),
            shape((seqs, full, width), BF16),
            shape((seqs, full, width), BF16),
            shape((seqs, full, width), BF16),
            shape((seqs, size, width), F32),
            shape((seqs, full, 384), F32),
            shape((seqs, full, 256), BF16),
            shape((seqs, full, 128), BF16),
            shape((seqs, full, 128), BF16),
            shape((seqs, full, 256), BF16),
            shape((seqs, full, 256), F32),
        ),
        in_specs=[SMEM, VMEM] + [ANY] * 3 + [VMEM] * 6,
        out_specs=(ANY,) * 5 + (VMEM,) * 7,
        scratch_shapes=[
            pltpu.VMEM((seqs, full, width), BF16),
            pltpu.VMEM((dp * shard, cols), BF16),
            pltpu.VMEM((4, full, LANES), BF16),
            pltpu.VMEM((4, full, 2 * LANES), BF16),
            pltpu.VMEM((2, size, 2 * LANES), F32),
            pltpu.VMEM((seqs, parts, size, width), BF16),
            pltpu.VMEM((seqs, 2, size, width), BF16),
            pltpu.VMEM((seqs, size, width), BF16),
            pltpu.VMEM((seqs, size, width), BF16),
            pltpu.SemaphoreType.DMA((2, n_sems)),
            pltpu.SemaphoreType.DMA((2 + 3 * seqs + n_c,)),
        ],
        compiler_params=pltpu.CompilerParams(
            vmem_limit_bytes=VMEM_LIMIT, collective_id=0, has_side_effects=True
        ),
        cost_estimate=pl.CostEstimate(flops=16_000_000_000, bytes_accessed=40_000_000, transcendentals=6_000_000),
        name="forward",
    )(lengths, x, aw, up, fw, *tabs, *gains)


def swap(values, axis, bits):
    return lax.ppermute(values, axis, [(i, i ^ bits) for i in range(lax.axis_size(axis))])


def gather_tokens(block):
    far = swap(block, "tensor", 2)
    return [block, swap(block, "tensor", 1), far, swap(far, "tensor", 1)]


def scatter_tokens(keep, send):
    near = swap(send, "tensor", 1)
    middle = (keep[1].astype(F32) + near[1].astype(F32)).astype(BF16)
    far = swap(middle, "tensor", 2)
    return keep[0].astype(F32) + near[0].astype(F32) + far.astype(F32)


def gather_shards(shard):
    if lax.axis_size("dp") != 8 or shard.shape[0] % LANES:
        return [lax.all_gather(shard, "dp", axis=0, tiled=True)]
    slots = [shard, swap(shard, "dp", 1)]
    for bits in (2, 4, 6):
        there = swap(shard, "dp", bits)
        slots += [there, swap(there, "dp", 1)]
    return slots


def scatter_shards(grads):
    if len(grads) == 1:
        return lax.psum_scatter(grads[0].astype(F32), "dp", scatter_dimension=0, tiled=True)
    keep, send = grads
    near = swap(send, "dp", 1)
    both = keep.astype(F32) + near.astype(F32)
    total = both[0]
    for slot in (1, 2, 3):
        total = total + swap(both[slot].astype(BF16), "dp", 2 * slot).astype(F32)
    return total


def sum_everywhere(values):
    for axis in ("tensor", "dp"):
        bits = 1
        while bits < lax.axis_size(axis):
            values = values + swap(values, axis, bits)
            bits *= 2
    return values


def norm_rows(values, gain):
    factor = lax.rsqrt(jnp.mean(values * values, axis=-1, keepdims=True) + EPS)
    return (values * factor * gain, factor)


def norm_back(values, factor, gain, upstream):
    weighted = upstream * gain
    inner = jnp.mean(values * weighted, axis=-1, keepdims=True)
    return factor * weighted - values * factor * factor * factor * inner


def tables(full, head_width):
    half = head_width // 2
    freqs = THETA ** (-jnp.arange(half, dtype=F32) * 2.0 / head_width)
    angles = jnp.arange(full, dtype=F32)[:, None] * freqs[None, :]
    cosines, sines = jnp.cos(angles), jnp.sin(angles)
    return (jnp.tile(cosines, (1, 4)), jnp.tile(jnp.concatenate([-sines, sines], axis=1), (1, 2)))


def local_plain(
    inputs,
    lengths,
    query_weight,
    key_value_weight,
    output_weight,
    inner_weight,
    down_weight,
    mixer_gain,
    query_gain,
    key_gain,
    dense_gain,
    cotangent,
):
    size, seqs, width = inputs.shape
    parts = lax.axis_size("tensor")
    full = size * parts
    head = query_gain.shape[0]
    query_cols = query_weight.shape[1]
    pair_cols = key_value_weight.shape[2]
    hidden = inner_weight.shape[2]
    shard = query_weight.shape[0]
    me_t, me_d = lax.axis_index("tensor"), lax.axis_index("dp")
    n_c = 3
    cols = hidden // n_c
    cosines, sines = tables(full, head)
    gq = jnp.tile(query_gain, 2)[None, :]
    gk = jnp.tile(key_gain, 2)[None, :]

    down_turned = down_weight.T
    attn_shard = jnp.concatenate(
        [query_weight, key_value_weight.reshape(shard, 2 * pair_cols), output_weight.T], axis=1
    )
    attn_w = gather_shards(attn_shard)
    positions = me_t * size + jnp.arange(size, dtype=jnp.int32)
    scals = [
        jnp.stack([me_t.astype(jnp.int32), me_d.astype(jnp.int32), lengths[s], jnp.int32(0)])
        for s in range(seqs)
    ]
    tokens = [inputs[:, s].astype(F32) for s in range(seqs)]
    valid = [(positions < lengths[s])[:, None] for s in range(seqs)]
    firsts = [norm_rows(tokens[s], mixer_gain) for s in range(seqs)]
    normed = [gather_tokens(firsts[s][0].astype(BF16)) for s in range(seqs)]
    ff_w = []
    for c in range(n_c):
        part = slice(c * cols, (c + 1) * cols)
        ff_w.append(
            gather_shards(
                jnp.concatenate(
                    [inner_weight[:, 0, part], inner_weight[:, 1, part], down_turned[:, part]], axis=1
                )
            )
        )
    upstream = [jnp.where(valid[s], cotangent[:, s].astype(F32), 0.0) for s in range(seqs)]
    up_parts = [gather_tokens(upstream[s].astype(BF16)) for s in range(seqs)]

    saved, residual, seconds, dense = [], [], [], []
    for s in range(seqs):
        outs = attn_fwd(scals[s], cosines, sines, gq, gk, normed[s], attn_w)
        saved.append(outs[:6])
        residual.append(tokens[s] + scatter_tokens(outs[6], outs[7]))
        dense_in, factor = norm_rows(residual[s], dense_gain)
        seconds.append(factor)
        dense.append(gather_tokens(dense_in.astype(BF16)))

    x_parts = [part for s in range(seqs) for part in dense[s]]
    u_parts = [part for s in range(seqs) for part in up_parts[s]]
    hids, ggus, ff_grads = [], [], []
    for c in range(n_c):
        hid, ggu, grads = feed_forward(scals[0], x_parts, u_parts, ff_w[c])
        hids.append(hid)
        ggus.append(ggu)
        ff_grads.append(scatter_shards(grads))

    block_out, input_gradient, attn_grads = [], [], []
    mixer_part = dense_part = gain_part = 0.0
    for s in range(seqs):
        ykeep, ysend, gkeep, gsend = ff_out(s, scals[s], parts, size, hids, ggus, ff_w)
        grad_dense = scatter_tokens(gkeep, gsend)
        dense_part = dense_part + jnp.sum(grad_dense * residual[s] * seconds[s], axis=0)
        grad_residual = upstream[s] + norm_back(residual[s], seconds[s], dense_gain, grad_dense)
        r_parts = gather_tokens(grad_residual.astype(BF16))
        nkeep, nsend, gains, grads = attn_bwd(
            scals[s], cosines, sines, gq, gk, saved[s], normed[s], r_parts, attn_w
        )
        attn_grads.append(grads)
        gain_part = gain_part + gains
        grad_normed = scatter_tokens(nkeep, nsend)
        factor = firsts[s][1]
        mixer_part = mixer_part + jnp.sum(grad_normed * tokens[s] * factor, axis=0)
        input_gradient.append(grad_residual + norm_back(tokens[s], factor, mixer_gain, grad_normed))
        out_sum = scatter_tokens(ykeep, ysend)
        block_out.append(jnp.where(valid[s], residual[s] + out_sum, 0.0).astype(BF16))

    summed = [
        sum(part.astype(F32) for part in parts_of).astype(BF16) for parts_of in zip(*attn_grads)
    ]
    attn_grad = scatter_shards(summed)
    early = sum_everywhere(jnp.concatenate([dense_part.reshape(-1, LANES), gain_part], axis=0))
    mixer = sum_everywhere(mixer_part.reshape(-1, LANES)).reshape(-1)
    dense_rows = width // LANES
    folded = early[dense_rows:, :head] + early[dense_rows:, head:]
    inner_gradient = jnp.stack(
        [
            jnp.concatenate([grad[:, p * cols : (p + 1) * cols] for grad in ff_grads], axis=1)
            for p in range(2)
        ],
        axis=1,
    )
    down_gradient = jnp.concatenate([grad[:, 2 * cols :] for grad in ff_grads], axis=1).T
    return (
        jnp.stack(block_out, axis=1),
        jnp.stack(input_gradient, axis=1),
        attn_grad[:, :query_cols],
        attn_grad[:, query_cols : query_cols + 2 * pair_cols].reshape(shard, 2, pair_cols),
        attn_grad[:, query_cols + 2 * pair_cols :].T,
        inner_gradient,
        down_gradient,
        mixer,
        folded[0],
        folded[1],
        early[:dense_rows].reshape(-1),
    )


def local(*args):
    inputs, shard = args[0], args[2].shape[0]
    if lax.axis_size("dp") == 8 and lax.axis_size("tensor") == 4 and shard % LANES == 0:
        return local_fused(*args)
    return local_plain(*args)


def rope_tables(full, head):
    half = head // 2
    freqs = np.float32(THETA) ** (-np.arange(half, dtype=np.float32) * np.float32(2.0) / np.float32(head))
    angles = np.arange(full, dtype=np.float32)[:, None] * freqs[None, :].astype(np.float32)
    cosines, sines = np.cos(angles), np.sin(angles)
    return (
        jnp.asarray(np.tile(cosines, (1, 4)), F32),
        jnp.asarray(np.tile(np.concatenate([-sines, sines], axis=1), (1, 2)), F32),
    )


def local_fused(
    inputs,
    lengths,
    query_weight,
    key_value_weight,
    output_weight,
    inner_weight,
    down_weight,
    mixer_gain,
    query_gain,
    key_gain,
    dense_gain,
    cotangent,
):
    size, seqs, width = inputs.shape
    parts = lax.axis_size("tensor")
    full = size * parts
    head = query_gain.shape[0]
    query_cols = query_weight.shape[1]
    pair_cols = key_value_weight.shape[2]
    hidden = inner_weight.shape[2]
    shard = query_weight.shape[0]
    me_t, me_d = lax.axis_index("tensor"), lax.axis_index("dp")
    n_c = 3
    cols = hidden // n_c
    tabs = rope_tables(full, head)
    gq = jnp.tile(query_gain, 2)[None, :]
    gk = jnp.tile(key_gain, 2)[None, :]
    gains = (gq, gk, mixer_gain[None, :], dense_gain[None, :])
    down_turned = down_weight.T
    attn_shard = jnp.concatenate(
        [query_weight, key_value_weight.reshape(shard, 2 * pair_cols), output_weight.T], axis=1
    )
    ff_shard = jnp.stack(
        [
            jnp.concatenate(
                [inner_weight[:, 0, part], inner_weight[:, 1, part], down_turned[:, part]], axis=1
            )
            for part in (slice(c * cols, (c + 1) * cols) for c in range(n_c))
        ]
    )
    positions = me_t * size + jnp.arange(size, dtype=jnp.int32)
    valid = [(positions < lengths[s])[:, None] for s in range(seqs)]
    upstream = jnp.stack([jnp.where(valid[s], cotangent[:, s], 0) for s in range(seqs)])
    x = inputs.reshape(size, seqs * width)

    (aw, fw, normed, ups, dense, resid, *saved) = fused_forward(
        lengths, x, attn_shard, upstream, ff_shard, tabs, gains
    )
    cosines, sines = tabs
    scals = [
        jnp.stack([me_t.astype(jnp.int32), me_d.astype(jnp.int32), lengths[s], jnp.int32(0)])
        for s in range(seqs)
    ]
    def sl(a,n,me,cnt):
        return [lax.dynamic_slice_in_dim(a,(me^j)*n,n,0) for j in range(cnt)]
    attn_w=sl(aw,shard,me_d,8)
    ff_w=[sl(fw[c],shard,me_d,8) for c in range(n_c)]
    tokens = [inputs[:, s].astype(F32) for s in range(seqs)]
    normed=[sl(normed[s],size,me_t,4) for s in range(seqs)]
    up_parts=[sl(ups[s],size,me_t,4) for s in range(seqs)]
    dense=[sl(dense[s],size,me_t,4) for s in range(seqs)]
    residual=[resid[s] for s in range(seqs)]
    saved=[[a[s] for a in saved] for s in range(seqs)]
    seconds=[lax.rsqrt(jnp.mean(r*r,axis=-1,keepdims=True)+EPS) for r in residual]
    firsts=[(None,lax.rsqrt(jnp.mean(r*r,axis=-1,keepdims=True)+EPS)) for r in tokens]
    upstream=[upstream[s].astype(F32) for s in range(seqs)]
    x_parts = [part for s in range(seqs) for part in dense[s]]
    u_parts = [part for s in range(seqs) for part in up_parts[s]]
    hids, ggus, ff_grads = [], [], []
    for c in range(n_c):
        hid, ggu, grads = feed_forward(scals[0], x_parts, u_parts, ff_w[c])
        hids.append(hid)
        ggus.append(ggu)
        ff_grads.append(scatter_shards(grads))

    block_out, input_gradient, attn_grads = [], [], []
    mixer_part = dense_part = gain_part = 0.0
    for s in range(seqs):
        ykeep, ysend, gkeep, gsend = ff_out(s, scals[s], parts, size, hids, ggus, ff_w)
        grad_dense = scatter_tokens(gkeep, gsend)
        dense_part = dense_part + jnp.sum(grad_dense * residual[s] * seconds[s], axis=0)
        grad_residual = upstream[s] + norm_back(residual[s], seconds[s], dense_gain, grad_dense)
        r_parts = gather_tokens(grad_residual.astype(BF16))
        nkeep, nsend, gains, grads = attn_bwd(
            scals[s], cosines, sines, gq, gk, saved[s], normed[s], r_parts, attn_w
        )
        attn_grads.append(grads)
        gain_part = gain_part + gains
        grad_normed = scatter_tokens(nkeep, nsend)
        factor = firsts[s][1]
        mixer_part = mixer_part + jnp.sum(grad_normed * tokens[s] * factor, axis=0)
        input_gradient.append(grad_residual + norm_back(tokens[s], factor, mixer_gain, grad_normed))
        out_sum = scatter_tokens(ykeep, ysend)
        block_out.append(jnp.where(valid[s], residual[s] + out_sum, 0.0).astype(BF16))

    summed = [
        sum(part.astype(F32) for part in parts_of).astype(BF16) for parts_of in zip(*attn_grads)
    ]
    attn_grad = scatter_shards(summed)
    early = sum_everywhere(jnp.concatenate([dense_part.reshape(-1, LANES), gain_part], axis=0))
    mixer = sum_everywhere(mixer_part.reshape(-1, LANES)).reshape(-1)
    dense_rows = width // LANES
    folded = early[dense_rows:, :head] + early[dense_rows:, head:]
    inner_gradient = jnp.stack(
        [
            jnp.concatenate([grad[:, p * cols : (p + 1) * cols] for grad in ff_grads], axis=1)
            for p in range(2)
        ],
        axis=1,
    )
    down_gradient = jnp.concatenate([grad[:, 2 * cols :] for grad in ff_grads], axis=1).T
    return (
        jnp.stack(block_out, axis=1),
        jnp.stack(input_gradient, axis=1),
        attn_grad[:, :query_cols],
        attn_grad[:, query_cols : query_cols + 2 * pair_cols].reshape(shard, 2, pair_cols),
        attn_grad[:, query_cols + 2 * pair_cols :].T,
        inner_gradient,
        down_gradient,
        mixer,
        folded[0],
        folded[1],
        early[:dense_rows].reshape(-1),
    )


def solution(mesh):
    return jax.shard_map(
        local,
        mesh=mesh,
        in_specs=(
            P("tensor", "dp", None),
            P("dp"),
            P("dp", "tensor"),
            P("dp", None, "tensor"),
            P("tensor", "dp"),
            P("dp", None, "tensor"),
            P("tensor", "dp"),
            P(),
            P(),
            P(),
            P(),
            P("tensor", "dp", None),
        ),
        out_specs=(
            P("tensor", "dp", None),
            P("tensor", "dp", None),
            P("dp", "tensor"),
            P("dp", None, "tensor"),
            P("tensor", "dp"),
            P("dp", None, "tensor"),
            P("tensor", "dp"),
            P(),
            P(),
            P(),
            P(),
        ),
        check_vma=False,
    )
```

```python
import functools

import jax
import jax.numpy as jnp
import numpy as np
from jax import lax
from jax.experimental import pallas as pl
from jax.experimental.pallas import tpu as pltpu
from jax.sharding import PartitionSpec as P

EPS = 1e-05
THETA = 1000000.0
LOG2E = 1.4426950408889634
F32 = jnp.float32
BF16 = jnp.bfloat16
HIGH = lax.Precision.HIGHEST
LANES = 128
VMEM_LIMIT = 56 * 1024 * 1024
DENSE_LIMIT = 62 * 1024 * 1024
ANY = pl.BlockSpec(memory_space=pl.ANY)
VMEM = pl.BlockSpec(memory_space=pltpu.VMEM)
SMEM = pl.BlockSpec(memory_space=pltpu.SMEM)


def dot(a, b, **kw):
    return lax.dot_general(
        a, b, (((1,), (0,)), ((), ())), preferred_element_type=F32, **kw
    )


def dot_nt(a, b, **kw):
    return lax.dot_general(
        a, b, (((1,), (1,)), ((), ())), preferred_element_type=F32, **kw
    )


def dot_tn(a, b, **kw):
    return lax.dot_general(
        a, b, (((0,), (0,)), ((), ())), preferred_element_type=F32, **kw
    )


def iota(shape, axis):
    return lax.broadcasted_iota(jnp.int32, shape, axis)


def low_half(shape):
    return iota(shape, 1) % LANES < LANES // 2


def head_blocks(scale):
    shape = (LANES, LANES)
    return jnp.where(iota(shape, 0) // 64 == iota(shape, 1) // 64, scale, 0.0).astype(F32)


def partner(values):
    first = iota(values.shape, 1) % 64 < 32
    return jnp.where(first, pltpu.roll(values, LANES - 32, 1), pltpu.roll(values, 32, 1))


def rows_of(index, size):
    return pl.ds(pl.multiple_of(index * size, size), size)


def load_all(sources, targets, sems, first):
    copies = []
    for number, (source, target) in enumerate(zip(sources, targets)):
        copy = pltpu.make_async_copy(source, target, sems.at[first + number])
        copy.start()
        copies.append(copy)
    return copies


def shard_targets(w_refs, ws, me):
    size = w_refs[0].shape[0]
    if len(w_refs) == 1:
        return [ws]
    return [ws.at[rows_of(me ^ slot, size)] for slot in range(len(w_refs))]


def store_slots(whole, out_refs, me):
    if len(out_refs) == 1:
        out_refs[0][...] = whole[...]
        return
    keep_ref, send_ref = out_refs
    size = keep_ref.shape[1]
    for slot in range(2 * keep_ref.shape[0]):
        (send_ref if slot % 2 else keep_ref)[slot // 2] = whole[rows_of(me ^ slot, size), :]


def padded_heads(first, second, low, g, e):
    here = low if e == 0 else jnp.logical_not(low)
    return jnp.where(here, first if g == e else second, 0.0).astype(BF16)


def project_rows(r, size, length, xs, ws, tabs, gains, raw_ref, q_ref, k_ref, v_ref, kp, vp):
    rows = rows_of(r, size)
    cos_ref, sin_ref = tabs
    gq_ref, gk_ref = gains
    mean_of = head_blocks(1.0 / 64)
    low = low_half((size, LANES))
    projected = dot(xs[rows, :], ws[:, :512])
    raw_ref[rows, :] = projected[:, :384]
    cosines, sines = cos_ref[rows, :], sin_ref[rows, :]

    def turned(values, gain):
        mean = dot(values * values, mean_of, precision=HIGH)
        normed = values * lax.rsqrt(mean + EPS) * gain
        return normed * cosines + partner(normed) * sines

    for g in range(2):
        lanes = slice(LANES * g, LANES * (g + 1))
        q_ref[rows, lanes] = turned(projected[:, lanes], gq_ref[...]).astype(BF16)
    keys = turned(projected[:, 256:384], gk_ref[...])
    values = projected[:, 384:512]
    k_ref[rows, :] = keys.astype(BF16)
    v_ref[rows, :] = values.astype(BF16)
    live = r * size + iota((size, LANES), 0) < length
    ones = jnp.where(live, 1.0, 0.0)
    values = jnp.where(live, values, 0.0)
    keys_swap, values_swap = pltpu.roll(keys, 64, 1), pltpu.roll(values, 64, 1)
    for g in range(2):
        for e in range(2):
            kp[2 * g + e, rows, :] = padded_heads(keys, keys_swap, low, g, e)
            vp[2 * g + e, rows, :LANES] = padded_heads(values, values_swap, low, g, e)
            vp[2 * g + e, rows, LANES:] = padded_heads(ones, ones, low, g, e)


def attend_rows(i, size, q_ref, kp, vp, acc, att_ref, lse_ref):
    rows = rows_of(i, size)
    factor = LOG2E / 8.0
    causal = iota((size, size), 1) <= iota((size, size), 0)
    queries = [q_ref[rows, LANES * g : LANES * (g + 1)] for g in range(2)]

    def block(kb, masked):
        cols = rows_of(kb, size)
        sums = []
        for g in range(2):
            total = None
            for e in range(2):
                weights = jnp.exp2(dot_nt(queries[g], kp[2 * g + e, cols, :]) * factor)
                if masked:
                    weights = jnp.where(causal, weights, 0.0)
                part = dot(weights.astype(BF16), vp[2 * g + e, cols, :])
                total = part if total is None else total + part
            sums.append(total)
        return sums

    for g, total in enumerate(block(i, True)):
        acc[g] = total

    def more(kb, carry):
        for g, total in enumerate(block(kb, False)):
            acc[g] += total
        return carry

    lax.fori_loop(0, i, more, 0)
    for g in range(2):
        lanes = slice(LANES * g, LANES * (g + 1))
        summed = acc[g, :, LANES:]
        att_ref[rows, lanes] = (acc[g, :, :LANES] / summed).astype(BF16)
        lse_ref[rows, lanes] = jnp.log2(summed)


def attn_fwd_kernel(parts, n_w, scal, cos_ref, sin_ref, gq_ref, gk_ref, *refs):
    x_refs, refs = refs[:parts], refs[parts:]
    w_refs, refs = refs[:n_w], refs[n_w:]
    (raw_ref, q_ref, k_ref, v_ref, att_ref, lse_ref, keep_ref, send_ref, xs, ws, kp, vp, acc, sems) = refs
    size = x_refs[0].shape[0]
    me_t, me_d, length = scal[0], scal[1], scal[2]
    copies = load_all(w_refs, shard_targets(w_refs, ws, me_d), sems, 0)
    copies += load_all(x_refs, [xs.at[rows_of(me_t ^ j, size)] for j in range(parts)], sems, n_w)
    for copy in copies:
        copy.wait()

    def project(r, carry):
        project_rows(
            r, size, length, xs, ws, (cos_ref, sin_ref), (gq_ref, gk_ref), raw_ref, q_ref, k_ref, v_ref, kp, vp
        )
        return carry

    def attend(i, carry):
        attend_rows(i, size, q_ref, kp, vp, acc, att_ref, lse_ref)
        return carry

    lax.fori_loop(0, parts, project, 0)
    lax.fori_loop(0, parts, attend, 0)
    for j in range(parts):
        out = dot_nt(att_ref[rows_of(me_t ^ j, size), :], ws[:, 512:])
        (send_ref if j % 2 else keep_ref)[j // 2] = out.astype(BF16)


def attn_fwd(scal, cosines, sines, gq, gk, x_parts, w_parts):
    parts, n_w = len(x_parts), len(w_parts)
    size, width = x_parts[0].shape
    full = parts * size
    cols = w_parts[0].shape[1]
    pair = jax.ShapeDtypeStruct((parts // 2, size, width), BF16)
    return pl.pallas_call(
        functools.partial(attn_fwd_kernel, parts, n_w),
        out_shape=(
            jax.ShapeDtypeStruct((full, 384), F32),
            jax.ShapeDtypeStruct((full, 256), BF16),
            jax.ShapeDtypeStruct((full, 128), BF16),
            jax.ShapeDtypeStruct((full, 128), BF16),
            jax.ShapeDtypeStruct((full, 256), BF16),
            jax.ShapeDtypeStruct((full, 256), F32),
            pair,
            pair,
        ),
        in_specs=[SMEM] + [VMEM] * 4 + [ANY] * (parts + n_w),
        out_specs=(VMEM,) * 8,
        scratch_shapes=[
            pltpu.VMEM((full, width), BF16),
            pltpu.VMEM((width, cols), BF16),
            pltpu.VMEM((4, full, LANES), BF16),
            pltpu.VMEM((4, full, 2 * LANES), BF16),
            pltpu.VMEM((2, size, 2 * LANES), F32),
            pltpu.SemaphoreType.DMA((n_w + parts,)),
        ],
        compiler_params=pltpu.CompilerParams(vmem_limit_bytes=VMEM_LIMIT),
        cost_estimate=pl.CostEstimate(flops=8_000_000_000, bytes_accessed=12_000_000, transcendentals=3_000_000),
        name="attention_forward",
    )(scal, cosines, sines, gq, gk, *x_parts, *w_parts)


def prepare_rows(r, size, length, gs, ws, k_ref, v_ref, att_ref, lse_ref, ga, drow, lrow, kp, kt, vp):
    rows = rows_of(r, size)
    low = low_half((size, LANES))
    pick = jnp.where(iota((8, 256), 0) == iota((8, 256), 1) // 64, 1.0, 0.0).astype(F32)
    grad = dot(gs[rows, :], ws[:, 512:]).astype(BF16)
    ga[rows, :] = grad
    drow[:, rows] = dot_nt(pick, grad.astype(F32) * att_ref[rows, :].astype(F32), precision=HIGH)
    lrow[:, rows] = dot_nt(pick * (1.0 / 64), lse_ref[rows, :], precision=HIGH)
    live = r * size + iota((size, LANES), 0) < length
    keys = jnp.where(live, k_ref[rows, :].astype(F32), 0.0)
    values = jnp.where(live, v_ref[rows, :].astype(F32), 0.0)
    keys_swap, values_swap = pltpu.roll(keys, 64, 1), pltpu.roll(values, 64, 1)
    for g in range(2):
        for e in range(2):
            here = low if e == 0 else jnp.logical_not(low)
            padded = jnp.where(here, keys if g == e else keys_swap, 0.0)
            kp[2 * g + e, rows, :] = padded.astype(BF16)
            kt[2 * g + e, :, rows] = padded.T.astype(BF16)
            vp[2 * g + e, rows, :] = padded_heads(values, values_swap, low, g, e)


def sweep_rows(i, size, q_ref, ga, kp, kt, vp, drow, lrow, acc, dq, dk, dv):
    rows = rows_of(i, size)
    factor = LOG2E / 8.0
    causal = iota((size, size), 0) <= iota((size, size), 1)
    low2 = iota((2 * size, LANES), 0) // size == iota((2 * size, LANES), 1) // 64
    queries, grads, queries2, grads2 = [], [], [], []
    for g in range(2):
        lanes = slice(LANES * g, LANES * (g + 1))
        queries.append(q_ref[rows, lanes])
        grads.append(ga[rows, lanes])
        for source, target in ((queries, queries2), (grads, grads2)):
            both = jnp.concatenate([source[g], source[g]], axis=0)
            target.append(jnp.where(low2, both, jnp.zeros_like(both)))

    def block(kb, masked):
        cols = rows_of(kb, size)
        parts_t = []
        for g in range(2):
            weights2, scores2, turned = [], [], None
            for e in range(2):
                h = 2 * g + e
                weights = jnp.exp2(dot_nt(kp[h, cols, :], queries[g]) * factor - lrow[h : h + 1, rows])
                if masked:
                    weights = jnp.where(causal, weights, 0.0)
                grad_weights = dot_nt(vp[h, cols, :], grads[g])
                grad_scores = (weights * (grad_weights - drow[h : h + 1, rows])).astype(BF16)
                weights2.append(weights.astype(BF16))
                scores2.append(grad_scores)
                part = dot(kt[h, :, cols], grad_scores)
                turned = part if turned is None else turned + part
            dv[g, cols, :] += dot(jnp.concatenate(weights2, axis=1), grads2[g])
            dk[g, cols, :] += dot(jnp.concatenate(scores2, axis=1), queries2[g])
            parts_t.append(turned)
        return parts_t

    for g, total in enumerate(block(i, True)):
        acc[g] = total

    def more(kb, carry):
        for g, total in enumerate(block(kb, False)):
            acc[g] += total
        return carry

    lax.fori_loop(0, i, more, 0)
    for g in range(2):
        dq[rows, LANES * g : LANES * (g + 1)] = acc[g].T


def unproject_rows(r, size, length, tabs, gains, raw_ref, dq, dk, dv, gp, gains_ref):
    rows = rows_of(r, size)
    cosines, sines = tabs[0][rows, :], tabs[1][rows, :]
    low = low_half((size, LANES))
    mean_of = head_blocks(1.0 / 64)
    live = r * size + iota((size, LANES), 0) < length

    def back(grad, lanes, gain, row):
        raw = raw_ref[rows, lanes]
        rms = lax.rsqrt(dot(raw * raw, mean_of, precision=HIGH) + EPS)
        turned = grad * cosines - partner(grad) * sines
        gains_ref[row : row + 1, :] += jnp.sum(turned * raw * rms, axis=0, keepdims=True)
        weighted = turned * gain
        inner = dot(raw * weighted, mean_of, precision=HIGH)
        gp[rows, lanes] = (rms * weighted - raw * (rms * rms * rms) * inner).astype(BF16)

    def folded(ref):
        first, second = ref[0, rows, :], ref[1, rows, :]
        both = jnp.where(low, first + pltpu.roll(first, 64, 1), second + pltpu.roll(second, 64, 1))
        return jnp.where(live, both, 0.0)

    for g in range(2):
        lanes = slice(LANES * g, LANES * (g + 1))
        back(dq[rows, lanes] * 0.125, lanes, gains[0][...], 0)
    back(folded(dk) * 0.125, slice(256, 384), gains[1][...], 1)
    gp[rows, 384:512] = folded(dv).astype(BF16)


def attn_bwd_kernel(parts, n_w, scal, cos_ref, sin_ref, gq_ref, gk_ref, raw_ref, q_ref, k_ref, v_ref, att_ref, lse_ref, *refs):
    x_refs, refs = refs[:parts], refs[parts:]
    r_refs, refs = refs[:parts], refs[parts:]
    w_refs, refs = refs[:n_w], refs[n_w:]
    n_g = 1 if n_w == 1 else 2
    keep_ref, send_ref, gains_ref = refs[:3]
    g_refs, refs = refs[3 : 3 + n_g], refs[3 + n_g :]
    xs, gs, ws, kp, vp, kt, ga, dq, dk, dv, gp, whole, lrow, drow, acc, sems = refs
    size = x_refs[0].shape[0]
    me_t, me_d, length = scal[0], scal[1], scal[2]
    copies = load_all(w_refs, shard_targets(w_refs, ws, me_d), sems, 0)
    copies += load_all(r_refs, [gs.at[rows_of(me_t ^ j, size)] for j in range(parts)], sems, n_w)
    copies += load_all(x_refs, [xs.at[rows_of(me_t ^ j, size)] for j in range(parts)], sems, n_w + parts)
    for copy in copies:
        copy.wait()

    def prepare(r, carry):
        prepare_rows(r, size, length, gs, ws, k_ref, v_ref, att_ref, lse_ref, ga, drow, lrow, kp, kt, vp)
        return carry

    def sweep(i, carry):
        sweep_rows(i, size, q_ref, ga, kp, kt, vp, drow, lrow, acc, dq, dk, dv)
        return carry

    def unproject(r, carry):
        unproject_rows(r, size, length, (cos_ref, sin_ref), (gq_ref, gk_ref), raw_ref, dq, dk, dv, gp, gains_ref)
        return carry

    lax.fori_loop(0, parts, prepare, 0)
    dk[...] = jnp.zeros_like(dk)
    dv[...] = jnp.zeros_like(dv)
    lax.fori_loop(0, parts, sweep, 0)
    gains_ref[...] = jnp.zeros_like(gains_ref)
    lax.fori_loop(0, parts, unproject, 0)
    for j in range(parts):
        out = dot_nt(gp[rows_of(me_t ^ j, size), :], ws[:, :512])
        (send_ref if j % 2 else keep_ref)[j // 2] = out.astype(BF16)

    def weigh(b, carry):
        rows = rows_of(b, 256)
        whole[rows, :512] = dot_tn(xs[:, rows], gp[...]).astype(BF16)
        whole[rows, 512:] = dot_tn(gs[:, rows], att_ref[...]).astype(BF16)
        return carry

    lax.fori_loop(0, whole.shape[0] // 256, weigh, 0)
    store_slots(whole, g_refs, me_d)


def slot_shapes(n_w, width, cols):
    if n_w == 1:
        return (jax.ShapeDtypeStruct((width, cols), BF16),)
    return (jax.ShapeDtypeStruct((n_w // 2, width // n_w, cols), BF16),) * 2


def attn_bwd(scal, cosines, sines, gq, gk, saved, x_parts, r_parts, w_parts):
    parts, n_w = len(x_parts), len(w_parts)
    size, width = x_parts[0].shape
    full = parts * size
    cols = w_parts[0].shape[1]
    pair = jax.ShapeDtypeStruct((parts // 2, size, width), BF16)
    g_shapes = slot_shapes(n_w, width, cols)
    outs = pl.pallas_call(
        functools.partial(attn_bwd_kernel, parts, n_w),
        out_shape=(pair, pair, jax.ShapeDtypeStruct((8, LANES), F32)) + g_shapes,
        in_specs=[SMEM] + [VMEM] * 10 + [ANY] * (2 * parts + n_w),
        out_specs=(VMEM,) * (3 + len(g_shapes)),
        scratch_shapes=[
            pltpu.VMEM((full, width), BF16),
            pltpu.VMEM((full, width), BF16),
            pltpu.VMEM((width, cols), BF16),
            pltpu.VMEM((4, full, LANES), BF16),
            pltpu.VMEM((4, full, LANES), BF16),
            pltpu.VMEM((4, LANES, full), BF16),
            pltpu.VMEM((full, 256), BF16),
            pltpu.VMEM((full, 256), F32),
            pltpu.VMEM((2, full, LANES), F32),
            pltpu.VMEM((2, full, LANES), F32),
            pltpu.VMEM((full, 512), BF16),
            pltpu.VMEM((width, cols), BF16),
            pltpu.VMEM((8, full), F32),
            pltpu.VMEM((8, full), F32),
            pltpu.VMEM((2, LANES, size), F32),
            pltpu.SemaphoreType.DMA((n_w + 2 * parts,)),
        ],
        compiler_params=pltpu.CompilerParams(vmem_limit_bytes=VMEM_LIMIT),
        cost_estimate=pl.CostEstimate(flops=14_000_000_000, bytes_accessed=15_000_000, transcendentals=3_000_000),
        name="attention_backward",
    )(scal, cosines, sines, gq, gk, *saved, *x_parts, *r_parts, *w_parts)
    return outs[0], outs[1], outs[2], outs[3:]


def ff_kernel(n_x, n_w, scal, *refs):
    x_refs, refs = refs[:n_x], refs[n_x:]
    u_refs, refs = refs[:n_x], refs[n_x:]
    w_refs, refs = refs[:n_w], refs[n_w:]
    n_g = 1 if n_w == 1 else 2
    hid_ref, ggu_ref = refs[:2]
    g_refs, refs = refs[2 : 2 + n_g], refs[2 + n_g :]
    xs, us, ws, whole, sems = refs
    size = x_refs[0].shape[0]
    me_d = scal[1]
    cols = ws.shape[1] // 3
    copies = load_all(w_refs, shard_targets(w_refs, ws, me_d), sems, 0)
    x_copies = load_all(x_refs, [xs.at[pl.ds(j * size, size)] for j in range(n_x)], sems, n_w)
    u_copies = load_all(u_refs, [us.at[pl.ds(j * size, size)] for j in range(n_x)], sems, n_w + n_x)
    for copy in copies + x_copies + u_copies:
        copy.wait()

    def tokens(r, carry):
        rows = rows_of(r, size)
        gate_up = dot(xs[rows, :], ws[:, : 2 * cols])
        grad = dot(us[rows, :], ws[:, 2 * cols :])
        gate, up = gate_up[:, :cols], gate_up[:, cols:]
        sig = 1.0 / (1.0 + jnp.exp2(gate * -LOG2E))
        silu = gate * sig
        hid_ref[rows, :] = (silu * up).astype(BF16)
        ggu_ref[rows, :cols] = (grad * up * (sig + silu * (1.0 - sig))).astype(BF16)
        ggu_ref[rows, cols:] = (grad * silu).astype(BF16)
        return carry

    lax.fori_loop(0, n_x, tokens, 0)

    def weigh(b, carry):
        rows = rows_of(b, 256)
        whole[rows, : 2 * cols] = dot_tn(xs[:, rows], ggu_ref[...]).astype(BF16)
        whole[rows, 2 * cols :] = dot_tn(us[:, rows], hid_ref[...]).astype(BF16)
        return carry

    lax.fori_loop(0, whole.shape[0] // 256, weigh, 0)
    store_slots(whole, g_refs, me_d)


def feed_forward(scal, x_parts, u_parts, w_parts):
    n_x, n_w = len(x_parts), len(w_parts)
    size, width = x_parts[0].shape
    full = n_x * size
    wide = w_parts[0].shape[1]
    cols = wide // 3
    g_shapes = slot_shapes(n_w, width, wide)
    outs = pl.pallas_call(
        functools.partial(ff_kernel, n_x, n_w),
        out_shape=(
            jax.ShapeDtypeStruct((full, cols), BF16),
            jax.ShapeDtypeStruct((full, 2 * cols), BF16),
        )
        + g_shapes,
        in_specs=[SMEM] + [ANY] * (2 * n_x + n_w),
        out_specs=(VMEM,) * (2 + len(g_shapes)),
        scratch_shapes=[
            pltpu.VMEM((full, width), BF16),
            pltpu.VMEM((full, width), BF16),
            pltpu.VMEM((width, wide), BF16),
            pltpu.VMEM((width, wide), BF16),
            pltpu.SemaphoreType.DMA((n_w + 2 * n_x,)),
        ],
        compiler_params=pltpu.CompilerParams(vmem_limit_bytes=VMEM_LIMIT),
        cost_estimate=pl.CostEstimate(flops=4 * full * width * wide, bytes_accessed=20_000_000, transcendentals=full * cols),
        name="feed_forward",
    )(scal, *x_parts, *u_parts, *w_parts)
    return outs[0], outs[1], outs[2:]


def ff_out_kernel(parts, n_c, n_w, seq, scal, *refs):
    hid_refs, refs = refs[:n_c], refs[n_c:]
    ggu_refs, refs = refs[:n_c], refs[n_c:]
    w_refs, refs = refs[: n_c * n_w], refs[n_c * n_w :]
    ykeep_ref, ysend_ref, gkeep_ref, gsend_ref, hs, gs, ws, sems = refs
    size = ykeep_ref.shape[1]
    full = parts * size
    me_d = scal[1]
    wide = ws.shape[2]
    cols = wide // 3
    copies = []
    first = 0
    for c in range(n_c):
        targets = shard_targets(w_refs[c * n_w : (c + 1) * n_w], ws.at[c], me_d)
        copies += load_all(w_refs[c * n_w : (c + 1) * n_w], targets, sems, first)
        first += n_w
    mine = pl.ds(seq * full, full)
    copies += load_all([ref.at[mine] for ref in ggu_refs], [gs.at[c] for c in range(n_c)], sems, first)
    copies += load_all([ref.at[mine] for ref in hid_refs], [hs.at[c] for c in range(n_c)], sems, first + n_c)
    for copy in copies:
        copy.wait()
    for j in range(parts):
        rows = pl.ds(j * size, size)
        grad = sum(dot_nt(gs[c, rows, :], ws[c, :, : 2 * cols]) for c in range(n_c))
        (gsend_ref if j % 2 else gkeep_ref)[j // 2] = grad.astype(BF16)
        out = sum(dot_nt(hs[c, rows, :], ws[c, :, 2 * cols :]) for c in range(n_c))
        (ysend_ref if j % 2 else ykeep_ref)[j // 2] = out.astype(BF16)


def ff_out(seq, scal, parts, size, hids, ggus, w_chunks):
    n_c, n_w = len(w_chunks), len(w_chunks[0])
    wide = w_chunks[0][0].shape[1]
    width = w_chunks[0][0].shape[0] * n_w
    full = parts * size
    cols = wide // 3
    pair = jax.ShapeDtypeStruct((parts // 2, size, width), BF16)
    return pl.pallas_call(
        functools.partial(ff_out_kernel, parts, n_c, n_w, seq),
        out_shape=(pair,) * 4,
        in_specs=[SMEM] + [ANY] * (2 * n_c + n_c * n_w),
        out_specs=(VMEM,) * 4,
        scratch_shapes=[
            pltpu.VMEM((n_c, full, cols), BF16),
            pltpu.VMEM((n_c, full, 2 * cols), BF16),
            pltpu.VMEM((n_c, width, wide), BF16),
            pltpu.SemaphoreType.DMA((n_c * n_w + 2 * n_c,)),
        ],
        compiler_params=pltpu.CompilerParams(vmem_limit_bytes=VMEM_LIMIT),
        cost_estimate=pl.CostEstimate(flops=2 * full * width * wide * n_c, bytes_accessed=22_000_000, transcendentals=0),
        name="feed_forward_out",
    )(scal, *hids, *ggus, *[shard for chunk in w_chunks for shard in chunk])


def flip(index, bits):
    for bit in (1, 2, 4):
        if bits & bit:
            index = index + bit - 2 * bit * lax.rem(lax.div(index, bit), 2)
    return index


def enter(me_d, me_t):
    barrier = pltpu.get_barrier_semaphore()
    devices = [{"dp": flip(me_d, bits)} for bits in (1, 2, 4, 6)]
    devices += [{"tensor": flip(me_t, bits)} for bits in (1, 2)]
    for device in devices:
        pl.semaphore_signal(barrier, inc=1, device_id=device, device_id_type=pl.DeviceIdType.MESH)
    return lambda: pl.semaphore_wait(barrier, len(devices))


def remote(source, target, sems, number, device):
    return pltpu.make_async_remote_copy(
        src_ref=source,
        dst_ref=target,
        send_sem=sems.at[0, number],
        recv_sem=sems.at[1, number],
        device_id=device,
        device_id_type=pl.DeviceIdType.MESH,
    )


class ShardGather:
    COPIES = 7

    def __init__(self, shard, whole, sems, first, me_d):
        size = shard.shape[0]
        mine = whole.at[rows_of(me_d, size)]
        beside = {"dp": flip(me_d, 1)}
        self.own = [
            remote(shard, mine, sems, first + n, {"dp": flip(me_d, bits)})
            for n, bits in enumerate((1, 2, 4, 6))
        ]
        self.passed = []
        for n, bits in enumerate((2, 4, 6)):
            there = whole.at[rows_of(flip(me_d, bits), size)]
            self.passed.append(remote(there, there, sems, first + 4 + n, beside))

    def start(self):
        for copy in self.own:
            copy.start()

    def forward(self):
        for come, onward in zip(self.own[1:], self.passed):
            come.wait_recv()
            onward.start()

    def arrive(self):
        self.own[0].wait_recv()
        for copy in self.passed:
            copy.wait_recv()

    def drain(self):
        for copy in self.own + self.passed:
            copy.wait_send()


class TokenGather:
    COPIES = 3

    def __init__(self, block, whole, sems, first, me_t):
        size = block.shape[0]
        mine = whole.at[rows_of(me_t, size)]
        there = whole.at[rows_of(flip(me_t, 2), size)]
        near = {"tensor": flip(me_t, 1)}
        self.near = remote(block, mine, sems, first, near)
        self.far = remote(block, mine, sems, first + 1, {"tensor": flip(me_t, 2)})
        self.passed = remote(there, there, sems, first + 2, near)

    def start(self):
        self.far.start()
        self.near.start()

    def forward(self):
        self.far.wait_recv()
        self.passed.start()

    def arrive(self):
        self.near.wait_recv()
        self.passed.wait_recv()

    def drain(self):
        for copy in (self.near, self.far, self.passed):
            copy.wait_send()


class TokenReduce:
    COPIES = 3

    def __init__(self, blocks, near, far, sems, first, me_t):
        device = {"tensor": flip(me_t, 1)}
        self.blocks, self.near_ref, self.far_ref = blocks, near, far
        self.me = me_t
        self.across = flip(me_t, 2)
        size = far.shape[0]
        self.size = size
        self.near = [
            remote(blocks.at[rows_of(flip(me_t, 1 + 2 * n), size)], near.at[n], sems, first + n, device)
            for n in range(2)
        ]
        self.far = remote(near.at[1], far, sems, first + 2, {"tensor": flip(me_t, 2)})

    def start(self, n):
        self.near[n].start()

    def middle(self):
        self.near[1].wait_recv()

        def step(b, carry):
            rows = rows_of(b, 32)
            total = self.part(self.across, rows) + self.near_ref[1, rows, :].astype(F32)
            self.near_ref[1, rows, :] = total.astype(BF16)
            return carry

        lax.fori_loop(0, self.near_ref.shape[1] // 32, step, 0)
        self.far.start()

    def arrive(self):
        self.near[0].wait_recv()
        self.far.wait_recv()

    def part(self, block, rows):
        start = pl.multiple_of(block * self.size + rows.start, 32)
        return self.blocks[pl.ds(start, rows.size), :].astype(F32)

    def rows(self, rows):
        total = self.part(self.me, rows) + self.near_ref[0, rows, :].astype(F32)
        return total + self.far_ref[rows, :].astype(F32)

    def drain(self):
        for copy in self.near + [self.far]:
            copy.wait_send()


class ShardReduce:
    COPIES = 4

    def __init__(self, whole, near, far, out, sems, first, me_d):
        self.whole, self.near_ref, self.far_ref, self.out = whole, near, far, out
        self.z, self.x = lax.div(me_d, 2), lax.rem(me_d, 2)
        self.size = near.shape[1]
        self.near = remote(whole.at[:, 1 - self.x], near, sems, first, {"dp": flip(me_d, 1)})
        self.far = [
            remote(near.at[flip(self.z, k)], far.at[k - 1], sems, first + k, {"dp": flip(me_d, 2 * k)})
            for k in (1, 2, 3)
        ]

    def start(self):
        self.near.start()

    def middle(self):
        self.near.wait_recv()
        for k in (1, 2, 3, 0):
            there = flip(self.z, k)

            def step(rows):
                total = self.whole[there, self.x, rows, :].astype(F32) + self.near_ref[there, rows, :].astype(F32)
                if k:
                    self.near_ref[there, rows, :] = total.astype(BF16)
                else:
                    self.out[rows, :] = total

            by_rows(self.size, 32, step)
            if k:
                self.far[k - 1].start()

    def finish(self):
        for copy in self.far:
            copy.wait_recv()

        def step(rows):
            total = self.out[rows, :]
            for k in range(3):
                total = total + self.far_ref[k, rows, :].astype(F32)
            self.out[rows, :] = total

        by_rows(self.size, 32, step)

    def drain(self):
        for copy in [self.near] + self.far:
            copy.wait_send()


def by_rows(count, step, body):
    def run(b, carry):
        body(rows_of(b, step))
        return carry

    lax.fori_loop(0, count // step, run, 0)


def rms_factor(values):
    return lax.rsqrt(jnp.mean(values * values, axis=-1, keepdims=True) + EPS)


def forward_kernel(
    lengths, x_ref, aw_ref, up_ref, fw_ref, cos_ref, sin_ref, gq_ref, gk_ref, mg_ref, dg_ref,
    aw_out, fw_out, normed_out, up_out, dense_out, resid_ref, raw_ref, q_ref, k_ref, v_ref, att_ref, lse_ref,
    xs, ws, kp, vp, acc, outp, near, far, dense, sems, local_sems,
):
    seqs, size, width = resid_ref.shape
    parts = xs.shape[1] // size
    n_c = fw_ref.shape[0]
    me_t, me_d = lax.axis_index("tensor"), lax.axis_index("dp")
    entered = enter(me_d, me_t)
    mine_t, mine_d = rows_of(me_t, size), rows_of(me_d, aw_ref.shape[0])

    first = 0
    attn_w = ShardGather(aw_ref, ws, sems, first, me_d)
    first += ShardGather.COPIES
    ff_w = []
    for c in range(n_c):
        ff_w.append(ShardGather(fw_ref.at[c], fw_out.at[c], sems, first, me_d))
        first += ShardGather.COPIES
    normed, ups, denses, outs = [], [], [], []
    for s in range(seqs):
        normed.append(TokenGather(xs.at[s, mine_t], xs.at[s], sems, first, me_t))
        ups.append(TokenGather(up_ref.at[s], up_out.at[s], sems, first + 3, me_t))
        denses.append(TokenGather(dense.at[s], dense_out.at[s], sems, first + 6, me_t))
        outs.append(TokenReduce(outp.at[s], near.at[s], far.at[s], sems, first + 9, me_t))
        first += 12

    def here(source, target, number):
        copy = pltpu.make_async_copy(source, target, local_sems.at[number])
        copy.start()
        return copy

    mine = here(aw_ref, ws.at[mine_d], 0)
    stays = [here(up_ref.at[s], up_out.at[s, mine_t], 1 + s) for s in range(seqs)]
    stays += [here(fw_ref.at[c], fw_out.at[c, mine_d], 1 + seqs + c) for c in range(n_c)]
    used = 1 + seqs + n_c

    for s in range(seqs):

        def norm(rows):
            values = x_ref[rows, width * s : width * (s + 1)].astype(F32)
            target = pl.ds(pl.multiple_of(me_t * size + rows.start, 32), 32)
            xs[s, target, :] = (values * rms_factor(values) * mg_ref[...]).astype(BF16)

        by_rows(size, 32, norm)
    entered()
    normed[0].start()
    attn_w.start()
    normed[1].start()
    attn_w.forward()
    normed[0].forward()
    normed[0].arrive()
    mine.wait()
    attn_w.arrive()
    ff_w[0].start()
    stays.append(here(ws, aw_out, used))
    used += 1

    def project(s):
        def run(r, carry):
            project_rows(
                r, size, lengths[s], xs.at[s], ws, (cos_ref, sin_ref), (gq_ref, gk_ref),
                raw_ref.at[s], q_ref.at[s], k_ref.at[s], v_ref.at[s], kp, vp,
            )
            return carry

        lax.fori_loop(0, parts, run, 0)

    def attend(s, start, stop):
        def run(i, carry):
            attend_rows(i, size, q_ref.at[s], kp, vp, acc, att_ref.at[s], lse_ref.at[s])
            return carry

        lax.fori_loop(start, stop, run, 0)

    def out(s):
        for n, bits in enumerate((1, 3, 2, 0)):
            block = flip(me_t, bits)
            result = dot_nt(att_ref[s, rows_of(block, size), :], ws[:, 512:])
            outp[s, rows_of(block, size), :] = result.astype(BF16)
            if n < 2:
                outs[s].start(n)

    def after(s):
        outs[s].arrive()

        def norm(rows):
            values = x_ref[rows, width * s : width * (s + 1)].astype(F32) + outs[s].rows(rows)
            resid_ref[s, rows, :] = values
            dense[s, rows, :] = (values * rms_factor(values) * dg_ref[...]).astype(BF16)

        by_rows(size, 32, norm)
        denses[s].start()
        stays.append(here(dense.at[s], dense_out.at[s, mine_t], used + s))

    project(0)
    normed[1].forward()
    for s in range(seqs):
        ups[s].start()
    attend(0, 0, 3)
    ff_w[0].forward()
    if n_c > 1:
        ff_w[1].start()
    attend(0, 3, parts)
    out(0)
    normed[1].arrive()
    for s in range(seqs):
        ups[s].forward()
    outs[0].middle()
    project(1)
    attend(1, 0, 3)
    after(0)
    attend(1, 3, parts)
    out(1)
    outs[1].middle()
    denses[0].forward()
    for c in range(1, n_c):
        ff_w[c].forward()
        if c + 1 < n_c:
            ff_w[c + 1].start()
    after(1)
    denses[1].forward()
    used += seqs
    stays += [here(xs.at[s], normed_out.at[s], used + s) for s in range(seqs)]
    for c in range(n_c):
        ff_w[c].arrive()
    for s in range(seqs):
        ups[s].arrive()
        denses[s].arrive()
    for copy in stays:
        copy.wait()
    attn_w.drain()
    for exchange in ff_w + normed + ups + denses + outs:
        exchange.drain()


def fused_forward(lengths, x, aw, up, fw, tabs, gains):
    seqs, size, width = up.shape
    parts = 4
    full = parts * size
    shard, cols = aw.shape
    n_c, _, wide = fw.shape
    dp = 8

    def shape(dims, kind):
        return jax.ShapeDtypeStruct(dims, kind)

    n_sems = ShardGather.COPIES * (1 + n_c) + 12 * seqs
    return pl.pallas_call(
        forward_kernel,
        out_shape=(
            shape((dp * shard, cols), BF16),
            shape((n_c, dp * shard, wide), BF16),
            shape((seqs, full, width), BF16),
            shape((seqs, full, width), BF16),
            shape((seqs, full, width), BF16),
            shape((seqs, size, width), F32),
            shape((seqs, full, 384), F32),
            shape((seqs, full, 256), BF16),
            shape((seqs, full, 128), BF16),
            shape((seqs, full, 128), BF16),
            shape((seqs, full, 256), BF16),
            shape((seqs, full, 256), F32),
        ),
        in_specs=[SMEM, VMEM] + [ANY] * 3 + [VMEM] * 6,
        out_specs=(ANY,) * 5 + (VMEM,) * 7,
        scratch_shapes=[
            pltpu.VMEM((seqs, full, width), BF16),
            pltpu.VMEM((dp * shard, cols), BF16),
            pltpu.VMEM((4, full, LANES), BF16),
            pltpu.VMEM((4, full, 2 * LANES), BF16),
            pltpu.VMEM((2, size, 2 * LANES), F32),
            pltpu.VMEM((seqs, full, width), BF16),
            pltpu.VMEM((seqs, 2, size, width), BF16),
            pltpu.VMEM((seqs, size, width), BF16),
            pltpu.VMEM((seqs, size, width), BF16),
            pltpu.SemaphoreType.DMA((2, n_sems)),
            pltpu.SemaphoreType.DMA((2 + 3 * seqs + n_c,)),
        ],
        compiler_params=pltpu.CompilerParams(
            vmem_limit_bytes=VMEM_LIMIT, collective_id=0, has_side_effects=True
        ),
        cost_estimate=pl.CostEstimate(flops=16_000_000_000, bytes_accessed=40_000_000, transcendentals=6_000_000),
        name="forward",
    )(lengths, x, aw, up, fw, *tabs, *gains)


def dense_kernel(
    x_ref, u_ref, fw_ref, last_ref, up_ref, resid_ref, dg_ref,
    r_out, gres_ref, blk_ref, dgain_ref, ffg_ref,
    xs, us, ws, hid, ggu, whole, wnear, wfar, gnear, gfar, ynear, yfar, low_grad, sems, local_sems,
):
    seqs, size, width = resid_ref.shape
    full = x_ref.shape[1]
    parts = full // size
    early = fw_ref.shape[0]
    n_c = early + 1
    wide = ws.shape[2]
    cols = wide // 3
    me_t, me_d = lax.axis_index("tensor"), lax.axis_index("dp")
    entered = enter(me_d, me_t)

    first = 0
    last_w = ShardGather(last_ref, ws.at[early], sems, first, me_d)
    first += ShardGather.COPIES
    weights = []
    for c in range(n_c):
        out = ffg_ref.at[:, wide * c : wide * (c + 1)]
        weights.append(ShardReduce(whole.at[c % 2], wnear.at[c], wfar.at[c], out, sems, first, me_d))
        first += ShardReduce.COPIES
    grads, outs, resids = [], [], []
    for s in range(seqs):
        mine = pl.ds(s * full, full)
        grads.append(TokenReduce(xs.at[mine], gnear.at[s], gfar.at[s], sems, first, me_t))
        outs.append(TokenReduce(us.at[mine], ynear.at[s], yfar.at[s], sems, first + 3, me_t))
        resids.append(TokenGather(low_grad.at[s], r_out.at[s], sems, first + 6, me_t))
        first += 9

    def here(source, target, number):
        copy = pltpu.make_async_copy(source, target, local_sems.at[number])
        copy.start()
        return copy

    loads = [here(fw_ref.at[0], ws.at[0], 0)]
    for s in range(seqs):
        loads.append(here(x_ref.at[s], xs.at[pl.ds(s * full, full)], 1 + 2 * s))
        loads.append(here(u_ref.at[s], us.at[pl.ds(s * full, full)], 2 + 2 * s))
    used = 1 + 2 * seqs
    stays = [here(last_ref, ws.at[early, rows_of(me_d, last_ref.shape[0])], used)]
    used += 1
    later = [here(fw_ref.at[c], ws.at[c], used + c) for c in range(1, early)]
    used += early
    entered()
    last_w.start()
    for copy in loads:
        copy.wait()

    def tokens(c, start, stop):
        def run(r, carry):
            rows = rows_of(r, size)
            gate_up = dot(xs[rows, :], ws[c, :, : 2 * cols])
            grad = dot(us[rows, :], ws[c, :, 2 * cols :])
            gate, up = gate_up[:, :cols], gate_up[:, cols:]
            sig = 1.0 / (1.0 + jnp.exp2(gate * -LOG2E))
            silu = gate * sig
            hid[c, rows, :] = (silu * up).astype(BF16)
            ggu[c, rows, :cols] = (grad * up * (sig + silu * (1.0 - sig))).astype(BF16)
            ggu[c, rows, cols:] = (grad * silu).astype(BF16)
            return carry

        lax.fori_loop(start, stop, run, 0)

    def weigh(c):
        def run(b, carry):
            rows = rows_of(b, 256)
            shape = whole.shape[2:4]
            inner = dot_tn(xs[:, rows], ggu[c]).astype(BF16)
            whole[c % 2, b, :, :, : 2 * cols] = inner.reshape(shape + (2 * cols,))
            down = dot_tn(us[:, rows], hid[c]).astype(BF16)
            whole[c % 2, b, :, :, 2 * cols :] = down.reshape(shape + (cols,))
            return carry

        lax.fori_loop(0, whole.shape[1], run, 0)

    blocks = seqs * parts
    for c in range(n_c):
        if c == early:
            last_w.arrive()
            for copy in stays:
                copy.wait()
        elif c:
            later[c - 1].wait()
        tokens(c, 0, blocks)
        if c == 0:
            last_w.forward()
        if c >= 1:
            weights[c - 1].middle()
        if c >= 2:
            weights[c - 2].near.wait_send()
        weigh(c)
        weights[c].start()

    def grad_block(s, bits):
        block = flip(me_t, bits)
        rows = rows_of(s * parts + block, size)
        total = sum(dot_nt(ggu[c, rows, :], ws[c, :, : 2 * cols]) for c in range(n_c))
        xs[rows, :] = total.astype(BF16)

    def out_block(s, bits):
        block = flip(me_t, bits)
        rows = rows_of(s * parts + block, size)
        total = sum(dot_nt(hid[c, rows, :], ws[c, :, 2 * cols :]) for c in range(n_c))
        us[rows, :] = total.astype(BF16)

    def after_grad(s):
        grads[s].arrive()

        def step(rows):
            grad = grads[s].rows(rows)
            values = resid_ref[s, rows, :]
            factor = rms_factor(values)
            product = grad * values * factor
            dgain_ref[...] += jnp.sum(product.reshape(-1, 8, width), axis=0)
            weighted = grad * dg_ref[...]
            inner = jnp.mean(values * weighted, axis=-1, keepdims=True)
            total = up_ref[s, rows, :].astype(F32) + factor * weighted - values * (factor * factor * factor) * inner
            gres_ref[s, rows, :] = total
            low_grad[s, rows, :] = total.astype(BF16)

        by_rows(size, 32, step)
        resids[s].start()
        return here(low_grad.at[s], r_out.at[s, rows_of(me_t, size)], used + s)

    def after_out(s):
        outs[s].arrive()

        def step(rows):
            blk_ref[s, rows, :] = (resid_ref[s, rows, :] + outs[s].rows(rows)).astype(BF16)

        by_rows(size, 32, step)

    dgain_ref[...] = jnp.zeros_like(dgain_ref)
    for n, bits in enumerate((3, 1, 2, 0)):
        grad_block(0, bits)
        if n < 2:
            grads[0].start(1 - n)
    grad_block(1, 3)
    grads[1].start(1)
    grads[0].middle()
    weights[n_c - 1].middle()
    grad_block(1, 1)
    grads[1].start(0)
    grad_block(1, 2)
    grad_block(1, 0)
    grads[1].middle()
    out_block(0, 3)
    outs[0].start(1)
    out_block(0, 1)
    outs[0].start(0)
    final = [after_grad(0)]
    out_block(0, 2)
    out_block(0, 0)
    out_block(1, 3)
    outs[1].start(1)
    out_block(1, 1)
    outs[1].start(0)
    out_block(1, 2)
    out_block(1, 0)
    final.append(after_grad(1))
    resids[0].forward()
    for s in range(seqs):
        outs[s].middle()
    for c in range(n_c):
        weights[c].finish()
    resids[1].forward()
    for s in range(seqs):
        after_out(s)
    for s in range(seqs):
        resids[s].arrive()
    for copy in final:
        copy.wait()
    for c in range(n_c):
        if c + 2 < n_c:
            for copy in weights[c].far:
                copy.wait_send()
        else:
            weights[c].drain()
    for exchange in [last_w] + grads + outs + resids:
        exchange.drain()


def fused_dense(dense, ups, fw, last, upstream, resid, dense_gain):
    seqs, size, width = resid.shape
    full = dense.shape[1]
    shard, wide = last.shape
    early = fw.shape[0]
    n_c = early + 1
    cols = wide // 3
    tokens = seqs * full

    def shape(dims, kind):
        return jax.ShapeDtypeStruct(dims, kind)

    n_sems = ShardGather.COPIES + ShardReduce.COPIES * n_c + 9 * seqs
    return pl.pallas_call(
        dense_kernel,
        out_shape=(
            shape((seqs, full, width), BF16),
            shape((seqs, size, width), F32),
            shape((seqs, size, width), BF16),
            shape((8, width), F32),
            shape((shard, n_c * wide), F32),
        ),
        in_specs=[ANY] * 4 + [VMEM] * 3,
        out_specs=(ANY,) + (VMEM,) * 4,
        scratch_shapes=[
            pltpu.VMEM((tokens, width), BF16),
            pltpu.VMEM((tokens, width), BF16),
            pltpu.VMEM((n_c, width, wide), BF16),
            pltpu.VMEM((n_c, tokens, cols), BF16),
            pltpu.VMEM((n_c, tokens, 2 * cols), BF16),
            pltpu.VMEM((2, 4, 2, shard, wide), BF16),
            pltpu.VMEM((n_c, 4, shard, wide), BF16),
            pltpu.VMEM((n_c, 3, shard, wide), BF16),
            pltpu.VMEM((seqs, 2, size, width), BF16),
            pltpu.VMEM((seqs, size, width), BF16),
            pltpu.VMEM((seqs, 2, size, width), BF16),
            pltpu.VMEM((seqs, size, width), BF16),
            pltpu.VMEM((seqs, size, width), BF16),
            pltpu.SemaphoreType.DMA((2, n_sems)),
            pltpu.SemaphoreType.DMA((2 + 3 * seqs + early,)),
        ],
        compiler_params=pltpu.CompilerParams(
            vmem_limit_bytes=DENSE_LIMIT, collective_id=1, has_side_effects=True
        ),
        cost_estimate=pl.CostEstimate(flops=6 * tokens * width * wide * n_c, bytes_accessed=40_000_000, transcendentals=tokens * cols * n_c),
        name="feed_forward",
    )(dense, ups, fw, last, upstream, resid, dense_gain)


def backward_kernel(
    lengths, n_ref, r_ref, aw_ref, x_ref, gres_ref, dgain_ref, cos_ref, sin_ref, gq_ref, gk_ref, mg_ref,
    raw_ref, q_ref, k_ref, v_ref, att_ref, lse_ref,
    ig_ref, awg_ref, sums_ref,
    xs, gs, ws, kp, vp, kt, ga, dq, dk, dv, gp, lrow, drow, acc, gains, mixer,
    wo, wo_near, wo_far, wp, wp_near, wp_far, blocks, near, far, put, got, sems, local_sems,
):
    seqs, size, width = gres_ref.shape
    full = n_ref.shape[1]
    parts = full // size
    me_t, me_d = lax.axis_index("tensor"), lax.axis_index("dp")
    entered = enter(me_d, me_t)

    first = 0
    out_w = ShardReduce(wo, wo_near, wo_far, awg_ref.at[:, 512:768], sems, first, me_d)
    first += ShardReduce.COPIES
    pro_w = ShardReduce(wp, wp_near, wp_far, awg_ref.at[:, :512], sems, first, me_d)
    first += ShardReduce.COPIES
    grads = []
    for s in range(seqs):
        grads.append(TokenReduce(blocks.at[s], near.at[s], far.at[s], sems, first, me_t))
        first += TokenReduce.COPIES
    steps = []
    for n, (axis, bits) in enumerate((("tensor", 1), ("tensor", 2), ("dp", 1), ("dp", 2), ("dp", 4))):
        device = {axis: flip(me_t if axis == "tensor" else me_d, bits)}
        steps.append(remote(put.at[n], got.at[n], sems, first + n, device))

    def here(source, target, number):
        copy = pltpu.make_async_copy(source, target, local_sems.at[number])
        copy.start()
        return copy

    load_w = here(aw_ref, ws, 0)
    load_r = [here(r_ref.at[s], gs.at[s], 1 + s) for s in range(seqs)]
    load_x = [here(n_ref.at[s], xs.at[s], 1 + seqs + s) for s in range(seqs)]
    gains[...] = jnp.zeros_like(gains)
    mixer[...] = jnp.zeros_like(mixer)
    load_w.wait()
    entered()

    def prepare(s):
        def run(r, carry):
            prepare_rows(
                r, size, lengths[s], gs.at[s], ws, k_ref.at[s], v_ref.at[s], att_ref.at[s], lse_ref.at[s],
                ga, drow, lrow, kp, kt, vp,
            )
            return carry

        lax.fori_loop(0, parts, run, 0)
        dk[...] = jnp.zeros_like(dk)
        dv[...] = jnp.zeros_like(dv)

    def sweep(s, start, stop):
        def run(i, carry):
            sweep_rows(i, size, q_ref.at[s], ga, kp, kt, vp, drow, lrow, acc, dq, dk, dv)
            return carry

        lax.fori_loop(start, stop, run, 0)

    def unproject(s):
        def run(r, carry):
            unproject_rows(
                r, size, lengths[s], (cos_ref, sin_ref), (gq_ref, gk_ref), raw_ref.at[s], dq, dk, dv,
                gp.at[s], gains,
            )
            return carry

        lax.fori_loop(0, parts, run, 0)

    def grad_blocks(s):
        for n, bits in enumerate((3, 1, 2, 0)):
            rows = rows_of(flip(me_t, bits), size)
            blocks[s, rows, :] = dot_nt(gp[s, rows, :], ws[:, :512]).astype(BF16)
            if n < 2:
                grads[s].start(1 - n)

    def weigh(target, lefts, rights):
        def run(b, carry):
            rows = rows_of(b, 256)
            total = sum(dot_tn(lefts[s, :, rows], rights[s]) for s in range(seqs))
            target[b] = total.astype(BF16).reshape(target.shape[1:])
            return carry

        lax.fori_loop(0, target.shape[0], run, 0)

    def after(s):
        grads[s].arrive()
        lanes = slice(width * s, width * (s + 1))

        def step(rows):
            grad = grads[s].rows(rows)
            values = x_ref[rows, lanes].astype(F32)
            factor = rms_factor(values)
            product = grad * values * factor
            mixer[...] += jnp.sum(product.reshape(-1, 8, width), axis=0)
            weighted = grad * mg_ref[...]
            inner = jnp.mean(values * weighted, axis=-1, keepdims=True)
            ig_ref[rows, lanes] = gres_ref[s, rows, :] + factor * weighted - values * (factor * factor * factor) * inner

        by_rows(size, 32, step)

    load_r[0].wait()
    prepare(0)
    sweep(0, 0, parts)
    unproject(0)
    grad_blocks(0)
    load_r[1].wait()
    weigh(wo, gs, att_ref)
    out_w.start()
    grads[0].middle()
    prepare(1)
    sweep(1, 0, 3)
    out_w.middle()
    after(0)
    sweep(1, 3, parts)
    unproject(1)
    for copy in load_x:
        copy.wait()
    weigh(wp, xs, gp)
    pro_w.start()
    grad_blocks(1)
    grads[1].middle()
    out_w.finish()
    pro_w.middle()
    after(1)
    for row, vector in ((0, mixer), (8, dgain_ref)):
        total = jnp.sum(vector[...], axis=0, keepdims=True)
        for i in range(8):
            put[0, row + i : row + i + 1, :] = total[:, LANES * i : LANES * (i + 1)]
    put[0, 16:, :] = gains[...]
    for n, copy in enumerate(steps):
        copy.start()
        copy.wait_recv()
        total = put[n] + got[n]
        if n + 1 < len(steps):
            put[n + 1] = total
        else:
            sums_ref[...] = total
    pro_w.finish()
    for copy in steps:
        copy.wait_send()
    for exchange in [out_w, pro_w] + grads:
        exchange.drain()


def fused_backward(lengths, normed, resids, aw, x, gres, dgain, tabs, gains, saved):
    seqs, size, width = gres.shape
    full = normed.shape[1]
    cols = aw.shape[1]
    shard = aw.shape[0] // 8

    def shape(dims, kind):
        return jax.ShapeDtypeStruct(dims, kind)

    n_sems = 2 * ShardReduce.COPIES + TokenReduce.COPIES * seqs + 5
    return pl.pallas_call(
        backward_kernel,
        out_shape=(
            shape((size, seqs * width), F32),
            shape((shard, cols), F32),
            shape((24, LANES), F32),
        ),
        in_specs=[SMEM] + [ANY] * 3 + [VMEM] * 14,
        out_specs=(VMEM,) * 3,
        scratch_shapes=[
            pltpu.VMEM((seqs, full, width), BF16),
            pltpu.VMEM((seqs, full, width), BF16),
            pltpu.VMEM((width, cols), BF16),
            pltpu.VMEM((4, full, LANES), BF16),
            pltpu.VMEM((4, full, LANES), BF16),
            pltpu.VMEM((4, LANES, full), BF16),
            pltpu.VMEM((full, 256), BF16),
            pltpu.VMEM((full, 256), F32),
            pltpu.VMEM((2, full, LANES), F32),
            pltpu.VMEM((2, full, LANES), F32),
            pltpu.VMEM((seqs, full, 512), BF16),
            pltpu.VMEM((8, full), F32),
            pltpu.VMEM((8, full), F32),
            pltpu.VMEM((2, LANES, size), F32),
            pltpu.VMEM((8, LANES), F32),
            pltpu.VMEM((8, width), F32),
            pltpu.VMEM((4, 2, shard, 256), BF16),
            pltpu.VMEM((4, shard, 256), BF16),
            pltpu.VMEM((3, shard, 256), BF16),
            pltpu.VMEM((4, 2, shard, 512), BF16),
            pltpu.VMEM((4, shard, 512), BF16),
            pltpu.VMEM((3, shard, 512), BF16),
            pltpu.VMEM((seqs, full, width), BF16),
            pltpu.VMEM((seqs, 2, size, width), BF16),
            pltpu.VMEM((seqs, size, width), BF16),
            pltpu.VMEM((5, 24, LANES), F32),
            pltpu.VMEM((5, 24, LANES), F32),
            pltpu.SemaphoreType.DMA((2, n_sems)),
            pltpu.SemaphoreType.DMA((1 + 2 * seqs,)),
        ],
        compiler_params=pltpu.CompilerParams(
            vmem_limit_bytes=VMEM_LIMIT, collective_id=2, has_side_effects=True
        ),
        cost_estimate=pl.CostEstimate(flops=28_000_000_000, bytes_accessed=40_000_000, transcendentals=6_000_000),
        name="backward",
    )(lengths, normed, resids, aw, x, gres, dgain, *tabs, *gains[:3], *saved)


def swap(values, axis, bits):
    return lax.ppermute(values, axis, [(i, i ^ bits) for i in range(lax.axis_size(axis))])


def gather_tokens(block):
    far = swap(block, "tensor", 2)
    return [block, swap(block, "tensor", 1), far, swap(far, "tensor", 1)]


def scatter_tokens(keep, send):
    near = swap(send, "tensor", 1)
    middle = (keep[1].astype(F32) + near[1].astype(F32)).astype(BF16)
    far = swap(middle, "tensor", 2)
    return keep[0].astype(F32) + near[0].astype(F32) + far.astype(F32)


def gather_shards(shard):
    if lax.axis_size("dp") != 8 or shard.shape[0] % LANES:
        return [lax.all_gather(shard, "dp", axis=0, tiled=True)]
    slots = [shard, swap(shard, "dp", 1)]
    for bits in (2, 4, 6):
        there = swap(shard, "dp", bits)
        slots += [there, swap(there, "dp", 1)]
    return slots


def scatter_shards(grads):
    if len(grads) == 1:
        return lax.psum_scatter(grads[0].astype(F32), "dp", scatter_dimension=0, tiled=True)
    keep, send = grads
    near = swap(send, "dp", 1)
    both = keep.astype(F32) + near.astype(F32)
    total = both[0]
    for slot in (1, 2, 3):
        total = total + swap(both[slot].astype(BF16), "dp", 2 * slot).astype(F32)
    return total


def sum_everywhere(values):
    for axis in ("tensor", "dp"):
        bits = 1
        while bits < lax.axis_size(axis):
            values = values + swap(values, axis, bits)
            bits *= 2
    return values


def norm_rows(values, gain):
    factor = lax.rsqrt(jnp.mean(values * values, axis=-1, keepdims=True) + EPS)
    return (values * factor * gain, factor)


def norm_back(values, factor, gain, upstream):
    weighted = upstream * gain
    inner = jnp.mean(values * weighted, axis=-1, keepdims=True)
    return factor * weighted - values * factor * factor * factor * inner


def tables(full, head_width):
    half = head_width // 2
    freqs = THETA ** (-jnp.arange(half, dtype=F32) * 2.0 / head_width)
    angles = jnp.arange(full, dtype=F32)[:, None] * freqs[None, :]
    cosines, sines = jnp.cos(angles), jnp.sin(angles)
    return (jnp.tile(cosines, (1, 4)), jnp.tile(jnp.concatenate([-sines, sines], axis=1), (1, 2)))


def local_plain(
    inputs,
    lengths,
    query_weight,
    key_value_weight,
    output_weight,
    inner_weight,
    down_weight,
    mixer_gain,
    query_gain,
    key_gain,
    dense_gain,
    cotangent,
):
    size, seqs, width = inputs.shape
    parts = lax.axis_size("tensor")
    full = size * parts
    head = query_gain.shape[0]
    query_cols = query_weight.shape[1]
    pair_cols = key_value_weight.shape[2]
    hidden = inner_weight.shape[2]
    shard = query_weight.shape[0]
    me_t, me_d = lax.axis_index("tensor"), lax.axis_index("dp")
    n_c = 3
    cols = hidden // n_c
    cosines, sines = tables(full, head)
    gq = jnp.tile(query_gain, 2)[None, :]
    gk = jnp.tile(key_gain, 2)[None, :]

    down_turned = down_weight.T
    attn_shard = jnp.concatenate(
        [query_weight, key_value_weight.reshape(shard, 2 * pair_cols), output_weight.T], axis=1
    )
    attn_w = gather_shards(attn_shard)
    positions = me_t * size + jnp.arange(size, dtype=jnp.int32)
    scals = [
        jnp.stack([me_t.astype(jnp.int32), me_d.astype(jnp.int32), lengths[s], jnp.int32(0)])
        for s in range(seqs)
    ]
    tokens = [inputs[:, s].astype(F32) for s in range(seqs)]
    valid = [(positions < lengths[s])[:, None] for s in range(seqs)]
    firsts = [norm_rows(tokens[s], mixer_gain) for s in range(seqs)]
    normed = [gather_tokens(firsts[s][0].astype(BF16)) for s in range(seqs)]
    ff_w = []
    for c in range(n_c):
        part = slice(c * cols, (c + 1) * cols)
        ff_w.append(
            gather_shards(
                jnp.concatenate(
                    [inner_weight[:, 0, part], inner_weight[:, 1, part], down_turned[:, part]], axis=1
                )
            )
        )
    upstream = [jnp.where(valid[s], cotangent[:, s].astype(F32), 0.0) for s in range(seqs)]
    up_parts = [gather_tokens(upstream[s].astype(BF16)) for s in range(seqs)]

    saved, residual, seconds, dense = [], [], [], []
    for s in range(seqs):
        outs = attn_fwd(scals[s], cosines, sines, gq, gk, normed[s], attn_w)
        saved.append(outs[:6])
        residual.append(tokens[s] + scatter_tokens(outs[6], outs[7]))
        dense_in, factor = norm_rows(residual[s], dense_gain)
        seconds.append(factor)
        dense.append(gather_tokens(dense_in.astype(BF16)))

    x_parts = [part for s in range(seqs) for part in dense[s]]
    u_parts = [part for s in range(seqs) for part in up_parts[s]]
    hids, ggus, ff_grads = [], [], []
    for c in range(n_c):
        hid, ggu, grads = feed_forward(scals[0], x_parts, u_parts, ff_w[c])
        hids.append(hid)
        ggus.append(ggu)
        ff_grads.append(scatter_shards(grads))

    block_out, input_gradient, attn_grads = [], [], []
    mixer_part = dense_part = gain_part = 0.0
    for s in range(seqs):
        ykeep, ysend, gkeep, gsend = ff_out(s, scals[s], parts, size, hids, ggus, ff_w)
        grad_dense = scatter_tokens(gkeep, gsend)
        dense_part = dense_part + jnp.sum(grad_dense * residual[s] * seconds[s], axis=0)
        grad_residual = upstream[s] + norm_back(residual[s], seconds[s], dense_gain, grad_dense)
        r_parts = gather_tokens(grad_residual.astype(BF16))
        nkeep, nsend, gains, grads = attn_bwd(
            scals[s], cosines, sines, gq, gk, saved[s], normed[s], r_parts, attn_w
        )
        attn_grads.append(grads)
        gain_part = gain_part + gains
        grad_normed = scatter_tokens(nkeep, nsend)
        factor = firsts[s][1]
        mixer_part = mixer_part + jnp.sum(grad_normed * tokens[s] * factor, axis=0)
        input_gradient.append(grad_residual + norm_back(tokens[s], factor, mixer_gain, grad_normed))
        out_sum = scatter_tokens(ykeep, ysend)
        block_out.append(jnp.where(valid[s], residual[s] + out_sum, 0.0).astype(BF16))

    summed = [
        sum(part.astype(F32) for part in parts_of).astype(BF16) for parts_of in zip(*attn_grads)
    ]
    attn_grad = scatter_shards(summed)
    early = sum_everywhere(jnp.concatenate([dense_part.reshape(-1, LANES), gain_part], axis=0))
    mixer = sum_everywhere(mixer_part.reshape(-1, LANES)).reshape(-1)
    dense_rows = width // LANES
    folded = early[dense_rows:, :head] + early[dense_rows:, head:]
    inner_gradient = jnp.stack(
        [
            jnp.concatenate([grad[:, p * cols : (p + 1) * cols] for grad in ff_grads], axis=1)
            for p in range(2)
        ],
        axis=1,
    )
    down_gradient = jnp.concatenate([grad[:, 2 * cols :] for grad in ff_grads], axis=1).T
    return (
        jnp.stack(block_out, axis=1),
        jnp.stack(input_gradient, axis=1),
        attn_grad[:, :query_cols],
        attn_grad[:, query_cols : query_cols + 2 * pair_cols].reshape(shard, 2, pair_cols),
        attn_grad[:, query_cols + 2 * pair_cols :].T,
        inner_gradient,
        down_gradient,
        mixer,
        folded[0],
        folded[1],
        early[:dense_rows].reshape(-1),
    )


def local(*args):
    inputs, shard = args[0], args[2].shape[0]
    if lax.axis_size("dp") == 8 and lax.axis_size("tensor") == 4 and shard % LANES == 0:
        return local_fused(*args)
    return local_plain(*args)


def rope_tables(full, head):
    half = head // 2
    freqs = np.float32(THETA) ** (-np.arange(half, dtype=np.float32) * np.float32(2.0) / np.float32(head))
    angles = np.arange(full, dtype=np.float32)[:, None] * freqs[None, :].astype(np.float32)
    cosines, sines = np.cos(angles), np.sin(angles)
    return (
        jnp.asarray(np.tile(cosines, (1, 4)), F32),
        jnp.asarray(np.tile(np.concatenate([-sines, sines], axis=1), (1, 2)), F32),
    )


def local_fused(
    inputs,
    lengths,
    query_weight,
    key_value_weight,
    output_weight,
    inner_weight,
    down_weight,
    mixer_gain,
    query_gain,
    key_gain,
    dense_gain,
    cotangent,
):
    size, seqs, width = inputs.shape
    parts = lax.axis_size("tensor")
    full = size * parts
    head = query_gain.shape[0]
    query_cols = query_weight.shape[1]
    pair_cols = key_value_weight.shape[2]
    hidden = inner_weight.shape[2]
    shard = query_weight.shape[0]
    me_t, me_d = lax.axis_index("tensor"), lax.axis_index("dp")
    n_c = 3
    cols = hidden // n_c
    tabs = rope_tables(full, head)
    gq = jnp.tile(query_gain, 2)[None, :]
    gk = jnp.tile(key_gain, 2)[None, :]
    gains = (gq, gk, mixer_gain[None, :], dense_gain[None, :])
    down_turned = down_weight.T
    attn_shard = jnp.concatenate(
        [query_weight, key_value_weight.reshape(shard, 2 * pair_cols), output_weight.T], axis=1
    )
    ff_shard = jnp.stack(
        [
            jnp.concatenate(
                [inner_weight[:, 0, part], inner_weight[:, 1, part], down_turned[:, part]], axis=1
            )
            for part in (slice(c * cols, (c + 1) * cols) for c in range(n_c))
        ]
    )
    positions = me_t * size + jnp.arange(size, dtype=jnp.int32)
    valid = [(positions < lengths[s])[:, None] for s in range(seqs)]
    upstream = jnp.stack([jnp.where(valid[s], cotangent[:, s], 0) for s in range(seqs)])
    x = inputs.reshape(size, seqs * width)

    (aw, fw, normed, ups, dense, resid, *saved) = fused_forward(
        lengths, x, attn_shard, upstream, ff_shard[: n_c - 1], tabs, gains
    )
    resids, gres, blk, dgain, ff_grad = fused_dense(
        dense, ups, fw, ff_shard[n_c - 1], upstream, resid, gains[3]
    )
    input_gradient, attn_grad, sums = fused_backward(
        lengths, normed, resids, aw, x, gres, dgain, tabs, gains, saved
    )
    block_out = jnp.stack([jnp.where(valid[s], blk[s], 0) for s in range(seqs)], axis=1)
    ff_grad = ff_grad.reshape(shard, n_c, 3, cols)
    inner_gradient = jnp.moveaxis(ff_grad[:, :, :2], 1, 2).reshape(shard, 2, hidden)
    down_gradient = ff_grad[:, :, 2].reshape(shard, hidden).T
    folded = sums[16:, :head] + sums[16:, head:]
    return (
        block_out,
        input_gradient.reshape(size, seqs, width),
        attn_grad[:, :query_cols],
        attn_grad[:, query_cols : query_cols + 2 * pair_cols].reshape(shard, 2, pair_cols),
        attn_grad[:, query_cols + 2 * pair_cols :].T,
        inner_gradient,
        down_gradient,
        sums[:8].reshape(-1),
        folded[0],
        folded[1],
        sums[8:16].reshape(-1),
    )


def solution(mesh):
    return jax.shard_map(
        local,
        mesh=mesh,
        in_specs=(
            P("tensor", "dp", None),
            P("dp"),
            P("dp", "tensor"),
            P("dp", None, "tensor"),
            P("tensor", "dp"),
            P("dp", None, "tensor"),
            P("tensor", "dp"),
            P(),
            P(),
            P(),
            P(),
            P("tensor", "dp", None),
        ),
        out_specs=(
            P("tensor", "dp", None),
            P("tensor", "dp", None),
            P("dp", "tensor"),
            P("dp", None, "tensor"),
            P("tensor", "dp"),
            P("dp", None, "tensor"),
            P("tensor", "dp"),
            P(),
            P(),
            P(),
            P(),
        ),
        check_vma=False,
    )
```

```python
import functools

import jax
import jax.numpy as jnp
import numpy as np
from jax import lax
from jax.experimental import pallas as pl
from jax.experimental.pallas import tpu as pltpu
from jax.sharding import PartitionSpec as P

EPS = 1e-05
THETA = 1000000.0
LOG2E = 1.4426950408889634
F32 = jnp.float32
BF16 = jnp.bfloat16
HIGH = lax.Precision.HIGHEST
LANES = 128
VMEM_LIMIT = 56 * 1024 * 1024
DENSE_LIMIT = 62 * 1024 * 1024
ANY = pl.BlockSpec(memory_space=pl.ANY)
VMEM = pl.BlockSpec(memory_space=pltpu.VMEM)
SMEM = pl.BlockSpec(memory_space=pltpu.SMEM)


def dot(a, b, **kw):
    return lax.dot_general(
        a, b, (((1,), (0,)), ((), ())), preferred_element_type=F32, **kw
    )


def dot_nt(a, b, **kw):
    return lax.dot_general(
        a, b, (((1,), (1,)), ((), ())), preferred_element_type=F32, **kw
    )


def dot_tn(a, b, **kw):
    return lax.dot_general(
        a, b, (((0,), (0,)), ((), ())), preferred_element_type=F32, **kw
    )


def iota(shape, axis):
    return lax.broadcasted_iota(jnp.int32, shape, axis)


def low_half(shape):
    return iota(shape, 1) % LANES < LANES // 2


def head_blocks(scale):
    shape = (LANES, LANES)
    return jnp.where(iota(shape, 0) // 64 == iota(shape, 1) // 64, scale, 0.0).astype(F32)


def head_rows(scale):
    return jnp.where(iota((8, 256), 0) == iota((8, 256), 1) // 64, scale, 0.0).astype(F32)


def partner(values):
    first = iota(values.shape, 1) % 64 < 32
    return jnp.where(first, pltpu.roll(values, LANES - 32, 1), pltpu.roll(values, 32, 1))


def rows_of(index, size):
    return pl.ds(pl.multiple_of(index * size, size), size)


def load_all(sources, targets, sems, first):
    copies = []
    for number, (source, target) in enumerate(zip(sources, targets)):
        copy = pltpu.make_async_copy(source, target, sems.at[first + number])
        copy.start()
        copies.append(copy)
    return copies


def shard_targets(w_refs, ws, me):
    size = w_refs[0].shape[0]
    if len(w_refs) == 1:
        return [ws]
    return [ws.at[rows_of(me ^ slot, size)] for slot in range(len(w_refs))]


def store_slots(whole, out_refs, me):
    if len(out_refs) == 1:
        out_refs[0][...] = whole[...]
        return
    keep_ref, send_ref = out_refs
    size = keep_ref.shape[1]
    for slot in range(2 * keep_ref.shape[0]):
        (send_ref if slot % 2 else keep_ref)[slot // 2] = whole[rows_of(me ^ slot, size), :]


def padded_heads(first, second, low, g, e):
    here = low if e == 0 else jnp.logical_not(low)
    return jnp.where(here, first if g == e else second, 0.0).astype(BF16)


def project_rows(r, size, length, xs, ws, tabs, gains, raw_ref, q_ref, k_ref, v_ref, kp, vp):
    rows = rows_of(r, size)
    cos_ref, sin_ref = tabs
    gq_ref, gk_ref = gains
    mean_of = head_blocks(1.0 / 64)
    low = low_half((size, LANES))
    projected = dot(xs[rows, :], ws[:, :512])
    raw_ref[rows, :] = projected[:, :384]
    cosines, sines = cos_ref[rows, :], sin_ref[rows, :]

    def turned(values, gain):
        mean = dot(values * values, mean_of, precision=HIGH)
        normed = values * lax.rsqrt(mean + EPS) * gain
        return normed * cosines + partner(normed) * sines

    for g in range(2):
        lanes = slice(LANES * g, LANES * (g + 1))
        q_ref[rows, lanes] = turned(projected[:, lanes], gq_ref[...]).astype(BF16)
    keys = turned(projected[:, 256:384], gk_ref[...])
    values = projected[:, 384:512]
    k_ref[rows, :] = keys.astype(BF16)
    v_ref[rows, :] = values.astype(BF16)
    live = r * size + iota((size, LANES), 0) < length
    ones = jnp.where(live, 1.0, 0.0)
    values = jnp.where(live, values, 0.0)
    keys_swap, values_swap = pltpu.roll(keys, 64, 1), pltpu.roll(values, 64, 1)
    for g in range(2):
        for e in range(2):
            kp[2 * g + e, rows, :] = padded_heads(keys, keys_swap, low, g, e)
            vp[2 * g + e, rows, :LANES] = padded_heads(values, values_swap, low, g, e)
            vp[2 * g + e, rows, LANES:] = padded_heads(ones, ones, low, g, e)


def attend_rows(i, size, q_ref, kp, vp, acc, att_ref, lse_ref):
    rows = rows_of(i, size)
    factor = LOG2E / 8.0
    causal = iota((size, size), 1) <= iota((size, size), 0)
    queries = [q_ref[rows, LANES * g : LANES * (g + 1)] for g in range(2)]

    def block(kb, masked):
        cols = rows_of(kb, size)
        sums = []
        for g in range(2):
            total = None
            for e in range(2):
                weights = jnp.exp2(dot_nt(queries[g], kp[2 * g + e, cols, :]) * factor)
                if masked:
                    weights = jnp.where(causal, weights, 0.0)
                part = dot(weights.astype(BF16), vp[2 * g + e, cols, :])
                total = part if total is None else total + part
            sums.append(total)
        return sums

    for g, total in enumerate(block(i, True)):
        acc[g] = total

    def more(kb, carry):
        for g, total in enumerate(block(kb, False)):
            acc[g] += total
        return carry

    lax.fori_loop(0, i, more, 0)
    logs = []
    for g in range(2):
        lanes = slice(LANES * g, LANES * (g + 1))
        summed = acc[g, :, LANES:]
        att_ref[rows, lanes] = (acc[g, :, :LANES] / summed).astype(BF16)
        logs.append(jnp.log2(summed))
    lse_ref[:, rows] = dot_nt(head_rows(1.0 / 64), jnp.concatenate(logs, axis=1), precision=HIGH)


def attn_fwd_kernel(parts, n_w, scal, cos_ref, sin_ref, gq_ref, gk_ref, *refs):
    x_refs, refs = refs[:parts], refs[parts:]
    w_refs, refs = refs[:n_w], refs[n_w:]
    (raw_ref, q_ref, k_ref, v_ref, att_ref, lse_ref, keep_ref, send_ref, xs, ws, kp, vp, acc, sems) = refs
    size = x_refs[0].shape[0]
    me_t, me_d, length = scal[0], scal[1], scal[2]
    copies = load_all(w_refs, shard_targets(w_refs, ws, me_d), sems, 0)
    copies += load_all(x_refs, [xs.at[rows_of(me_t ^ j, size)] for j in range(parts)], sems, n_w)
    for copy in copies:
        copy.wait()

    def project(r, carry):
        project_rows(
            r, size, length, xs, ws, (cos_ref, sin_ref), (gq_ref, gk_ref), raw_ref, q_ref, k_ref, v_ref, kp, vp
        )
        return carry

    def attend(i, carry):
        attend_rows(i, size, q_ref, kp, vp, acc, att_ref, lse_ref)
        return carry

    lax.fori_loop(0, parts, project, 0)
    lax.fori_loop(0, parts, attend, 0)
    for j in range(parts):
        out = dot_nt(att_ref[rows_of(me_t ^ j, size), :], ws[:, 512:])
        (send_ref if j % 2 else keep_ref)[j // 2] = out.astype(BF16)


def attn_fwd(scal, cosines, sines, gq, gk, x_parts, w_parts):
    parts, n_w = len(x_parts), len(w_parts)
    size, width = x_parts[0].shape
    full = parts * size
    cols = w_parts[0].shape[1]
    pair = jax.ShapeDtypeStruct((parts // 2, size, width), BF16)
    return pl.pallas_call(
        functools.partial(attn_fwd_kernel, parts, n_w),
        out_shape=(
            jax.ShapeDtypeStruct((full, 384), F32),
            jax.ShapeDtypeStruct((full, 256), BF16),
            jax.ShapeDtypeStruct((full, 128), BF16),
            jax.ShapeDtypeStruct((full, 128), BF16),
            jax.ShapeDtypeStruct((full, 256), BF16),
            jax.ShapeDtypeStruct((8, full), F32),
            pair,
            pair,
        ),
        in_specs=[SMEM] + [VMEM] * 4 + [ANY] * (parts + n_w),
        out_specs=(VMEM,) * 8,
        scratch_shapes=[
            pltpu.VMEM((full, width), BF16),
            pltpu.VMEM((width, cols), BF16),
            pltpu.VMEM((4, full, LANES), BF16),
            pltpu.VMEM((4, full, 2 * LANES), BF16),
            pltpu.VMEM((2, size, 2 * LANES), F32),
            pltpu.SemaphoreType.DMA((n_w + parts,)),
        ],
        compiler_params=pltpu.CompilerParams(vmem_limit_bytes=VMEM_LIMIT),
        cost_estimate=pl.CostEstimate(flops=8_000_000_000, bytes_accessed=12_000_000, transcendentals=3_000_000),
        name="attention_forward",
    )(scal, cosines, sines, gq, gk, *x_parts, *w_parts)


def prepare_rows(r, size, length, gs, ws, k_ref, v_ref, att_ref, ga, drow, kp, kt, vp):
    rows = rows_of(r, size)
    low = low_half((size, LANES))
    grad = dot(gs[rows, :], ws[:, 512:]).astype(BF16)
    ga[rows, :] = grad
    drow[:, rows] = dot_nt(head_rows(1.0), grad.astype(F32) * att_ref[rows, :].astype(F32), precision=HIGH)
    live = r * size + iota((size, LANES), 0) < length
    keys = jnp.where(live, k_ref[rows, :].astype(F32), 0.0)
    values = jnp.where(live, v_ref[rows, :].astype(F32), 0.0)
    keys_swap, values_swap = pltpu.roll(keys, 64, 1), pltpu.roll(values, 64, 1)
    for g in range(2):
        for e in range(2):
            here = low if e == 0 else jnp.logical_not(low)
            padded = jnp.where(here, keys if g == e else keys_swap, 0.0)
            kp[2 * g + e, rows, :] = padded.astype(BF16)
            kt[2 * g + e, :, rows] = padded.T.astype(BF16)
            vp[2 * g + e, rows, :] = padded_heads(values, values_swap, low, g, e)


def sweep_rows(i, size, q_ref, ga, kp, kt, vp, drow, lrow, acc, dq, dk, dv):
    rows = rows_of(i, size)
    factor = LOG2E / 8.0
    causal = iota((size, size), 0) <= iota((size, size), 1)
    low2 = iota((2 * size, LANES), 0) // size == iota((2 * size, LANES), 1) // 64
    queries, grads, queries2, grads2 = [], [], [], []
    for g in range(2):
        lanes = slice(LANES * g, LANES * (g + 1))
        queries.append(q_ref[rows, lanes])
        grads.append(ga[rows, lanes])
        for source, target in ((queries, queries2), (grads, grads2)):
            both = jnp.concatenate([source[g], source[g]], axis=0)
            target.append(jnp.where(low2, both, jnp.zeros_like(both)))

    def block(kb, masked):
        cols = rows_of(kb, size)
        parts_t = []
        for g in range(2):
            weights2, scores2, turned = [], [], None
            for e in range(2):
                h = 2 * g + e
                weights = jnp.exp2(dot_nt(kp[h, cols, :], queries[g]) * factor - lrow[h : h + 1, rows])
                if masked:
                    weights = jnp.where(causal, weights, 0.0)
                grad_weights = dot_nt(vp[h, cols, :], grads[g])
                grad_scores = (weights * (grad_weights - drow[h : h + 1, rows])).astype(BF16)
                weights2.append(weights.astype(BF16))
                scores2.append(grad_scores)
                part = dot(kt[h, :, cols], grad_scores)
                turned = part if turned is None else turned + part
            dv[g, cols, :] += dot(jnp.concatenate(weights2, axis=1), grads2[g])
            dk[g, cols, :] += dot(jnp.concatenate(scores2, axis=1), queries2[g])
            parts_t.append(turned)
        return parts_t

    for g, total in enumerate(block(i, True)):
        acc[g] = total

    def more(kb, carry):
        for g, total in enumerate(block(kb, False)):
            acc[g] += total
        return carry

    lax.fori_loop(0, i, more, 0)
    for g in range(2):
        dq[rows, LANES * g : LANES * (g + 1)] = acc[g].T


def unproject_rows(r, size, length, tabs, gains, raw_ref, dq, dk, dv, gp, gains_ref):
    rows = rows_of(r, size)
    cosines, sines = tabs[0][rows, :], tabs[1][rows, :]
    low = low_half((size, LANES))
    mean_of = head_blocks(1.0 / 64)
    live = r * size + iota((size, LANES), 0) < length

    def back(grad, lanes, gain, row):
        raw = raw_ref[rows, lanes]
        rms = lax.rsqrt(dot(raw * raw, mean_of, precision=HIGH) + EPS)
        turned = grad * cosines - partner(grad) * sines
        gains_ref[row : row + 1, :] += jnp.sum(turned * raw * rms, axis=0, keepdims=True)
        weighted = turned * gain
        inner = dot(raw * weighted, mean_of, precision=HIGH)
        gp[rows, lanes] = (rms * weighted - raw * (rms * rms * rms) * inner).astype(BF16)

    def folded(ref):
        first, second = ref[0, rows, :], ref[1, rows, :]
        both = jnp.where(low, first + pltpu.roll(first, 64, 1), second + pltpu.roll(second, 64, 1))
        return jnp.where(live, both, 0.0)

    for g in range(2):
        lanes = slice(LANES * g, LANES * (g + 1))
        back(dq[rows, lanes] * 0.125, lanes, gains[0][...], 0)
    back(folded(dk) * 0.125, slice(256, 384), gains[1][...], 1)
    gp[rows, 384:512] = folded(dv).astype(BF16)


def attn_bwd_kernel(parts, n_w, scal, cos_ref, sin_ref, gq_ref, gk_ref, raw_ref, q_ref, k_ref, v_ref, att_ref, lse_ref, *refs):
    x_refs, refs = refs[:parts], refs[parts:]
    r_refs, refs = refs[:parts], refs[parts:]
    w_refs, refs = refs[:n_w], refs[n_w:]
    n_g = 1 if n_w == 1 else 2
    keep_ref, send_ref, gains_ref = refs[:3]
    g_refs, refs = refs[3 : 3 + n_g], refs[3 + n_g :]
    xs, gs, ws, kp, vp, kt, ga, dq, dk, dv, gp, whole, drow, acc, sems = refs
    size = x_refs[0].shape[0]
    me_t, me_d, length = scal[0], scal[1], scal[2]
    copies = load_all(w_refs, shard_targets(w_refs, ws, me_d), sems, 0)
    copies += load_all(r_refs, [gs.at[rows_of(me_t ^ j, size)] for j in range(parts)], sems, n_w)
    copies += load_all(x_refs, [xs.at[rows_of(me_t ^ j, size)] for j in range(parts)], sems, n_w + parts)
    for copy in copies:
        copy.wait()

    def prepare(r, carry):
        prepare_rows(r, size, length, gs, ws, k_ref, v_ref, att_ref, ga, drow, kp, kt, vp)
        return carry

    def sweep(i, carry):
        sweep_rows(i, size, q_ref, ga, kp, kt, vp, drow, lse_ref, acc, dq, dk, dv)
        return carry

    def unproject(r, carry):
        unproject_rows(r, size, length, (cos_ref, sin_ref), (gq_ref, gk_ref), raw_ref, dq, dk, dv, gp, gains_ref)
        return carry

    lax.fori_loop(0, parts, prepare, 0)
    dk[...] = jnp.zeros_like(dk)
    dv[...] = jnp.zeros_like(dv)
    lax.fori_loop(0, parts, sweep, 0)
    gains_ref[...] = jnp.zeros_like(gains_ref)
    lax.fori_loop(0, parts, unproject, 0)
    for j in range(parts):
        out = dot_nt(gp[rows_of(me_t ^ j, size), :], ws[:, :512])
        (send_ref if j % 2 else keep_ref)[j // 2] = out.astype(BF16)

    def weigh(b, carry):
        rows = rows_of(b, 256)
        whole[rows, :512] = dot_tn(xs[:, rows], gp[...]).astype(BF16)
        whole[rows, 512:] = dot_tn(gs[:, rows], att_ref[...]).astype(BF16)
        return carry

    lax.fori_loop(0, whole.shape[0] // 256, weigh, 0)
    store_slots(whole, g_refs, me_d)


def slot_shapes(n_w, width, cols):
    if n_w == 1:
        return (jax.ShapeDtypeStruct((width, cols), BF16),)
    return (jax.ShapeDtypeStruct((n_w // 2, width // n_w, cols), BF16),) * 2


def attn_bwd(scal, cosines, sines, gq, gk, saved, x_parts, r_parts, w_parts):
    parts, n_w = len(x_parts), len(w_parts)
    size, width = x_parts[0].shape
    full = parts * size
    cols = w_parts[0].shape[1]
    pair = jax.ShapeDtypeStruct((parts // 2, size, width), BF16)
    g_shapes = slot_shapes(n_w, width, cols)
    outs = pl.pallas_call(
        functools.partial(attn_bwd_kernel, parts, n_w),
        out_shape=(pair, pair, jax.ShapeDtypeStruct((8, LANES), F32)) + g_shapes,
        in_specs=[SMEM] + [VMEM] * 10 + [ANY] * (2 * parts + n_w),
        out_specs=(VMEM,) * (3 + len(g_shapes)),
        scratch_shapes=[
            pltpu.VMEM((full, width), BF16),
            pltpu.VMEM((full, width), BF16),
            pltpu.VMEM((width, cols), BF16),
            pltpu.VMEM((4, full, LANES), BF16),
            pltpu.VMEM((4, full, LANES), BF16),
            pltpu.VMEM((4, LANES, full), BF16),
            pltpu.VMEM((full, 256), BF16),
            pltpu.VMEM((full, 256), F32),
            pltpu.VMEM((2, full, LANES), F32),
            pltpu.VMEM((2, full, LANES), F32),
            pltpu.VMEM((full, 512), BF16),
            pltpu.VMEM((width, cols), BF16),
            pltpu.VMEM((8, full), F32),
            pltpu.VMEM((2, LANES, size), F32),
            pltpu.SemaphoreType.DMA((n_w + 2 * parts,)),
        ],
        compiler_params=pltpu.CompilerParams(vmem_limit_bytes=VMEM_LIMIT),
        cost_estimate=pl.CostEstimate(flops=14_000_000_000, bytes_accessed=15_000_000, transcendentals=3_000_000),
        name="attention_backward",
    )(scal, cosines, sines, gq, gk, *saved, *x_parts, *r_parts, *w_parts)
    return outs[0], outs[1], outs[2], outs[3:]


def ff_kernel(n_x, n_w, scal, *refs):
    x_refs, refs = refs[:n_x], refs[n_x:]
    u_refs, refs = refs[:n_x], refs[n_x:]
    w_refs, refs = refs[:n_w], refs[n_w:]
    n_g = 1 if n_w == 1 else 2
    hid_ref, ggu_ref = refs[:2]
    g_refs, refs = refs[2 : 2 + n_g], refs[2 + n_g :]
    xs, us, ws, whole, sems = refs
    size = x_refs[0].shape[0]
    me_d = scal[1]
    cols = ws.shape[1] // 3
    copies = load_all(w_refs, shard_targets(w_refs, ws, me_d), sems, 0)
    x_copies = load_all(x_refs, [xs.at[pl.ds(j * size, size)] for j in range(n_x)], sems, n_w)
    u_copies = load_all(u_refs, [us.at[pl.ds(j * size, size)] for j in range(n_x)], sems, n_w + n_x)
    for copy in copies + x_copies + u_copies:
        copy.wait()

    def tokens(r, carry):
        rows = rows_of(r, size)
        gate_up = dot(xs[rows, :], ws[:, : 2 * cols])
        grad = dot(us[rows, :], ws[:, 2 * cols :])
        gate, up = gate_up[:, :cols], gate_up[:, cols:]
        sig = 1.0 / (1.0 + jnp.exp2(gate * -LOG2E))
        silu = gate * sig
        hid_ref[rows, :] = (silu * up).astype(BF16)
        ggu_ref[rows, :cols] = (grad * up * (sig + silu * (1.0 - sig))).astype(BF16)
        ggu_ref[rows, cols:] = (grad * silu).astype(BF16)
        return carry

    lax.fori_loop(0, n_x, tokens, 0)

    def weigh(b, carry):
        rows = rows_of(b, 256)
        whole[rows, : 2 * cols] = dot_tn(xs[:, rows], ggu_ref[...]).astype(BF16)
        whole[rows, 2 * cols :] = dot_tn(us[:, rows], hid_ref[...]).astype(BF16)
        return carry

    lax.fori_loop(0, whole.shape[0] // 256, weigh, 0)
    store_slots(whole, g_refs, me_d)


def feed_forward(scal, x_parts, u_parts, w_parts):
    n_x, n_w = len(x_parts), len(w_parts)
    size, width = x_parts[0].shape
    full = n_x * size
    wide = w_parts[0].shape[1]
    cols = wide // 3
    g_shapes = slot_shapes(n_w, width, wide)
    outs = pl.pallas_call(
        functools.partial(ff_kernel, n_x, n_w),
        out_shape=(
            jax.ShapeDtypeStruct((full, cols), BF16),
            jax.ShapeDtypeStruct((full, 2 * cols), BF16),
        )
        + g_shapes,
        in_specs=[SMEM] + [ANY] * (2 * n_x + n_w),
        out_specs=(VMEM,) * (2 + len(g_shapes)),
        scratch_shapes=[
            pltpu.VMEM((full, width), BF16),
            pltpu.VMEM((full, width), BF16),
            pltpu.VMEM((width, wide), BF16),
            pltpu.VMEM((width, wide), BF16),
            pltpu.SemaphoreType.DMA((n_w + 2 * n_x,)),
        ],
        compiler_params=pltpu.CompilerParams(vmem_limit_bytes=VMEM_LIMIT),
        cost_estimate=pl.CostEstimate(flops=4 * full * width * wide, bytes_accessed=20_000_000, transcendentals=full * cols),
        name="feed_forward",
    )(scal, *x_parts, *u_parts, *w_parts)
    return outs[0], outs[1], outs[2:]


def ff_out_kernel(parts, n_c, n_w, seq, scal, *refs):
    hid_refs, refs = refs[:n_c], refs[n_c:]
    ggu_refs, refs = refs[:n_c], refs[n_c:]
    w_refs, refs = refs[: n_c * n_w], refs[n_c * n_w :]
    ykeep_ref, ysend_ref, gkeep_ref, gsend_ref, hs, gs, ws, sems = refs
    size = ykeep_ref.shape[1]
    full = parts * size
    me_d = scal[1]
    wide = ws.shape[2]
    cols = wide // 3
    copies = []
    first = 0
    for c in range(n_c):
        targets = shard_targets(w_refs[c * n_w : (c + 1) * n_w], ws.at[c], me_d)
        copies += load_all(w_refs[c * n_w : (c + 1) * n_w], targets, sems, first)
        first += n_w
    mine = pl.ds(seq * full, full)
    copies += load_all([ref.at[mine] for ref in ggu_refs], [gs.at[c] for c in range(n_c)], sems, first)
    copies += load_all([ref.at[mine] for ref in hid_refs], [hs.at[c] for c in range(n_c)], sems, first + n_c)
    for copy in copies:
        copy.wait()
    for j in range(parts):
        rows = pl.ds(j * size, size)
        grad = sum(dot_nt(gs[c, rows, :], ws[c, :, : 2 * cols]) for c in range(n_c))
        (gsend_ref if j % 2 else gkeep_ref)[j // 2] = grad.astype(BF16)
        out = sum(dot_nt(hs[c, rows, :], ws[c, :, 2 * cols :]) for c in range(n_c))
        (ysend_ref if j % 2 else ykeep_ref)[j // 2] = out.astype(BF16)


def ff_out(seq, scal, parts, size, hids, ggus, w_chunks):
    n_c, n_w = len(w_chunks), len(w_chunks[0])
    wide = w_chunks[0][0].shape[1]
    width = w_chunks[0][0].shape[0] * n_w
    full = parts * size
    cols = wide // 3
    pair = jax.ShapeDtypeStruct((parts // 2, size, width), BF16)
    return pl.pallas_call(
        functools.partial(ff_out_kernel, parts, n_c, n_w, seq),
        out_shape=(pair,) * 4,
        in_specs=[SMEM] + [ANY] * (2 * n_c + n_c * n_w),
        out_specs=(VMEM,) * 4,
        scratch_shapes=[
            pltpu.VMEM((n_c, full, cols), BF16),
            pltpu.VMEM((n_c, full, 2 * cols), BF16),
            pltpu.VMEM((n_c, width, wide), BF16),
            pltpu.SemaphoreType.DMA((n_c * n_w + 2 * n_c,)),
        ],
        compiler_params=pltpu.CompilerParams(vmem_limit_bytes=VMEM_LIMIT),
        cost_estimate=pl.CostEstimate(flops=2 * full * width * wide * n_c, bytes_accessed=22_000_000, transcendentals=0),
        name="feed_forward_out",
    )(scal, *hids, *ggus, *[shard for chunk in w_chunks for shard in chunk])


def flip(index, bits):
    for bit in (1, 2, 4):
        if bits & bit:
            index = index + bit - 2 * bit * lax.rem(lax.div(index, bit), 2)
    return index


def enter(me_d, me_t):
    barrier = pltpu.get_barrier_semaphore()
    devices = [{"dp": flip(me_d, bits)} for bits in (1, 2, 4, 6)]
    devices += [{"tensor": flip(me_t, bits)} for bits in (1, 2)]
    for device in devices:
        pl.semaphore_signal(barrier, inc=1, device_id=device, device_id_type=pl.DeviceIdType.MESH)
    return lambda: pl.semaphore_wait(barrier, len(devices))


def remote(source, target, sems, number, device):
    return pltpu.make_async_remote_copy(
        src_ref=source,
        dst_ref=target,
        send_sem=sems.at[0, number],
        recv_sem=sems.at[1, number],
        device_id=device,
        device_id_type=pl.DeviceIdType.MESH,
    )


class Remote:
    LIMIT = 64

    def __init__(self, sems):
        self.sems, self.used = sems, 0

    def __call__(self, source, target, device):
        assert self.used < self.LIMIT
        self.used += 1
        return remote(source, target, self.sems, self.used - 1, device)


class Local:
    LIMIT = 64

    def __init__(self, sems):
        self.sems, self.used = sems, 0

    def __call__(self, source, target):
        assert self.used < self.LIMIT
        copy = pltpu.make_async_copy(source, target, self.sems.at[self.used])
        self.used += 1
        copy.start()
        return copy


COPY_SEMS = [
    pltpu.SemaphoreType.DMA((2, Remote.LIMIT)),
    pltpu.SemaphoreType.DMA((Local.LIMIT,)),
]


class ShardGather:
    def __init__(self, shard, whole, send, me_d):
        size = shard.shape[0]
        mine = whole.at[rows_of(me_d, size)]
        self.own = [send(shard, mine, {"dp": flip(me_d, bits)}) for bits in (1, 2, 4, 6)]
        self.passed = []
        for bits in (2, 4, 6):
            there = whole.at[rows_of(flip(me_d, bits), size)]
            self.passed.append(send(there, there, {"dp": flip(me_d, 1)}))

    def start(self):
        for copy in self.own:
            copy.start()

    def forward(self, *which):
        for n in which or (0, 1, 2):
            self.own[1 + n].wait_recv()
            self.passed[n].start()

    def arrive(self):
        self.own[0].wait_recv()
        for copy in self.passed:
            copy.wait_recv()

    def drain(self):
        for copy in self.own + self.passed:
            copy.wait_send()


class TokenGather:
    def __init__(self, block, whole, send, me_t):
        size = block.shape[0]
        mine = whole.at[rows_of(me_t, size)]
        there = whole.at[rows_of(flip(me_t, 2), size)]
        near = {"tensor": flip(me_t, 1)}
        self.near = send(block, mine, near)
        self.far = send(block, mine, {"tensor": flip(me_t, 2)})
        self.passed = send(there, there, near)

    def start(self):
        self.far.start()
        self.near.start()

    def forward(self):
        self.far.wait_recv()
        self.passed.start()

    def arrive(self):
        self.near.wait_recv()
        self.passed.wait_recv()

    def drain(self):
        for copy in (self.near, self.far, self.passed):
            copy.wait_send()


class TokenReduce:
    def __init__(self, blocks, near, far, send, me_t, mine=None):
        device = {"tensor": flip(me_t, 1)}
        self.blocks, self.near_ref, self.far_ref, self.mine = blocks, near, far, mine
        self.places = (me_t, flip(me_t, 2))
        self.size = far.shape[0]
        self.near = [
            send(blocks.at[rows_of(flip(me_t, 1 + 2 * n), self.size)], near.at[n], device) for n in range(2)
        ]
        self.far = send(near.at[1], far, {"tensor": flip(me_t, 2)})

    def load(self, here):
        return [here(self.blocks.at[rows_of(place, self.size)], self.mine.at[n]) for n, place in enumerate(self.places)]

    def start(self, *which):
        for n in which or (1, 0):
            self.near[n].start()

    def part(self, n, rows):
        if self.mine is not None:
            return self.mine[n, rows, :].astype(F32)
        start = pl.multiple_of(self.places[n] * self.size + rows.start, 32)
        return self.blocks[pl.ds(start, rows.size), :].astype(F32)

    def middle(self):
        self.near[1].wait_recv()

        def step(rows):
            total = self.part(1, rows) + self.near_ref[1, rows, :].astype(F32)
            self.near_ref[1, rows, :] = total.astype(BF16)

        by_rows(self.size, 32, step)
        self.far.start()

    def arrive(self):
        self.near[0].wait_recv()
        self.far.wait_recv()

    def rows(self, rows):
        total = self.part(0, rows) + self.near_ref[0, rows, :].astype(F32)
        return total + self.far_ref[rows, :].astype(F32)

    def drain(self):
        for copy in self.near + [self.far]:
            copy.wait_send()


class ShardNear:
    def __init__(self, whole, near, out, send, me_d, mine=None):
        self.whole, self.near_ref, self.out, self.mine = whole, near, out, mine
        self.z, self.x = lax.div(me_d, 2), lax.rem(me_d, 2)
        self.size = near.shape[1]
        self.near = send(whole.at[:, 1 - self.x], near, {"dp": flip(me_d, 1)})

    def load(self, here):
        return [here(self.whole.at[:, self.x], self.mine)]

    def start(self):
        self.near.start()

    def part(self, there, rows):
        if self.mine is not None:
            return self.mine[there, rows, :].astype(F32)
        return self.whole[there, self.x, rows, :].astype(F32)

    def middle(self, far=None):
        self.near.wait_recv()
        for k in (1, 2, 3, 0):
            there = flip(self.z, k)

            def step(rows):
                total = self.part(there, rows) + self.near_ref[there, rows, :].astype(F32)
                if k:
                    self.near_ref[there, rows, :] = total.astype(BF16)
                else:
                    self.out[rows, :] = total

            by_rows(self.size, 32, step)
            if k and far is not None:
                far.far[k - 1].start()

    def drain(self):
        self.near.wait_send()


class ShardFar:
    def __init__(self, near, far, out, send, me_d):
        self.far_ref, self.out = far, out
        z = lax.div(me_d, 2)
        self.size = far.shape[1]
        self.far = [send(near.at[flip(z, k)], far.at[k - 1], {"dp": flip(me_d, 2 * k)}) for k in (1, 2, 3)]

    def start(self):
        for copy in self.far:
            copy.start()

    def finish(self):
        for copy in self.far:
            copy.wait_recv()

        def step(rows):
            total = self.out[rows, :]
            for k in range(3):
                total = total + self.far_ref[k, rows, :].astype(F32)
            self.out[rows, :] = total

        by_rows(self.size, 32, step)

    def drain(self):
        for copy in self.far:
            copy.wait_send()


def by_rows(count, step, body):
    def run(b, carry):
        body(rows_of(b, step))
        return carry

    lax.fori_loop(0, count // step, run, 0)


def loop(start, stop, body):
    def run(i, carry):
        body(i)
        return carry

    lax.fori_loop(start, stop, run, 0)


def rms_factor(values):
    return lax.rsqrt(jnp.mean(values * values, axis=-1, keepdims=True) + EPS)


def shape(dims, kind):
    return jax.ShapeDtypeStruct(dims, kind)


def forward_kernel(
    lengths, x_ref, aw_ref, up_ref, fw_ref, cos_ref, sin_ref, gq_ref, gk_ref, mg_ref, dg_ref,
    aw_out, fw_out, normed_out, up_out, dense_out, outb_out, raw_out, q_out, k_out, v_out, att_out, lse_out, resid_ref,
    xs, ws, kp, vp, acc, outp, near, far, dense, raw, q, k, v, att, lse, sems, local_sems,
):
    size, width = resid_ref.shape
    seqs, full = xs.shape[:2]
    parts = full // size
    n_c = fw_ref.shape[0]
    me_t, me_d = lax.axis_index("tensor"), lax.axis_index("dp")
    entered = enter(me_d, me_t)
    send, here = Remote(sems), Local(local_sems)
    mine_t, mine_d = rows_of(me_t, size), rows_of(me_d, aw_ref.shape[0])
    kept = ((raw, raw_out), (q, q_out), (k, k_out), (v, v_out), (att, att_out), (lse, lse_out))

    pro_w = ShardGather(aw_ref.at[:, :512], ws.at[:, :512], send, me_d)
    out_w = ShardGather(aw_ref.at[:, 512:], ws.at[:, 512:], send, me_d)
    ff_w = [ShardGather(fw_ref.at[c], fw_out.at[c], send, me_d) for c in range(n_c)]
    normed = [TokenGather(xs.at[s, mine_t], xs.at[s], send, me_t) for s in range(seqs)]
    ups = [TokenGather(up_ref.at[s], up_out.at[s], send, me_t) for s in range(seqs)]
    denses = TokenGather(dense, dense_out, send, me_t)
    outs = TokenReduce(outp.at[0], near, far, send, me_t)

    loads = [here(aw_ref, ws.at[mine_d])]
    stays = [here(up_ref.at[s], up_out.at[s, mine_t]) for s in range(seqs)]
    stays += [here(fw_ref.at[c], fw_out.at[c, mine_d]) for c in range(n_c)]

    def norm_first(s):
        def norm(rows):
            values = x_ref[rows, width * s : width * (s + 1)].astype(F32)
            target = pl.ds(pl.multiple_of(me_t * size + rows.start, 32), 32)
            xs[s, target, :] = (values * rms_factor(values) * mg_ref[...]).astype(BF16)

        by_rows(size, 32, norm)

    def project(s):
        loop(0, parts, lambda r: project_rows(
            r, size, lengths[s], xs.at[s], ws, (cos_ref, sin_ref), (gq_ref, gk_ref),
            raw.at[s], q.at[s], k.at[s], v.at[s], kp, vp,
        ))

    def attend(s, start, stop):
        loop(start, stop, lambda i: attend_rows(i, size, q.at[s], kp, vp, acc, att.at[s], lse.at[s]))

    def out_block(s, bits):
        rows = rows_of(flip(me_t, bits), size)
        outp[s, rows, :] = dot_nt(att[s, rows, :], ws[:, 512:]).astype(BF16)

    def after():
        outs.arrive()

        def norm(rows):
            values = x_ref[rows, :width].astype(F32) + outs.rows(rows)
            resid_ref[rows, :] = values
            dense[rows, :] = (values * rms_factor(values) * dg_ref[...]).astype(BF16)

        by_rows(size, 32, norm)
        denses.start()
        stays.append(here(dense, dense_out.at[mine_t]))

    norm_first(0)
    entered()
    normed[0].start()
    pro_w.start()
    norm_first(1)
    pro_w.forward()
    normed[0].forward()
    normed[1].start()
    out_w.start()
    normed[0].arrive()
    for copy in loads:
        copy.wait()
    pro_w.arrive()
    project(0)
    out_w.forward()
    ff_w[0].start()
    attend(0, 0, 3)
    normed[1].forward()
    for s in range(seqs):
        ups[s].start()
    attend(0, 3, parts)
    out_w.arrive()
    for n, bits in enumerate((3, 1, 2, 0)):
        out_block(0, bits)
        if n < 2:
            outs.start(1 - n)
    stays.append(here(ws, aw_out))
    stays += [here(source.at[0], target.at[0]) for source, target in kept]
    outs.middle()
    ff_w[0].forward()
    ff_w[1].start()
    normed[1].arrive()
    project(1)
    attend(1, 0, 2)
    for s in range(seqs):
        ups[s].forward()
    after()
    attend(1, 2, parts)
    stays += [here(source.at[1], target.at[1]) for source, target in kept]
    stays += [here(xs.at[s], normed_out.at[s]) for s in range(seqs)]
    ff_w[1].forward()
    for bits in (0, 1, 2, 3):
        out_block(1, bits)
    stays.append(here(outp.at[1], outb_out))
    denses.forward()
    for exchange in ff_w + ups + [denses]:
        exchange.arrive()
    for copy in stays:
        copy.wait()
    for exchange in [pro_w, out_w] + ff_w + normed + ups + [denses, outs]:
        exchange.drain()


def fused_forward(lengths, x, aw, up, fw, tabs, gains):
    seqs, size, width = up.shape
    full = 4 * size
    shard, cols = aw.shape
    n_c, _, wide = fw.shape
    dp = 8
    kept = [
        ((seqs, full, 384), F32),
        ((seqs, full, 256), BF16),
        ((seqs, full, 128), BF16),
        ((seqs, full, 128), BF16),
        ((seqs, full, 256), BF16),
        ((seqs, 8, full), F32),
    ]
    return pl.pallas_call(
        forward_kernel,
        out_shape=(
            shape((dp * shard, cols), BF16),
            shape((n_c, dp * shard, wide), BF16),
            shape((seqs, full, width), BF16),
            shape((seqs, full, width), BF16),
            shape((full, width), BF16),
            shape((full, width), BF16),
        )
        + tuple(shape(*item) for item in kept)
        + (shape((size, width), F32),),
        in_specs=[SMEM, VMEM] + [ANY] * 3 + [VMEM] * 6,
        out_specs=(ANY,) * 12 + (VMEM,),
        scratch_shapes=[
            pltpu.VMEM((seqs, full, width), BF16),
            pltpu.VMEM((dp * shard, cols), BF16),
            pltpu.VMEM((4, full, LANES), BF16),
            pltpu.VMEM((4, full, 2 * LANES), BF16),
            pltpu.VMEM((2, size, 2 * LANES), F32),
            pltpu.VMEM((seqs, full, width), BF16),
            pltpu.VMEM((2, size, width), BF16),
            pltpu.VMEM((size, width), BF16),
            pltpu.VMEM((size, width), BF16),
        ]
        + [pltpu.VMEM(*item) for item in kept]
        + COPY_SEMS,
        compiler_params=pltpu.CompilerParams(
            vmem_limit_bytes=VMEM_LIMIT, collective_id=0, has_side_effects=True
        ),
        cost_estimate=pl.CostEstimate(flops=16_000_000_000, bytes_accessed=40_000_000, transcendentals=6_000_000),
        name="forward",
    )(lengths, x, aw, up, fw, *tabs, *gains)


def dense_kernel(
    x_ref, xa_ref, u_ref, outb_ref, fw_ref, last_ref, up_ref, resa_ref, dg_ref,
    ra_out, gb_out, y_out, wn_out, w_out, gresa_ref, resb_ref, dgain_ref, own_ref,
    xs, us, ws, hid, ggu, whole, wnear, blocks, bnear, bfar, bmine, gnear, gfar, low_grad, sems, local_sems,
):
    size, width = resa_ref.shape
    full = xa_ref.shape[0]
    parts = full // size
    early = fw_ref.shape[0]
    n_c = early + 1
    wide = ws.shape[2]
    cols = wide // 3
    me_t, me_d = lax.axis_index("tensor"), lax.axis_index("dp")
    entered = enter(me_d, me_t)
    send, here = Remote(sems), Local(local_sems)
    first, second = pl.ds(0, full), pl.ds(full, full)
    mine_b = rows_of(parts + me_t, size)

    outs = TokenReduce(outb_ref, bnear, bfar, send, me_t, bmine)
    denses = TokenGather(xs.at[mine_b], xs.at[second], send, me_t)
    grads = TokenReduce(blocks, gnear, gfar, send, me_t)
    resids = TokenGather(low_grad, ra_out, send, me_t)
    last_w = ShardGather(last_ref, ws.at[early], send, me_d)
    weights = ShardNear(whole.at[0], wnear, own_ref, send, me_d)

    loads = [here(fw_ref.at[0], ws.at[0]), here(xa_ref, xs.at[first]), here(u_ref.at[0], us.at[first])]
    loads_b = outs.load(here)
    loads_1 = [here(fw_ref.at[1], ws.at[1])]
    loads_u = [here(u_ref.at[1], us.at[second])]
    stays = [here(last_ref, ws.at[early, rows_of(me_d, last_ref.shape[0])])]

    def tokens(c, s):
        def run(r):
            rows = rows_of(r, size)
            gate_up = dot(xs[rows, :], ws[c, :, : 2 * cols])
            grad = dot(us[rows, :], ws[c, :, 2 * cols :])
            gate, up = gate_up[:, :cols], gate_up[:, cols:]
            sig = 1.0 / (1.0 + jnp.exp2(gate * -LOG2E))
            silu = gate * sig
            hid[c, rows, :] = (silu * up).astype(BF16)
            ggu[c, rows, :cols] = (grad * up * (sig + silu * (1.0 - sig))).astype(BF16)
            ggu[c, rows, cols:] = (grad * silu).astype(BF16)

        loop(s * parts, (s + 1) * parts, run)

    def weigh(c):
        def run(b):
            rows = rows_of(b, 256)
            dims = whole.shape[2:4]
            inner = dot_tn(xs[:, rows], ggu[c]).astype(BF16)
            whole[c, b, :, :, : 2 * cols] = inner.reshape(dims + (2 * cols,))
            down = dot_tn(us[:, rows], hid[c]).astype(BF16)
            whole[c, b, :, :, 2 * cols :] = down.reshape(dims + (cols,))

        loop(0, whole.shape[1], run)

    def grad_block(s, block, target):
        rows = rows_of(s * parts + block, size)
        total = sum(dot_nt(ggu[c, rows, :], ws[c, :, : 2 * cols]) for c in range(n_c))
        target[rows_of(block, size), :] = total.astype(BF16)

    def out_block(r):
        rows = rows_of(r, size)
        total = sum(dot_nt(hid[c, rows, :], ws[c, :, 2 * cols :]) for c in range(n_c))
        us[rows, :] = total.astype(BF16)

    def after_out():
        outs.arrive()

        def norm(rows):
            values = x_ref[rows, width:].astype(F32) + outs.rows(rows)
            resb_ref[rows, :] = values
            target = pl.ds(pl.multiple_of((parts + me_t) * size + rows.start, 32), 32)
            xs[target, :] = (values * rms_factor(values) * dg_ref[...]).astype(BF16)

        by_rows(size, 32, norm)
        denses.start()

    def after_grad():
        grads.arrive()
        dgain_ref[...] = jnp.zeros_like(dgain_ref)
        by_rows(size, 32, lambda rows: residual_back(
            rows, grads, resa_ref, up_ref.at[0], dg_ref, dgain_ref, gresa_ref, low_grad
        ))
        resids.start()
        stays.append(here(low_grad, ra_out.at[rows_of(me_t, size)]))

    entered()
    outs.start()
    last_w.start()
    for copy in loads:
        copy.wait()
    tokens(0, 0)
    for copy in loads_b:
        copy.wait()
    outs.middle()
    last_w.forward(0)
    for copy in loads_1:
        copy.wait()
    tokens(1, 0)
    after_out()
    last_w.forward(1, 2)
    denses.forward()
    last_w.arrive()
    for copy in stays:
        copy.wait()
    stays = []
    tokens(2, 0)
    for n, bits in enumerate((3, 1, 2, 0)):
        grad_block(0, flip(me_t, bits), blocks)
        if n < 2:
            grads.start(1 - n)
    denses.arrive()
    for copy in loads_u:
        copy.wait()
    tokens(0, 1)
    grads.middle()
    weigh(0)
    weights.start()
    tokens(1, 1)
    weigh(1)
    after_grad()
    stays.append(here(whole.at[1], w_out.at[0]))
    tokens(2, 1)
    weigh(2)
    resids.forward()
    stays.append(here(whole.at[2], w_out.at[1]))
    denses.drain()
    loop(0, parts, lambda r: grad_block(1, r, xs.at[second]))
    stays.append(here(xs.at[second], gb_out))
    loop(0, 2 * parts, out_block)
    stays += [here(us.at[first], y_out.at[0]), here(us.at[second], y_out.at[1])]
    weights.middle()
    stays.append(here(wnear, wn_out))
    resids.arrive()
    for copy in stays:
        copy.wait()
    for exchange in (outs, grads, resids, last_w, weights):
        exchange.drain()


def residual_back(rows, grads, resid_ref, up_ref, dg_ref, dgain_ref, gres_ref, low_ref):
    grad = grads.rows(rows)
    values = resid_ref[rows, :]
    factor = rms_factor(values)
    product = grad * values * factor
    dgain_ref[...] += jnp.sum(product.reshape(-1, 8, values.shape[1]), axis=0)
    weighted = grad * dg_ref[...]
    inner = jnp.mean(values * weighted, axis=-1, keepdims=True)
    total = up_ref[rows, :].astype(F32) + factor * weighted - values * (factor * factor * factor) * inner
    gres_ref[rows, :] = total
    low_ref[rows, :] = total.astype(BF16)


def fused_dense(x, dense, ups, outb, fw, last, upstream, resid, dense_gain):
    seqs, size, width = upstream.shape
    full = dense.shape[0]
    shard, wide = last.shape
    early = fw.shape[0]
    n_c = early + 1
    cols = wide // 3
    tokens = seqs * full
    return pl.pallas_call(
        dense_kernel,
        out_shape=(
            shape((full, width), BF16),
            shape((full, width), BF16),
            shape((seqs, full, width), BF16),
            shape((4, shard, wide), BF16),
            shape((n_c - 1, 4, 2, shard, wide), BF16),
            shape((size, width), F32),
            shape((size, width), F32),
            shape((8, width), F32),
            shape((shard, wide), F32),
        ),
        in_specs=[VMEM] + [ANY] * 5 + [VMEM] * 3,
        out_specs=(ANY,) * 5 + (VMEM,) * 4,
        scratch_shapes=[
            pltpu.VMEM((tokens, width), BF16),
            pltpu.VMEM((tokens, width), BF16),
            pltpu.VMEM((n_c, width, wide), BF16),
            pltpu.VMEM((n_c, tokens, cols), BF16),
            pltpu.VMEM((n_c, tokens, 2 * cols), BF16),
            pltpu.VMEM((n_c, 4, 2, shard, wide), BF16),
            pltpu.VMEM((4, shard, wide), BF16),
            pltpu.VMEM((full, width), BF16),
            pltpu.VMEM((2, size, width), BF16),
            pltpu.VMEM((size, width), BF16),
            pltpu.VMEM((2, size, width), BF16),
            pltpu.VMEM((2, size, width), BF16),
            pltpu.VMEM((size, width), BF16),
            pltpu.VMEM((size, width), BF16),
        ]
        + COPY_SEMS,
        compiler_params=pltpu.CompilerParams(
            vmem_limit_bytes=DENSE_LIMIT, collective_id=1, has_side_effects=True
        ),
        cost_estimate=pl.CostEstimate(flops=6 * tokens * width * wide * n_c, bytes_accessed=40_000_000, transcendentals=tokens * cols * n_c),
        name="feed_forward",
    )(x, dense, ups, outb, fw, last, upstream, resid, dense_gain)


def backward_kernel(
    lengths, n_ref, ra_ref, aw_ref, gb_ref, y_ref, wn_ref, w_ref, own_ref, gresa_ref, raw_ref, q_ref, k_ref, v_ref, att_ref, lse_ref,
    x_ref, up_ref, resa_ref, resb_ref, dgain_ref, cos_ref, sin_ref, gq_ref, gk_ref, mg_ref, dg_ref,
    ig_ref, blk_ref, awg_ref, ffg_ref, sums_ref,
    xs, gs, ws, kp, vp, kt, ga, dq, dk, dv, gp, drow, acc, gains, mixer, dgain,
    raw, q, k, v, att, lse,
    wo, wo_near, wo_far, wp, wp_near, wp_far, wf_near, wf_far, wf_mine,
    blocks, near, far, gnear, gfar, gmine, ynear, yfar, ymine, put, got, sems, local_sems,
):
    size, width = resa_ref.shape
    seqs, full = n_ref.shape[:2]
    parts = full // size
    n_late = w_ref.shape[0]
    wide = wn_ref.shape[2]
    me_t, me_d = lax.axis_index("tensor"), lax.axis_index("dp")
    entered = enter(me_d, me_t)
    send, here = Remote(sems), Local(local_sems)
    mine_t = rows_of(me_t, size)
    resid_refs = (resa_ref, resb_ref)

    late = TokenReduce(gb_ref, gnear, gfar, send, me_t, gmine)
    resids = TokenGather(gs.at[1, mine_t], gs.at[1], send, me_t)
    outs = [TokenReduce(y_ref.at[s], ynear.at[s], yfar.at[s], send, me_t, ymine.at[s]) for s in range(seqs)]
    places = (blocks, gs.at[0])
    grads = [TokenReduce(places[s], near.at[s], far.at[s], send, me_t) for s in range(seqs)]
    sums = [ffg_ref.at[:, wide * c : wide * (c + 1)] for c in range(n_late + 1)]
    ff_near = [
        ShardNear(w_ref.at[c], wf_near.at[c], sums[c + 1], send, me_d, wf_mine) for c in range(n_late)
    ]
    ff_far = [
        ShardFar(wn_ref if c == 0 else wf_near.at[c - 1], wf_far.at[c], sums[c], send, me_d)
        for c in range(n_late + 1)
    ]
    out_near = ShardNear(wo, wo_near, awg_ref.at[:, 512:], send, me_d)
    out_far = ShardFar(wo_near, wo_far, awg_ref.at[:, 512:], send, me_d)
    pro_near = ShardNear(wp, wp_near, awg_ref.at[:, :512], send, me_d)
    pro_far = ShardFar(wp_near, wp_far, awg_ref.at[:, :512], send, me_d)
    steps = []
    for n, (axis, bits) in enumerate((("tensor", 1), ("tensor", 2), ("dp", 1), ("dp", 2), ("dp", 4))):
        device = {axis: flip(me_t if axis == "tensor" else me_d, bits)}
        steps.append(send(put.at[n], got.at[n], device))

    kept = ((k_ref, k), (v_ref, v), (att_ref, att), (lse_ref, lse), (q_ref, q))
    load_w = [here(aw_ref, ws), here(ra_ref, gs.at[0])]
    load_s = [[here(source.at[s], target.at[s]) for source, target in kept] for s in range(seqs)]
    load_raw = [here(raw_ref.at[0], raw)]
    load_late = late.load(here)
    load_f = ff_near[0].load(here)
    load_y = [exchange.load(here) for exchange in outs]
    load_x = [here(n_ref.at[s], xs.at[s]) for s in range(seqs)]
    load_own = [here(own_ref, sums[0]), here(gresa_ref, ig_ref.at[:, :width])]
    gains[...] = jnp.zeros_like(gains)
    mixer[...] = jnp.zeros_like(mixer)
    dgain[...] = dgain_ref[...]

    def wait(copies):
        for copy in copies:
            copy.wait()

    def prepare(s):
        loop(0, parts, lambda r: prepare_rows(
            r, size, lengths[s], gs.at[s], ws, k.at[s], v.at[s], att.at[s], ga, drow, kp, kt, vp
        ))
        dk[...] = jnp.zeros_like(dk)
        dv[...] = jnp.zeros_like(dv)

    def sweep(s, start, stop):
        loop(start, stop, lambda i: sweep_rows(i, size, q.at[s], ga, kp, kt, vp, drow, lse.at[s], acc, dq, dk, dv))

    def unproject(s):
        loop(0, parts, lambda r: unproject_rows(
            r, size, lengths[s], (cos_ref, sin_ref), (gq_ref, gk_ref), raw, dq, dk, dv, gp.at[s], gains
        ))

    def grad_blocks(s):
        for n, bits in enumerate((3, 1, 2, 0)):
            rows = rows_of(flip(me_t, bits), size)
            places[s][rows, :] = dot_nt(gp[s, rows, :], ws[:, :512]).astype(BF16)
            if n < 2:
                grads[s].start(1 - n)

    def weigh(target, lefts, rights):
        def run(b):
            rows = rows_of(b, 256)
            total = sum(dot_tn(lefts[s, :, rows], rights[s]) for s in range(seqs))
            target[b] = total.astype(BF16).reshape(target.shape[1:])

        loop(0, target.shape[0], run)

    def after_late():
        late.arrive()
        by_rows(size, 32, lambda rows: residual_back(
            rows, late, resb_ref, up_ref.at[1], dg_ref, dgain, ig_ref.at[:, width:], gs.at[1, mine_t]
        ))
        resids.start()

    def after_out(s):
        outs[s].arrive()

        def step(rows):
            total = resid_refs[s][rows, :] + outs[s].rows(rows)
            blk_ref[rows, width * s : width * (s + 1)] = total.astype(BF16)

        by_rows(size, 32, step)

    def after(s):
        grads[s].arrive()
        lanes = slice(width * s, width * (s + 1))

        def step(rows):
            grad = grads[s].rows(rows)
            values = x_ref[rows, lanes].astype(F32)
            factor = rms_factor(values)
            product = grad * values * factor
            mixer[...] += jnp.sum(product.reshape(-1, 8, width), axis=0)
            weighted = grad * mg_ref[...]
            inner = jnp.mean(values * weighted, axis=-1, keepdims=True)
            ig_ref[rows, lanes] += factor * weighted - values * (factor * factor * factor) * inner

        by_rows(size, 32, step)

    entered()
    late.start()
    ff_far[0].start()
    ff_near[0].start()
    wait(load_w + load_s[0])
    prepare(0)
    wait(load_late)
    late.middle()
    for exchange in outs:
        exchange.start()
    sweep(0, 0, 3)
    after_late()
    sweep(0, 3, parts)
    wait(load_y[0])
    outs[0].middle()
    wait(load_raw)
    unproject(0)
    load_raw = [here(raw_ref.at[1], raw)]
    grad_blocks(0)
    wait(load_f)
    ff_near[0].middle(ff_far[1])
    load_f = ff_near[1].load(here)
    ff_near[1].start()
    resids.forward()
    grads[0].middle()
    resids.arrive()
    wait(load_s[1])
    prepare(1)
    weigh(wo, gs, att)
    out_near.start()
    sweep(1, 0, 3)
    wait(load_y[1])
    outs[1].middle()
    after_out(0)
    wait(load_own)
    after(0)
    ff_far[0].finish()
    sweep(1, 3, parts)
    wait(load_raw)
    unproject(1)
    wait(load_x)
    weigh(wp, xs, gp)
    pro_near.start()
    grad_blocks(1)
    grads[1].middle()
    wait(load_f)
    ff_near[1].middle(ff_far[2])
    out_near.middle(out_far)
    after_out(1)
    ff_far[1].finish()
    pro_near.middle(pro_far)
    after(1)
    for row, vector in ((0, mixer), (8, dgain)):
        total = jnp.sum(vector[...], axis=0, keepdims=True)
        for i in range(8):
            put[0, row + i : row + i + 1, :] = total[:, LANES * i : LANES * (i + 1)]
    put[0, 16:, :] = gains[...]
    for n, copy in enumerate(steps):
        copy.start()
        copy.wait_recv()
        total = put[n] + got[n]
        if n + 1 < len(steps):
            put[n + 1] = total
        else:
            sums_ref[...] = total
    ff_far[2].finish()
    out_far.finish()
    pro_far.finish()
    for copy in steps:
        copy.wait_send()
    for exchange in [late, resids, out_near, out_far, pro_near, pro_far] + outs + grads + ff_near + ff_far:
        exchange.drain()


def fused_backward(lengths, in_hbm, in_vmem):
    normed, aw, w = in_hbm[0], in_hbm[2], in_hbm[6]
    size, width = in_vmem[2].shape
    seqs, full = normed.shape[:2]
    cols = aw.shape[1]
    shard = aw.shape[0] // 8
    n_late, wide = w.shape[0], w.shape[4]
    kept = [
        ((full, 384), F32),
        ((seqs, full, 256), BF16),
        ((seqs, full, 128), BF16),
        ((seqs, full, 128), BF16),
        ((seqs, full, 256), BF16),
        ((seqs, 8, full), F32),
    ]
    return pl.pallas_call(
        backward_kernel,
        out_shape=(
            shape((size, seqs * width), F32),
            shape((size, seqs * width), BF16),
            shape((shard, cols), F32),
            shape((shard, (n_late + 1) * wide), F32),
            shape((24, LANES), F32),
        ),
        in_specs=[SMEM] + [ANY] * len(in_hbm) + [VMEM] * len(in_vmem),
        out_specs=(VMEM,) * 5,
        scratch_shapes=[
            pltpu.VMEM((seqs, full, width), BF16),
            pltpu.VMEM((seqs, full, width), BF16),
            pltpu.VMEM((width, cols), BF16),
            pltpu.VMEM((4, full, LANES), BF16),
            pltpu.VMEM((4, full, LANES), BF16),
            pltpu.VMEM((4, LANES, full), BF16),
            pltpu.VMEM((full, 256), BF16),
            pltpu.VMEM((full, 256), F32),
            pltpu.VMEM((2, full, LANES), F32),
            pltpu.VMEM((2, full, LANES), F32),
            pltpu.VMEM((seqs, full, 512), BF16),
            pltpu.VMEM((8, full), F32),
            pltpu.VMEM((2, LANES, size), F32),
            pltpu.VMEM((8, LANES), F32),
            pltpu.VMEM((8, width), F32),
            pltpu.VMEM((8, width), F32),
        ]
        + [pltpu.VMEM(*item) for item in kept]
        + [
            pltpu.VMEM((4, 2, shard, 256), BF16),
            pltpu.VMEM((4, shard, 256), BF16),
            pltpu.VMEM((3, shard, 256), BF16),
            pltpu.VMEM((4, 2, shard, 512), BF16),
            pltpu.VMEM((4, shard, 512), BF16),
            pltpu.VMEM((3, shard, 512), BF16),
            pltpu.VMEM((n_late, 4, shard, wide), BF16),
            pltpu.VMEM((n_late + 1, 3, shard, wide), BF16),
            pltpu.VMEM((4, shard, wide), BF16),
            pltpu.VMEM((full, width), BF16),
            pltpu.VMEM((seqs, 2, size, width), BF16),
            pltpu.VMEM((seqs, size, width), BF16),
            pltpu.VMEM((2, size, width), BF16),
            pltpu.VMEM((size, width), BF16),
            pltpu.VMEM((2, size, width), BF16),
            pltpu.VMEM((seqs, 2, size, width), BF16),
            pltpu.VMEM((seqs, size, width), BF16),
            pltpu.VMEM((seqs, 2, size, width), BF16),
            pltpu.VMEM((5, 24, LANES), F32),
            pltpu.VMEM((5, 24, LANES), F32),
        ]
        + COPY_SEMS,
        compiler_params=pltpu.CompilerParams(
            vmem_limit_bytes=DENSE_LIMIT, collective_id=2, has_side_effects=True
        ),
        cost_estimate=pl.CostEstimate(flops=28_000_000_000, bytes_accessed=40_000_000, transcendentals=6_000_000),
        name="backward",
    )(lengths, *in_hbm, *in_vmem)


def swap(values, axis, bits):
    return lax.ppermute(values, axis, [(i, i ^ bits) for i in range(lax.axis_size(axis))])


def gather_tokens(block):
    far = swap(block, "tensor", 2)
    return [block, swap(block, "tensor", 1), far, swap(far, "tensor", 1)]


def scatter_tokens(keep, send):
    near = swap(send, "tensor", 1)
    middle = (keep[1].astype(F32) + near[1].astype(F32)).astype(BF16)
    far = swap(middle, "tensor", 2)
    return keep[0].astype(F32) + near[0].astype(F32) + far.astype(F32)


def gather_shards(shard):
    if lax.axis_size("dp") != 8 or shard.shape[0] % LANES:
        return [lax.all_gather(shard, "dp", axis=0, tiled=True)]
    slots = [shard, swap(shard, "dp", 1)]
    for bits in (2, 4, 6):
        there = swap(shard, "dp", bits)
        slots += [there, swap(there, "dp", 1)]
    return slots


def scatter_shards(grads):
    if len(grads) == 1:
        return lax.psum_scatter(grads[0].astype(F32), "dp", scatter_dimension=0, tiled=True)
    keep, send = grads
    near = swap(send, "dp", 1)
    both = keep.astype(F32) + near.astype(F32)
    total = both[0]
    for slot in (1, 2, 3):
        total = total + swap(both[slot].astype(BF16), "dp", 2 * slot).astype(F32)
    return total


def sum_everywhere(values):
    for axis in ("tensor", "dp"):
        bits = 1
        while bits < lax.axis_size(axis):
            values = values + swap(values, axis, bits)
            bits *= 2
    return values


def norm_rows(values, gain):
    factor = lax.rsqrt(jnp.mean(values * values, axis=-1, keepdims=True) + EPS)
    return (values * factor * gain, factor)


def norm_back(values, factor, gain, upstream):
    weighted = upstream * gain
    inner = jnp.mean(values * weighted, axis=-1, keepdims=True)
    return factor * weighted - values * factor * factor * factor * inner


def tables(full, head_width):
    half = head_width // 2
    freqs = THETA ** (-jnp.arange(half, dtype=F32) * 2.0 / head_width)
    angles = jnp.arange(full, dtype=F32)[:, None] * freqs[None, :]
    cosines, sines = jnp.cos(angles), jnp.sin(angles)
    return (jnp.tile(cosines, (1, 4)), jnp.tile(jnp.concatenate([-sines, sines], axis=1), (1, 2)))


def local_plain(
    inputs,
    lengths,
    query_weight,
    key_value_weight,
    output_weight,
    inner_weight,
    down_weight,
    mixer_gain,
    query_gain,
    key_gain,
    dense_gain,
    cotangent,
):
    size, seqs, width = inputs.shape
    parts = lax.axis_size("tensor")
    full = size * parts
    head = query_gain.shape[0]
    query_cols = query_weight.shape[1]
    pair_cols = key_value_weight.shape[2]
    hidden = inner_weight.shape[2]
    shard = query_weight.shape[0]
    me_t, me_d = lax.axis_index("tensor"), lax.axis_index("dp")
    n_c = 3
    cols = hidden // n_c
    cosines, sines = tables(full, head)
    gq = jnp.tile(query_gain, 2)[None, :]
    gk = jnp.tile(key_gain, 2)[None, :]

    down_turned = down_weight.T
    attn_shard = jnp.concatenate(
        [query_weight, key_value_weight.reshape(shard, 2 * pair_cols), output_weight.T], axis=1
    )
    attn_w = gather_shards(attn_shard)
    positions = me_t * size + jnp.arange(size, dtype=jnp.int32)
    scals = [
        jnp.stack([me_t.astype(jnp.int32), me_d.astype(jnp.int32), lengths[s], jnp.int32(0)])
        for s in range(seqs)
    ]
    tokens = [inputs[:, s].astype(F32) for s in range(seqs)]
    valid = [(positions < lengths[s])[:, None] for s in range(seqs)]
    firsts = [norm_rows(tokens[s], mixer_gain) for s in range(seqs)]
    normed = [gather_tokens(firsts[s][0].astype(BF16)) for s in range(seqs)]
    ff_w = []
    for c in range(n_c):
        part = slice(c * cols, (c + 1) * cols)
        ff_w.append(
            gather_shards(
                jnp.concatenate(
                    [inner_weight[:, 0, part], inner_weight[:, 1, part], down_turned[:, part]], axis=1
                )
            )
        )
    upstream = [jnp.where(valid[s], cotangent[:, s].astype(F32), 0.0) for s in range(seqs)]
    up_parts = [gather_tokens(upstream[s].astype(BF16)) for s in range(seqs)]

    saved, residual, seconds, dense = [], [], [], []
    for s in range(seqs):
        outs = attn_fwd(scals[s], cosines, sines, gq, gk, normed[s], attn_w)
        saved.append(outs[:6])
        residual.append(tokens[s] + scatter_tokens(outs[6], outs[7]))
        dense_in, factor = norm_rows(residual[s], dense_gain)
        seconds.append(factor)
        dense.append(gather_tokens(dense_in.astype(BF16)))

    x_parts = [part for s in range(seqs) for part in dense[s]]
    u_parts = [part for s in range(seqs) for part in up_parts[s]]
    hids, ggus, ff_grads = [], [], []
    for c in range(n_c):
        hid, ggu, grads = feed_forward(scals[0], x_parts, u_parts, ff_w[c])
        hids.append(hid)
        ggus.append(ggu)
        ff_grads.append(scatter_shards(grads))

    block_out, input_gradient, attn_grads = [], [], []
    mixer_part = dense_part = gain_part = 0.0
    for s in range(seqs):
        ykeep, ysend, gkeep, gsend = ff_out(s, scals[s], parts, size, hids, ggus, ff_w)
        grad_dense = scatter_tokens(gkeep, gsend)
        dense_part = dense_part + jnp.sum(grad_dense * residual[s] * seconds[s], axis=0)
        grad_residual = upstream[s] + norm_back(residual[s], seconds[s], dense_gain, grad_dense)
        r_parts = gather_tokens(grad_residual.astype(BF16))
        nkeep, nsend, gains, grads = attn_bwd(
            scals[s], cosines, sines, gq, gk, saved[s], normed[s], r_parts, attn_w
        )
        attn_grads.append(grads)
        gain_part = gain_part + gains
        grad_normed = scatter_tokens(nkeep, nsend)
        factor = firsts[s][1]
        mixer_part = mixer_part + jnp.sum(grad_normed * tokens[s] * factor, axis=0)
        input_gradient.append(grad_residual + norm_back(tokens[s], factor, mixer_gain, grad_normed))
        out_sum = scatter_tokens(ykeep, ysend)
        block_out.append(jnp.where(valid[s], residual[s] + out_sum, 0.0).astype(BF16))

    summed = [
        sum(part.astype(F32) for part in parts_of).astype(BF16) for parts_of in zip(*attn_grads)
    ]
    attn_grad = scatter_shards(summed)
    early = sum_everywhere(jnp.concatenate([dense_part.reshape(-1, LANES), gain_part], axis=0))
    mixer = sum_everywhere(mixer_part.reshape(-1, LANES)).reshape(-1)
    dense_rows = width // LANES
    folded = early[dense_rows:, :head] + early[dense_rows:, head:]
    inner_gradient = jnp.stack(
        [
            jnp.concatenate([grad[:, p * cols : (p + 1) * cols] for grad in ff_grads], axis=1)
            for p in range(2)
        ],
        axis=1,
    )
    down_gradient = jnp.concatenate([grad[:, 2 * cols :] for grad in ff_grads], axis=1).T
    return (
        jnp.stack(block_out, axis=1),
        jnp.stack(input_gradient, axis=1),
        attn_grad[:, :query_cols],
        attn_grad[:, query_cols : query_cols + 2 * pair_cols].reshape(shard, 2, pair_cols),
        attn_grad[:, query_cols + 2 * pair_cols :].T,
        inner_gradient,
        down_gradient,
        mixer,
        folded[0],
        folded[1],
        early[:dense_rows].reshape(-1),
    )


def local(*args):
    inputs, shard = args[0], args[2].shape[0]
    if lax.axis_size("dp") == 8 and lax.axis_size("tensor") == 4 and shard % LANES == 0 and inputs.shape[1] == 2:
        return local_fused(*args)
    return local_plain(*args)


def rope_tables(full, head):
    half = head // 2
    freqs = np.float32(THETA) ** (-np.arange(half, dtype=np.float32) * np.float32(2.0) / np.float32(head))
    angles = np.arange(full, dtype=np.float32)[:, None] * freqs[None, :].astype(np.float32)
    cosines, sines = np.cos(angles), np.sin(angles)
    return (
        jnp.asarray(np.tile(cosines, (1, 4)), F32),
        jnp.asarray(np.tile(np.concatenate([-sines, sines], axis=1), (1, 2)), F32),
    )


def local_fused(
    inputs,
    lengths,
    query_weight,
    key_value_weight,
    output_weight,
    inner_weight,
    down_weight,
    mixer_gain,
    query_gain,
    key_gain,
    dense_gain,
    cotangent,
):
    size, seqs, width = inputs.shape
    parts = lax.axis_size("tensor")
    full = size * parts
    head = query_gain.shape[0]
    query_cols = query_weight.shape[1]
    pair_cols = key_value_weight.shape[2]
    hidden = inner_weight.shape[2]
    shard = query_weight.shape[0]
    me_t, me_d = lax.axis_index("tensor"), lax.axis_index("dp")
    n_c = 3
    cols = hidden // n_c
    tabs = rope_tables(full, head)
    gq = jnp.tile(query_gain, 2)[None, :]
    gk = jnp.tile(key_gain, 2)[None, :]
    gains = (gq, gk, mixer_gain[None, :], dense_gain[None, :])
    down_turned = down_weight.T
    attn_shard = jnp.concatenate(
        [query_weight, key_value_weight.reshape(shard, 2 * pair_cols), output_weight.T], axis=1
    )
    ff_shard = jnp.stack(
        [
            jnp.concatenate(
                [inner_weight[:, 0, part], inner_weight[:, 1, part], down_turned[:, part]], axis=1
            )
            for part in (slice(c * cols, (c + 1) * cols) for c in range(n_c))
        ]
    )
    positions = me_t * size + jnp.arange(size, dtype=jnp.int32)
    valid = [(positions < lengths[s])[:, None] for s in range(seqs)]
    upstream = jnp.stack([jnp.where(valid[s], cotangent[:, s], 0) for s in range(seqs)])
    x = inputs.reshape(size, seqs * width)

    (aw, fw, normed, ups, dense, outb, *saved, resid) = fused_forward(
        lengths, x, attn_shard, upstream, ff_shard[: n_c - 1], tabs, gains
    )
    grad_a, grad_b, ys, near, wholes, gres, resid_b, dgain, own = fused_dense(
        x, dense, ups, outb, fw, ff_shard[n_c - 1], upstream, resid, gains[3]
    )
    input_gradient, blk, attn_grad, ff_grad, sums = fused_backward(
        lengths,
        (normed, grad_a, aw, grad_b, ys, near, wholes, own, gres, *saved),
        (x, upstream, resid, resid_b, dgain, *tabs, *gains),
    )
    block_out = jnp.where(jnp.stack(valid, axis=1), blk.reshape(size, seqs, width), 0)
    ff_grad = ff_grad.reshape(shard, n_c, 3, cols)
    inner_gradient = jnp.moveaxis(ff_grad[:, :, :2], 1, 2).reshape(shard, 2, hidden)
    down_gradient = ff_grad[:, :, 2].reshape(shard, hidden).T
    folded = sums[16:, :head] + sums[16:, head:]
    return (
        block_out,
        input_gradient.reshape(size, seqs, width),
        attn_grad[:, :query_cols],
        attn_grad[:, query_cols : query_cols + 2 * pair_cols].reshape(shard, 2, pair_cols),
        attn_grad[:, query_cols + 2 * pair_cols :].T,
        inner_gradient,
        down_gradient,
        sums[:8].reshape(-1),
        folded[0],
        folded[1],
        sums[8:16].reshape(-1),
    )


def solution(mesh):
    return jax.shard_map(
        local,
        mesh=mesh,
        in_specs=(
            P("tensor", "dp", None),
            P("dp"),
            P("dp", "tensor"),
            P("dp", None, "tensor"),
            P("tensor", "dp"),
            P("dp", None, "tensor"),
            P("tensor", "dp"),
            P(),
            P(),
            P(),
            P(),
            P("tensor", "dp", None),
        ),
        out_specs=(
            P("tensor", "dp", None),
            P("tensor", "dp", None),
            P("dp", "tensor"),
            P("dp", None, "tensor"),
            P("tensor", "dp"),
            P("dp", None, "tensor"),
            P("tensor", "dp"),
            P(),
            P(),
            P(),
            P(),
        ),
        check_vma=False,
    )
```

```python
import functools

import jax
import jax.numpy as jnp
import numpy as np
from jax import lax
from jax.experimental import pallas as pl
from jax.experimental.pallas import tpu as pltpu
from jax.sharding import PartitionSpec as P

EPS = 1e-05
THETA = 1000000.0
LOG2E = 1.4426950408889634
F32 = jnp.float32
BF16 = jnp.bfloat16
HIGH = lax.Precision.HIGHEST
LANES = 128
VMEM_LIMIT = 56 * 1024 * 1024
FRONT_LIMIT = 62 * 1024 * 1024
ANY = pl.BlockSpec(memory_space=pl.ANY)
VMEM = pl.BlockSpec(memory_space=pltpu.VMEM)
SMEM = pl.BlockSpec(memory_space=pltpu.SMEM)


def dot(a, b, **kw):
    return lax.dot_general(
        a, b, (((1,), (0,)), ((), ())), preferred_element_type=F32, **kw
    )


def dot_nt(a, b, **kw):
    return lax.dot_general(
        a, b, (((1,), (1,)), ((), ())), preferred_element_type=F32, **kw
    )


def dot_tn(a, b, **kw):
    return lax.dot_general(
        a, b, (((0,), (0,)), ((), ())), preferred_element_type=F32, **kw
    )


def iota(shape, axis):
    return lax.broadcasted_iota(jnp.int32, shape, axis)


def low_half(shape):
    return iota(shape, 1) % LANES < LANES // 2


def head_blocks(scale):
    shape = (LANES, LANES)
    return jnp.where(iota(shape, 0) // 64 == iota(shape, 1) // 64, scale, 0.0).astype(F32)


def head_rows(scale):
    return jnp.where(iota((8, 256), 0) == iota((8, 256), 1) // 64, scale, 0.0).astype(F32)


def partner(values):
    first = iota(values.shape, 1) % 64 < 32
    return jnp.where(first, pltpu.roll(values, LANES - 32, 1), pltpu.roll(values, 32, 1))


def rows_of(index, size):
    return pl.ds(pl.multiple_of(index * size, size), size)


def load_all(sources, targets, sems, first):
    copies = []
    for number, (source, target) in enumerate(zip(sources, targets)):
        copy = pltpu.make_async_copy(source, target, sems.at[first + number])
        copy.start()
        copies.append(copy)
    return copies


def shard_targets(w_refs, ws, me):
    size = w_refs[0].shape[0]
    if len(w_refs) == 1:
        return [ws]
    return [ws.at[rows_of(me ^ slot, size)] for slot in range(len(w_refs))]


def store_slots(whole, out_refs, me):
    if len(out_refs) == 1:
        out_refs[0][...] = whole[...]
        return
    keep_ref, send_ref = out_refs
    size = keep_ref.shape[1]
    for slot in range(2 * keep_ref.shape[0]):
        (send_ref if slot % 2 else keep_ref)[slot // 2] = whole[rows_of(me ^ slot, size), :]


def padded_heads(first, second, low, g, e):
    here = low if e == 0 else jnp.logical_not(low)
    return jnp.where(here, first if g == e else second, 0.0).astype(BF16)


def project_rows(r, size, length, xs, ws, tabs, gains, raw_ref, q_ref, k_ref, v_ref, kp, vp):
    rows = rows_of(r, size)
    cos_ref, sin_ref = tabs
    gq_ref, gk_ref = gains
    mean_of = head_blocks(1.0 / 64)
    low = low_half((size, LANES))
    projected = dot(xs[rows, :], ws[:, :512])
    raw_ref[rows, :] = projected[:, :384]
    cosines, sines = cos_ref[rows, :], sin_ref[rows, :]

    def turned(values, gain):
        mean = dot(values * values, mean_of, precision=HIGH)
        normed = values * lax.rsqrt(mean + EPS) * gain
        return normed * cosines + partner(normed) * sines

    for g in range(2):
        lanes = slice(LANES * g, LANES * (g + 1))
        q_ref[rows, lanes] = turned(projected[:, lanes], gq_ref[...]).astype(BF16)
    keys = turned(projected[:, 256:384], gk_ref[...])
    values = projected[:, 384:512]
    k_ref[rows, :] = keys.astype(BF16)
    v_ref[rows, :] = values.astype(BF16)
    live = r * size + iota((size, LANES), 0) < length
    ones = jnp.where(live, 1.0, 0.0)
    values = jnp.where(live, values, 0.0)
    keys_swap, values_swap = pltpu.roll(keys, 64, 1), pltpu.roll(values, 64, 1)
    for g in range(2):
        for e in range(2):
            kp[2 * g + e, rows, :] = padded_heads(keys, keys_swap, low, g, e)
            vp[2 * g + e, rows, :LANES] = padded_heads(values, values_swap, low, g, e)
            vp[2 * g + e, rows, LANES:] = padded_heads(ones, ones, low, g, e)


def attend_rows(i, size, q_ref, kp, vp, acc, att_ref, lse_ref):
    rows = rows_of(i, size)
    factor = LOG2E / 8.0
    causal = iota((size, size), 1) <= iota((size, size), 0)
    queries = [q_ref[rows, LANES * g : LANES * (g + 1)] for g in range(2)]

    def block(kb, masked):
        cols = rows_of(kb, size)
        sums = []
        for g in range(2):
            total = None
            for e in range(2):
                weights = jnp.exp2(dot_nt(queries[g], kp[2 * g + e, cols, :]) * factor)
                if masked:
                    weights = jnp.where(causal, weights, 0.0)
                part = dot(weights.astype(BF16), vp[2 * g + e, cols, :])
                total = part if total is None else total + part
            sums.append(total)
        return sums

    for g, total in enumerate(block(i, True)):
        acc[g] = total

    def more(kb, carry):
        for g, total in enumerate(block(kb, False)):
            acc[g] += total
        return carry

    lax.fori_loop(i - i, i, more, None)
    logs = []
    for g in range(2):
        lanes = slice(LANES * g, LANES * (g + 1))
        summed = acc[g, :, LANES:]
        att_ref[rows, lanes] = (acc[g, :, :LANES] / summed).astype(BF16)
        logs.append(jnp.log2(summed))
    lse_ref[:, rows] = dot_nt(head_rows(1.0 / 64), jnp.concatenate(logs, axis=1), precision=HIGH)


def attn_fwd_kernel(parts, n_w, scal, cos_ref, sin_ref, gq_ref, gk_ref, *refs):
    x_refs, refs = refs[:parts], refs[parts:]
    w_refs, refs = refs[:n_w], refs[n_w:]
    (raw_ref, q_ref, k_ref, v_ref, att_ref, lse_ref, keep_ref, send_ref, xs, ws, kp, vp, acc, sems) = refs
    size = x_refs[0].shape[0]
    me_t, me_d, length = scal[0], scal[1], scal[2]
    copies = load_all(w_refs, shard_targets(w_refs, ws, me_d), sems, 0)
    copies += load_all(x_refs, [xs.at[rows_of(me_t ^ j, size)] for j in range(parts)], sems, n_w)
    for copy in copies:
        copy.wait()

    def project(r, carry):
        project_rows(
            r, size, length, xs, ws, (cos_ref, sin_ref), (gq_ref, gk_ref), raw_ref, q_ref, k_ref, v_ref, kp, vp
        )
        return carry

    def attend(i, carry):
        attend_rows(i, size, q_ref, kp, vp, acc, att_ref, lse_ref)
        return carry

    lax.fori_loop(0, parts, project, 0)
    lax.fori_loop(0, parts, attend, 0)
    for j in range(parts):
        out = dot_nt(att_ref[rows_of(me_t ^ j, size), :], ws[:, 512:])
        (send_ref if j % 2 else keep_ref)[j // 2] = out.astype(BF16)


def attn_fwd(scal, cosines, sines, gq, gk, x_parts, w_parts):
    parts, n_w = len(x_parts), len(w_parts)
    size, width = x_parts[0].shape
    full = parts * size
    cols = w_parts[0].shape[1]
    pair = jax.ShapeDtypeStruct((parts // 2, size, width), BF16)
    return pl.pallas_call(
        functools.partial(attn_fwd_kernel, parts, n_w),
        out_shape=(
            jax.ShapeDtypeStruct((full, 384), F32),
            jax.ShapeDtypeStruct((full, 256), BF16),
            jax.ShapeDtypeStruct((full, 128), BF16),
            jax.ShapeDtypeStruct((full, 128), BF16),
            jax.ShapeDtypeStruct((full, 256), BF16),
            jax.ShapeDtypeStruct((8, full), F32),
            pair,
            pair,
        ),
        in_specs=[SMEM] + [VMEM] * 4 + [ANY] * (parts + n_w),
        out_specs=(VMEM,) * 8,
        scratch_shapes=[
            pltpu.VMEM((full, width), BF16),
            pltpu.VMEM((width, cols), BF16),
            pltpu.VMEM((4, full, LANES), BF16),
            pltpu.VMEM((4, full, 2 * LANES), BF16),
            pltpu.VMEM((2, size, 2 * LANES), F32),
            pltpu.SemaphoreType.DMA((n_w + parts,)),
        ],
        compiler_params=pltpu.CompilerParams(vmem_limit_bytes=VMEM_LIMIT),
        cost_estimate=pl.CostEstimate(flops=8_000_000_000, bytes_accessed=12_000_000, transcendentals=3_000_000),
        name="attention_forward",
    )(scal, cosines, sines, gq, gk, *x_parts, *w_parts)


def prepare_rows(r, size, length, gs, ws, k_ref, v_ref, att_ref, ga, drow, kp, kt, vp):
    rows = rows_of(r, size)
    low = low_half((size, LANES))
    grad = dot(gs[rows, :], ws[:, 512:]).astype(BF16)
    ga[rows, :] = grad
    drow[:, rows] = dot_nt(head_rows(1.0), grad.astype(F32) * att_ref[rows, :].astype(F32), precision=HIGH)
    live = r * size + iota((size, LANES), 0) < length
    keys = jnp.where(live, k_ref[rows, :].astype(F32), 0.0)
    values = jnp.where(live, v_ref[rows, :].astype(F32), 0.0)
    keys_swap, values_swap = pltpu.roll(keys, 64, 1), pltpu.roll(values, 64, 1)
    for g in range(2):
        for e in range(2):
            here = low if e == 0 else jnp.logical_not(low)
            padded = jnp.where(here, keys if g == e else keys_swap, 0.0)
            kp[2 * g + e, rows, :] = padded.astype(BF16)
            kt[2 * g + e, :, rows] = padded.T.astype(BF16)
            vp[2 * g + e, rows, :] = padded_heads(values, values_swap, low, g, e)


def sweep_rows(i, size, q_ref, ga, kp, kt, vp, drow, lrow, acc, dq, dk, dv):
    rows = rows_of(i, size)
    factor = LOG2E / 8.0
    causal = iota((size, size), 0) <= iota((size, size), 1)
    low2 = iota((2 * size, LANES), 0) // size == iota((2 * size, LANES), 1) // 64
    queries, grads, queries2, grads2 = [], [], [], []
    for g in range(2):
        lanes = slice(LANES * g, LANES * (g + 1))
        queries.append(q_ref[rows, lanes])
        grads.append(ga[rows, lanes])
        for source, target in ((queries, queries2), (grads, grads2)):
            both = jnp.concatenate([source[g], source[g]], axis=0)
            target.append(jnp.where(low2, both, jnp.zeros_like(both)))

    def block(kb, masked):
        cols = rows_of(kb, size)
        parts_t = []
        for g in range(2):
            weights2, scores2, turned = [], [], None
            for e in range(2):
                h = 2 * g + e
                weights = jnp.exp2(dot_nt(kp[h, cols, :], queries[g]) * factor - lrow[h : h + 1, rows])
                if masked:
                    weights = jnp.where(causal, weights, 0.0)
                grad_weights = dot_nt(vp[h, cols, :], grads[g])
                grad_scores = (weights * (grad_weights - drow[h : h + 1, rows])).astype(BF16)
                weights2.append(weights.astype(BF16))
                scores2.append(grad_scores)
                part = dot(kt[h, :, cols], grad_scores)
                turned = part if turned is None else turned + part
            dv[g, cols, :] += dot(jnp.concatenate(weights2, axis=1), grads2[g])
            dk[g, cols, :] += dot(jnp.concatenate(scores2, axis=1), queries2[g])
            parts_t.append(turned)
        return parts_t

    for g, total in enumerate(block(i, True)):
        acc[g] = total

    def more(kb, carry):
        for g, total in enumerate(block(kb, False)):
            acc[g] += total
        return carry

    lax.fori_loop(i - i, i, more, None)
    for g in range(2):
        dq[rows, LANES * g : LANES * (g + 1)] = acc[g].T


def unproject_rows(r, size, length, tabs, gains, raw_ref, dq, dk, dv, gp, gains_ref):
    rows = rows_of(r, size)
    cosines, sines = tabs[0][rows, :], tabs[1][rows, :]
    low = low_half((size, LANES))
    mean_of = head_blocks(1.0 / 64)
    live = r * size + iota((size, LANES), 0) < length

    def back(grad, lanes, gain, row):
        raw = raw_ref[rows, lanes]
        rms = lax.rsqrt(dot(raw * raw, mean_of, precision=HIGH) + EPS)
        turned = grad * cosines - partner(grad) * sines
        gains_ref[row : row + 1, :] += jnp.sum(turned * raw * rms, axis=0, keepdims=True)
        weighted = turned * gain
        inner = dot(raw * weighted, mean_of, precision=HIGH)
        gp[rows, lanes] = (rms * weighted - raw * (rms * rms * rms) * inner).astype(BF16)

    def folded(ref):
        first, second = ref[0, rows, :], ref[1, rows, :]
        both = jnp.where(low, first + pltpu.roll(first, 64, 1), second + pltpu.roll(second, 64, 1))
        return jnp.where(live, both, 0.0)

    for g in range(2):
        lanes = slice(LANES * g, LANES * (g + 1))
        back(dq[rows, lanes] * 0.125, lanes, gains[0][...], 0)
    back(folded(dk) * 0.125, slice(256, 384), gains[1][...], 1)
    gp[rows, 384:512] = folded(dv).astype(BF16)


def attn_bwd_kernel(parts, n_w, scal, cos_ref, sin_ref, gq_ref, gk_ref, raw_ref, q_ref, k_ref, v_ref, att_ref, lse_ref, *refs):
    x_refs, refs = refs[:parts], refs[parts:]
    r_refs, refs = refs[:parts], refs[parts:]
    w_refs, refs = refs[:n_w], refs[n_w:]
    n_g = 1 if n_w == 1 else 2
    keep_ref, send_ref, gains_ref = refs[:3]
    g_refs, refs = refs[3 : 3 + n_g], refs[3 + n_g :]
    xs, gs, ws, kp, vp, kt, ga, dq, dk, dv, gp, whole, drow, acc, sems = refs
    size = x_refs[0].shape[0]
    me_t, me_d, length = scal[0], scal[1], scal[2]
    copies = load_all(w_refs, shard_targets(w_refs, ws, me_d), sems, 0)
    copies += load_all(r_refs, [gs.at[rows_of(me_t ^ j, size)] for j in range(parts)], sems, n_w)
    copies += load_all(x_refs, [xs.at[rows_of(me_t ^ j, size)] for j in range(parts)], sems, n_w + parts)
    for copy in copies:
        copy.wait()

    def prepare(r, carry):
        prepare_rows(r, size, length, gs, ws, k_ref, v_ref, att_ref, ga, drow, kp, kt, vp)
        return carry

    def sweep(i, carry):
        sweep_rows(i, size, q_ref, ga, kp, kt, vp, drow, lse_ref, acc, dq, dk, dv)
        return carry

    def unproject(r, carry):
        unproject_rows(r, size, length, (cos_ref, sin_ref), (gq_ref, gk_ref), raw_ref, dq, dk, dv, gp, gains_ref)
        return carry

    lax.fori_loop(0, parts, prepare, 0)
    dk[...] = jnp.zeros_like(dk)
    dv[...] = jnp.zeros_like(dv)
    lax.fori_loop(0, parts, sweep, 0)
    gains_ref[...] = jnp.zeros_like(gains_ref)
    lax.fori_loop(0, parts, unproject, 0)
    for j in range(parts):
        out = dot_nt(gp[rows_of(me_t ^ j, size), :], ws[:, :512])
        (send_ref if j % 2 else keep_ref)[j // 2] = out.astype(BF16)

    def weigh(b, carry):
        rows = rows_of(b, 256)
        whole[rows, :512] = dot_tn(xs[:, rows], gp[...]).astype(BF16)
        whole[rows, 512:] = dot_tn(gs[:, rows], att_ref[...]).astype(BF16)
        return carry

    lax.fori_loop(0, whole.shape[0] // 256, weigh, 0)
    store_slots(whole, g_refs, me_d)


def slot_shapes(n_w, width, cols):
    if n_w == 1:
        return (jax.ShapeDtypeStruct((width, cols), BF16),)
    return (jax.ShapeDtypeStruct((n_w // 2, width // n_w, cols), BF16),) * 2


def attn_bwd(scal, cosines, sines, gq, gk, saved, x_parts, r_parts, w_parts):
    parts, n_w = len(x_parts), len(w_parts)
    size, width = x_parts[0].shape
    full = parts * size
    cols = w_parts[0].shape[1]
    pair = jax.ShapeDtypeStruct((parts // 2, size, width), BF16)
    g_shapes = slot_shapes(n_w, width, cols)
    outs = pl.pallas_call(
        functools.partial(attn_bwd_kernel, parts, n_w),
        out_shape=(pair, pair, jax.ShapeDtypeStruct((8, LANES), F32)) + g_shapes,
        in_specs=[SMEM] + [VMEM] * 10 + [ANY] * (2 * parts + n_w),
        out_specs=(VMEM,) * (3 + len(g_shapes)),
        scratch_shapes=[
            pltpu.VMEM((full, width), BF16),
            pltpu.VMEM((full, width), BF16),
            pltpu.VMEM((width, cols), BF16),
            pltpu.VMEM((4, full, LANES), BF16),
            pltpu.VMEM((4, full, LANES), BF16),
            pltpu.VMEM((4, LANES, full), BF16),
            pltpu.VMEM((full, 256), BF16),
            pltpu.VMEM((full, 256), F32),
            pltpu.VMEM((2, full, LANES), F32),
            pltpu.VMEM((2, full, LANES), F32),
            pltpu.VMEM((full, 512), BF16),
            pltpu.VMEM((width, cols), BF16),
            pltpu.VMEM((8, full), F32),
            pltpu.VMEM((2, LANES, size), F32),
            pltpu.SemaphoreType.DMA((n_w + 2 * parts,)),
        ],
        compiler_params=pltpu.CompilerParams(vmem_limit_bytes=VMEM_LIMIT),
        cost_estimate=pl.CostEstimate(flops=14_000_000_000, bytes_accessed=15_000_000, transcendentals=3_000_000),
        name="attention_backward",
    )(scal, cosines, sines, gq, gk, *saved, *x_parts, *r_parts, *w_parts)
    return outs[0], outs[1], outs[2], outs[3:]


def ff_kernel(n_x, n_w, scal, *refs):
    x_refs, refs = refs[:n_x], refs[n_x:]
    u_refs, refs = refs[:n_x], refs[n_x:]
    w_refs, refs = refs[:n_w], refs[n_w:]
    n_g = 1 if n_w == 1 else 2
    hid_ref, ggu_ref = refs[:2]
    g_refs, refs = refs[2 : 2 + n_g], refs[2 + n_g :]
    xs, us, ws, whole, sems = refs
    size = x_refs[0].shape[0]
    me_d = scal[1]
    cols = ws.shape[1] // 3
    copies = load_all(w_refs, shard_targets(w_refs, ws, me_d), sems, 0)
    x_copies = load_all(x_refs, [xs.at[pl.ds(j * size, size)] for j in range(n_x)], sems, n_w)
    u_copies = load_all(u_refs, [us.at[pl.ds(j * size, size)] for j in range(n_x)], sems, n_w + n_x)
    for copy in copies + x_copies + u_copies:
        copy.wait()

    def tokens(r, carry):
        rows = rows_of(r, size)
        gate_up = dot(xs[rows, :], ws[:, : 2 * cols])
        grad = dot(us[rows, :], ws[:, 2 * cols :])
        gate, up = gate_up[:, :cols], gate_up[:, cols:]
        sig = 1.0 / (1.0 + jnp.exp2(gate * -LOG2E))
        silu = gate * sig
        hid_ref[rows, :] = (silu * up).astype(BF16)
        ggu_ref[rows, :cols] = (grad * up * (sig + silu * (1.0 - sig))).astype(BF16)
        ggu_ref[rows, cols:] = (grad * silu).astype(BF16)
        return carry

    lax.fori_loop(0, n_x, tokens, 0)

    def weigh(b, carry):
        rows = rows_of(b, 256)
        whole[rows, : 2 * cols] = dot_tn(xs[:, rows], ggu_ref[...]).astype(BF16)
        whole[rows, 2 * cols :] = dot_tn(us[:, rows], hid_ref[...]).astype(BF16)
        return carry

    lax.fori_loop(0, whole.shape[0] // 256, weigh, 0)
    store_slots(whole, g_refs, me_d)


def feed_forward(scal, x_parts, u_parts, w_parts):
    n_x, n_w = len(x_parts), len(w_parts)
    size, width = x_parts[0].shape
    full = n_x * size
    wide = w_parts[0].shape[1]
    cols = wide // 3
    g_shapes = slot_shapes(n_w, width, wide)
    outs = pl.pallas_call(
        functools.partial(ff_kernel, n_x, n_w),
        out_shape=(
            jax.ShapeDtypeStruct((full, cols), BF16),
            jax.ShapeDtypeStruct((full, 2 * cols), BF16),
        )
        + g_shapes,
        in_specs=[SMEM] + [ANY] * (2 * n_x + n_w),
        out_specs=(VMEM,) * (2 + len(g_shapes)),
        scratch_shapes=[
            pltpu.VMEM((full, width), BF16),
            pltpu.VMEM((full, width), BF16),
            pltpu.VMEM((width, wide), BF16),
            pltpu.VMEM((width, wide), BF16),
            pltpu.SemaphoreType.DMA((n_w + 2 * n_x,)),
        ],
        compiler_params=pltpu.CompilerParams(vmem_limit_bytes=VMEM_LIMIT),
        cost_estimate=pl.CostEstimate(flops=4 * full * width * wide, bytes_accessed=20_000_000, transcendentals=full * cols),
        name="feed_forward",
    )(scal, *x_parts, *u_parts, *w_parts)
    return outs[0], outs[1], outs[2:]


def ff_out_kernel(parts, n_c, n_w, seq, scal, *refs):
    hid_refs, refs = refs[:n_c], refs[n_c:]
    ggu_refs, refs = refs[:n_c], refs[n_c:]
    w_refs, refs = refs[: n_c * n_w], refs[n_c * n_w :]
    ykeep_ref, ysend_ref, gkeep_ref, gsend_ref, hs, gs, ws, sems = refs
    size = ykeep_ref.shape[1]
    full = parts * size
    me_d = scal[1]
    wide = ws.shape[2]
    cols = wide // 3
    copies = []
    first = 0
    for c in range(n_c):
        targets = shard_targets(w_refs[c * n_w : (c + 1) * n_w], ws.at[c], me_d)
        copies += load_all(w_refs[c * n_w : (c + 1) * n_w], targets, sems, first)
        first += n_w
    mine = pl.ds(seq * full, full)
    copies += load_all([ref.at[mine] for ref in ggu_refs], [gs.at[c] for c in range(n_c)], sems, first)
    copies += load_all([ref.at[mine] for ref in hid_refs], [hs.at[c] for c in range(n_c)], sems, first + n_c)
    for copy in copies:
        copy.wait()
    for j in range(parts):
        rows = pl.ds(j * size, size)
        grad = sum(dot_nt(gs[c, rows, :], ws[c, :, : 2 * cols]) for c in range(n_c))
        (gsend_ref if j % 2 else gkeep_ref)[j // 2] = grad.astype(BF16)
        out = sum(dot_nt(hs[c, rows, :], ws[c, :, 2 * cols :]) for c in range(n_c))
        (ysend_ref if j % 2 else ykeep_ref)[j // 2] = out.astype(BF16)


def ff_out(seq, scal, parts, size, hids, ggus, w_chunks):
    n_c, n_w = len(w_chunks), len(w_chunks[0])
    wide = w_chunks[0][0].shape[1]
    width = w_chunks[0][0].shape[0] * n_w
    full = parts * size
    cols = wide // 3
    pair = jax.ShapeDtypeStruct((parts // 2, size, width), BF16)
    return pl.pallas_call(
        functools.partial(ff_out_kernel, parts, n_c, n_w, seq),
        out_shape=(pair,) * 4,
        in_specs=[SMEM] + [ANY] * (2 * n_c + n_c * n_w),
        out_specs=(VMEM,) * 4,
        scratch_shapes=[
            pltpu.VMEM((n_c, full, cols), BF16),
            pltpu.VMEM((n_c, full, 2 * cols), BF16),
            pltpu.VMEM((n_c, width, wide), BF16),
            pltpu.SemaphoreType.DMA((n_c * n_w + 2 * n_c,)),
        ],
        compiler_params=pltpu.CompilerParams(vmem_limit_bytes=VMEM_LIMIT),
        cost_estimate=pl.CostEstimate(flops=2 * full * width * wide * n_c, bytes_accessed=22_000_000, transcendentals=0),
        name="feed_forward_out",
    )(scal, *hids, *ggus, *[shard for chunk in w_chunks for shard in chunk])


def flip(index, bits):
    for bit in (1, 2, 4):
        if bits & bit:
            index = index + bit - 2 * bit * lax.rem(lax.div(index, bit), 2)
    return index


class Spot:
    def __init__(self, index, choices):
        self.index = index
        self.flips = {0: index}
        for bits in choices:
            self.flips[bits] = flip(index, bits)


def spots():
    me_t = Spot(lax.axis_index("tensor"), (1, 2, 3))
    me_d = Spot(lax.axis_index("dp"), (1, 2, 4, 6))
    me_d.x = lax.rem(me_d.index, 2)
    me_d.beside = 1 - me_d.x
    me_d.z = Spot(lax.div(me_d.index, 2), (1, 2, 3))
    return me_t, me_d


def enter(me_d, me_t):
    barrier = pltpu.get_barrier_semaphore()
    devices = [{"dp": me_d.flips[bits]} for bits in (1, 2, 4, 6)]
    devices += [{"tensor": me_t.flips[bits]} for bits in (1, 2)]
    for device in devices:
        pl.semaphore_signal(barrier, inc=1, device_id=device, device_id_type=pl.DeviceIdType.MESH)
    return lambda: pl.semaphore_wait(barrier, len(devices))


def remote(source, target, sems, number, device):
    return pltpu.make_async_remote_copy(
        src_ref=source,
        dst_ref=target,
        send_sem=sems.at[0, number],
        recv_sem=sems.at[1, number],
        device_id=device,
        device_id_type=pl.DeviceIdType.MESH,
    )


class Remote:
    LIMIT = 80

    def __init__(self, sems):
        self.sems, self.used = sems, 0

    def __call__(self, source, target, device):
        assert self.used < self.LIMIT
        self.used += 1
        return remote(source, target, self.sems, self.used - 1, device)


class Local:
    LIMIT = 64

    def __init__(self, sems):
        self.sems, self.used = sems, 0

    def make(self, source, target):
        assert self.used < self.LIMIT
        self.used += 1
        return pltpu.make_async_copy(source, target, self.sems.at[self.used - 1])

    def __call__(self, source, target):
        copy = self.make(source, target)
        copy.start()
        return copy


COPY_SEMS = [
    pltpu.SemaphoreType.DMA((2, Remote.LIMIT)),
    pltpu.SemaphoreType.DMA((Local.LIMIT,)),
]


class ShardGather:
    def __init__(self, shard, whole, send, me_d):
        size = shard.shape[0]
        mine = whole.at[rows_of(me_d.index, size)]
        self.own = [send(shard, mine, {"dp": me_d.flips[bits]}) for bits in (1, 2, 4, 6)]
        self.passed = []
        for bits in (2, 4, 6):
            there = whole.at[rows_of(me_d.flips[bits], size)]
            self.passed.append(send(there, there, {"dp": me_d.flips[1]}))

    def start(self):
        for copy in self.own:
            copy.start()

    def forward(self, *which):
        for n in which or (0, 1, 2):
            self.own[1 + n].wait_recv()
            self.passed[n].start()

    def arrive(self):
        self.own[0].wait_recv()
        for copy in self.passed:
            copy.wait_recv()

    def drain(self):
        for copy in self.own + self.passed:
            copy.wait_send()


class TokenGather:
    def __init__(self, block, whole, send, me_t):
        size = block.shape[0]
        mine = whole.at[rows_of(me_t.index, size)]
        there = whole.at[rows_of(me_t.flips[2], size)]
        near = {"tensor": me_t.flips[1]}
        self.near = send(block, mine, near)
        self.far = send(block, mine, {"tensor": me_t.flips[2]})
        self.passed = send(there, there, near)

    def start(self):
        self.far.start()
        self.near.start()

    def forward(self):
        self.far.wait_recv()
        self.passed.start()

    def arrive(self):
        self.near.wait_recv()
        self.passed.wait_recv()

    def drain(self):
        for copy in (self.near, self.far, self.passed):
            copy.wait_send()


class TokenReduce:
    def __init__(self, blocks, near, far, send, me_t, mine=None):
        device = {"tensor": me_t.flips[1]}
        self.blocks, self.near_ref, self.far_ref, self.mine = blocks, near, far, mine
        self.places = (me_t.index, me_t.flips[2])
        self.size = far.shape[0]
        self.near = [
            send(blocks.at[rows_of(me_t.flips[1 + 2 * n], self.size)], near.at[n], device) for n in range(2)
        ]
        self.far = send(near.at[1], far, {"tensor": me_t.flips[2]})

    def load(self, here):
        return [here(self.blocks.at[rows_of(place, self.size)], self.mine.at[n]) for n, place in enumerate(self.places)]

    def start(self, *which):
        for n in which or (1, 0):
            self.near[n].start()

    def part(self, n, rows):
        if self.mine is not None:
            return self.mine[n, rows, :].astype(F32)
        start = pl.multiple_of(self.places[n] * self.size + rows.start, 32)
        return self.blocks[pl.ds(start, rows.size), :].astype(F32)

    def middle(self):
        self.near[1].wait_recv()

        def step(rows):
            total = self.part(1, rows) + self.near_ref[1, rows, :].astype(F32)
            self.near_ref[1, rows, :] = total.astype(BF16)

        by_rows(self.size, 32, step)
        self.far.start()

    def arrive(self):
        self.near[0].wait_recv()
        self.far.wait_recv()

    def rows(self, rows):
        total = self.part(0, rows) + self.near_ref[0, rows, :].astype(F32)
        return total + self.far_ref[rows, :].astype(F32)

    def drain(self):
        for copy in self.near + [self.far]:
            copy.wait_send()


class ShardNear:
    def __init__(self, whole, near, out, send, me_d, mine=None):
        self.whole, self.near_ref, self.out, self.mine = whole, near, out, mine
        self.z, self.x = me_d.z, me_d.x
        self.size = near.shape[1]
        self.near = send(whole.at[:, me_d.beside], near, {"dp": me_d.flips[1]})

    def load(self, here):
        return [here(self.whole.at[:, self.x], self.mine)]

    def start(self):
        self.near.start()

    def part(self, there, rows):
        if self.mine is not None:
            return self.mine[there, rows, :].astype(F32)
        return self.whole[there, self.x, rows, :].astype(F32)

    def middle(self, far=None):
        self.near.wait_recv()
        for k in (1, 2, 3, 0):
            there = self.z.flips[k]

            def step(rows):
                total = self.part(there, rows) + self.near_ref[there, rows, :].astype(F32)
                if k:
                    self.near_ref[there, rows, :] = total.astype(BF16)
                else:
                    self.out[rows, :] = total

            by_rows(self.size, 32, step)
            if k and far is not None:
                far.far[k - 1].start()

    def drain(self):
        self.near.wait_send()


class ShardFar:
    def __init__(self, near, far, out, send, me_d):
        self.far_ref, self.out = far, out
        self.size = far.shape[1]
        self.far = [send(near.at[me_d.z.flips[k]], far.at[k - 1], {"dp": me_d.flips[2 * k]}) for k in (1, 2, 3)]

    def start(self):
        for copy in self.far:
            copy.start()

    def finish(self):
        for copy in self.far:
            copy.wait_recv()

        def step(rows):
            total = self.out[rows, :]
            for k in range(3):
                total = total + self.far_ref[k, rows, :].astype(F32)
            self.out[rows, :] = total

        by_rows(self.size, 32, step)

    def drain(self):
        for copy in self.far:
            copy.wait_send()


def by_rows(count, step, body):
    def run(b, carry):
        body(rows_of(b, step))
        return carry

    lax.fori_loop(0, count // step, run, None)


def loop(start, stop, body):
    def run(i, carry):
        body(i)
        return carry

    lax.fori_loop(start, stop, run, None)


def rms_factor(values):
    return lax.rsqrt(jnp.mean(values * values, axis=-1, keepdims=True) + EPS)


def shape(dims, kind):
    return jax.ShapeDtypeStruct(dims, kind)


def residual_back(rows, grads, resid_ref, up_ref, dg_ref, dgain_ref, gres_ref, low_ref):
    grad = grads.rows(rows)
    values = resid_ref[rows, :]
    factor = rms_factor(values)
    product = grad * values * factor
    dgain_ref[...] += jnp.sum(product.reshape(-1, 8, values.shape[1]), axis=0)
    weighted = grad * dg_ref[...]
    inner = jnp.mean(values * weighted, axis=-1, keepdims=True)
    total = up_ref[rows, :].astype(F32) + factor * weighted - values * (factor * factor * factor) * inner
    gres_ref[rows, :] = total
    low_ref[rows, :] = total.astype(BF16)


def front_kernel(
    lengths, x_ref, aw_ref, up_ref, fw_ref, cos_ref, sin_ref, gq_ref, gk_ref, mg_ref, dg_ref,
    aw_out, normed_out, raw_out, q_out, k_out, v_out, att_out, lse_out, ra_out, gb_out, y_out, wn_out, w_out,
    resa_ref, resb_ref, gres_ref, dgain_ref, sum_ref, own_ref,
    xs, ws, dn, us, wf, outp, onear, ofar, gnear, gfar, low_grad, wnear, wfar, sems, local_sems,
):
    size, width = resa_ref.shape
    seqs, full = xs.shape[:2]
    parts = full // size
    n_c, shard, wide = fw_ref.shape
    cols = wide // 3
    me_t, me_d = spots()
    entered = enter(me_d, me_t)
    send, here = Remote(sems), Local(local_sems)
    mine_t, mine_d = rows_of(me_t.index, size), rows_of(me_d.index, shard)
    resid_refs = (resa_ref, resb_ref)
    halves = [pl.ds(s * full, full) for s in range(seqs)]
    own_rows = [rows_of(s * parts + me_t.index, size) for s in range(seqs)]

    pro_w = ShardGather(aw_ref.at[:, :512], ws.at[:, :512], send, me_d)
    out_w = ShardGather(aw_ref.at[:, 512:], ws.at[:, 512:], send, me_d)
    ff_w = [ShardGather(fw_ref.at[c], wf.at[c], send, me_d) for c in range(n_c)]
    normed = [TokenGather(xs.at[s, mine_t], xs.at[s], send, me_t) for s in range(seqs)]
    ups = [TokenGather(up_ref.at[s], us.at[halves[s]], send, me_t) for s in range(seqs)]
    denses = [TokenGather(dn.at[own_rows[s]], dn.at[halves[s]], send, me_t) for s in range(seqs)]
    places = (outp, xs.at[0])
    outs = [TokenReduce(places[s], onear.at[s], ofar.at[s], send, me_t) for s in range(seqs)]
    grads = TokenReduce(outp, gnear, gfar, send, me_t)
    resids = TokenGather(low_grad, ra_out, send, me_t)

    loads = [here(aw_ref, ws.at[mine_d])]
    loads_u = [here(up_ref.at[s], us.at[own_rows[s]]) for s in range(seqs)]
    loads_f = [here(fw_ref.at[c], wf.at[c, mine_d]) for c in range(n_c)]
    keeps = [here.make(xs.at[s], normed_out.at[s]) for s in range(seqs)]
    stays = []

    def norm_first(s):
        def norm(rows):
            values = x_ref[rows, width * s : width * (s + 1)].astype(F32)
            target = pl.ds(pl.multiple_of(me_t.index * size + rows.start, 32), 32)
            xs[s, target, :] = (values * rms_factor(values) * mg_ref[...]).astype(BF16)

        by_rows(size, 32, norm)

    def after_out(s):
        outs[s].arrive()

        def norm(rows):
            values = x_ref[rows, width * s : width * (s + 1)].astype(F32) + outs[s].rows(rows)
            resid_refs[s][rows, :] = values
            target = pl.ds(pl.multiple_of((s * parts + me_t.index) * size + rows.start, 32), 32)
            dn[target, :] = (values * rms_factor(values) * dg_ref[...]).astype(BF16)

        by_rows(size, 32, norm)
        denses[s].start()

    def attention(kp, vp, acc, raw, q, k, v, att, lse):
        kept = ((raw, raw_out), (q, q_out), (k, k_out), (v, v_out), (att, att_out), (lse, lse_out))
        flushes = []

        def project(s):
            loop(0, parts, lambda r: project_rows(
                r, size, lengths[s], xs.at[s], ws, (cos_ref, sin_ref), (gq_ref, gk_ref),
                raw.at[s], q.at[s], k.at[s], v.at[s], kp, vp,
            ))

        def attend(s, start, stop):
            loop(start, stop, lambda i: attend_rows(i, size, q.at[s], kp, vp, acc, att.at[s], lse.at[s]))

        def out_block(s, bits):
            rows = rows_of(me_t.flips[bits], size)
            places[s][rows, :] = dot_nt(att[s, rows, :], ws[:, 512:]).astype(BF16)

        def out(s):
            for n, bits in enumerate((3, 1, 2, 0)):
                out_block(s, bits)
                if n < 2:
                    outs[s].start(1 - n)

        norm_first(0)
        entered()
        normed[0].start()
        pro_w.start()
        norm_first(1)
        pro_w.forward()
        out_w.start()
        normed[0].forward()
        normed[1].start()
        normed[0].arrive()
        for copy in loads:
            copy.wait()
        ff_w[0].start()
        pro_w.arrive()
        project(0)
        keeps[0].start()
        out_w.forward()
        attend(0, 0, 3)
        normed[1].forward()
        ups[0].start()
        attend(0, 3, parts)
        out_w.arrive()
        out(0)
        outs[0].middle()
        flushes.append(here(ws, aw_out))
        for source, target in kept:
            flushes.append(here(source.at[0], target.at[0]))
        normed[1].arrive()
        project(1)
        keeps[1].start()
        attend(1, 0, 3)
        ups[0].forward()
        ff_w[0].forward()
        ff_w[1].start()
        attend(1, 3, parts)
        normed[0].drain()
        keeps[0].wait()
        out(1)
        for source, target in kept:
            flushes.append(here(source.at[1], target.at[1]))
        after_out(0)
        outs[1].middle()
        for copy in flushes:
            copy.wait()

    pl.run_scoped(
        attention,
        pltpu.VMEM((4, full, LANES), BF16),
        pltpu.VMEM((4, full, 2 * LANES), BF16),
        pltpu.VMEM((2, size, 2 * LANES), F32),
        pltpu.VMEM((seqs, full, 384), F32),
        pltpu.VMEM((seqs, full, 256), BF16),
        pltpu.VMEM((seqs, full, 128), BF16),
        pltpu.VMEM((seqs, full, 128), BF16),
        pltpu.VMEM((seqs, full, 256), BF16),
        pltpu.VMEM((seqs, 8, full), F32),
    )

    def feed_forward(hid, ggu, whole):
        sums = (sum_ref, own_ref)
        near = [ShardNear(whole.at[c], wnear.at[c], sums[c], send, me_d) for c in range(2)]
        far = ShardFar(wnear.at[0], wfar, sum_ref, send, me_d)

        def tokens(c, s):
            def run(r):
                rows = rows_of(r, size)
                gate_up = dot(dn[rows, :], wf[c, :, : 2 * cols])
                grad = dot(us[rows, :], wf[c, :, 2 * cols :])
                gate, up = gate_up[:, :cols], gate_up[:, cols:]
                sig = 1.0 / (1.0 + jnp.exp2(gate * -LOG2E))
                silu = gate * sig
                hid[c, rows, :] = (silu * up).astype(BF16)
                ggu[c, rows, :cols] = (grad * up * (sig + silu * (1.0 - sig))).astype(BF16)
                ggu[c, rows, cols:] = (grad * silu).astype(BF16)

            loop(s * parts, (s + 1) * parts, run)

        def weigh(c):
            def run(b):
                rows = rows_of(b, 256)
                dims = whole.shape[2:4]
                inner = dot_tn(dn[:, rows], ggu[c]).astype(BF16)
                whole[c % 2, b, :, :, : 2 * cols] = inner.reshape(dims + (2 * cols,))
                down = dot_tn(us[:, rows], hid[c]).astype(BF16)
                whole[c % 2, b, :, :, 2 * cols :] = down.reshape(dims + (cols,))

            loop(0, whole.shape[1], run)

        def grad_block(s, block, target):
            rows = rows_of(s * parts + block, size)
            total = sum(dot_nt(ggu[c, rows, :], wf[c, :, : 2 * cols]) for c in range(n_c))
            target[rows_of(block, size), :] = total.astype(BF16)

        def down_block(r):
            rows = rows_of(r, size)
            total = sum(dot_nt(hid[c, rows, :], wf[c, :, 2 * cols :]) for c in range(n_c))
            us[rows, :] = total.astype(BF16)

        def after_grad():
            grads.arrive()
            dgain_ref[...] = jnp.zeros_like(dgain_ref)

            def step(rows):
                residual_back(
                    rows, grads, resa_ref, us.at[own_rows[0]], dg_ref, dgain_ref, gres_ref, low_grad
                )

            by_rows(size, 32, step)
            resids.start()
            stays.append(here(low_grad, ra_out.at[mine_t]))

        for copy in loads_u + loads_f:
            copy.wait()
        denses[0].forward()
        ups[1].start()
        ups[0].arrive()
        ff_w[0].arrive()
        denses[0].arrive()
        tokens(0, 0)
        ff_w[1].forward()
        ff_w[2].start()
        after_out(1)
        ff_w[1].arrive()
        tokens(1, 0)
        ups[1].forward()
        denses[1].forward()
        ff_w[2].forward()
        ups[1].arrive()
        denses[1].arrive()
        tokens(0, 1)
        weigh(0)
        near[0].start()
        tokens(1, 1)
        weigh(1)
        ff_w[2].arrive()
        tokens(2, 0)
        outs[0].drain()
        for n, bits in enumerate((3, 1, 2, 0)):
            grad_block(0, me_t.flips[bits], outp)
            if n < 2:
                grads.start(1 - n)
        tokens(2, 1)
        grads.middle()
        normed[1].drain()
        keeps[1].wait()
        loop(0, parts, lambda r: grad_block(1, r, xs.at[1]))
        stays.append(here(xs.at[1], gb_out))
        near[0].middle(far)
        near[1].start()
        near[0].drain()
        weigh(2)
        stays.append(here(whole.at[0], w_out))
        after_grad()
        for exchange in ups:
            exchange.drain()
        loop(0, 2 * parts, down_block)
        for s in range(seqs):
            stays.append(here(us.at[halves[s]], y_out.at[s]))
        resids.forward()
        far.finish()
        near[1].middle()
        stays.append(here(wnear.at[1], wn_out))
        resids.arrive()
        for copy in stays:
            copy.wait()
        for exchange in (near[1], far):
            exchange.drain()

    pl.run_scoped(
        feed_forward,
        pltpu.VMEM((n_c, seqs * full, cols), BF16),
        pltpu.VMEM((n_c, seqs * full, 2 * cols), BF16),
        pltpu.VMEM((2, 4, 2, shard, wide), BF16),
    )
    for exchange in [pro_w, out_w] + ff_w + denses + [outs[1], grads, resids]:
        exchange.drain()


def fused_front(lengths, x, aw, up, fw, tabs, gains):
    seqs, size, width = up.shape
    full = 4 * size
    shard, cols = aw.shape
    n_c, _, wide = fw.shape
    dp = 8
    return pl.pallas_call(
        front_kernel,
        out_shape=(
            shape((dp * shard, cols), BF16),
            shape((seqs, full, width), BF16),
            shape((seqs, full, 384), F32),
            shape((seqs, full, 256), BF16),
            shape((seqs, full, 128), BF16),
            shape((seqs, full, 128), BF16),
            shape((seqs, full, 256), BF16),
            shape((seqs, 8, full), F32),
            shape((full, width), BF16),
            shape((full, width), BF16),
            shape((seqs, full, width), BF16),
            shape((4, shard, wide), BF16),
            shape((4, 2, shard, wide), BF16),
            shape((size, width), F32),
            shape((size, width), F32),
            shape((size, width), F32),
            shape((8, width), F32),
            shape((shard, wide), F32),
            shape((shard, wide), F32),
        ),
        in_specs=[SMEM, VMEM] + [ANY] * 3 + [VMEM] * 6,
        out_specs=(ANY,) * 13 + (VMEM,) * 6,
        scratch_shapes=[
            pltpu.VMEM((seqs, full, width), BF16),
            pltpu.VMEM((dp * shard, cols), BF16),
            pltpu.VMEM((seqs * full, width), BF16),
            pltpu.VMEM((seqs * full, width), BF16),
            pltpu.VMEM((n_c, dp * shard, wide), BF16),
            pltpu.VMEM((full, width), BF16),
            pltpu.VMEM((seqs, 2, size, width), BF16),
            pltpu.VMEM((seqs, size, width), BF16),
            pltpu.VMEM((2, size, width), BF16),
            pltpu.VMEM((size, width), BF16),
            pltpu.VMEM((size, width), BF16),
            pltpu.VMEM((2, 4, shard, wide), BF16),
            pltpu.VMEM((3, shard, wide), BF16),
        ]
        + COPY_SEMS,
        compiler_params=pltpu.CompilerParams(
            vmem_limit_bytes=FRONT_LIMIT, collective_id=0, has_side_effects=True
        ),
        cost_estimate=pl.CostEstimate(flops=60_000_000_000, bytes_accessed=60_000_000, transcendentals=10_000_000),
        name="front",
    )(lengths, x, aw, up, fw, *tabs, *gains)


def backward_kernel(
    lengths, n_ref, ra_ref, aw_ref, gb_ref, y_ref, wn_ref, w_ref, own_ref, gresa_ref, raw_ref, q_ref, k_ref, v_ref, att_ref, lse_ref,
    x_ref, up_ref, resa_ref, resb_ref, dgain_ref, cos_ref, sin_ref, gq_ref, gk_ref, mg_ref, dg_ref,
    ig_ref, blk_ref, awg_ref, ffg_ref, sums_ref,
    xs, gs, ws, kp, vp, kt, ga, dq, dk, dv, gp, drow, acc, gains, mixer, dgain,
    raw, q, k, v, att, lse,
    wo, wo_near, wo_far, wp, wp_near, wp_far, wf_near, wf_far, wf_mine,
    blocks, near, far, gnear, gfar, gmine, ynear, yfar, ymine, put, got, sems, local_sems,
):
    size, width = resa_ref.shape
    seqs, full = n_ref.shape[:2]
    parts = full // size
    wide = wn_ref.shape[2]
    me_t, me_d = spots()
    entered = enter(me_d, me_t)
    send, here = Remote(sems), Local(local_sems)
    mine_t = rows_of(me_t.index, size)
    resid_refs = (resa_ref, resb_ref)

    late = TokenReduce(gb_ref, gnear, gfar, send, me_t, gmine)
    resids = TokenGather(gs.at[1, mine_t], gs.at[1], send, me_t)
    outs = [TokenReduce(y_ref.at[s], ynear.at[s], yfar.at[s], send, me_t, ymine.at[s]) for s in range(seqs)]
    places = (blocks, gs.at[0])
    grads = [TokenReduce(places[s], near.at[s], far.at[s], send, me_t) for s in range(seqs)]
    sums = [ffg_ref.at[:, wide * c : wide * (c + 1)] for c in range(2)]
    ff_near = ShardNear(w_ref, wf_near, sums[1], send, me_d, wf_mine)
    ff_far = [ShardFar(source, wf_far.at[c], sums[c], send, me_d) for c, source in enumerate((wn_ref, wf_near))]
    out_near = ShardNear(wo, wo_near, awg_ref.at[:, 512:], send, me_d)
    out_far = ShardFar(wo_near, wo_far, awg_ref.at[:, 512:], send, me_d)
    pro_near = ShardNear(wp, wp_near, awg_ref.at[:, :512], send, me_d)
    pro_far = ShardFar(wp_near, wp_far, awg_ref.at[:, :512], send, me_d)
    steps = []
    for n, (axis, bits) in enumerate((("tensor", 1), ("tensor", 2), ("dp", 1), ("dp", 2), ("dp", 4))):
        device = {axis: (me_t if axis == "tensor" else me_d).flips[bits]}
        steps.append(send(put.at[n], got.at[n], device))

    kept = ((k_ref, k), (v_ref, v), (att_ref, att), (lse_ref, lse), (q_ref, q))
    load_w = [here(aw_ref, ws), here(ra_ref, gs.at[0])]
    load_s = [[here(source.at[s], target.at[s]) for source, target in kept] for s in range(seqs)]
    load_raw = [here(raw_ref.at[0], raw)]
    load_late = late.load(here)
    load_f = ff_near.load(here)
    load_y = [exchange.load(here) for exchange in outs]
    load_x = [here(n_ref.at[s], xs.at[s]) for s in range(seqs)]
    load_own = [here(own_ref, sums[0]), here(gresa_ref, ig_ref.at[:, :width])]
    gains[...] = jnp.zeros_like(gains)
    mixer[...] = jnp.zeros_like(mixer)
    dgain[...] = dgain_ref[...]

    def wait(copies):
        for copy in copies:
            copy.wait()

    def prepare(s):
        loop(0, parts, lambda r: prepare_rows(
            r, size, lengths[s], gs.at[s], ws, k.at[s], v.at[s], att.at[s], ga, drow, kp, kt, vp
        ))
        dk[...] = jnp.zeros_like(dk)
        dv[...] = jnp.zeros_like(dv)

    def sweep(s, start, stop):
        loop(start, stop, lambda i: sweep_rows(i, size, q.at[s], ga, kp, kt, vp, drow, lse.at[s], acc, dq, dk, dv))

    def unproject(s):
        loop(0, parts, lambda r: unproject_rows(
            r, size, lengths[s], (cos_ref, sin_ref), (gq_ref, gk_ref), raw, dq, dk, dv, gp.at[s], gains
        ))

    def grad_blocks(s):
        for n, bits in enumerate((3, 1, 2, 0)):
            rows = rows_of(me_t.flips[bits], size)
            places[s][rows, :] = dot_nt(gp[s, rows, :], ws[:, :512]).astype(BF16)
            if n < 2:
                grads[s].start(1 - n)

    def weigh(target, lefts, rights):
        def run(b):
            rows = rows_of(b, 256)
            total = sum(dot_tn(lefts[s, :, rows], rights[s]) for s in range(seqs))
            target[b] = total.astype(BF16).reshape(target.shape[1:])

        loop(0, target.shape[0], run)

    def after_late():
        late.arrive()
        by_rows(size, 32, lambda rows: residual_back(
            rows, late, resb_ref, up_ref.at[1], dg_ref, dgain, ig_ref.at[:, width:], gs.at[1, mine_t]
        ))
        resids.start()

    def after_out(s):
        outs[s].arrive()

        def step(rows):
            total = resid_refs[s][rows, :] + outs[s].rows(rows)
            blk_ref[rows, width * s : width * (s + 1)] = total.astype(BF16)

        by_rows(size, 32, step)

    def after(s):
        grads[s].arrive()
        lanes = slice(width * s, width * (s + 1))

        def step(rows):
            grad = grads[s].rows(rows)
            values = x_ref[rows, lanes].astype(F32)
            factor = rms_factor(values)
            product = grad * values * factor
            mixer[...] += jnp.sum(product.reshape(-1, 8, width), axis=0)
            weighted = grad * mg_ref[...]
            inner = jnp.mean(values * weighted, axis=-1, keepdims=True)
            ig_ref[rows, lanes] += factor * weighted - values * (factor * factor * factor) * inner

        by_rows(size, 32, step)

    entered()
    late.start()
    ff_far[0].start()
    ff_near.start()
    wait(load_w + load_s[0])
    prepare(0)
    wait(load_late)
    late.middle()
    for exchange in outs:
        exchange.start()
    sweep(0, 0, 3)
    after_late()
    sweep(0, 3, parts)
    wait(load_y[0])
    outs[0].middle()
    wait(load_raw)
    unproject(0)
    load_raw = [here(raw_ref.at[1], raw)]
    grad_blocks(0)
    wait(load_f)
    ff_near.middle(ff_far[1])
    resids.forward()
    grads[0].middle()
    resids.arrive()
    wait(load_s[1])
    prepare(1)
    weigh(wo, gs, att)
    out_near.start()
    sweep(1, 0, 3)
    wait(load_y[1])
    outs[1].middle()
    after_out(0)
    wait(load_own)
    after(0)
    ff_far[0].finish()
    sweep(1, 3, parts)
    wait(load_raw)
    unproject(1)
    wait(load_x)
    weigh(wp, xs, gp)
    pro_near.start()
    grad_blocks(1)
    grads[1].middle()
    out_near.middle(out_far)
    after_out(1)
    pro_near.middle(pro_far)
    after(1)
    for row, vector in ((0, mixer), (8, dgain)):
        total = jnp.sum(vector[...], axis=0, keepdims=True)
        for i in range(8):
            put[0, row + i : row + i + 1, :] = total[:, LANES * i : LANES * (i + 1)]
    put[0, 16:, :] = gains[...]
    for n, copy in enumerate(steps):
        copy.start()
        copy.wait_recv()
        total = put[n] + got[n]
        if n + 1 < len(steps):
            put[n + 1] = total
        else:
            sums_ref[...] = total
    ff_far[1].finish()
    out_far.finish()
    pro_far.finish()
    for copy in steps:
        copy.wait_send()
    for exchange in [late, resids, out_near, out_far, pro_near, pro_far, ff_near] + outs + grads + ff_far:
        exchange.drain()


def fused_backward(lengths, in_hbm, in_vmem):
    normed, aw, w = in_hbm[0], in_hbm[2], in_hbm[6]
    size, width = in_vmem[2].shape
    seqs, full = normed.shape[:2]
    cols = aw.shape[1]
    shard = aw.shape[0] // 8
    wide = w.shape[3]
    kept = [
        ((full, 384), F32),
        ((seqs, full, 256), BF16),
        ((seqs, full, 128), BF16),
        ((seqs, full, 128), BF16),
        ((seqs, full, 256), BF16),
        ((seqs, 8, full), F32),
    ]
    return pl.pallas_call(
        backward_kernel,
        out_shape=(
            shape((size, seqs * width), F32),
            shape((size, seqs * width), BF16),
            shape((shard, cols), F32),
            shape((shard, 2 * wide), F32),
            shape((24, LANES), F32),
        ),
        in_specs=[SMEM] + [ANY] * len(in_hbm) + [VMEM] * len(in_vmem),
        out_specs=(VMEM,) * 5,
        scratch_shapes=[
            pltpu.VMEM((seqs, full, width), BF16),
            pltpu.VMEM((seqs, full, width), BF16),
            pltpu.VMEM((width, cols), BF16),
            pltpu.VMEM((4, full, LANES), BF16),
            pltpu.VMEM((4, full, LANES), BF16),
            pltpu.VMEM((4, LANES, full), BF16),
            pltpu.VMEM((full, 256), BF16),
            pltpu.VMEM((full, 256), F32),
            pltpu.VMEM((2, full, LANES), F32),
            pltpu.VMEM((2, full, LANES), F32),
            pltpu.VMEM((seqs, full, 512), BF16),
            pltpu.VMEM((8, full), F32),
            pltpu.VMEM((2, LANES, size), F32),
            pltpu.VMEM((8, LANES), F32),
            pltpu.VMEM((8, width), F32),
            pltpu.VMEM((8, width), F32),
        ]
        + [pltpu.VMEM(*item) for item in kept]
        + [
            pltpu.VMEM((4, 2, shard, 256), BF16),
            pltpu.VMEM((4, shard, 256), BF16),
            pltpu.VMEM((3, shard, 256), BF16),
            pltpu.VMEM((4, 2, shard, 512), BF16),
            pltpu.VMEM((4, shard, 512), BF16),
            pltpu.VMEM((3, shard, 512), BF16),
            pltpu.VMEM((4, shard, wide), BF16),
            pltpu.VMEM((2, 3, shard, wide), BF16),
            pltpu.VMEM((4, shard, wide), BF16),
            pltpu.VMEM((full, width), BF16),
            pltpu.VMEM((seqs, 2, size, width), BF16),
            pltpu.VMEM((seqs, size, width), BF16),
            pltpu.VMEM((2, size, width), BF16),
            pltpu.VMEM((size, width), BF16),
            pltpu.VMEM((2, size, width), BF16),
            pltpu.VMEM((seqs, 2, size, width), BF16),
            pltpu.VMEM((seqs, size, width), BF16),
            pltpu.VMEM((seqs, 2, size, width), BF16),
            pltpu.VMEM((5, 24, LANES), F32),
            pltpu.VMEM((5, 24, LANES), F32),
        ]
        + COPY_SEMS,
        compiler_params=pltpu.CompilerParams(
            vmem_limit_bytes=FRONT_LIMIT, collective_id=1, has_side_effects=True
        ),
        cost_estimate=pl.CostEstimate(flops=28_000_000_000, bytes_accessed=40_000_000, transcendentals=6_000_000),
        name="backward",
    )(lengths, *in_hbm, *in_vmem)


def swap(values, axis, bits):
    return lax.ppermute(values, axis, [(i, i ^ bits) for i in range(lax.axis_size(axis))])


def gather_tokens(block):
    far = swap(block, "tensor", 2)
    return [block, swap(block, "tensor", 1), far, swap(far, "tensor", 1)]


def scatter_tokens(keep, send):
    near = swap(send, "tensor", 1)
    middle = (keep[1].astype(F32) + near[1].astype(F32)).astype(BF16)
    far = swap(middle, "tensor", 2)
    return keep[0].astype(F32) + near[0].astype(F32) + far.astype(F32)


def gather_shards(shard):
    if lax.axis_size("dp") != 8 or shard.shape[0] % LANES:
        return [lax.all_gather(shard, "dp", axis=0, tiled=True)]
    slots = [shard, swap(shard, "dp", 1)]
    for bits in (2, 4, 6):
        there = swap(shard, "dp", bits)
        slots += [there, swap(there, "dp", 1)]
    return slots


def scatter_shards(grads):
    if len(grads) == 1:
        return lax.psum_scatter(grads[0].astype(F32), "dp", scatter_dimension=0, tiled=True)
    keep, send = grads
    near = swap(send, "dp", 1)
    both = keep.astype(F32) + near.astype(F32)
    total = both[0]
    for slot in (1, 2, 3):
        total = total + swap(both[slot].astype(BF16), "dp", 2 * slot).astype(F32)
    return total


def sum_everywhere(values):
    for axis in ("tensor", "dp"):
        bits = 1
        while bits < lax.axis_size(axis):
            values = values + swap(values, axis, bits)
            bits *= 2
    return values


def norm_rows(values, gain):
    factor = lax.rsqrt(jnp.mean(values * values, axis=-1, keepdims=True) + EPS)
    return (values * factor * gain, factor)


def norm_back(values, factor, gain, upstream):
    weighted = upstream * gain
    inner = jnp.mean(values * weighted, axis=-1, keepdims=True)
    return factor * weighted - values * factor * factor * factor * inner


def tables(full, head_width):
    half = head_width // 2
    freqs = THETA ** (-jnp.arange(half, dtype=F32) * 2.0 / head_width)
    angles = jnp.arange(full, dtype=F32)[:, None] * freqs[None, :]
    cosines, sines = jnp.cos(angles), jnp.sin(angles)
    return (jnp.tile(cosines, (1, 4)), jnp.tile(jnp.concatenate([-sines, sines], axis=1), (1, 2)))


def local_plain(
    inputs,
    lengths,
    query_weight,
    key_value_weight,
    output_weight,
    inner_weight,
    down_weight,
    mixer_gain,
    query_gain,
    key_gain,
    dense_gain,
    cotangent,
):
    size, seqs, width = inputs.shape
    parts = lax.axis_size("tensor")
    full = size * parts
    head = query_gain.shape[0]
    query_cols = query_weight.shape[1]
    pair_cols = key_value_weight.shape[2]
    hidden = inner_weight.shape[2]
    shard = query_weight.shape[0]
    me_t, me_d = lax.axis_index("tensor"), lax.axis_index("dp")
    n_c = 3
    cols = hidden // n_c
    cosines, sines = tables(full, head)
    gq = jnp.tile(query_gain, 2)[None, :]
    gk = jnp.tile(key_gain, 2)[None, :]

    down_turned = down_weight.T
    attn_shard = jnp.concatenate(
        [query_weight, key_value_weight.reshape(shard, 2 * pair_cols), output_weight.T], axis=1
    )
    attn_w = gather_shards(attn_shard)
    positions = me_t * size + jnp.arange(size, dtype=jnp.int32)
    scals = [
        jnp.stack([me_t.astype(jnp.int32), me_d.astype(jnp.int32), lengths[s], jnp.int32(0)])
        for s in range(seqs)
    ]
    tokens = [inputs[:, s].astype(F32) for s in range(seqs)]
    valid = [(positions < lengths[s])[:, None] for s in range(seqs)]
    firsts = [norm_rows(tokens[s], mixer_gain) for s in range(seqs)]
    normed = [gather_tokens(firsts[s][0].astype(BF16)) for s in range(seqs)]
    ff_w = []
    for c in range(n_c):
        part = slice(c * cols, (c + 1) * cols)
        ff_w.append(
            gather_shards(
                jnp.concatenate(
                    [inner_weight[:, 0, part], inner_weight[:, 1, part], down_turned[:, part]], axis=1
                )
            )
        )
    upstream = [jnp.where(valid[s], cotangent[:, s].astype(F32), 0.0) for s in range(seqs)]
    up_parts = [gather_tokens(upstream[s].astype(BF16)) for s in range(seqs)]

    saved, residual, seconds, dense = [], [], [], []
    for s in range(seqs):
        outs = attn_fwd(scals[s], cosines, sines, gq, gk, normed[s], attn_w)
        saved.append(outs[:6])
        residual.append(tokens[s] + scatter_tokens(outs[6], outs[7]))
        dense_in, factor = norm_rows(residual[s], dense_gain)
        seconds.append(factor)
        dense.append(gather_tokens(dense_in.astype(BF16)))

    x_parts = [part for s in range(seqs) for part in dense[s]]
    u_parts = [part for s in range(seqs) for part in up_parts[s]]
    hids, ggus, ff_grads = [], [], []
    for c in range(n_c):
        hid, ggu, grads = feed_forward(scals[0], x_parts, u_parts, ff_w[c])
        hids.append(hid)
        ggus.append(ggu)
        ff_grads.append(scatter_shards(grads))

    block_out, input_gradient, attn_grads = [], [], []
    mixer_part = dense_part = gain_part = 0.0
    for s in range(seqs):
        ykeep, ysend, gkeep, gsend = ff_out(s, scals[s], parts, size, hids, ggus, ff_w)
        grad_dense = scatter_tokens(gkeep, gsend)
        dense_part = dense_part + jnp.sum(grad_dense * residual[s] * seconds[s], axis=0)
        grad_residual = upstream[s] + norm_back(residual[s], seconds[s], dense_gain, grad_dense)
        r_parts = gather_tokens(grad_residual.astype(BF16))
        nkeep, nsend, gains, grads = attn_bwd(
            scals[s], cosines, sines, gq, gk, saved[s], normed[s], r_parts, attn_w
        )
        attn_grads.append(grads)
        gain_part = gain_part + gains
        grad_normed = scatter_tokens(nkeep, nsend)
        factor = firsts[s][1]
        mixer_part = mixer_part + jnp.sum(grad_normed * tokens[s] * factor, axis=0)
        input_gradient.append(grad_residual + norm_back(tokens[s], factor, mixer_gain, grad_normed))
        out_sum = scatter_tokens(ykeep, ysend)
        block_out.append(jnp.where(valid[s], residual[s] + out_sum, 0.0).astype(BF16))

    summed = [
        sum(part.astype(F32) for part in parts_of).astype(BF16) for parts_of in zip(*attn_grads)
    ]
    attn_grad = scatter_shards(summed)
    early = sum_everywhere(jnp.concatenate([dense_part.reshape(-1, LANES), gain_part], axis=0))
    mixer = sum_everywhere(mixer_part.reshape(-1, LANES)).reshape(-1)
    dense_rows = width // LANES
    folded = early[dense_rows:, :head] + early[dense_rows:, head:]
    inner_gradient = jnp.stack(
        [
            jnp.concatenate([grad[:, p * cols : (p + 1) * cols] for grad in ff_grads], axis=1)
            for p in range(2)
        ],
        axis=1,
    )
    down_gradient = jnp.concatenate([grad[:, 2 * cols :] for grad in ff_grads], axis=1).T
    return (
        jnp.stack(block_out, axis=1),
        jnp.stack(input_gradient, axis=1),
        attn_grad[:, :query_cols],
        attn_grad[:, query_cols : query_cols + 2 * pair_cols].reshape(shard, 2, pair_cols),
        attn_grad[:, query_cols + 2 * pair_cols :].T,
        inner_gradient,
        down_gradient,
        mixer,
        folded[0],
        folded[1],
        early[:dense_rows].reshape(-1),
    )


def local(*args):
    inputs, shard = args[0], args[2].shape[0]
    if lax.axis_size("dp") == 8 and lax.axis_size("tensor") == 4 and shard % LANES == 0 and inputs.shape[1] == 2:
        return local_fused(*args)
    return local_plain(*args)


def rope_tables(full, head):
    half = head // 2
    freqs = np.float32(THETA) ** (-np.arange(half, dtype=np.float32) * np.float32(2.0) / np.float32(head))
    angles = np.arange(full, dtype=np.float32)[:, None] * freqs[None, :].astype(np.float32)
    cosines, sines = np.cos(angles), np.sin(angles)
    return (
        jnp.asarray(np.tile(cosines, (1, 4)), F32),
        jnp.asarray(np.tile(np.concatenate([-sines, sines], axis=1), (1, 2)), F32),
    )


def local_fused(
    inputs,
    lengths,
    query_weight,
    key_value_weight,
    output_weight,
    inner_weight,
    down_weight,
    mixer_gain,
    query_gain,
    key_gain,
    dense_gain,
    cotangent,
):
    size, seqs, width = inputs.shape
    parts = lax.axis_size("tensor")
    full = size * parts
    head = query_gain.shape[0]
    query_cols = query_weight.shape[1]
    pair_cols = key_value_weight.shape[2]
    hidden = inner_weight.shape[2]
    shard = query_weight.shape[0]
    me_t, me_d = lax.axis_index("tensor"), lax.axis_index("dp")
    n_c = 3
    cols = hidden // n_c
    tabs = rope_tables(full, head)
    gq = jnp.tile(query_gain, 2)[None, :]
    gk = jnp.tile(key_gain, 2)[None, :]
    gains = (gq, gk, mixer_gain[None, :], dense_gain[None, :])
    down_turned = down_weight.T
    attn_shard = jnp.concatenate(
        [query_weight, key_value_weight.reshape(shard, 2 * pair_cols), output_weight.T], axis=1
    )
    ff_shard = jnp.stack(
        [
            jnp.concatenate(
                [inner_weight[:, 0, part], inner_weight[:, 1, part], down_turned[:, part]], axis=1
            )
            for part in (slice(c * cols, (c + 1) * cols) for c in range(n_c))
        ]
    )
    positions = me_t * size + jnp.arange(size, dtype=jnp.int32)
    valid = [(positions < lengths[s])[:, None] for s in range(seqs)]
    upstream = jnp.stack([jnp.where(valid[s], cotangent[:, s], 0) for s in range(seqs)])
    x = inputs.reshape(size, seqs * width)

    (aw, normed, *saved, grad_a, grad_b, ys, near, whole, resid, resid_b, gres, dgain, first_sum, own) = fused_front(
        lengths, x, attn_shard, upstream, ff_shard, tabs, gains
    )
    input_gradient, blk, attn_grad, ff_grad, sums = fused_backward(
        lengths,
        (normed, grad_a, aw, grad_b, ys, near, whole, own, gres, *saved),
        (x, upstream, resid, resid_b, dgain, *tabs, *gains),
    )
    block_out = jnp.where(jnp.stack(valid, axis=1), blk.reshape(size, seqs, width), 0)
    ff_grad = jnp.concatenate([first_sum, ff_grad], axis=1).reshape(shard, n_c, 3, cols)
    inner_gradient = jnp.moveaxis(ff_grad[:, :, :2], 1, 2).reshape(shard, 2, hidden)
    down_gradient = ff_grad[:, :, 2].reshape(shard, hidden).T
    folded = sums[16:, :head] + sums[16:, head:]
    return (
        block_out,
        input_gradient.reshape(size, seqs, width),
        attn_grad[:, :query_cols],
        attn_grad[:, query_cols : query_cols + 2 * pair_cols].reshape(shard, 2, pair_cols),
        attn_grad[:, query_cols + 2 * pair_cols :].T,
        inner_gradient,
        down_gradient,
        sums[:8].reshape(-1),
        folded[0],
        folded[1],
        sums[8:16].reshape(-1),
    )


def solution(mesh):
    return jax.shard_map(
        local,
        mesh=mesh,
        in_specs=(
            P("tensor", "dp", None),
            P("dp"),
            P("dp", "tensor"),
            P("dp", None, "tensor"),
            P("tensor", "dp"),
            P("dp", None, "tensor"),
            P("tensor", "dp"),
            P(),
            P(),
            P(),
            P(),
            P("tensor", "dp", None),
        ),
        out_specs=(
            P("tensor", "dp", None),
            P("tensor", "dp", None),
            P("dp", "tensor"),
            P("dp", None, "tensor"),
            P("tensor", "dp"),
            P("dp", None, "tensor"),
            P("tensor", "dp"),
            P(),
            P(),
            P(),
            P(),
        ),
        check_vma=False,
    )
```

```python
import functools

import jax
import jax.numpy as jnp
import numpy as np
from jax import lax
from jax.experimental import pallas as pl
from jax.experimental.pallas import tpu as pltpu
from jax.sharding import PartitionSpec as P

EPS = 1e-05
THETA = 1000000.0
LOG2E = 1.4426950408889634
F32 = jnp.float32
BF16 = jnp.bfloat16
HIGH = lax.Precision.HIGHEST
LANES = 128
VMEM_LIMIT = 56 * 1024 * 1024
FRONT_LIMIT = 62 * 1024 * 1024
ANY = pl.BlockSpec(memory_space=pl.ANY)
VMEM = pl.BlockSpec(memory_space=pltpu.VMEM)
SMEM = pl.BlockSpec(memory_space=pltpu.SMEM)


def dot(a, b, **kw):
    return lax.dot_general(
        a, b, (((1,), (0,)), ((), ())), preferred_element_type=F32, **kw
    )


def dot_nt(a, b, **kw):
    return lax.dot_general(
        a, b, (((1,), (1,)), ((), ())), preferred_element_type=F32, **kw
    )


def dot_tn(a, b, **kw):
    return lax.dot_general(
        a, b, (((0,), (0,)), ((), ())), preferred_element_type=F32, **kw
    )


def iota(shape, axis):
    return lax.broadcasted_iota(jnp.int32, shape, axis)


def low_half(shape):
    return iota(shape, 1) % LANES < LANES // 2


def head_blocks(scale):
    shape = (LANES, LANES)
    return jnp.where(iota(shape, 0) // 64 == iota(shape, 1) // 64, scale, 0.0).astype(F32)


def head_rows(scale):
    return jnp.where(iota((8, 256), 0) == iota((8, 256), 1) // 64, scale, 0.0).astype(F32)


def partner(values):
    first = iota(values.shape, 1) % 64 < 32
    return jnp.where(first, pltpu.roll(values, LANES - 32, 1), pltpu.roll(values, 32, 1))


def rows_of(index, size):
    return pl.ds(pl.multiple_of(index * size, size), size)


def load_all(sources, targets, sems, first):
    copies = []
    for number, (source, target) in enumerate(zip(sources, targets)):
        copy = pltpu.make_async_copy(source, target, sems.at[first + number])
        copy.start()
        copies.append(copy)
    return copies


def shard_targets(w_refs, ws, me):
    size = w_refs[0].shape[0]
    if len(w_refs) == 1:
        return [ws]
    return [ws.at[rows_of(me ^ slot, size)] for slot in range(len(w_refs))]


def store_slots(whole, out_refs, me):
    if len(out_refs) == 1:
        out_refs[0][...] = whole[...]
        return
    keep_ref, send_ref = out_refs
    size = keep_ref.shape[1]
    for slot in range(2 * keep_ref.shape[0]):
        (send_ref if slot % 2 else keep_ref)[slot // 2] = whole[rows_of(me ^ slot, size), :]


def padded_heads(first, second, low, g, e):
    here = low if e == 0 else jnp.logical_not(low)
    return jnp.where(here, first if g == e else second, 0.0).astype(BF16)


def project_rows(r, size, length, xs, ws, tabs, gains, raw_ref, q_ref, k_ref, v_ref, kp, vp):
    rows = rows_of(r, size)
    cos_ref, sin_ref = tabs
    gq_ref, gk_ref = gains
    mean_of = head_blocks(1.0 / 64)
    low = low_half((size, LANES))
    projected = dot(xs[rows, :], ws[:, :512])
    raw_ref[rows, :] = projected[:, :384]
    cosines, sines = cos_ref[rows, :], sin_ref[rows, :]

    def turned(values, gain):
        mean = dot(values * values, mean_of, precision=HIGH)
        normed = values * lax.rsqrt(mean + EPS) * gain
        return normed * cosines + partner(normed) * sines

    for g in range(2):
        lanes = slice(LANES * g, LANES * (g + 1))
        q_ref[rows, lanes] = turned(projected[:, lanes], gq_ref[...]).astype(BF16)
    keys = turned(projected[:, 256:384], gk_ref[...])
    values = projected[:, 384:512]
    k_ref[rows, :] = keys.astype(BF16)
    v_ref[rows, :] = values.astype(BF16)
    live = r * size + iota((size, LANES), 0) < length
    ones = jnp.where(live, 1.0, 0.0)
    values = jnp.where(live, values, 0.0)
    keys_swap, values_swap = pltpu.roll(keys, 64, 1), pltpu.roll(values, 64, 1)
    for g in range(2):
        for e in range(2):
            kp[2 * g + e, rows, :] = padded_heads(keys, keys_swap, low, g, e)
            vp[2 * g + e, rows, :LANES] = padded_heads(values, values_swap, low, g, e)
            vp[2 * g + e, rows, LANES:] = padded_heads(ones, ones, low, g, e)


def attend_rows(i, size, q_ref, kp, vp, acc, att_ref, lse_ref):
    rows = rows_of(i, size)
    factor = LOG2E / 8.0
    causal = iota((size, size), 1) <= iota((size, size), 0)
    queries = [q_ref[rows, LANES * g : LANES * (g + 1)] for g in range(2)]

    def block(kb, masked):
        cols = rows_of(kb, size)
        sums = []
        for g in range(2):
            total = None
            for e in range(2):
                weights = jnp.exp2(dot_nt(queries[g], kp[2 * g + e, cols, :]) * factor)
                if masked:
                    weights = jnp.where(causal, weights, 0.0)
                part = dot(weights.astype(BF16), vp[2 * g + e, cols, :])
                total = part if total is None else total + part
            sums.append(total)
        return sums

    for g, total in enumerate(block(i, True)):
        acc[g] = total

    def more(kb, carry):
        for g, total in enumerate(block(kb, False)):
            acc[g] += total
        return carry

    lax.fori_loop(i - i, i, more, None)
    logs = []
    for g in range(2):
        lanes = slice(LANES * g, LANES * (g + 1))
        summed = acc[g, :, LANES:]
        att_ref[rows, lanes] = (acc[g, :, :LANES] / summed).astype(BF16)
        logs.append(jnp.log2(summed))
    lse_ref[:, rows] = dot_nt(head_rows(1.0 / 64), jnp.concatenate(logs, axis=1), precision=HIGH)


def attn_fwd_kernel(parts, n_w, scal, cos_ref, sin_ref, gq_ref, gk_ref, *refs):
    x_refs, refs = refs[:parts], refs[parts:]
    w_refs, refs = refs[:n_w], refs[n_w:]
    (raw_ref, q_ref, k_ref, v_ref, att_ref, lse_ref, keep_ref, send_ref, xs, ws, kp, vp, acc, sems) = refs
    size = x_refs[0].shape[0]
    me_t, me_d, length = scal[0], scal[1], scal[2]
    copies = load_all(w_refs, shard_targets(w_refs, ws, me_d), sems, 0)
    copies += load_all(x_refs, [xs.at[rows_of(me_t ^ j, size)] for j in range(parts)], sems, n_w)
    for copy in copies:
        copy.wait()

    def project(r, carry):
        project_rows(
            r, size, length, xs, ws, (cos_ref, sin_ref), (gq_ref, gk_ref), raw_ref, q_ref, k_ref, v_ref, kp, vp
        )
        return carry

    def attend(i, carry):
        attend_rows(i, size, q_ref, kp, vp, acc, att_ref, lse_ref)
        return carry

    lax.fori_loop(0, parts, project, 0)
    lax.fori_loop(0, parts, attend, 0)
    for j in range(parts):
        out = dot_nt(att_ref[rows_of(me_t ^ j, size), :], ws[:, 512:])
        (send_ref if j % 2 else keep_ref)[j // 2] = out.astype(BF16)


def attn_fwd(scal, cosines, sines, gq, gk, x_parts, w_parts):
    parts, n_w = len(x_parts), len(w_parts)
    size, width = x_parts[0].shape
    full = parts * size
    cols = w_parts[0].shape[1]
    pair = jax.ShapeDtypeStruct((parts // 2, size, width), BF16)
    return pl.pallas_call(
        functools.partial(attn_fwd_kernel, parts, n_w),
        out_shape=(
            jax.ShapeDtypeStruct((full, 384), F32),
            jax.ShapeDtypeStruct((full, 256), BF16),
            jax.ShapeDtypeStruct((full, 128), BF16),
            jax.ShapeDtypeStruct((full, 128), BF16),
            jax.ShapeDtypeStruct((full, 256), BF16),
            jax.ShapeDtypeStruct((8, full), F32),
            pair,
            pair,
        ),
        in_specs=[SMEM] + [VMEM] * 4 + [ANY] * (parts + n_w),
        out_specs=(VMEM,) * 8,
        scratch_shapes=[
            pltpu.VMEM((full, width), BF16),
            pltpu.VMEM((width, cols), BF16),
            pltpu.VMEM((4, full, LANES), BF16),
            pltpu.VMEM((4, full, 2 * LANES), BF16),
            pltpu.VMEM((2, size, 2 * LANES), F32),
            pltpu.SemaphoreType.DMA((n_w + parts,)),
        ],
        compiler_params=pltpu.CompilerParams(vmem_limit_bytes=VMEM_LIMIT),
        cost_estimate=pl.CostEstimate(flops=8_000_000_000, bytes_accessed=12_000_000, transcendentals=3_000_000),
        name="attention_forward",
    )(scal, cosines, sines, gq, gk, *x_parts, *w_parts)


def prepare_rows(r, size, length, gs, ws, k_ref, v_ref, att_ref, ga, drow, kp, kt, vp):
    rows = rows_of(r, size)
    low = low_half((size, LANES))
    grad = dot(gs[rows, :], ws[:, 512:]).astype(BF16)
    ga[rows, :] = grad
    drow[:, rows] = dot_nt(head_rows(1.0), grad.astype(F32) * att_ref[rows, :].astype(F32), precision=HIGH)
    live = r * size + iota((size, LANES), 0) < length
    keys = jnp.where(live, k_ref[rows, :].astype(F32), 0.0)
    values = jnp.where(live, v_ref[rows, :].astype(F32), 0.0)
    keys_swap, values_swap = pltpu.roll(keys, 64, 1), pltpu.roll(values, 64, 1)
    for g in range(2):
        for e in range(2):
            here = low if e == 0 else jnp.logical_not(low)
            padded = jnp.where(here, keys if g == e else keys_swap, 0.0)
            kp[2 * g + e, rows, :] = padded.astype(BF16)
            kt[2 * g + e, :, rows] = padded.T.astype(BF16)
            vp[2 * g + e, rows, :] = padded_heads(values, values_swap, low, g, e)


def sweep_rows(i, size, q_ref, ga, kp, kt, vp, drow, lrow, acc, dq, dk, dv):
    rows = rows_of(i, size)
    factor = LOG2E / 8.0
    causal = iota((size, size), 0) <= iota((size, size), 1)
    low2 = iota((2 * size, LANES), 0) // size == iota((2 * size, LANES), 1) // 64
    queries, grads, queries2, grads2 = [], [], [], []
    for g in range(2):
        lanes = slice(LANES * g, LANES * (g + 1))
        queries.append(q_ref[rows, lanes])
        grads.append(ga[rows, lanes])
        for source, target in ((queries, queries2), (grads, grads2)):
            both = jnp.concatenate([source[g], source[g]], axis=0)
            target.append(jnp.where(low2, both, jnp.zeros_like(both)))

    def block(kb, masked):
        cols = rows_of(kb, size)
        parts_t = []
        for g in range(2):
            weights2, scores2, turned = [], [], None
            for e in range(2):
                h = 2 * g + e
                weights = jnp.exp2(dot_nt(kp[h, cols, :], queries[g]) * factor - lrow[h : h + 1, rows])
                if masked:
                    weights = jnp.where(causal, weights, 0.0)
                grad_weights = dot_nt(vp[h, cols, :], grads[g])
                grad_scores = (weights * (grad_weights - drow[h : h + 1, rows])).astype(BF16)
                weights2.append(weights.astype(BF16))
                scores2.append(grad_scores)
                part = dot(kt[h, :, cols], grad_scores)
                turned = part if turned is None else turned + part
            dv[g, cols, :] += dot(jnp.concatenate(weights2, axis=1), grads2[g])
            dk[g, cols, :] += dot(jnp.concatenate(scores2, axis=1), queries2[g])
            parts_t.append(turned)
        return parts_t

    for g, total in enumerate(block(i, True)):
        acc[g] = total

    def more(kb, carry):
        for g, total in enumerate(block(kb, False)):
            acc[g] += total
        return carry

    lax.fori_loop(i - i, i, more, None)
    for g in range(2):
        dq[rows, LANES * g : LANES * (g + 1)] = acc[g].T


def unproject_rows(r, size, length, tabs, gains, raw_ref, dq, dk, dv, gp, gains_ref):
    rows = rows_of(r, size)
    cosines, sines = tabs[0][rows, :], tabs[1][rows, :]
    low = low_half((size, LANES))
    mean_of = head_blocks(1.0 / 64)
    live = r * size + iota((size, LANES), 0) < length

    def back(grad, lanes, gain, row):
        raw = raw_ref[rows, lanes]
        rms = lax.rsqrt(dot(raw * raw, mean_of, precision=HIGH) + EPS)
        turned = grad * cosines - partner(grad) * sines
        gains_ref[row : row + 1, :] += jnp.sum(turned * raw * rms, axis=0, keepdims=True)
        weighted = turned * gain
        inner = dot(raw * weighted, mean_of, precision=HIGH)
        gp[rows, lanes] = (rms * weighted - raw * (rms * rms * rms) * inner).astype(BF16)

    def folded(ref):
        first, second = ref[0, rows, :], ref[1, rows, :]
        both = jnp.where(low, first + pltpu.roll(first, 64, 1), second + pltpu.roll(second, 64, 1))
        return jnp.where(live, both, 0.0)

    for g in range(2):
        lanes = slice(LANES * g, LANES * (g + 1))
        back(dq[rows, lanes] * 0.125, lanes, gains[0][...], 0)
    back(folded(dk) * 0.125, slice(256, 384), gains[1][...], 1)
    gp[rows, 384:512] = folded(dv).astype(BF16)


def attn_bwd_kernel(parts, n_w, scal, cos_ref, sin_ref, gq_ref, gk_ref, raw_ref, q_ref, k_ref, v_ref, att_ref, lse_ref, *refs):
    x_refs, refs = refs[:parts], refs[parts:]
    r_refs, refs = refs[:parts], refs[parts:]
    w_refs, refs = refs[:n_w], refs[n_w:]
    n_g = 1 if n_w == 1 else 2
    keep_ref, send_ref, gains_ref = refs[:3]
    g_refs, refs = refs[3 : 3 + n_g], refs[3 + n_g :]
    xs, gs, ws, kp, vp, kt, ga, dq, dk, dv, gp, whole, drow, acc, sems = refs
    size = x_refs[0].shape[0]
    me_t, me_d, length = scal[0], scal[1], scal[2]
    copies = load_all(w_refs, shard_targets(w_refs, ws, me_d), sems, 0)
    copies += load_all(r_refs, [gs.at[rows_of(me_t ^ j, size)] for j in range(parts)], sems, n_w)
    copies += load_all(x_refs, [xs.at[rows_of(me_t ^ j, size)] for j in range(parts)], sems, n_w + parts)
    for copy in copies:
        copy.wait()

    def prepare(r, carry):
        prepare_rows(r, size, length, gs, ws, k_ref, v_ref, att_ref, ga, drow, kp, kt, vp)
        return carry

    def sweep(i, carry):
        sweep_rows(i, size, q_ref, ga, kp, kt, vp, drow, lse_ref, acc, dq, dk, dv)
        return carry

    def unproject(r, carry):
        unproject_rows(r, size, length, (cos_ref, sin_ref), (gq_ref, gk_ref), raw_ref, dq, dk, dv, gp, gains_ref)
        return carry

    lax.fori_loop(0, parts, prepare, 0)
    dk[...] = jnp.zeros_like(dk)
    dv[...] = jnp.zeros_like(dv)
    lax.fori_loop(0, parts, sweep, 0)
    gains_ref[...] = jnp.zeros_like(gains_ref)
    lax.fori_loop(0, parts, unproject, 0)
    for j in range(parts):
        out = dot_nt(gp[rows_of(me_t ^ j, size), :], ws[:, :512])
        (send_ref if j % 2 else keep_ref)[j // 2] = out.astype(BF16)

    def weigh(b, carry):
        rows = rows_of(b, 256)
        whole[rows, :512] = dot_tn(xs[:, rows], gp[...]).astype(BF16)
        whole[rows, 512:] = dot_tn(gs[:, rows], att_ref[...]).astype(BF16)
        return carry

    lax.fori_loop(0, whole.shape[0] // 256, weigh, 0)
    store_slots(whole, g_refs, me_d)


def slot_shapes(n_w, width, cols):
    if n_w == 1:
        return (jax.ShapeDtypeStruct((width, cols), BF16),)
    return (jax.ShapeDtypeStruct((n_w // 2, width // n_w, cols), BF16),) * 2


def attn_bwd(scal, cosines, sines, gq, gk, saved, x_parts, r_parts, w_parts):
    parts, n_w = len(x_parts), len(w_parts)
    size, width = x_parts[0].shape
    full = parts * size
    cols = w_parts[0].shape[1]
    pair = jax.ShapeDtypeStruct((parts // 2, size, width), BF16)
    g_shapes = slot_shapes(n_w, width, cols)
    outs = pl.pallas_call(
        functools.partial(attn_bwd_kernel, parts, n_w),
        out_shape=(pair, pair, jax.ShapeDtypeStruct((8, LANES), F32)) + g_shapes,
        in_specs=[SMEM] + [VMEM] * 10 + [ANY] * (2 * parts + n_w),
        out_specs=(VMEM,) * (3 + len(g_shapes)),
        scratch_shapes=[
            pltpu.VMEM((full, width), BF16),
            pltpu.VMEM((full, width), BF16),
            pltpu.VMEM((width, cols), BF16),
            pltpu.VMEM((4, full, LANES), BF16),
            pltpu.VMEM((4, full, LANES), BF16),
            pltpu.VMEM((4, LANES, full), BF16),
            pltpu.VMEM((full, 256), BF16),
            pltpu.VMEM((full, 256), F32),
            pltpu.VMEM((2, full, LANES), F32),
            pltpu.VMEM((2, full, LANES), F32),
            pltpu.VMEM((full, 512), BF16),
            pltpu.VMEM((width, cols), BF16),
            pltpu.VMEM((8, full), F32),
            pltpu.VMEM((2, LANES, size), F32),
            pltpu.SemaphoreType.DMA((n_w + 2 * parts,)),
        ],
        compiler_params=pltpu.CompilerParams(vmem_limit_bytes=VMEM_LIMIT),
        cost_estimate=pl.CostEstimate(flops=14_000_000_000, bytes_accessed=15_000_000, transcendentals=3_000_000),
        name="attention_backward",
    )(scal, cosines, sines, gq, gk, *saved, *x_parts, *r_parts, *w_parts)
    return outs[0], outs[1], outs[2], outs[3:]


def ff_kernel(n_x, n_w, scal, *refs):
    x_refs, refs = refs[:n_x], refs[n_x:]
    u_refs, refs = refs[:n_x], refs[n_x:]
    w_refs, refs = refs[:n_w], refs[n_w:]
    n_g = 1 if n_w == 1 else 2
    hid_ref, ggu_ref = refs[:2]
    g_refs, refs = refs[2 : 2 + n_g], refs[2 + n_g :]
    xs, us, ws, whole, sems = refs
    size = x_refs[0].shape[0]
    me_d = scal[1]
    cols = ws.shape[1] // 3
    copies = load_all(w_refs, shard_targets(w_refs, ws, me_d), sems, 0)
    x_copies = load_all(x_refs, [xs.at[pl.ds(j * size, size)] for j in range(n_x)], sems, n_w)
    u_copies = load_all(u_refs, [us.at[pl.ds(j * size, size)] for j in range(n_x)], sems, n_w + n_x)
    for copy in copies + x_copies + u_copies:
        copy.wait()

    def tokens(r, carry):
        rows = rows_of(r, size)
        gate_up = dot(xs[rows, :], ws[:, : 2 * cols])
        grad = dot(us[rows, :], ws[:, 2 * cols :])
        gate, up = gate_up[:, :cols], gate_up[:, cols:]
        sig = 1.0 / (1.0 + jnp.exp2(gate * -LOG2E))
        silu = gate * sig
        hid_ref[rows, :] = (silu * up).astype(BF16)
        ggu_ref[rows, :cols] = (grad * up * (sig + silu * (1.0 - sig))).astype(BF16)
        ggu_ref[rows, cols:] = (grad * silu).astype(BF16)
        return carry

    lax.fori_loop(0, n_x, tokens, 0)

    def weigh(b, carry):
        rows = rows_of(b, 256)
        whole[rows, : 2 * cols] = dot_tn(xs[:, rows], ggu_ref[...]).astype(BF16)
        whole[rows, 2 * cols :] = dot_tn(us[:, rows], hid_ref[...]).astype(BF16)
        return carry

    lax.fori_loop(0, whole.shape[0] // 256, weigh, 0)
    store_slots(whole, g_refs, me_d)


def feed_forward(scal, x_parts, u_parts, w_parts):
    n_x, n_w = len(x_parts), len(w_parts)
    size, width = x_parts[0].shape
    full = n_x * size
    wide = w_parts[0].shape[1]
    cols = wide // 3
    g_shapes = slot_shapes(n_w, width, wide)
    outs = pl.pallas_call(
        functools.partial(ff_kernel, n_x, n_w),
        out_shape=(
            jax.ShapeDtypeStruct((full, cols), BF16),
            jax.ShapeDtypeStruct((full, 2 * cols), BF16),
        )
        + g_shapes,
        in_specs=[SMEM] + [ANY] * (2 * n_x + n_w),
        out_specs=(VMEM,) * (2 + len(g_shapes)),
        scratch_shapes=[
            pltpu.VMEM((full, width), BF16),
            pltpu.VMEM((full, width), BF16),
            pltpu.VMEM((width, wide), BF16),
            pltpu.VMEM((width, wide), BF16),
            pltpu.SemaphoreType.DMA((n_w + 2 * n_x,)),
        ],
        compiler_params=pltpu.CompilerParams(vmem_limit_bytes=VMEM_LIMIT),
        cost_estimate=pl.CostEstimate(flops=4 * full * width * wide, bytes_accessed=20_000_000, transcendentals=full * cols),
        name="feed_forward",
    )(scal, *x_parts, *u_parts, *w_parts)
    return outs[0], outs[1], outs[2:]


def ff_out_kernel(parts, n_c, n_w, seq, scal, *refs):
    hid_refs, refs = refs[:n_c], refs[n_c:]
    ggu_refs, refs = refs[:n_c], refs[n_c:]
    w_refs, refs = refs[: n_c * n_w], refs[n_c * n_w :]
    ykeep_ref, ysend_ref, gkeep_ref, gsend_ref, hs, gs, ws, sems = refs
    size = ykeep_ref.shape[1]
    full = parts * size
    me_d = scal[1]
    wide = ws.shape[2]
    cols = wide // 3
    copies = []
    first = 0
    for c in range(n_c):
        targets = shard_targets(w_refs[c * n_w : (c + 1) * n_w], ws.at[c], me_d)
        copies += load_all(w_refs[c * n_w : (c + 1) * n_w], targets, sems, first)
        first += n_w
    mine = pl.ds(seq * full, full)
    copies += load_all([ref.at[mine] for ref in ggu_refs], [gs.at[c] for c in range(n_c)], sems, first)
    copies += load_all([ref.at[mine] for ref in hid_refs], [hs.at[c] for c in range(n_c)], sems, first + n_c)
    for copy in copies:
        copy.wait()
    for j in range(parts):
        rows = pl.ds(j * size, size)
        grad = sum(dot_nt(gs[c, rows, :], ws[c, :, : 2 * cols]) for c in range(n_c))
        (gsend_ref if j % 2 else gkeep_ref)[j // 2] = grad.astype(BF16)
        out = sum(dot_nt(hs[c, rows, :], ws[c, :, 2 * cols :]) for c in range(n_c))
        (ysend_ref if j % 2 else ykeep_ref)[j // 2] = out.astype(BF16)


def ff_out(seq, scal, parts, size, hids, ggus, w_chunks):
    n_c, n_w = len(w_chunks), len(w_chunks[0])
    wide = w_chunks[0][0].shape[1]
    width = w_chunks[0][0].shape[0] * n_w
    full = parts * size
    cols = wide // 3
    pair = jax.ShapeDtypeStruct((parts // 2, size, width), BF16)
    return pl.pallas_call(
        functools.partial(ff_out_kernel, parts, n_c, n_w, seq),
        out_shape=(pair,) * 4,
        in_specs=[SMEM] + [ANY] * (2 * n_c + n_c * n_w),
        out_specs=(VMEM,) * 4,
        scratch_shapes=[
            pltpu.VMEM((n_c, full, cols), BF16),
            pltpu.VMEM((n_c, full, 2 * cols), BF16),
            pltpu.VMEM((n_c, width, wide), BF16),
            pltpu.SemaphoreType.DMA((n_c * n_w + 2 * n_c,)),
        ],
        compiler_params=pltpu.CompilerParams(vmem_limit_bytes=VMEM_LIMIT),
        cost_estimate=pl.CostEstimate(flops=2 * full * width * wide * n_c, bytes_accessed=22_000_000, transcendentals=0),
        name="feed_forward_out",
    )(scal, *hids, *ggus, *[shard for chunk in w_chunks for shard in chunk])


def flip(index, bits):
    for bit in (1, 2, 4):
        if bits & bit:
            index = index + bit - 2 * bit * lax.rem(lax.div(index, bit), 2)
    return index


class Spot:
    def __init__(self, index, choices):
        self.index = index
        self.flips = {0: index}
        for bits in choices:
            self.flips[bits] = flip(index, bits)


def spots():
    me_t = Spot(lax.axis_index("tensor"), (1, 2, 3))
    me_d = Spot(lax.axis_index("dp"), (1, 2, 3, 4, 5, 6, 7))
    me_d.x = lax.rem(me_d.index, 2)
    me_d.beside = 1 - me_d.x
    me_d.z = Spot(lax.div(me_d.index, 2), (1, 2, 3))
    return me_t, me_d


def enter(me_d, me_t, along_d=(1, 2, 4, 6), along_t=(1, 2)):
    barrier = pltpu.get_barrier_semaphore()
    devices = [{"dp": me_d.flips[bits]} for bits in along_d]
    devices += [{"tensor": me_t.flips[bits]} for bits in along_t]
    for device in devices:
        pl.semaphore_signal(barrier, inc=1, device_id=device, device_id_type=pl.DeviceIdType.MESH)
    return lambda: pl.semaphore_wait(barrier, len(devices))


def remote(source, target, sems, number, device):
    return pltpu.make_async_remote_copy(
        src_ref=source,
        dst_ref=target,
        send_sem=sems.at[0, number],
        recv_sem=sems.at[1, number],
        device_id=device,
        device_id_type=pl.DeviceIdType.MESH,
    )


class Remote:
    LIMIT = 80

    def __init__(self, sems):
        self.sems, self.used = sems, 0

    def __call__(self, source, target, device):
        assert self.used < self.LIMIT
        self.used += 1
        return remote(source, target, self.sems, self.used - 1, device)


class Local:
    LIMIT = 64

    def __init__(self, sems):
        self.sems, self.used = sems, 0

    def make(self, source, target):
        assert self.used < self.LIMIT
        self.used += 1
        return pltpu.make_async_copy(source, target, self.sems.at[self.used - 1])

    def __call__(self, source, target):
        copy = self.make(source, target)
        copy.start()
        return copy


COPY_SEMS = [
    pltpu.SemaphoreType.DMA((2, Remote.LIMIT)),
    pltpu.SemaphoreType.DMA((Local.LIMIT,)),
]


class ShardGather:
    def __init__(self, shard, whole, send, me_d):
        size = shard.shape[0]
        mine = whole.at[rows_of(me_d.index, size)]
        self.own = [send(shard, mine, {"dp": me_d.flips[bits]}) for bits in (1, 2, 4, 6)]
        self.passed = []
        for bits in (2, 4, 6):
            there = whole.at[rows_of(me_d.flips[bits], size)]
            self.passed.append(send(there, there, {"dp": me_d.flips[1]}))

    def start_x(self):
        self.own[0].start()

    def start_z(self):
        for copy in self.own[1:]:
            copy.start()

    def start(self):
        self.start_x()
        self.start_z()

    def forward(self, *which):
        for n in which or (0, 1, 2):
            self.own[1 + n].wait_recv()
            self.passed[n].start()

    def arrive(self):
        self.own[0].wait_recv()
        for copy in self.passed:
            copy.wait_recv()

    def drain(self):
        for copy in self.own + self.passed:
            copy.wait_send()


class TokenGather:
    def __init__(self, block, whole, send, me_t):
        size = block.shape[0]
        mine = whole.at[rows_of(me_t.index, size)]
        there = whole.at[rows_of(me_t.flips[2], size)]
        near = {"tensor": me_t.flips[1]}
        self.near = send(block, mine, near)
        self.far = send(block, mine, {"tensor": me_t.flips[2]})
        self.passed = send(there, there, near)

    def start(self):
        self.far.start()
        self.near.start()

    def forward(self):
        self.far.wait_recv()
        self.passed.start()

    def arrive(self):
        self.near.wait_recv()
        self.passed.wait_recv()

    def drain(self):
        for copy in (self.near, self.far, self.passed):
            copy.wait_send()


class TokenReduce:
    def __init__(self, blocks, near, far, send, me_t, mine=None):
        device = {"tensor": me_t.flips[1]}
        self.blocks, self.near_ref, self.far_ref, self.mine = blocks, near, far, mine
        self.places = (me_t.index, me_t.flips[2])
        self.size = far.shape[0]
        self.near = [
            send(blocks.at[rows_of(me_t.flips[1 + 2 * n], self.size)], near.at[n], device) for n in range(2)
        ]
        self.far = send(near.at[1], far, {"tensor": me_t.flips[2]})

    def load(self, here):
        return [here(self.blocks.at[rows_of(place, self.size)], self.mine.at[n]) for n, place in enumerate(self.places)]

    def start(self, *which):
        for n in which or (1, 0):
            self.near[n].start()

    def part(self, n, rows):
        if self.mine is not None:
            return self.mine[n, rows, :].astype(F32)
        start = pl.multiple_of(self.places[n] * self.size + rows.start, 32)
        return self.blocks[pl.ds(start, rows.size), :].astype(F32)

    def middle(self):
        self.near[1].wait_recv()

        def step(rows):
            total = self.part(1, rows) + self.near_ref[1, rows, :].astype(F32)
            self.near_ref[1, rows, :] = total.astype(BF16)

        by_rows(self.size, 32, step)
        self.far.start()

    def arrive(self):
        self.near[0].wait_recv()
        self.far.wait_recv()

    def rows(self, rows):
        total = self.part(0, rows) + self.near_ref[0, rows, :].astype(F32)
        return total + self.far_ref[rows, :].astype(F32)

    def drain(self):
        for copy in self.near + [self.far]:
            copy.wait_send()


class ShardNear:
    def __init__(self, whole, near, out, send, me_d, mine=None):
        self.whole, self.near_ref, self.out, self.mine = whole, near, out, mine
        self.z, self.x = me_d.z, me_d.x
        self.size = near.shape[1]
        self.near = send(whole.at[:, me_d.beside], near, {"dp": me_d.flips[1]})

    def load(self, here):
        return [here(self.whole.at[:, self.x], self.mine)]

    def start(self):
        self.near.start()

    def part(self, there, rows):
        if self.mine is not None:
            return self.mine[there, rows, :].astype(F32)
        return self.whole[there, self.x, rows, :].astype(F32)

    def middle(self, far=None):
        self.near.wait_recv()
        for k in (1, 2, 3, 0):
            there = self.z.flips[k]

            def step(rows):
                total = self.part(there, rows) + self.near_ref[there, rows, :].astype(F32)
                if k:
                    self.near_ref[there, rows, :] = total.astype(BF16)
                else:
                    self.out[rows, :] = total

            by_rows(self.size, 32, step)
            if k and far is not None:
                far.far[k - 1].start()

    def drain(self):
        self.near.wait_send()


class ShardFar:
    def __init__(self, near, far, out, send, me_d):
        self.far_ref, self.out = far, out
        self.size = far.shape[1]
        self.far = [send(near.at[me_d.z.flips[k]], far.at[k - 1], {"dp": me_d.flips[2 * k]}) for k in (1, 2, 3)]

    def start(self):
        for copy in self.far:
            copy.start()

    def finish(self):
        for copy in self.far:
            copy.wait_recv()

        def step(rows):
            total = self.out[rows, :]
            for k in range(3):
                total = total + self.far_ref[k, rows, :].astype(F32)
            self.out[rows, :] = total

        by_rows(self.size, 32, step)

    def drain(self):
        for copy in self.far:
            copy.wait_send()


def by_rows(count, step, body):
    def run(b, carry):
        body(rows_of(b, step))
        return carry

    lax.fori_loop(0, count // step, run, None)


def loop(start, stop, body):
    def run(i, carry):
        body(i)
        return carry

    lax.fori_loop(start, stop, run, None)


def rms_factor(values):
    return lax.rsqrt(jnp.mean(values * values, axis=-1, keepdims=True) + EPS)


def shape(dims, kind):
    return jax.ShapeDtypeStruct(dims, kind)


def residual_back(rows, grads, resid_ref, up_ref, dg_ref, dgain_ref, gres_ref, low_ref):
    grad = grads.rows(rows)
    values = resid_ref[rows, :]
    factor = rms_factor(values)
    product = grad * values * factor
    dgain_ref[...] += jnp.sum(product.reshape(-1, 8, values.shape[1]), axis=0)
    weighted = grad * dg_ref[...]
    inner = jnp.mean(values * weighted, axis=-1, keepdims=True)
    total = up_ref[rows, :].astype(F32) + factor * weighted - values * (factor * factor * factor) * inner
    gres_ref[rows, :] = total
    low_ref[rows, :] = total.astype(BF16)


def front_kernel(
    lengths, x_ref, aw_ref, up_ref, fw_ref, cos_ref, sin_ref, gq_ref, gk_ref, mg_ref, dg_ref,
    aw_out, normed_out, raw_out, q_out, k_out, v_out, att_out, lse_out, ra_out, rb_out, y_out, wn_out, w_out,
    resa_ref, resb_ref, gres_ref, dgain_ref, sum_ref, own_ref,
    xs, ws, dn, us, wf, outp, onear, ofar, low_grad, wnear, wfar, sems, local_sems,
):
    size, width = resa_ref.shape
    seqs, full = xs.shape[:2]
    parts = full // size
    n_c, shard, wide = fw_ref.shape
    cols = wide // 3
    me_t, me_d = spots()
    entered = enter(me_d, me_t)
    send, here = Remote(sems), Local(local_sems)
    mine_t, mine_d = rows_of(me_t.index, size), rows_of(me_d.index, shard)
    resid_refs = (resa_ref, resb_ref)
    halves = [pl.ds(s * full, full) for s in range(seqs)]
    own_rows = [rows_of(s * parts + me_t.index, size) for s in range(seqs)]

    pro_w = ShardGather(aw_ref.at[:, :512], ws.at[:, :512], send, me_d)
    out_w = ShardGather(aw_ref.at[:, 512:], ws.at[:, 512:], send, me_d)
    ff_w = [ShardGather(fw_ref.at[c], wf.at[c], send, me_d) for c in range(n_c)]
    normed = [TokenGather(xs.at[s, mine_t], xs.at[s], send, me_t) for s in range(seqs)]
    ups = [TokenGather(up_ref.at[s], us.at[halves[s]], send, me_t) for s in range(seqs)]
    denses = [TokenGather(dn.at[own_rows[s]], dn.at[halves[s]], send, me_t) for s in range(seqs)]
    places = (outp, xs.at[0])
    outs = [TokenReduce(places[s], onear.at[s], ofar.at[s], send, me_t) for s in range(seqs)]
    grads = [TokenReduce((outp, xs.at[1])[s], onear.at[s], ofar.at[s], send, me_t) for s in range(seqs)]
    resids = TokenGather(low_grad.at[0], ra_out, send, me_t)

    loads = [here(aw_ref, ws.at[mine_d])]
    loads_u = [here(up_ref.at[s], us.at[own_rows[s]]) for s in range(seqs)]
    loads_f = [here(fw_ref.at[c], wf.at[c, mine_d]) for c in range(n_c)]
    keeps = [here.make(xs.at[s], normed_out.at[s]) for s in range(seqs)]
    stays = []

    def norm_first(s):
        def norm(rows):
            values = x_ref[rows, width * s : width * (s + 1)].astype(F32)
            target = pl.ds(pl.multiple_of(me_t.index * size + rows.start, 32), 32)
            xs[s, target, :] = (values * rms_factor(values) * mg_ref[...]).astype(BF16)

        by_rows(size, 32, norm)

    def after_out(s):
        outs[s].arrive()
        outs[s].drain()

        def norm(rows):
            values = x_ref[rows, width * s : width * (s + 1)].astype(F32) + outs[s].rows(rows)
            resid_refs[s][rows, :] = values
            target = pl.ds(pl.multiple_of((s * parts + me_t.index) * size + rows.start, 32), 32)
            dn[target, :] = (values * rms_factor(values) * dg_ref[...]).astype(BF16)

        by_rows(size, 32, norm)
        denses[s].start()

    def attention(kp, vp, acc, raw, q, k, v, att, lse):
        kept = ((raw, raw_out), (q, q_out), (k, k_out), (v, v_out), (att, att_out), (lse, lse_out))
        flushes = []

        def project(s):
            loop(0, parts, lambda r: project_rows(
                r, size, lengths[s], xs.at[s], ws, (cos_ref, sin_ref), (gq_ref, gk_ref),
                raw.at[s], q.at[s], k.at[s], v.at[s], kp, vp,
            ))

        def attend(s, start, stop):
            loop(start, stop, lambda i: attend_rows(i, size, q.at[s], kp, vp, acc, att.at[s], lse.at[s]))

        def out_block(s, bits):
            rows = rows_of(me_t.flips[bits], size)
            places[s][rows, :] = dot_nt(att[s, rows, :], ws[:, 512:]).astype(BF16)

        def out(s):
            for n, bits in enumerate((3, 1, 2, 0)):
                out_block(s, bits)
                if n < 2:
                    outs[s].start(1 - n)

        norm_first(0)
        entered()
        normed[0].start()
        pro_w.start()
        norm_first(1)
        pro_w.forward()
        out_w.start()
        normed[0].forward()
        normed[1].start()
        normed[0].arrive()
        for copy in loads:
            copy.wait()
        ff_w[0].start_z()
        pro_w.arrive()
        project(0)
        keeps[0].start()
        out_w.forward()
        attend(0, 0, 3)
        for exchange in ff_w[:2]:
            exchange.start_x()
        normed[1].forward()
        ups[0].start()
        attend(0, 3, parts)
        out_w.arrive()
        out(0)
        outs[0].middle()
        flushes.append(here(ws, aw_out))
        for source, target in kept:
            flushes.append(here(source.at[0], target.at[0]))
        normed[1].arrive()
        project(1)
        keeps[1].start()
        attend(1, 0, 3)
        ups[0].forward()
        ff_w[0].forward()
        ff_w[1].start_z()
        attend(1, 3, parts)
        normed[0].drain()
        keeps[0].wait()
        out(1)
        for source, target in kept:
            flushes.append(here(source.at[1], target.at[1]))
        after_out(0)
        outs[1].middle()
        for copy in flushes:
            copy.wait()

    pl.run_scoped(
        attention,
        pltpu.VMEM((4, full, LANES), BF16),
        pltpu.VMEM((4, full, 2 * LANES), BF16),
        pltpu.VMEM((2, size, 2 * LANES), F32),
        pltpu.VMEM((seqs, full, 384), F32),
        pltpu.VMEM((seqs, full, 256), BF16),
        pltpu.VMEM((seqs, full, 128), BF16),
        pltpu.VMEM((seqs, full, 128), BF16),
        pltpu.VMEM((seqs, full, 256), BF16),
        pltpu.VMEM((seqs, 8, full), F32),
    )

    def feed_forward(hid, ggu, whole):
        sums = (sum_ref, own_ref)
        near = [ShardNear(whole.at[c], wnear.at[c], sums[c], send, me_d) for c in range(2)]
        far = ShardFar(wnear.at[0], wfar, sum_ref, send, me_d)

        def tokens(c, s):
            def run(r):
                rows = rows_of(r, size)
                gate_up = dot(dn[rows, :], wf[c, :, : 2 * cols])
                grad = dot(us[rows, :], wf[c, :, 2 * cols :])
                gate, up = gate_up[:, :cols], gate_up[:, cols:]
                sig = 1.0 / (1.0 + jnp.exp2(gate * -LOG2E))
                silu = gate * sig
                hid[c, rows, :] = (silu * up).astype(BF16)
                ggu[c, rows, :cols] = (grad * up * (sig + silu * (1.0 - sig))).astype(BF16)
                ggu[c, rows, cols:] = (grad * silu).astype(BF16)

            loop(s * parts, (s + 1) * parts, run)

        def weigh(c, tokens, more=False):
            def run(b):
                rows = rows_of(b, 256)
                dims = whole.shape[2:4]
                inner = dot_tn(dn[tokens, rows], ggu[c, tokens, :]).reshape(dims + (2 * cols,))
                down = dot_tn(us[tokens, rows], hid[c, tokens, :]).reshape(dims + (cols,))
                if more:
                    inner = inner + whole[c % 2, b, :, :, : 2 * cols].astype(F32)
                    down = down + whole[c % 2, b, :, :, 2 * cols :].astype(F32)
                whole[c % 2, b, :, :, : 2 * cols] = inner.astype(BF16)
                whole[c % 2, b, :, :, 2 * cols :] = down.astype(BF16)

            loop(0, whole.shape[1], run)

        def grad_block(s, block, target):
            rows = rows_of(s * parts + block, size)
            total = sum(dot_nt(ggu[c, rows, :], wf[c, :, : 2 * cols]) for c in range(n_c))
            target[rows_of(block, size), :] = total.astype(BF16)

        def down_block(r):
            rows = rows_of(r, size)
            total = sum(dot_nt(hid[c, rows, :], wf[c, :, 2 * cols :]) for c in range(n_c))
            us[rows, :] = total.astype(BF16)

        def after_grad(s):
            grads[s].arrive()
            lanes = slice(width * s, width * (s + 1))

            def step(rows):
                residual_back(
                    rows, grads[s], resid_refs[s], us.at[own_rows[s]], dg_ref, dgain_ref,
                    gres_ref.at[:, lanes], low_grad.at[s],
                )

            by_rows(size, 32, step)

        for copy in loads_u + loads_f:
            copy.wait()
        denses[0].forward()
        ups[1].start()
        ups[0].arrive()
        ff_w[0].arrive()
        denses[0].arrive()
        tokens(0, 0)
        ff_w[1].forward()
        ff_w[2].start()
        weigh(0, halves[0])
        after_out(1)
        ff_w[1].arrive()
        tokens(1, 0)
        weigh(1, halves[0])
        ups[1].forward()
        denses[1].forward()
        ff_w[2].forward()
        ups[1].arrive()
        denses[1].arrive()
        tokens(0, 1)
        weigh(0, halves[1], True)
        near[0].start()
        tokens(1, 1)
        weigh(1, halves[1], True)
        ff_w[2].arrive()
        tokens(2, 0)
        def grad_blocks(s):
            for n, bits in enumerate((3, 1, 2, 0)):
                grad_block(s, me_t.flips[bits], (outp, xs.at[1])[s])
                if n < 2:
                    grads[s].start(1 - n)

        grad_blocks(0)
        tokens(2, 1)
        grads[0].middle()
        normed[1].drain()
        keeps[1].wait()
        grad_blocks(1)
        dgain_ref[...] = jnp.zeros_like(dgain_ref)
        near[0].middle(far)
        near[1].start()
        near[0].drain()
        grads[1].middle()
        weigh(2, pl.ds(0, seqs * full))
        stays.append(here(whole.at[0], w_out))
        after_grad(0)
        resids.start()
        stays.append(here(low_grad.at[0], ra_out.at[mine_t]))
        after_grad(1)
        stays.append(here(low_grad.at[1], rb_out))
        for exchange in ups:
            exchange.drain()
        loop(0, 2 * parts, down_block)
        for s in range(seqs):
            stays.append(here(us.at[halves[s]], y_out.at[s]))
        resids.forward()
        far.finish()
        near[1].middle()
        stays.append(here(wnear.at[1], wn_out))
        resids.arrive()
        for copy in stays:
            copy.wait()
        for exchange in (near[1], far):
            exchange.drain()

    pl.run_scoped(
        feed_forward,
        pltpu.VMEM((n_c, seqs * full, cols), BF16),
        pltpu.VMEM((n_c, seqs * full, 2 * cols), BF16),
        pltpu.VMEM((2, 4, 2, shard, wide), BF16),
    )
    for exchange in [pro_w, out_w] + ff_w + denses + grads + [resids]:
        exchange.drain()


def fused_front(lengths, x, aw, up, fw, tabs, gains):
    seqs, size, width = up.shape
    full = 4 * size
    shard, cols = aw.shape
    n_c, _, wide = fw.shape
    dp = 8
    return pl.pallas_call(
        front_kernel,
        out_shape=(
            shape((dp * shard, cols), BF16),
            shape((seqs, full, width), BF16),
            shape((seqs, full, 384), F32),
            shape((seqs, full, 256), BF16),
            shape((seqs, full, 128), BF16),
            shape((seqs, full, 128), BF16),
            shape((seqs, full, 256), BF16),
            shape((seqs, 8, full), F32),
            shape((full, width), BF16),
            shape((size, width), BF16),
            shape((seqs, full, width), BF16),
            shape((4, shard, wide), BF16),
            shape((4, 2, shard, wide), BF16),
            shape((size, width), F32),
            shape((size, width), F32),
            shape((size, seqs * width), F32),
            shape((8, width), F32),
            shape((shard, wide), F32),
            shape((shard, wide), F32),
        ),
        in_specs=[SMEM, VMEM] + [ANY] * 3 + [VMEM] * 6,
        out_specs=(ANY,) * 13 + (VMEM,) * 6,
        scratch_shapes=[
            pltpu.VMEM((seqs, full, width), BF16),
            pltpu.VMEM((dp * shard, cols), BF16),
            pltpu.VMEM((seqs * full, width), BF16),
            pltpu.VMEM((seqs * full, width), BF16),
            pltpu.VMEM((n_c, dp * shard, wide), BF16),
            pltpu.VMEM((full, width), BF16),
            pltpu.VMEM((seqs, 2, size, width), BF16),
            pltpu.VMEM((seqs, size, width), BF16),
            pltpu.VMEM((seqs, size, width), BF16),
            pltpu.VMEM((2, 4, shard, wide), BF16),
            pltpu.VMEM((3, shard, wide), BF16),
        ]
        + COPY_SEMS,
        compiler_params=pltpu.CompilerParams(
            vmem_limit_bytes=FRONT_LIMIT, collective_id=0, has_side_effects=True
        ),
        cost_estimate=pl.CostEstimate(flops=60_000_000_000, bytes_accessed=60_000_000, transcendentals=10_000_000),
        name="front",
    )(lengths, x, aw, up, fw, *tabs, *gains)


def backward_kernel(
    lengths, n_ref, ra_ref, aw_ref, rb_ref, y_ref, wn_ref, w_ref, own_ref, gres_ref, raw_ref, q_ref, k_ref, v_ref, att_ref, lse_ref,
    x_ref, resa_ref, resb_ref, dgain_ref, cos_ref, sin_ref, gq_ref, gk_ref, mg_ref,
    ig_ref, blk_ref, awg_ref, ffg_ref, sums_ref,
    xs, gs, ws, kp, vp, kt, ga, dq, dk, dv, gp, drow, acc, gains, mixer,
    raw, q, k, v, att, lse,
    wo, wo_near, wo_far, wq, wq_near, wq_far, wk, wk_near, wk_far, wf_near, wf_far, wf_mine,
    blocks, near, far, ynear, yfar, ymine, put, got_t, got_d, sems, local_sems,
):
    size, width = resa_ref.shape
    seqs, full = n_ref.shape[:2]
    parts = full // size
    wide = wn_ref.shape[2]
    me_t, me_d = spots()
    entered = enter(me_d, me_t, (1, 2, 3, 4, 5, 6, 7), (1, 2, 3))
    send, here = Remote(sems), Local(local_sems)
    mine_t = rows_of(me_t.index, size)
    resid_refs = (resa_ref, resb_ref)

    resids = TokenGather(rb_ref, gs.at[1], send, me_t)
    outs = [TokenReduce(y_ref.at[s], ynear.at[s], yfar.at[s], send, me_t, ymine.at[s]) for s in range(seqs)]
    places = (blocks, gs.at[0])
    grads = [TokenReduce(places[s], near.at[s], far.at[s], send, me_t) for s in range(seqs)]
    sums = [ffg_ref.at[:, wide * c : wide * (c + 1)] for c in range(2)]
    ff_near = ShardNear(w_ref, wf_near, sums[1], send, me_d, wf_mine)
    ff_far = [ShardFar(source, wf_far.at[c], sums[c], send, me_d) for c, source in enumerate((wn_ref, wf_near))]
    out_near = ShardNear(wo, wo_near, awg_ref.at[:, 512:], send, me_d)
    out_far = ShardFar(wo_near, wo_far, awg_ref.at[:, 512:], send, me_d)
    pro_near = [
        ShardNear(wq, wq_near, awg_ref.at[:, :256], send, me_d),
        ShardNear(wk, wk_near, awg_ref.at[:, 256:512], send, me_d),
    ]
    pro_far = [
        ShardFar(wq_near, wq_far, awg_ref.at[:, :256], send, me_d),
        ShardFar(wk_near, wk_far, awg_ref.at[:, 256:512], send, me_d),
    ]
    steps = [
        [send(put.at[0], got_t.at[me_t.index], {"tensor": me_t.flips[bits]}) for bits in (1, 2, 3)],
        [send(put.at[1], got_d.at[me_d.index], {"dp": me_d.flips[bits]}) for bits in (1, 2, 3, 4, 5, 6, 7)],
    ]

    kept = ((k_ref, k), (v_ref, v), (att_ref, att), (lse_ref, lse), (q_ref, q))
    load_w = [here(aw_ref, ws), here(ra_ref, gs.at[0])]
    load_b = [here(rb_ref, gs.at[1, mine_t])]
    load_s = [[here(source.at[s], target.at[s]) for source, target in kept] for s in range(seqs)]
    load_raw = [here(raw_ref.at[0], raw)]
    load_f = ff_near.load(here)
    load_y = [exchange.load(here) for exchange in outs]
    load_x = [here(n_ref.at[s], xs.at[s]) for s in range(seqs)]
    load_own = [here(own_ref, sums[0]), here(gres_ref, ig_ref)]
    gains[...] = jnp.zeros_like(gains)
    mixer[...] = jnp.zeros_like(mixer)

    def wait(copies):
        for copy in copies:
            copy.wait()

    def prepare(s):
        loop(0, parts, lambda r: prepare_rows(
            r, size, lengths[s], gs.at[s], ws, k.at[s], v.at[s], att.at[s], ga, drow, kp, kt, vp
        ))
        dk[...] = jnp.zeros_like(dk)
        dv[...] = jnp.zeros_like(dv)

    def sweep(s, start, stop):
        loop(start, stop, lambda i: sweep_rows(i, size, q.at[s], ga, kp, kt, vp, drow, lse.at[s], acc, dq, dk, dv))

    def unproject(s):
        loop(0, parts, lambda r: unproject_rows(
            r, size, lengths[s], (cos_ref, sin_ref), (gq_ref, gk_ref), raw, dq, dk, dv, gp.at[s], gains
        ))

    def grad_blocks(s):
        for n, bits in enumerate((3, 1, 2, 0)):
            rows = rows_of(me_t.flips[bits], size)
            places[s][rows, :] = dot_nt(gp[s, rows, :], ws[:, :512]).astype(BF16)
            if n < 2:
                grads[s].start(1 - n)

    def weigh(target, lefts, rights, lanes=slice(0, 256)):
        def run(b):
            rows = rows_of(b, 256)
            total = sum(dot_tn(lefts[s, :, rows], rights[s, :, lanes]) for s in range(seqs))
            target[b] = total.astype(BF16).reshape(target.shape[1:])

        loop(0, target.shape[0], run)

    def after_out(s):
        outs[s].arrive()

        def step(rows):
            total = resid_refs[s][rows, :] + outs[s].rows(rows)
            blk_ref[rows, width * s : width * (s + 1)] = total.astype(BF16)

        by_rows(size, 32, step)

    def after(s):
        grads[s].arrive()
        lanes = slice(width * s, width * (s + 1))

        def step(rows):
            grad = grads[s].rows(rows)
            values = x_ref[rows, lanes].astype(F32)
            factor = rms_factor(values)
            product = grad * values * factor
            mixer[...] += jnp.sum(product.reshape(-1, 8, width), axis=0)
            weighted = grad * mg_ref[...]
            inner = jnp.mean(values * weighted, axis=-1, keepdims=True)
            ig_ref[rows, lanes] += factor * weighted - values * (factor * factor * factor) * inner

        by_rows(size, 32, step)

    entered()
    resids.start()
    ff_far[0].start()
    ff_near.start()
    for exchange in outs:
        exchange.start()
    wait(load_w + load_s[0])
    prepare(0)
    sweep(0, 0, 3)
    resids.forward()
    wait(load_y[0] + load_y[1])
    outs[0].middle()
    sweep(0, 3, parts)
    wait(load_raw)
    unproject(0)
    load_raw = [here(raw_ref.at[1], raw)]
    grad_blocks(0)
    wait(load_f)
    grads[0].middle()
    ff_near.middle(ff_far[1])
    resids.arrive()
    wait(load_s[1] + load_b)
    prepare(1)
    weigh(wo, gs, att)
    out_near.start()
    sweep(1, 0, 2)
    outs[1].middle()
    sweep(1, 2, 3)
    out_near.middle(out_far)
    sweep(1, 3, parts)
    wait(load_raw)
    unproject(1)
    grad_blocks(1)
    wait(load_x)
    weigh(wq, xs, gp)
    pro_near[0].start()
    grads[1].middle()
    weigh(wk, xs, gp, slice(256, 512))
    pro_near[1].start()
    wait(load_own)
    after(0)
    pro_near[0].middle(pro_far[0])
    after_out(0)
    after_out(1)
    ff_far[0].finish()
    ff_far[1].finish()
    out_far.finish()
    pro_near[1].middle(pro_far[1])
    after(1)
    for row, vector in ((0, mixer), (8, dgain_ref)):
        total = jnp.sum(vector[...], axis=0, keepdims=True)
        for i in range(8):
            put[0, row + i : row + i + 1, :] = total[:, LANES * i : LANES * (i + 1)]
    put[0, 16:, :] = gains[...]
    for n, (got, index) in enumerate(((got_t, me_t.index), (got_d, me_d.index))):
        for copy in steps[n]:
            copy.start()
        got[index] = put[n]
        for copy in steps[n]:
            copy.wait_recv()
        total = got[0]
        for place in range(1, got.shape[0]):
            total = total + got[place]
        if n == 0:
            put[1] = total
        else:
            sums_ref[...] = total
    for exchange in pro_far:
        exchange.finish()
    for copy in steps[0] + steps[1]:
        copy.wait_send()
    for exchange in [resids, out_near, out_far, ff_near] + pro_near + pro_far + outs + grads + ff_far:
        exchange.drain()


def fused_backward(lengths, in_hbm, in_vmem):
    normed, aw, w = in_hbm[0], in_hbm[2], in_hbm[6]
    size, width = in_vmem[1].shape
    seqs, full = normed.shape[:2]
    cols = aw.shape[1]
    shard = aw.shape[0] // 8
    wide = w.shape[3]
    kept = [
        ((full, 384), F32),
        ((seqs, full, 256), BF16),
        ((seqs, full, 128), BF16),
        ((seqs, full, 128), BF16),
        ((seqs, full, 256), BF16),
        ((seqs, 8, full), F32),
    ]
    return pl.pallas_call(
        backward_kernel,
        out_shape=(
            shape((size, seqs * width), F32),
            shape((size, seqs * width), BF16),
            shape((shard, cols), F32),
            shape((shard, 2 * wide), F32),
            shape((24, LANES), F32),
        ),
        in_specs=[SMEM] + [ANY] * len(in_hbm) + [VMEM] * len(in_vmem),
        out_specs=(VMEM,) * 5,
        scratch_shapes=[
            pltpu.VMEM((seqs, full, width), BF16),
            pltpu.VMEM((seqs, full, width), BF16),
            pltpu.VMEM((width, cols), BF16),
            pltpu.VMEM((4, full, LANES), BF16),
            pltpu.VMEM((4, full, LANES), BF16),
            pltpu.VMEM((4, LANES, full), BF16),
            pltpu.VMEM((full, 256), BF16),
            pltpu.VMEM((full, 256), F32),
            pltpu.VMEM((2, full, LANES), F32),
            pltpu.VMEM((2, full, LANES), F32),
            pltpu.VMEM((seqs, full, 512), BF16),
            pltpu.VMEM((8, full), F32),
            pltpu.VMEM((2, LANES, size), F32),
            pltpu.VMEM((8, LANES), F32),
            pltpu.VMEM((8, width), F32),
        ]
        + [pltpu.VMEM(*item) for item in kept]
        + [
            pltpu.VMEM((4, 2, shard, 256), BF16),
            pltpu.VMEM((4, shard, 256), BF16),
            pltpu.VMEM((3, shard, 256), BF16),
            pltpu.VMEM((4, 2, shard, 256), BF16),
            pltpu.VMEM((4, shard, 256), BF16),
            pltpu.VMEM((3, shard, 256), BF16),
            pltpu.VMEM((4, 2, shard, 256), BF16),
            pltpu.VMEM((4, shard, 256), BF16),
            pltpu.VMEM((3, shard, 256), BF16),
            pltpu.VMEM((4, shard, wide), BF16),
            pltpu.VMEM((2, 3, shard, wide), BF16),
            pltpu.VMEM((4, shard, wide), BF16),
            pltpu.VMEM((full, width), BF16),
            pltpu.VMEM((seqs, 2, size, width), BF16),
            pltpu.VMEM((seqs, size, width), BF16),
            pltpu.VMEM((seqs, 2, size, width), BF16),
            pltpu.VMEM((seqs, size, width), BF16),
            pltpu.VMEM((seqs, 2, size, width), BF16),
            pltpu.VMEM((2, 24, LANES), F32),
            pltpu.VMEM((4, 24, LANES), F32),
            pltpu.VMEM((8, 24, LANES), F32),
        ]
        + COPY_SEMS,
        compiler_params=pltpu.CompilerParams(
            vmem_limit_bytes=FRONT_LIMIT, collective_id=1, has_side_effects=True
        ),
        cost_estimate=pl.CostEstimate(flops=28_000_000_000, bytes_accessed=40_000_000, transcendentals=6_000_000),
        name="backward",
    )(lengths, *in_hbm, *in_vmem)


def begin_kernel(
    lengths, in_ref, cot_ref, qw_ref, kv_ref, ow_ref, iw_ref, dw_ref, qg_ref, kg_ref,
    x_out, up_out, aw_out, fw_out, gq_out, gk_out,
):
    size, seqs, width = in_ref.shape
    cols = fw_out.shape[2] // 3
    start = lax.axis_index("tensor") * size

    def step(rows):
        place = start + rows.start + iota((32, width), 0)
        values = in_ref[rows, :, :].astype(F32)
        grads = cot_ref[rows, :, :].astype(F32)
        for s in range(seqs):
            x_out[rows, width * s : width * (s + 1)] = values[:, s, :].astype(BF16)
            up_out[s, rows, :] = jnp.where(place < lengths[s], grads[:, s, :], 0.0).astype(BF16)

    by_rows(size, 32, step)
    aw_out[:, :256] = qw_ref[...]
    pair = kv_ref[...].astype(F32)
    for n in range(2):
        aw_out[:, 256 + 128 * n : 384 + 128 * n] = pair[:, n, :].astype(BF16)
    aw_out[:, 512:] = ow_ref[...].astype(F32).T.astype(BF16)

    def inner(rows):
        both = iw_ref[rows, :, :].astype(F32)
        for c in range(3):
            for n in range(2):
                fw_out[c, rows, cols * n : cols * (n + 1)] = both[:, n, cols * c : cols * (c + 1)].astype(BF16)

    by_rows(iw_ref.shape[0], 32, inner)
    for c in range(3):
        fw_out[c, :, 2 * cols :] = dw_ref[cols * c : cols * (c + 1), :].astype(F32).T.astype(BF16)
    for source, target in ((qg_ref, gq_out), (kg_ref, gk_out)):
        target[...] = jnp.concatenate([source[...], source[...]], axis=1)


def fused_begin(lengths, inputs, cotangent, weights, query_gain, key_gain, n_c):
    size, seqs, width = inputs.shape
    shard = weights[0].shape[0]
    hidden = weights[3].shape[2]
    return pl.pallas_call(
        begin_kernel,
        out_shape=(
            shape((size, seqs * width), BF16),
            shape((seqs, size, width), BF16),
            shape((shard, 768), BF16),
            shape((n_c, shard, 3 * hidden // n_c), BF16),
            shape((1, LANES), F32),
            shape((1, LANES), F32),
        ),
        in_specs=[SMEM] + [VMEM] * 9,
        out_specs=(VMEM,) * 6,
        compiler_params=pltpu.CompilerParams(vmem_limit_bytes=VMEM_LIMIT),
        name="begin",
    )(lengths, inputs, cotangent, *weights, query_gain[None, :], key_gain[None, :])


def finish_kernel(
    lengths, ig_ref, blk_ref, awg_ref, first_ref, ffg_ref,
    block_out, input_out, query_out, pair_out, output_out, inner_out, down_out,
):
    size, seqs, width = input_out.shape
    wide = first_ref.shape[1]
    cols = wide // 3
    start = lax.axis_index("tensor") * size

    def step(rows):
        place = start + rows.start + iota((32, width), 0)
        parts = []
        for s in range(seqs):
            lanes = slice(width * s, width * (s + 1))
            input_out[rows, s, :] = ig_ref[rows, lanes]
            parts.append(jnp.where(place < lengths[s], blk_ref[rows, lanes].astype(F32), 0.0))
        block_out[rows, :, :] = jnp.stack(parts, axis=1).astype(BF16)

    by_rows(size, 32, step)
    query_out[...] = awg_ref[:, :256]
    for n in range(2):
        pair_out[:, n, :] = awg_ref[:, 256 + 128 * n : 384 + 128 * n]
    output_out[...] = awg_ref[:, 512:].T
    for c in range(3):
        ref, base = (first_ref, 0) if c == 0 else (ffg_ref, wide * (c - 1))
        for n in range(2):
            inner_out[:, n, cols * c : cols * (c + 1)] = ref[:, base + cols * n : base + cols * (n + 1)]
        down_out[cols * c : cols * (c + 1), :] = ref[:, base + 2 * cols : base + 3 * cols].T


def fused_finish(lengths, ig, blk, awg, first, ffg, seqs):
    size, lanes = ig.shape
    width = lanes // seqs
    shard, wide = first.shape
    return pl.pallas_call(
        finish_kernel,
        out_shape=(
            shape((size, seqs, width), BF16),
            shape((size, seqs, width), F32),
            shape((shard, 256), F32),
            shape((shard, 2, 128), F32),
            shape((256, shard), F32),
            shape((shard, 2, wide), F32),
            shape((wide, shard), F32),
        ),
        in_specs=[SMEM] + [VMEM] * 5,
        out_specs=(VMEM,) * 7,
        compiler_params=pltpu.CompilerParams(vmem_limit_bytes=VMEM_LIMIT),
        name="finish",
    )(lengths, ig, blk, awg, first, ffg)


def swap(values, axis, bits):
    return lax.ppermute(values, axis, [(i, i ^ bits) for i in range(lax.axis_size(axis))])


def gather_tokens(block):
    far = swap(block, "tensor", 2)
    return [block, swap(block, "tensor", 1), far, swap(far, "tensor", 1)]


def scatter_tokens(keep, send):
    near = swap(send, "tensor", 1)
    middle = (keep[1].astype(F32) + near[1].astype(F32)).astype(BF16)
    far = swap(middle, "tensor", 2)
    return keep[0].astype(F32) + near[0].astype(F32) + far.astype(F32)


def gather_shards(shard):
    if lax.axis_size("dp") != 8 or shard.shape[0] % LANES:
        return [lax.all_gather(shard, "dp", axis=0, tiled=True)]
    slots = [shard, swap(shard, "dp", 1)]
    for bits in (2, 4, 6):
        there = swap(shard, "dp", bits)
        slots += [there, swap(there, "dp", 1)]
    return slots


def scatter_shards(grads):
    if len(grads) == 1:
        return lax.psum_scatter(grads[0].astype(F32), "dp", scatter_dimension=0, tiled=True)
    keep, send = grads
    near = swap(send, "dp", 1)
    both = keep.astype(F32) + near.astype(F32)
    total = both[0]
    for slot in (1, 2, 3):
        total = total + swap(both[slot].astype(BF16), "dp", 2 * slot).astype(F32)
    return total


def sum_everywhere(values):
    for axis in ("tensor", "dp"):
        bits = 1
        while bits < lax.axis_size(axis):
            values = values + swap(values, axis, bits)
            bits *= 2
    return values


def norm_rows(values, gain):
    factor = lax.rsqrt(jnp.mean(values * values, axis=-1, keepdims=True) + EPS)
    return (values * factor * gain, factor)


def norm_back(values, factor, gain, upstream):
    weighted = upstream * gain
    inner = jnp.mean(values * weighted, axis=-1, keepdims=True)
    return factor * weighted - values * factor * factor * factor * inner


def tables(full, head_width):
    half = head_width // 2
    freqs = THETA ** (-jnp.arange(half, dtype=F32) * 2.0 / head_width)
    angles = jnp.arange(full, dtype=F32)[:, None] * freqs[None, :]
    cosines, sines = jnp.cos(angles), jnp.sin(angles)
    return (jnp.tile(cosines, (1, 4)), jnp.tile(jnp.concatenate([-sines, sines], axis=1), (1, 2)))


def local_plain(
    inputs,
    lengths,
    query_weight,
    key_value_weight,
    output_weight,
    inner_weight,
    down_weight,
    mixer_gain,
    query_gain,
    key_gain,
    dense_gain,
    cotangent,
):
    size, seqs, width = inputs.shape
    parts = lax.axis_size("tensor")
    full = size * parts
    head = query_gain.shape[0]
    query_cols = query_weight.shape[1]
    pair_cols = key_value_weight.shape[2]
    hidden = inner_weight.shape[2]
    shard = query_weight.shape[0]
    me_t, me_d = lax.axis_index("tensor"), lax.axis_index("dp")
    n_c = 3
    cols = hidden // n_c
    cosines, sines = tables(full, head)
    gq = jnp.tile(query_gain, 2)[None, :]
    gk = jnp.tile(key_gain, 2)[None, :]

    down_turned = down_weight.T
    attn_shard = jnp.concatenate(
        [query_weight, key_value_weight.reshape(shard, 2 * pair_cols), output_weight.T], axis=1
    )
    attn_w = gather_shards(attn_shard)
    positions = me_t * size + jnp.arange(size, dtype=jnp.int32)
    scals = [
        jnp.stack([me_t.astype(jnp.int32), me_d.astype(jnp.int32), lengths[s], jnp.int32(0)])
        for s in range(seqs)
    ]
    tokens = [inputs[:, s].astype(F32) for s in range(seqs)]
    valid = [(positions < lengths[s])[:, None] for s in range(seqs)]
    firsts = [norm_rows(tokens[s], mixer_gain) for s in range(seqs)]
    normed = [gather_tokens(firsts[s][0].astype(BF16)) for s in range(seqs)]
    ff_w = []
    for c in range(n_c):
        part = slice(c * cols, (c + 1) * cols)
        ff_w.append(
            gather_shards(
                jnp.concatenate(
                    [inner_weight[:, 0, part], inner_weight[:, 1, part], down_turned[:, part]], axis=1
                )
            )
        )
    upstream = [jnp.where(valid[s], cotangent[:, s].astype(F32), 0.0) for s in range(seqs)]
    up_parts = [gather_tokens(upstream[s].astype(BF16)) for s in range(seqs)]

    saved, residual, seconds, dense = [], [], [], []
    for s in range(seqs):
        outs = attn_fwd(scals[s], cosines, sines, gq, gk, normed[s], attn_w)
        saved.append(outs[:6])
        residual.append(tokens[s] + scatter_tokens(outs[6], outs[7]))
        dense_in, factor = norm_rows(residual[s], dense_gain)
        seconds.append(factor)
        dense.append(gather_tokens(dense_in.astype(BF16)))

    x_parts = [part for s in range(seqs) for part in dense[s]]
    u_parts = [part for s in range(seqs) for part in up_parts[s]]
    hids, ggus, ff_grads = [], [], []
    for c in range(n_c):
        hid, ggu, grads = feed_forward(scals[0], x_parts, u_parts, ff_w[c])
        hids.append(hid)
        ggus.append(ggu)
        ff_grads.append(scatter_shards(grads))

    block_out, input_gradient, attn_grads = [], [], []
    mixer_part = dense_part = gain_part = 0.0
    for s in range(seqs):
        ykeep, ysend, gkeep, gsend = ff_out(s, scals[s], parts, size, hids, ggus, ff_w)
        grad_dense = scatter_tokens(gkeep, gsend)
        dense_part = dense_part + jnp.sum(grad_dense * residual[s] * seconds[s], axis=0)
        grad_residual = upstream[s] + norm_back(residual[s], seconds[s], dense_gain, grad_dense)
        r_parts = gather_tokens(grad_residual.astype(BF16))
        nkeep, nsend, gains, grads = attn_bwd(
            scals[s], cosines, sines, gq, gk, saved[s], normed[s], r_parts, attn_w
        )
        attn_grads.append(grads)
        gain_part = gain_part + gains
        grad_normed = scatter_tokens(nkeep, nsend)
        factor = firsts[s][1]
        mixer_part = mixer_part + jnp.sum(grad_normed * tokens[s] * factor, axis=0)
        input_gradient.append(grad_residual + norm_back(tokens[s], factor, mixer_gain, grad_normed))
        out_sum = scatter_tokens(ykeep, ysend)
        block_out.append(jnp.where(valid[s], residual[s] + out_sum, 0.0).astype(BF16))

    summed = [
        sum(part.astype(F32) for part in parts_of).astype(BF16) for parts_of in zip(*attn_grads)
    ]
    attn_grad = scatter_shards(summed)
    early = sum_everywhere(jnp.concatenate([dense_part.reshape(-1, LANES), gain_part], axis=0))
    mixer = sum_everywhere(mixer_part.reshape(-1, LANES)).reshape(-1)
    dense_rows = width // LANES
    folded = early[dense_rows:, :head] + early[dense_rows:, head:]
    inner_gradient = jnp.stack(
        [
            jnp.concatenate([grad[:, p * cols : (p + 1) * cols] for grad in ff_grads], axis=1)
            for p in range(2)
        ],
        axis=1,
    )
    down_gradient = jnp.concatenate([grad[:, 2 * cols :] for grad in ff_grads], axis=1).T
    return (
        jnp.stack(block_out, axis=1),
        jnp.stack(input_gradient, axis=1),
        attn_grad[:, :query_cols],
        attn_grad[:, query_cols : query_cols + 2 * pair_cols].reshape(shard, 2, pair_cols),
        attn_grad[:, query_cols + 2 * pair_cols :].T,
        inner_gradient,
        down_gradient,
        mixer,
        folded[0],
        folded[1],
        early[:dense_rows].reshape(-1),
    )


def local(*args):
    inputs, shard = args[0], args[2].shape[0]
    if lax.axis_size("dp") == 8 and lax.axis_size("tensor") == 4 and shard % LANES == 0 and inputs.shape[1] == 2:
        return local_fused(*args)
    return local_plain(*args)


def rope_tables(full, head):
    half = head // 2
    freqs = np.float32(THETA) ** (-np.arange(half, dtype=np.float32) * np.float32(2.0) / np.float32(head))
    angles = np.arange(full, dtype=np.float32)[:, None] * freqs[None, :].astype(np.float32)
    cosines, sines = np.cos(angles), np.sin(angles)
    return (
        jnp.asarray(np.tile(cosines, (1, 4)), F32),
        jnp.asarray(np.tile(np.concatenate([-sines, sines], axis=1), (1, 2)), F32),
    )


def local_fused(
    inputs,
    lengths,
    query_weight,
    key_value_weight,
    output_weight,
    inner_weight,
    down_weight,
    mixer_gain,
    query_gain,
    key_gain,
    dense_gain,
    cotangent,
):
    size, seqs, width = inputs.shape
    parts = lax.axis_size("tensor")
    full = size * parts
    head = query_gain.shape[0]
    tabs = rope_tables(full, head)
    weights = (query_weight, key_value_weight, output_weight, inner_weight, down_weight)
    x, upstream, attn_shard, ff_shard, gq, gk = fused_begin(
        lengths, inputs, cotangent, weights, query_gain, key_gain, 3
    )
    gains = (gq, gk, mixer_gain[None, :], dense_gain[None, :])
    (aw, normed, *saved, grad_a, grad_b, ys, near, whole, resid, resid_b, gres, dgain, first_sum, own) = fused_front(
        lengths, x, attn_shard, upstream, ff_shard, tabs, gains
    )
    input_gradient, blk, attn_grad, ff_grad, sums = fused_backward(
        lengths,
        (normed, grad_a, aw, grad_b, ys, near, whole, own, gres, *saved),
        (x, resid, resid_b, dgain, *tabs, *gains[:3]),
    )
    finished = fused_finish(lengths, input_gradient, blk, attn_grad, first_sum, ff_grad, seqs)
    folded = sums[16:, :head] + sums[16:, head:]
    return tuple(finished) + (
        sums[:8].reshape(-1),
        folded[0],
        folded[1],
        sums[8:16].reshape(-1),
    )


def solution(mesh):
    return jax.shard_map(
        local,
        mesh=mesh,
        in_specs=(
            P("tensor", "dp", None),
            P("dp"),
            P("dp", "tensor"),
            P("dp", None, "tensor"),
            P("tensor", "dp"),
            P("dp", None, "tensor"),
            P("tensor", "dp"),
            P(),
            P(),
            P(),
            P(),
            P("tensor", "dp", None),
        ),
        out_specs=(
            P("tensor", "dp", None),
            P("tensor", "dp", None),
            P("dp", "tensor"),
            P("dp", None, "tensor"),
            P("tensor", "dp"),
            P("dp", None, "tensor"),
            P("tensor", "dp"),
            P(),
            P(),
            P(),
            P(),
        ),
        check_vma=False,
    )
```

```python
import functools

import jax
import jax.numpy as jnp
import numpy as np
from jax import lax
from jax.experimental import pallas as pl
from jax.experimental.pallas import tpu as pltpu
from jax.sharding import PartitionSpec as P

EPS = 1e-05
THETA = 1000000.0
LOG2E = 1.4426950408889634
F32 = jnp.float32
BF16 = jnp.bfloat16
HIGH = lax.Precision.HIGHEST
LANES = 128
VMEM_LIMIT = 56 * 1024 * 1024
BLOCK_LIMIT = 62 * 1024 * 1024
ANY = pl.BlockSpec(memory_space=pl.ANY)
VMEM = pl.BlockSpec(memory_space=pltpu.VMEM)
SMEM = pl.BlockSpec(memory_space=pltpu.SMEM)


def dot(a, b, **kw):
    return lax.dot_general(
        a, b, (((1,), (0,)), ((), ())), preferred_element_type=F32, **kw
    )


def dot_nt(a, b, **kw):
    return lax.dot_general(
        a, b, (((1,), (1,)), ((), ())), preferred_element_type=F32, **kw
    )


def dot_tn(a, b, **kw):
    return lax.dot_general(
        a, b, (((0,), (0,)), ((), ())), preferred_element_type=F32, **kw
    )


def iota(shape, axis):
    return lax.broadcasted_iota(jnp.int32, shape, axis)


def low_half(shape):
    return iota(shape, 1) % LANES < LANES // 2


def head_blocks(scale):
    shape = (LANES, LANES)
    return jnp.where(iota(shape, 0) // 64 == iota(shape, 1) // 64, scale, 0.0).astype(F32)


def head_rows(scale):
    return jnp.where(iota((8, 256), 0) == iota((8, 256), 1) // 64, scale, 0.0).astype(F32)


def partner(values):
    first = iota(values.shape, 1) % 64 < 32
    return jnp.where(first, pltpu.roll(values, LANES - 32, 1), pltpu.roll(values, 32, 1))


def rows_of(index, size):
    return pl.ds(pl.multiple_of(index * size, size), size)


def load_all(sources, targets, sems, first):
    copies = []
    for number, (source, target) in enumerate(zip(sources, targets)):
        copy = pltpu.make_async_copy(source, target, sems.at[first + number])
        copy.start()
        copies.append(copy)
    return copies


def shard_targets(w_refs, ws, me):
    size = w_refs[0].shape[0]
    if len(w_refs) == 1:
        return [ws]
    return [ws.at[rows_of(me ^ slot, size)] for slot in range(len(w_refs))]


def store_slots(whole, out_refs, me):
    if len(out_refs) == 1:
        out_refs[0][...] = whole[...]
        return
    keep_ref, send_ref = out_refs
    size = keep_ref.shape[1]
    for slot in range(2 * keep_ref.shape[0]):
        (send_ref if slot % 2 else keep_ref)[slot // 2] = whole[rows_of(me ^ slot, size), :]


def padded_heads(first, second, low, g, e):
    here = low if e == 0 else jnp.logical_not(low)
    return jnp.where(here, first if g == e else second, 0.0).astype(BF16)


def project_rows(r, size, length, xs, ws, tabs, gains, raw_ref, q_ref, k_ref, v_ref, kp, vp):
    rows = rows_of(r, size)
    cos_ref, sin_ref = tabs
    gq_ref, gk_ref = gains
    mean_of = head_blocks(1.0 / 64)
    low = low_half((size, LANES))
    projected = dot(xs[rows, :], ws[:, :512])
    raw_ref[rows, :] = projected[:, :384]
    cosines, sines = cos_ref[rows, :], sin_ref[rows, :]

    def turned(values, gain):
        mean = dot(values * values, mean_of, precision=HIGH)
        normed = values * lax.rsqrt(mean + EPS) * gain
        return normed * cosines + partner(normed) * sines

    for g in range(2):
        lanes = slice(LANES * g, LANES * (g + 1))
        q_ref[rows, lanes] = turned(projected[:, lanes], gq_ref[...]).astype(BF16)
    keys = turned(projected[:, 256:384], gk_ref[...])
    values = projected[:, 384:512]
    k_ref[rows, :] = keys.astype(BF16)
    v_ref[rows, :] = values.astype(BF16)
    live = r * size + iota((size, LANES), 0) < length
    ones = jnp.where(live, 1.0, 0.0)
    values = jnp.where(live, values, 0.0)
    keys_swap, values_swap = pltpu.roll(keys, 64, 1), pltpu.roll(values, 64, 1)
    for g in range(2):
        for e in range(2):
            kp[2 * g + e, rows, :] = padded_heads(keys, keys_swap, low, g, e)
            vp[2 * g + e, rows, :LANES] = padded_heads(values, values_swap, low, g, e)
            vp[2 * g + e, rows, LANES:] = padded_heads(ones, ones, low, g, e)


def attend_rows(i, size, q_ref, kp, vp, acc, att_ref, lse_ref):
    rows = rows_of(i, size)
    factor = LOG2E / 8.0
    causal = iota((size, size), 1) <= iota((size, size), 0)
    queries = [q_ref[rows, LANES * g : LANES * (g + 1)] for g in range(2)]

    def block(kb, masked):
        cols = rows_of(kb, size)
        sums = []
        for g in range(2):
            total = None
            for e in range(2):
                weights = jnp.exp2(dot_nt(queries[g], kp[2 * g + e, cols, :]) * factor)
                if masked:
                    weights = jnp.where(causal, weights, 0.0)
                part = dot(weights.astype(BF16), vp[2 * g + e, cols, :])
                total = part if total is None else total + part
            sums.append(total)
        return sums

    for g, total in enumerate(block(i, True)):
        acc[g] = total

    def more(kb, carry):
        for g, total in enumerate(block(kb, False)):
            acc[g] += total
        return carry

    lax.fori_loop(i - i, i, more, None)
    logs = []
    for g in range(2):
        lanes = slice(LANES * g, LANES * (g + 1))
        summed = acc[g, :, LANES:]
        att_ref[rows, lanes] = (acc[g, :, :LANES] / summed).astype(BF16)
        logs.append(jnp.log2(summed))
    lse_ref[:, rows] = dot_nt(head_rows(1.0 / 64), jnp.concatenate(logs, axis=1), precision=HIGH)


def attn_fwd_kernel(parts, n_w, scal, cos_ref, sin_ref, gq_ref, gk_ref, *refs):
    x_refs, refs = refs[:parts], refs[parts:]
    w_refs, refs = refs[:n_w], refs[n_w:]
    (raw_ref, q_ref, k_ref, v_ref, att_ref, lse_ref, keep_ref, send_ref, xs, ws, kp, vp, acc, sems) = refs
    size = x_refs[0].shape[0]
    me_t, me_d, length = scal[0], scal[1], scal[2]
    copies = load_all(w_refs, shard_targets(w_refs, ws, me_d), sems, 0)
    copies += load_all(x_refs, [xs.at[rows_of(me_t ^ j, size)] for j in range(parts)], sems, n_w)
    for copy in copies:
        copy.wait()

    def project(r, carry):
        project_rows(
            r, size, length, xs, ws, (cos_ref, sin_ref), (gq_ref, gk_ref), raw_ref, q_ref, k_ref, v_ref, kp, vp
        )
        return carry

    def attend(i, carry):
        attend_rows(i, size, q_ref, kp, vp, acc, att_ref, lse_ref)
        return carry

    lax.fori_loop(0, parts, project, 0)
    lax.fori_loop(0, parts, attend, 0)
    for j in range(parts):
        out = dot_nt(att_ref[rows_of(me_t ^ j, size), :], ws[:, 512:])
        (send_ref if j % 2 else keep_ref)[j // 2] = out.astype(BF16)


def attn_fwd(scal, cosines, sines, gq, gk, x_parts, w_parts):
    parts, n_w = len(x_parts), len(w_parts)
    size, width = x_parts[0].shape
    full = parts * size
    cols = w_parts[0].shape[1]
    pair = jax.ShapeDtypeStruct((parts // 2, size, width), BF16)
    return pl.pallas_call(
        functools.partial(attn_fwd_kernel, parts, n_w),
        out_shape=(
            jax.ShapeDtypeStruct((full, 384), F32),
            jax.ShapeDtypeStruct((full, 256), BF16),
            jax.ShapeDtypeStruct((full, 128), BF16),
            jax.ShapeDtypeStruct((full, 128), BF16),
            jax.ShapeDtypeStruct((full, 256), BF16),
            jax.ShapeDtypeStruct((8, full), F32),
            pair,
            pair,
        ),
        in_specs=[SMEM] + [VMEM] * 4 + [ANY] * (parts + n_w),
        out_specs=(VMEM,) * 8,
        scratch_shapes=[
            pltpu.VMEM((full, width), BF16),
            pltpu.VMEM((width, cols), BF16),
            pltpu.VMEM((4, full, LANES), BF16),
            pltpu.VMEM((4, full, 2 * LANES), BF16),
            pltpu.VMEM((2, size, 2 * LANES), F32),
            pltpu.SemaphoreType.DMA((n_w + parts,)),
        ],
        compiler_params=pltpu.CompilerParams(vmem_limit_bytes=VMEM_LIMIT),
        cost_estimate=pl.CostEstimate(flops=8_000_000_000, bytes_accessed=12_000_000, transcendentals=3_000_000),
        name="attention_forward",
    )(scal, cosines, sines, gq, gk, *x_parts, *w_parts)


def prepare_rows(r, size, length, gs, ws, k_ref, v_ref, att_ref, ga, drow, kp, kt, vp):
    rows = rows_of(r, size)
    low = low_half((size, LANES))
    grad = dot(gs[rows, :], ws[:, 512:]).astype(BF16)
    ga[rows, :] = grad
    drow[:, rows] = dot_nt(head_rows(1.0), grad.astype(F32) * att_ref[rows, :].astype(F32), precision=HIGH)
    live = r * size + iota((size, LANES), 0) < length
    keys = jnp.where(live, k_ref[rows, :].astype(F32), 0.0)
    values = jnp.where(live, v_ref[rows, :].astype(F32), 0.0)
    keys_swap, values_swap = pltpu.roll(keys, 64, 1), pltpu.roll(values, 64, 1)
    for g in range(2):
        for e in range(2):
            here = low if e == 0 else jnp.logical_not(low)
            padded = jnp.where(here, keys if g == e else keys_swap, 0.0)
            kp[2 * g + e, rows, :] = padded.astype(BF16)
            kt[2 * g + e, :, rows] = padded.T.astype(BF16)
            vp[2 * g + e, rows, :] = padded_heads(values, values_swap, low, g, e)


def sweep_rows(i, size, q_ref, ga, kp, kt, vp, drow, lrow, acc, dq, dk, dv):
    rows = rows_of(i, size)
    factor = LOG2E / 8.0
    causal = iota((size, size), 0) <= iota((size, size), 1)
    low2 = iota((2 * size, LANES), 0) // size == iota((2 * size, LANES), 1) // 64
    queries, grads, queries2, grads2 = [], [], [], []
    for g in range(2):
        lanes = slice(LANES * g, LANES * (g + 1))
        queries.append(q_ref[rows, lanes])
        grads.append(ga[rows, lanes])
        for source, target in ((queries, queries2), (grads, grads2)):
            both = jnp.concatenate([source[g], source[g]], axis=0)
            target.append(jnp.where(low2, both, jnp.zeros_like(both)))

    def block(kb, masked):
        cols = rows_of(kb, size)
        parts_t = []
        for g in range(2):
            weights2, scores2, turned = [], [], None
            for e in range(2):
                h = 2 * g + e
                weights = jnp.exp2(dot_nt(kp[h, cols, :], queries[g]) * factor - lrow[h : h + 1, rows])
                if masked:
                    weights = jnp.where(causal, weights, 0.0)
                grad_weights = dot_nt(vp[h, cols, :], grads[g])
                grad_scores = (weights * (grad_weights - drow[h : h + 1, rows])).astype(BF16)
                weights2.append(weights.astype(BF16))
                scores2.append(grad_scores)
                part = dot(kt[h, :, cols], grad_scores)
                turned = part if turned is None else turned + part
            dv[g, cols, :] += dot(jnp.concatenate(weights2, axis=1), grads2[g])
            dk[g, cols, :] += dot(jnp.concatenate(scores2, axis=1), queries2[g])
            parts_t.append(turned)
        return parts_t

    for g, total in enumerate(block(i, True)):
        acc[g] = total

    def more(kb, carry):
        for g, total in enumerate(block(kb, False)):
            acc[g] += total
        return carry

    lax.fori_loop(i - i, i, more, None)
    for g in range(2):
        dq[rows, LANES * g : LANES * (g + 1)] = acc[g].T


def unproject_rows(r, size, length, tabs, gains, raw_ref, dq, dk, dv, gp, gains_ref):
    rows = rows_of(r, size)
    cosines, sines = tabs[0][rows, :], tabs[1][rows, :]
    low = low_half((size, LANES))
    mean_of = head_blocks(1.0 / 64)
    live = r * size + iota((size, LANES), 0) < length

    def back(grad, lanes, gain, row):
        raw = raw_ref[rows, lanes]
        rms = lax.rsqrt(dot(raw * raw, mean_of, precision=HIGH) + EPS)
        turned = grad * cosines - partner(grad) * sines
        gains_ref[row : row + 1, :] += jnp.sum(turned * raw * rms, axis=0, keepdims=True)
        weighted = turned * gain
        inner = dot(raw * weighted, mean_of, precision=HIGH)
        gp[rows, lanes] = (rms * weighted - raw * (rms * rms * rms) * inner).astype(BF16)

    def folded(ref):
        first, second = ref[0, rows, :], ref[1, rows, :]
        both = jnp.where(low, first + pltpu.roll(first, 64, 1), second + pltpu.roll(second, 64, 1))
        return jnp.where(live, both, 0.0)

    for g in range(2):
        lanes = slice(LANES * g, LANES * (g + 1))
        back(dq[rows, lanes] * 0.125, lanes, gains[0][...], 0)
    back(folded(dk) * 0.125, slice(256, 384), gains[1][...], 1)
    gp[rows, 384:512] = folded(dv).astype(BF16)


def attn_bwd_kernel(parts, n_w, scal, cos_ref, sin_ref, gq_ref, gk_ref, raw_ref, q_ref, k_ref, v_ref, att_ref, lse_ref, *refs):
    x_refs, refs = refs[:parts], refs[parts:]
    r_refs, refs = refs[:parts], refs[parts:]
    w_refs, refs = refs[:n_w], refs[n_w:]
    n_g = 1 if n_w == 1 else 2
    keep_ref, send_ref, gains_ref = refs[:3]
    g_refs, refs = refs[3 : 3 + n_g], refs[3 + n_g :]
    xs, gs, ws, kp, vp, kt, ga, dq, dk, dv, gp, whole, drow, acc, sems = refs
    size = x_refs[0].shape[0]
    me_t, me_d, length = scal[0], scal[1], scal[2]
    copies = load_all(w_refs, shard_targets(w_refs, ws, me_d), sems, 0)
    copies += load_all(r_refs, [gs.at[rows_of(me_t ^ j, size)] for j in range(parts)], sems, n_w)
    copies += load_all(x_refs, [xs.at[rows_of(me_t ^ j, size)] for j in range(parts)], sems, n_w + parts)
    for copy in copies:
        copy.wait()

    def prepare(r, carry):
        prepare_rows(r, size, length, gs, ws, k_ref, v_ref, att_ref, ga, drow, kp, kt, vp)
        return carry

    def sweep(i, carry):
        sweep_rows(i, size, q_ref, ga, kp, kt, vp, drow, lse_ref, acc, dq, dk, dv)
        return carry

    def unproject(r, carry):
        unproject_rows(r, size, length, (cos_ref, sin_ref), (gq_ref, gk_ref), raw_ref, dq, dk, dv, gp, gains_ref)
        return carry

    lax.fori_loop(0, parts, prepare, 0)
    dk[...] = jnp.zeros_like(dk)
    dv[...] = jnp.zeros_like(dv)
    lax.fori_loop(0, parts, sweep, 0)
    gains_ref[...] = jnp.zeros_like(gains_ref)
    lax.fori_loop(0, parts, unproject, 0)
    for j in range(parts):
        out = dot_nt(gp[rows_of(me_t ^ j, size), :], ws[:, :512])
        (send_ref if j % 2 else keep_ref)[j // 2] = out.astype(BF16)

    def weigh(b, carry):
        rows = rows_of(b, 256)
        whole[rows, :512] = dot_tn(xs[:, rows], gp[...]).astype(BF16)
        whole[rows, 512:] = dot_tn(gs[:, rows], att_ref[...]).astype(BF16)
        return carry

    lax.fori_loop(0, whole.shape[0] // 256, weigh, 0)
    store_slots(whole, g_refs, me_d)


def slot_shapes(n_w, width, cols):
    if n_w == 1:
        return (jax.ShapeDtypeStruct((width, cols), BF16),)
    return (jax.ShapeDtypeStruct((n_w // 2, width // n_w, cols), BF16),) * 2


def attn_bwd(scal, cosines, sines, gq, gk, saved, x_parts, r_parts, w_parts):
    parts, n_w = len(x_parts), len(w_parts)
    size, width = x_parts[0].shape
    full = parts * size
    cols = w_parts[0].shape[1]
    pair = jax.ShapeDtypeStruct((parts // 2, size, width), BF16)
    g_shapes = slot_shapes(n_w, width, cols)
    outs = pl.pallas_call(
        functools.partial(attn_bwd_kernel, parts, n_w),
        out_shape=(pair, pair, jax.ShapeDtypeStruct((8, LANES), F32)) + g_shapes,
        in_specs=[SMEM] + [VMEM] * 10 + [ANY] * (2 * parts + n_w),
        out_specs=(VMEM,) * (3 + len(g_shapes)),
        scratch_shapes=[
            pltpu.VMEM((full, width), BF16),
            pltpu.VMEM((full, width), BF16),
            pltpu.VMEM((width, cols), BF16),
            pltpu.VMEM((4, full, LANES), BF16),
            pltpu.VMEM((4, full, LANES), BF16),
            pltpu.VMEM((4, LANES, full), BF16),
            pltpu.VMEM((full, 256), BF16),
            pltpu.VMEM((full, 256), F32),
            pltpu.VMEM((2, full, LANES), F32),
            pltpu.VMEM((2, full, LANES), F32),
            pltpu.VMEM((full, 512), BF16),
            pltpu.VMEM((width, cols), BF16),
            pltpu.VMEM((8, full), F32),
            pltpu.VMEM((2, LANES, size), F32),
            pltpu.SemaphoreType.DMA((n_w + 2 * parts,)),
        ],
        compiler_params=pltpu.CompilerParams(vmem_limit_bytes=VMEM_LIMIT),
        cost_estimate=pl.CostEstimate(flops=14_000_000_000, bytes_accessed=15_000_000, transcendentals=3_000_000),
        name="attention_backward",
    )(scal, cosines, sines, gq, gk, *saved, *x_parts, *r_parts, *w_parts)
    return outs[0], outs[1], outs[2], outs[3:]


def ff_kernel(n_x, n_w, scal, *refs):
    x_refs, refs = refs[:n_x], refs[n_x:]
    u_refs, refs = refs[:n_x], refs[n_x:]
    w_refs, refs = refs[:n_w], refs[n_w:]
    n_g = 1 if n_w == 1 else 2
    hid_ref, ggu_ref = refs[:2]
    g_refs, refs = refs[2 : 2 + n_g], refs[2 + n_g :]
    xs, us, ws, whole, sems = refs
    size = x_refs[0].shape[0]
    me_d = scal[1]
    cols = ws.shape[1] // 3
    copies = load_all(w_refs, shard_targets(w_refs, ws, me_d), sems, 0)
    x_copies = load_all(x_refs, [xs.at[pl.ds(j * size, size)] for j in range(n_x)], sems, n_w)
    u_copies = load_all(u_refs, [us.at[pl.ds(j * size, size)] for j in range(n_x)], sems, n_w + n_x)
    for copy in copies + x_copies + u_copies:
        copy.wait()

    def tokens(r, carry):
        rows = rows_of(r, size)
        gate_up = dot(xs[rows, :], ws[:, : 2 * cols])
        grad = dot(us[rows, :], ws[:, 2 * cols :])
        gate, up = gate_up[:, :cols], gate_up[:, cols:]
        sig = 1.0 / (1.0 + jnp.exp2(gate * -LOG2E))
        silu = gate * sig
        hid_ref[rows, :] = (silu * up).astype(BF16)
        ggu_ref[rows, :cols] = (grad * up * (sig + silu * (1.0 - sig))).astype(BF16)
        ggu_ref[rows, cols:] = (grad * silu).astype(BF16)
        return carry

    lax.fori_loop(0, n_x, tokens, 0)

    def weigh(b, carry):
        rows = rows_of(b, 256)
        whole[rows, : 2 * cols] = dot_tn(xs[:, rows], ggu_ref[...]).astype(BF16)
        whole[rows, 2 * cols :] = dot_tn(us[:, rows], hid_ref[...]).astype(BF16)
        return carry

    lax.fori_loop(0, whole.shape[0] // 256, weigh, 0)
    store_slots(whole, g_refs, me_d)


def feed_forward(scal, x_parts, u_parts, w_parts):
    n_x, n_w = len(x_parts), len(w_parts)
    size, width = x_parts[0].shape
    full = n_x * size
    wide = w_parts[0].shape[1]
    cols = wide // 3
    g_shapes = slot_shapes(n_w, width, wide)
    outs = pl.pallas_call(
        functools.partial(ff_kernel, n_x, n_w),
        out_shape=(
            jax.ShapeDtypeStruct((full, cols), BF16),
            jax.ShapeDtypeStruct((full, 2 * cols), BF16),
        )
        + g_shapes,
        in_specs=[SMEM] + [ANY] * (2 * n_x + n_w),
        out_specs=(VMEM,) * (2 + len(g_shapes)),
        scratch_shapes=[
            pltpu.VMEM((full, width), BF16),
            pltpu.VMEM((full, width), BF16),
            pltpu.VMEM((width, wide), BF16),
            pltpu.VMEM((width, wide), BF16),
            pltpu.SemaphoreType.DMA((n_w + 2 * n_x,)),
        ],
        compiler_params=pltpu.CompilerParams(vmem_limit_bytes=VMEM_LIMIT),
        cost_estimate=pl.CostEstimate(flops=4 * full * width * wide, bytes_accessed=20_000_000, transcendentals=full * cols),
        name="feed_forward",
    )(scal, *x_parts, *u_parts, *w_parts)
    return outs[0], outs[1], outs[2:]


def ff_out_kernel(parts, n_c, n_w, seq, scal, *refs):
    hid_refs, refs = refs[:n_c], refs[n_c:]
    ggu_refs, refs = refs[:n_c], refs[n_c:]
    w_refs, refs = refs[: n_c * n_w], refs[n_c * n_w :]
    ykeep_ref, ysend_ref, gkeep_ref, gsend_ref, hs, gs, ws, sems = refs
    size = ykeep_ref.shape[1]
    full = parts * size
    me_d = scal[1]
    wide = ws.shape[2]
    cols = wide // 3
    copies = []
    first = 0
    for c in range(n_c):
        targets = shard_targets(w_refs[c * n_w : (c + 1) * n_w], ws.at[c], me_d)
        copies += load_all(w_refs[c * n_w : (c + 1) * n_w], targets, sems, first)
        first += n_w
    mine = pl.ds(seq * full, full)
    copies += load_all([ref.at[mine] for ref in ggu_refs], [gs.at[c] for c in range(n_c)], sems, first)
    copies += load_all([ref.at[mine] for ref in hid_refs], [hs.at[c] for c in range(n_c)], sems, first + n_c)
    for copy in copies:
        copy.wait()
    for j in range(parts):
        rows = pl.ds(j * size, size)
        grad = sum(dot_nt(gs[c, rows, :], ws[c, :, : 2 * cols]) for c in range(n_c))
        (gsend_ref if j % 2 else gkeep_ref)[j // 2] = grad.astype(BF16)
        out = sum(dot_nt(hs[c, rows, :], ws[c, :, 2 * cols :]) for c in range(n_c))
        (ysend_ref if j % 2 else ykeep_ref)[j // 2] = out.astype(BF16)


def ff_out(seq, scal, parts, size, hids, ggus, w_chunks):
    n_c, n_w = len(w_chunks), len(w_chunks[0])
    wide = w_chunks[0][0].shape[1]
    width = w_chunks[0][0].shape[0] * n_w
    full = parts * size
    cols = wide // 3
    pair = jax.ShapeDtypeStruct((parts // 2, size, width), BF16)
    return pl.pallas_call(
        functools.partial(ff_out_kernel, parts, n_c, n_w, seq),
        out_shape=(pair,) * 4,
        in_specs=[SMEM] + [ANY] * (2 * n_c + n_c * n_w),
        out_specs=(VMEM,) * 4,
        scratch_shapes=[
            pltpu.VMEM((n_c, full, cols), BF16),
            pltpu.VMEM((n_c, full, 2 * cols), BF16),
            pltpu.VMEM((n_c, width, wide), BF16),
            pltpu.SemaphoreType.DMA((n_c * n_w + 2 * n_c,)),
        ],
        compiler_params=pltpu.CompilerParams(vmem_limit_bytes=VMEM_LIMIT),
        cost_estimate=pl.CostEstimate(flops=2 * full * width * wide * n_c, bytes_accessed=22_000_000, transcendentals=0),
        name="feed_forward_out",
    )(scal, *hids, *ggus, *[shard for chunk in w_chunks for shard in chunk])


def flip(index, bits):
    for bit in (1, 2, 4):
        if bits & bit:
            index = index + bit - 2 * bit * lax.rem(lax.div(index, bit), 2)
    return index


class Spot:
    def __init__(self, index, choices):
        self.index = index
        self.flips = {0: index}
        for bits in choices:
            self.flips[bits] = flip(index, bits)


def spots():
    me_t = Spot(lax.axis_index("tensor"), (1, 2, 3))
    me_d = Spot(lax.axis_index("dp"), (1, 2, 3, 4, 5, 6, 7))
    me_d.x = lax.rem(me_d.index, 2)
    me_d.beside = 1 - me_d.x
    me_d.z = Spot(lax.div(me_d.index, 2), (1, 2, 3))
    return me_t, me_d


def greet(barrier, me_d, me_t, along_d, along_t):
    devices = [{"dp": me_d.flips[bits]} for bits in along_d]
    devices += [{"tensor": me_t.flips[bits]} for bits in along_t]
    for device in devices:
        pl.semaphore_signal(barrier, inc=1, device_id=device, device_id_type=pl.DeviceIdType.MESH)
    return lambda: pl.semaphore_wait(barrier, len(devices))


def remote(source, target, sems, number, device):
    return pltpu.make_async_remote_copy(
        src_ref=source,
        dst_ref=target,
        send_sem=sems.at[0, number],
        recv_sem=sems.at[1, number],
        device_id=device,
        device_id_type=pl.DeviceIdType.MESH,
    )


class Remote:
    LIMIT = 128

    def __init__(self, sems):
        self.sems, self.used = sems, 0

    def __call__(self, source, target, device):
        assert self.used < self.LIMIT
        self.used += 1
        return remote(source, target, self.sems, self.used - 1, device)


class Local:
    LIMIT = 64

    def __init__(self, sems):
        self.sems, self.used = sems, 0

    def make(self, source, target):
        assert self.used < self.LIMIT
        self.used += 1
        return pltpu.make_async_copy(source, target, self.sems.at[self.used - 1])

    def __call__(self, source, target):
        copy = self.make(source, target)
        copy.start()
        return copy


COPY_SEMS = [
    pltpu.SemaphoreType.DMA((2, Remote.LIMIT)),
    pltpu.SemaphoreType.DMA((Local.LIMIT,)),
]


class ShardGather:
    def __init__(self, shard, place, send, me_d, direct=False):
        def pass_on(bits, target):
            there = place(me_d.flips[bits])
            return send(there, there, {"dp": me_d.flips[target]})

        mine = place(me_d.index)
        self.beside, self.next, self.across = [send(shard, mine, {"dp": me_d.flips[bits]}) for bits in (1, 2, 4)]
        self.direct = direct
        self.on = send(shard, mine, {"dp": me_d.flips[6]}) if direct else pass_on(4, 2)
        self.passed = [pass_on(bits, 1) for bits in (4, 2, 6)]

    def start_x(self):
        self.beside.start()

    def start_z(self):
        self.next.start()
        self.across.start()
        if self.direct:
            self.on.start()

    def forward(self):
        self.next.wait_recv()
        self.passed[1].start()
        self.across.wait_recv()
        if not self.direct:
            self.on.start()
        self.passed[0].start()

    def forward_last(self):
        self.on.wait_recv()
        self.passed[2].start()

    def arrive(self):
        self.beside.wait_recv()
        for copy in self.passed:
            copy.wait_recv()

    def drain(self):
        for copy in [self.beside, self.next, self.across, self.on] + self.passed:
            copy.wait_send()


class TokenGather:
    def __init__(self, block, whole, send, me_t):
        size = block.shape[0]
        mine = whole.at[rows_of(me_t.index, size)]
        there = whole.at[rows_of(me_t.flips[2], size)]
        near = {"tensor": me_t.flips[1]}
        self.near = send(block, mine, near)
        self.far = send(block, mine, {"tensor": me_t.flips[2]})
        self.passed = send(there, there, near)

    def start(self):
        self.far.start()
        self.near.start()

    def forward(self):
        self.far.wait_recv()
        self.passed.start()

    def arrive(self):
        self.near.wait_recv()
        self.passed.wait_recv()

    def drain(self):
        for copy in (self.near, self.far, self.passed):
            copy.wait_send()


class TokenReduce:
    def __init__(self, blocks, near, far, send, me_t, mine=None):
        device = {"tensor": me_t.flips[1]}
        self.blocks, self.near_ref, self.far_ref, self.mine = blocks, near, far, mine
        self.places = (me_t.index, me_t.flips[2])
        self.size = far.shape[0]
        self.near = [
            send(blocks.at[rows_of(me_t.flips[1 + 2 * n], self.size)], near.at[n], device) for n in range(2)
        ]
        self.far = send(near.at[1], far, {"tensor": me_t.flips[2]})

    def load(self, here):
        return [here(self.blocks.at[rows_of(place, self.size)], self.mine.at[n]) for n, place in enumerate(self.places)]

    def start(self, *which):
        for n in which or (1, 0):
            self.near[n].start()

    def part(self, n, rows):
        if self.mine is not None:
            return self.mine[n, rows, :].astype(F32)
        start = pl.multiple_of(self.places[n] * self.size + rows.start, 32)
        return self.blocks[pl.ds(start, rows.size), :].astype(F32)

    def middle(self):
        self.near[1].wait_recv()

        def step(rows):
            total = self.part(1, rows) + self.near_ref[1, rows, :].astype(F32)
            self.near_ref[1, rows, :] = total.astype(BF16)

        by_rows(self.size, 32, step)
        self.far.start()

    def arrive(self):
        self.near[0].wait_recv()
        self.far.wait_recv()

    def rows(self, rows):
        total = self.part(0, rows) + self.near_ref[0, rows, :].astype(F32)
        return total + self.far_ref[rows, :].astype(F32)

    def drain(self):
        for copy in self.near + [self.far]:
            copy.wait_send()


class ShardNear:
    def __init__(self, whole, near, out, send, me_d, mine=None):
        self.whole, self.near_ref, self.out, self.mine = whole, near, out, mine
        self.z, self.x = me_d.z, me_d.x
        self.size = near.shape[1]
        self.near = send(whole.at[:, me_d.beside], near, {"dp": me_d.flips[1]})

    def load(self, here):
        return [here(self.whole.at[:, self.x], self.mine)]

    def start(self):
        self.near.start()

    def part(self, there, rows):
        if self.mine is not None:
            return self.mine[there, rows, :].astype(F32)
        return self.whole[there, self.x, rows, :].astype(F32)

    def middle(self, far=None):
        self.near.wait_recv()
        for k in (1, 3, 2, 0):
            there = self.z.flips[k]

            def step(rows):
                total = self.part(there, rows) + self.near_ref[there, rows, :].astype(F32)
                if k:
                    self.near_ref[there, rows, :] = total.astype(BF16)
                else:
                    self.out[rows, :] = total

            by_rows(self.size, 32, step)
            if k and far is not None:
                far.ready(k)

    def drain(self):
        self.near.wait_send()


class ShardFar:
    def __init__(self, near, far, out, send, me_d):
        self.far_ref, self.out = far, out
        self.size = far.shape[1]
        self.far = [send(near.at[me_d.z.flips[k]], far.at[k - 1], {"dp": me_d.flips[2 * k]}) for k in (1, 2, 3)]
        self.last = self.far
        self.terms = (0, 1, 2)

    def ready(self, k):
        self.far[k - 1].start()

    def finish(self):
        for copy in self.last:
            copy.wait_recv()

        def step(rows):
            total = self.out[rows, :]
            for k in self.terms:
                total = total + self.far_ref[k, rows, :].astype(F32)
            self.out[rows, :] = total

        by_rows(self.size, 32, step)

    def drain(self):
        for copy in self.far:
            copy.wait_send()


class ShardHalves(ShardFar):
    def __init__(self, near, far, out, send, me_d):
        self.near_ref, self.far_ref, self.out = near, far, out
        self.size = far.shape[1]
        z = me_d.z.flips
        self.across = z[2]
        self.far = [
            send(near.at[z[1]], far.at[0], {"dp": me_d.flips[2]}),
            send(near.at[z[3]], far.at[1], {"dp": me_d.flips[2]}),
            send(near.at[z[2]], far.at[2], {"dp": me_d.flips[4]}),
        ]
        self.last = (self.far[0], self.far[2])
        self.terms = (0, 2)

    def ready(self, k):
        if k != 2:
            self.far[k // 2].start()

    def middle(self):
        self.far[1].wait_recv()

        def step(rows):
            total = self.near_ref[self.across, rows, :].astype(F32) + self.far_ref[1, rows, :].astype(F32)
            self.near_ref[self.across, rows, :] = total.astype(BF16)

        by_rows(self.size, 32, step)
        self.far[2].start()


def by_rows(count, step, body):
    def run(b, carry):
        body(rows_of(b, step))
        return carry

    lax.fori_loop(0, count // step, run, None)


def loop(start, stop, body):
    def run(i, carry):
        body(i)
        return carry

    lax.fori_loop(start, stop, run, None)


def rms_factor(values):
    return lax.rsqrt(jnp.mean(values * values, axis=-1, keepdims=True) + EPS)


def shape(dims, kind):
    return jax.ShapeDtypeStruct(dims, kind)


def block_kernel(
    lengths, x_ref, aw_ref, up_ref, fw_ref, cos_ref, sin_ref, gq_ref, gk_ref, mg_ref, dg_ref,
    normed_out, raw_out, q_out, k_out, v_out, att_out, lse_out, r_out, blk_out,
    ig_ref, awg_ref, ffg_ref, sums_ref,
    xs, ws, dn, us, outp, onear, ofar, resid, wnear, wfar, whole, dgain, put, got_t, got_d, free, sems, local_sems,
):
    seqs, full, width = xs.shape
    size = resid.shape[1]
    parts = full // size
    n_c, shard, wide = fw_ref.shape
    cols = wide // 3
    me_t, me_d = spots()
    send, here = Remote(sems), Local(local_sems)
    mine_t, mine_d = rows_of(me_t.index, size), rows_of(me_d.index, shard)
    halves = [pl.ds(s * full, full) for s in range(seqs)]
    own_rows = [rows_of(s * parts + me_t.index, size) for s in range(seqs)]
    every_row = pl.ds(0, seqs * full)
    lanes_of = [slice(width * s, width * (s + 1)) for s in range(seqs)]

    def wait(copies):
        for copy in copies:
            copy.wait()

    pro_w = ShardGather(aw_ref.at[:, :512], lambda i: ws.at[rows_of(i, shard), :512], send, me_d)
    out_w = ShardGather(aw_ref.at[:, 512:], lambda i: ws.at[rows_of(i, shard), 512:], send, me_d, True)
    normed = [TokenGather(xs.at[s, mine_t], xs.at[s], send, me_t) for s in range(seqs)]
    ups = [TokenGather(up_ref.at[s], us.at[halves[s]], send, me_t) for s in range(seqs)]
    denses = [TokenGather(dn.at[own_rows[s]], dn.at[halves[s]], send, me_t) for s in range(seqs)]
    out_places = (outp, xs.at[0])
    back_places = (outp, xs.at[1])
    norm_places = (outp, dn.at[halves[0]])
    outs, backs, norms = [
        [TokenReduce(places[s], onear.at[s], ofar.at[s], send, me_t) for s in range(seqs)]
        for places in (out_places, back_places, norm_places)
    ]
    lows = [xs.at[0, pl.ds(s * size, size)] for s in range(seqs)]
    resids = [TokenGather(lows[s], r_out.at[s], send, me_t) for s in range(seqs)]
    ff_sums = [ffg_ref.at[:, wide * c : wide * (c + 1)] for c in range(n_c)]
    near = [ShardNear(whole.at[c], wnear.at[c], ff_sums[c], send, me_d) for c in range(2)]
    far = [ShardHalves(wnear.at[c], wfar.at[c], ff_sums[c], send, me_d) for c in range(2)]
    steps = [
        [send(put.at[0], got_t.at[me_t.index], {"tensor": me_t.flips[bits]}) for bits in (1, 2, 3)],
        [send(put.at[1], got_d.at[me_d.index], {"dp": me_d.flips[bits]}) for bits in (1, 2, 3, 4, 5, 6, 7)],
    ]
    load_w = [here(aw_ref, ws.at[mine_d])]
    load_u = [here(up_ref.at[s], us.at[own_rows[s]]) for s in range(seqs)]
    load_own = [here.make(up_ref.at[s], xs.at[0, pl.ds((seqs + s) * size, size)]) for s in range(seqs)]
    keeps = [here.make(xs.at[s], normed_out.at[s]) for s in range(seqs)]
    backup = [here.make(normed_out.at[s], xs.at[s]) for s in range(seqs)]
    low_keeps = [here.make(lows[s], r_out.at[s, mine_t]) for s in range(seqs)]

    def norm_first(s):
        def norm(rows):
            values = x_ref[rows, lanes_of[s]].astype(F32)
            target = pl.ds(pl.multiple_of(me_t.index * size + rows.start, 32), 32)
            xs[s, target, :] = (values * rms_factor(values) * mg_ref[...]).astype(BF16)

        by_rows(size, 32, norm)

    def after_out(s):
        outs[s].arrive()
        outs[s].drain()

        def norm(rows):
            values = x_ref[rows, lanes_of[s]].astype(F32) + outs[s].rows(rows)
            resid[s, rows, :] = values
            target = pl.ds(pl.multiple_of((s * parts + me_t.index) * size + rows.start, 32), 32)
            dn[target, :] = (values * rms_factor(values) * dg_ref[...]).astype(BF16)

        by_rows(size, 32, norm)
        denses[s].start()
        if s:
            for copy in load_own:
                copy.start()

    def after_back(s):
        backs[s].arrive()
        backs[s].drain()
        load_own[s].wait()

        def step(rows):
            grad = backs[s].rows(rows)
            values = resid[s, rows, :]
            factor = rms_factor(values)
            product = grad * values * factor
            dgain[...] += jnp.sum(product.reshape(-1, 8, width), axis=0)
            weighted = grad * dg_ref[...]
            inner = jnp.mean(values * weighted, axis=-1, keepdims=True)
            place = pl.ds(pl.multiple_of((seqs + s) * size + rows.start, 32), 32)
            total = xs[0, place, :].astype(F32) + factor * weighted - values * (factor * factor * factor) * inner
            ig_ref[rows, lanes_of[s]] = total
            lows[s][rows, :] = total.astype(BF16)

        by_rows(size, 32, step)
        resids[s].start()
        low_keeps[s].start()

    def after_norm(s):
        norms[s].arrive()

        def step(rows):
            values = x_ref[rows, lanes_of[s]].astype(F32)
            factor = rms_factor(values)
            weighted = norms[s].rows(rows) * mg_ref[...]
            inner = jnp.mean(values * weighted, axis=-1, keepdims=True)
            ig_ref[rows, lanes_of[s]] += factor * weighted - values * (factor * factor * factor) * inner

        by_rows(size, 32, step)

    def until_backward(wf):
        ff_w = [ShardGather(fw_ref.at[c], lambda i, c=c: wf.at[c, rows_of(i, shard)], send, me_d) for c in range(n_c)]
        load_f = [here(fw_ref.at[c], wf.at[c, mine_d]) for c in range(n_c)]

        def attention(kp, vp, acc, raw, q, k, v, att, lse):
            kept = ((raw, raw_out), (q, q_out), (k, k_out), (v, v_out), (att, att_out), (lse, lse_out))
            flushes = []

            def project(s):
                loop(0, parts, lambda r: project_rows(
                    r, size, lengths[s], xs.at[s], ws, (cos_ref, sin_ref), (gq_ref, gk_ref),
                    raw.at[s], q.at[s], k.at[s], v.at[s], kp, vp,
                ))

            def attend(s, start, stop):
                loop(start, stop, lambda i: attend_rows(i, size, q.at[s], kp, vp, acc, att.at[s], lse.at[s]))

            def out(s):
                for n, bits in enumerate((3, 1, 2, 0)):
                    rows = rows_of(me_t.flips[bits], size)
                    out_places[s][rows, :] = dot_nt(att[s, rows, :], ws[:, 512:]).astype(BF16)
                    if n < 2:
                        outs[s].start(1 - n)

            norm_first(0)
            entered = greet(
                pltpu.get_barrier_semaphore(), me_d, me_t, (1, 2, 3, 4, 5, 6, 7), (1, 2, 3)
            )
            entered()
            normed[0].start()
            pro_w.start_z()
            pro_w.start_x()
            norm_first(1)
            pro_w.forward()
            pro_w.forward_last()
            out_w.start_z()
            out_w.start_x()
            normed[0].forward()
            normed[1].start()
            normed[0].arrive()
            wait(load_w)
            ff_w[0].start_z()
            pro_w.arrive()
            ff_w[0].start_x()
            project(0)
            keeps[0].start()
            out_w.forward()
            out_w.forward_last()
            attend(0, 0, 3)
            normed[1].forward()
            ups[0].start()
            attend(0, 3, parts)
            ff_w[0].forward()
            out_w.arrive()
            out(0)
            outs[0].middle()
            for source, target in kept:
                flushes.append(here(source.at[0], target.at[0]))
            normed[1].arrive()
            project(1)
            keeps[1].start()
            ff_w[0].forward_last()
            ff_w[1].start_z()
            ff_w[1].start_x()
            attend(1, 0, 3)
            ups[0].forward()
            attend(1, 3, parts)
            normed[0].drain()
            keeps[0].wait()
            out(1)
            for source, target in kept:
                flushes.append(here(source.at[1], target.at[1]))
            after_out(0)
            outs[1].middle()
            ff_w[1].forward()
            ff_w[2].start_z()
            ff_w[2].start_x()
            wait(flushes)

        pl.run_scoped(
            attention,
            pltpu.VMEM((4, full, LANES), BF16),
            pltpu.VMEM((4, full, 2 * LANES), BF16),
            pltpu.VMEM((2, size, 2 * LANES), F32),
            pltpu.VMEM((seqs, full, 384), F32),
            pltpu.VMEM((seqs, full, 256), BF16),
            pltpu.VMEM((seqs, full, 128), BF16),
            pltpu.VMEM((seqs, full, 128), BF16),
            pltpu.VMEM((seqs, full, 256), BF16),
            pltpu.VMEM((seqs, 8, full), F32),
        )

        def feed_forward(hid, ggu):
            def tokens(c, s):
                def run(r):
                    rows = rows_of(r, size)
                    gate_up = dot(dn[rows, :], wf[c, :, : 2 * cols])
                    grad = dot(us[rows, :], wf[c, :, 2 * cols :])
                    gate, up = gate_up[:, :cols], gate_up[:, cols:]
                    sig = 1.0 / (1.0 + jnp.exp2(gate * -LOG2E))
                    silu = gate * sig
                    hid[c, rows, :] = (silu * up).astype(BF16)
                    ggu[c, rows, :cols] = (grad * up * (sig + silu * (1.0 - sig))).astype(BF16)
                    ggu[c, rows, cols:] = (grad * silu).astype(BF16)

                loop(s * parts, (s + 1) * parts, run)

            def weigh(c, tokens, more=False):
                def run(b):
                    rows = rows_of(b, 256)
                    dims = whole.shape[2:4]
                    inner = dot_tn(dn[tokens, rows], ggu[c, tokens, :]).reshape(dims + (2 * cols,))
                    down = dot_tn(us[tokens, rows], hid[c, tokens, :]).reshape(dims + (cols,))
                    if more:
                        inner = inner + whole[c % 2, b, :, :, : 2 * cols].astype(F32)
                        down = down + whole[c % 2, b, :, :, 2 * cols :].astype(F32)
                    whole[c % 2, b, :, :, : 2 * cols] = inner.astype(BF16)
                    whole[c % 2, b, :, :, 2 * cols :] = down.astype(BF16)

                loop(0, whole.shape[1], run)

            def grad_blocks(s):
                for n, bits in enumerate((3, 1, 2, 0)):
                    rows = rows_of(s * parts + me_t.flips[bits], size)
                    total = sum(dot_nt(ggu[c, rows, :], wf[c, :, : 2 * cols]) for c in range(n_c))
                    back_places[s][rows_of(me_t.flips[bits], size), :] = total.astype(BF16)
                    if n < 2:
                        backs[s].start(1 - n)

            def down_block(r):
                rows = rows_of(r, size)
                total = sum(dot_nt(hid[c, rows, :], wf[c, :, 2 * cols :]) for c in range(n_c))
                us[rows, :] = total.astype(BF16)

            wait(load_u + load_f)
            denses[0].forward()
            ups[1].start()
            ups[0].arrive()
            ff_w[0].arrive()
            denses[0].arrive()
            tokens(0, 0)
            ff_w[1].forward_last()
            ff_w[2].forward()
            weigh(0, halves[0])
            after_out(1)
            ff_w[1].arrive()
            tokens(1, 0)
            ff_w[2].forward_last()
            weigh(1, halves[0])
            ups[1].forward()
            denses[1].forward()
            ups[1].arrive()
            denses[1].arrive()
            tokens(0, 1)
            weigh(0, halves[1], True)
            near[0].start()
            ff_w[2].arrive()
            tokens(2, 0)
            grad_blocks(0)
            backs[0].middle()
            tokens(1, 1)
            weigh(1, halves[1], True)
            tokens(2, 1)
            normed[1].drain()
            keeps[1].wait()
            dgain[...] = jnp.zeros_like(dgain)
            after_back(0)
            grad_blocks(1)
            backs[1].middle()
            near[0].middle(far[0])
            near[1].start()
            near[0].drain()
            weigh(2, every_row)
            ups[0].drain()
            ups[1].drain()
            loop(0, parts, down_block)
            resids[0].forward()
            loop(parts, seqs * parts, down_block)
            far[0].middle()
            for exchange in ff_w + denses:
                exchange.drain()

        pl.run_scoped(
            feed_forward,
            pltpu.VMEM((n_c, seqs * full, cols), BF16),
            pltpu.VMEM((n_c, seqs * full, 2 * cols), BF16),
        )

    pl.run_scoped(until_backward, pltpu.VMEM((n_c, 8 * shard, wide), BF16))

    def backward(
        kp, vp, kt, ga, dq, dk, dv, gp, drow, acc, gains, mixer, raw, q, k, v, att, lse,
        wo, wq, wk, lnear, lfar, pnear, pfar, ynear, yfar,
    ):
        entered = greet(free, me_d, me_t, (1, 2, 4, 6), (1, 2))
        downs = [TokenReduce(us.at[halves[s]], ynear.at[s], yfar.at[s], send, me_t) for s in range(seqs)]
        late_near = ShardNear(whole.at[0], lnear, ff_sums[2], send, me_d)
        late_far = ShardHalves(lnear, lfar, ff_sums[2], send, me_d)
        pieces = ((wo, slice(512, 768)), (wq, slice(0, 256)), (wk, slice(256, 512)))
        pro_near = [ShardNear(part, pnear.at[n], awg_ref.at[:, lanes], send, me_d) for n, (part, lanes) in enumerate(pieces)]
        pro_far = [
            (ShardHalves if n else ShardFar)(pnear.at[n], pfar.at[n], awg_ref.at[:, lanes], send, me_d)
            for n, (part, lanes) in enumerate(pieces)
        ]
        kept = ((k_out, k), (v_out, v), (att_out, att), (lse_out, lse), (q_out, q))
        load_s = [[here(source.at[s], target.at[s]) for source, target in kept] for s in range(seqs)]
        load_raw = [here(raw_out.at[0], raw)]
        gains[...] = jnp.zeros_like(gains)
        mixer[...] = jnp.zeros_like(mixer)

        def load_grad(s):
            resids[s].arrive()
            low_keeps[s].wait()
            here(r_out.at[s], dn.at[halves[s]]).wait()

        def prepare(s):
            loop(0, parts, lambda r: prepare_rows(
                r, size, lengths[s], dn.at[halves[s]], ws, k.at[s], v.at[s], att.at[s], ga, drow, kp, kt, vp
            ))
            dk[...] = jnp.zeros_like(dk)
            dv[...] = jnp.zeros_like(dv)

        def sweep(s, start, stop):
            loop(start, stop, lambda i: sweep_rows(i, size, q.at[s], ga, kp, kt, vp, drow, lse.at[s], acc, dq, dk, dv))

        def unproject(s, start, stop):
            loop(start, stop, lambda r: unproject_rows(
                r, size, lengths[s], (cos_ref, sin_ref), (gq_ref, gk_ref), raw, dq, dk, dv, gp.at[s], gains
            ))

        def norm_blocks(s):
            for n, bits in enumerate((3, 1, 2, 0)):
                rows = rows_of(me_t.flips[bits], size)
                norm_places[s][rows, :] = dot_nt(gp[s, rows, :], ws[:, :512]).astype(BF16)
                if n < 2:
                    norms[s].start(1 - n)

        def weigh_out():
            def run(b):
                rows = rows_of(b, 256)
                total = sum(dot_tn(dn[halves[s], rows], att[s]) for s in range(seqs))
                wo[b] = total.astype(BF16).reshape(wo.shape[1:])

            loop(0, wo.shape[0], run)

        def weigh(target, lanes):
            def run(b):
                rows = rows_of(b, 256)
                total = sum(dot_tn(xs[s, :, rows], gp[s, :, lanes]) for s in range(seqs))
                target[b] = total.astype(BF16).reshape(target.shape[1:])
                product = total * ws[rows, lanes].astype(F32)
                high = product.astype(BF16)
                rest = (product - high.astype(F32)).astype(BF16)
                ones = jnp.ones((8, product.shape[1]), BF16)
                mixer[:, rows] += dot_nt(ones, high) + dot_nt(ones, rest)

            loop(0, target.shape[0], run)

        def after_down(s):
            downs[s].arrive()

            def step(rows):
                target = pl.ds(pl.multiple_of(s * size + rows.start, 32), 32)
                outp[target, :] = (resid[s, rows, :] + downs[s].rows(rows)).astype(BF16)

            by_rows(size, 32, step)
            return here(outp.at[pl.ds(s * size, size)], blk_out.at[s])

        def total_of(n, got, index):
            got[index] = put[n]
            for copy in steps[n]:
                copy.wait_recv()
            total = got[0]
            for place in range(1, got.shape[0]):
                total = total + got[place]
            return total

        wait(load_s[0])
        load_grad(0)
        prepare(0)
        entered()
        after_back(1)
        late_near.start()
        for exchange in downs:
            exchange.start()
        sweep(0, 0, 2)
        near[1].middle(far[1])
        sweep(0, 2, 3)
        downs[0].middle()
        sweep(0, 3, parts)
        wait(load_raw)
        unproject(0, 0, parts)
        resids[1].forward()
        load_raw = [here(raw_out.at[1], raw)]
        norm_blocks(0)
        norms[0].middle()
        far[1].middle()
        load_grad(1)
        for exchange in resids:
            exchange.drain()
        for copy in backup:
            copy.start()
        wait(load_s[1])
        prepare(1)
        far[0].finish()
        weigh_out()
        pro_near[0].start()
        late_near.middle(late_far)
        sweep(1, 0, 2)
        downs[1].middle()
        sweep(1, 2, 3)
        pro_near[0].middle(pro_far[0])
        sweep(1, 3, parts)
        wait(load_raw)
        unproject(1, 0, parts)
        wait(backup)
        weigh(wq, pieces[1][1])
        pro_near[1].start()
        late_far.middle()
        weigh(wk, pieces[2][1])
        pro_near[2].start()
        for row, vector in ((0, mixer[0:1, :] / mg_ref[...]), (8, jnp.sum(dgain[...], axis=0, keepdims=True))):
            for i in range(8):
                put[0, row + i : row + i + 1, :] = vector[:, LANES * i : LANES * (i + 1)]
        put[0, 16:, :] = gains[...]
        for copy in steps[0]:
            copy.start()
        norm_blocks(1)
        put[1] = total_of(0, got_t, me_t.index)
        for copy in steps[1]:
            copy.start()
        norms[1].middle()
        after_norm(0)
        far[1].finish()
        norms[0].drain()
        stays = [after_down(0)]
        pro_near[1].middle(pro_far[1])
        stays.append(after_down(1))
        pro_far[0].finish()
        pro_far[1].middle()
        pro_near[2].middle(pro_far[2])
        pro_far[2].middle()
        sums_ref[...] = total_of(1, got_d, me_d.index)
        late_far.finish()
        after_norm(1)
        pro_far[1].finish()
        pro_far[2].finish()
        wait(stays)
        for copy in steps[0] + steps[1]:
            copy.wait_send()
        for exchange in downs + [late_near, late_far] + pro_near + pro_far:
            exchange.drain()

    pl.run_scoped(
        backward,
        pltpu.VMEM((4, full, LANES), BF16),
        pltpu.VMEM((4, full, LANES), BF16),
        pltpu.VMEM((4, LANES, full), BF16),
        pltpu.VMEM((full, 256), BF16),
        pltpu.VMEM((full, 256), F32),
        pltpu.VMEM((2, full, LANES), F32),
        pltpu.VMEM((2, full, LANES), F32),
        pltpu.VMEM((seqs, full, 512), BF16),
        pltpu.VMEM((8, full), F32),
        pltpu.VMEM((2, LANES, size), F32),
        pltpu.VMEM((8, LANES), F32),
        pltpu.VMEM((8, width), F32),
        pltpu.VMEM((full, 384), F32),
        pltpu.VMEM((seqs, full, 256), BF16),
        pltpu.VMEM((seqs, full, 128), BF16),
        pltpu.VMEM((seqs, full, 128), BF16),
        pltpu.VMEM((seqs, full, 256), BF16),
        pltpu.VMEM((seqs, 8, full), F32),
        pltpu.VMEM((4, 2, shard, 256), BF16),
        pltpu.VMEM((4, 2, shard, 256), BF16),
        pltpu.VMEM((4, 2, shard, 256), BF16),
        pltpu.VMEM((4, shard, wide), BF16),
        pltpu.VMEM((3, shard, wide), BF16),
        pltpu.VMEM((3, 4, shard, 256), BF16),
        pltpu.VMEM((3, 3, shard, 256), BF16),
        pltpu.VMEM((seqs, 2, size, width), BF16),
        pltpu.VMEM((seqs, size, width), BF16),
    )
    for exchange in [pro_w, out_w, near[1]] + far + norms[1:]:
        exchange.drain()


def fused_block(lengths, x, aw, up, fw, tabs, gains):
    seqs, size, width = up.shape
    full = 4 * size
    shard, cols = aw.shape
    n_c, _, wide = fw.shape
    dp = 8
    return pl.pallas_call(
        block_kernel,
        out_shape=(
            shape((seqs, full, width), BF16),
            shape((seqs, full, 384), F32),
            shape((seqs, full, 256), BF16),
            shape((seqs, full, 128), BF16),
            shape((seqs, full, 128), BF16),
            shape((seqs, full, 256), BF16),
            shape((seqs, 8, full), F32),
            shape((seqs, full, width), BF16),
            shape((seqs, size, width), BF16),
            shape((size, seqs * width), F32),
            shape((shard, cols), F32),
            shape((shard, n_c * wide), F32),
            shape((24, LANES), F32),
        ),
        in_specs=[SMEM, VMEM] + [ANY] * 3 + [VMEM] * 6,
        out_specs=(ANY,) * 9 + (VMEM,) * 4,
        scratch_shapes=[
            pltpu.VMEM((seqs, full, width), BF16),
            pltpu.VMEM((dp * shard, cols), BF16),
            pltpu.VMEM((seqs * full, width), BF16),
            pltpu.VMEM((seqs * full, width), BF16),
            pltpu.VMEM((full, width), BF16),
            pltpu.VMEM((seqs, 2, size, width), BF16),
            pltpu.VMEM((seqs, size, width), BF16),
            pltpu.VMEM((seqs, size, width), F32),
            pltpu.VMEM((2, 4, shard, wide), BF16),
            pltpu.VMEM((2, 3, shard, wide), BF16),
            pltpu.VMEM((2, 4, 2, shard, wide), BF16),
            pltpu.VMEM((8, width), F32),
            pltpu.VMEM((2, 24, LANES), F32),
            pltpu.VMEM((4, 24, LANES), F32),
            pltpu.VMEM((8, 24, LANES), F32),
            pltpu.SemaphoreType.REGULAR,
        ]
        + COPY_SEMS,
        compiler_params=pltpu.CompilerParams(
            vmem_limit_bytes=BLOCK_LIMIT, collective_id=0, has_side_effects=True
        ),
        cost_estimate=pl.CostEstimate(flops=90_000_000_000, bytes_accessed=60_000_000, transcendentals=14_000_000),
        name="block",
    )(lengths, x, aw, up, fw, *tabs, *gains)


def begin_kernel(
    lengths, in_ref, cot_ref, qw_ref, kv_ref, ow_ref, iw_ref, dw_ref, qg_ref, kg_ref,
    x_out, up_out, aw_out, fw_out, gq_out, gk_out,
):
    size, seqs, width = in_ref.shape
    cols = fw_out.shape[2] // 3
    start = lax.axis_index("tensor") * size

    def step(rows):
        place = start + rows.start + iota((32, width), 0)
        values = in_ref[rows, :, :].astype(F32)
        grads = cot_ref[rows, :, :].astype(F32)
        for s in range(seqs):
            x_out[rows, width * s : width * (s + 1)] = values[:, s, :].astype(BF16)
            up_out[s, rows, :] = jnp.where(place < lengths[s], grads[:, s, :], 0.0).astype(BF16)

    by_rows(size, 32, step)
    aw_out[:, :256] = qw_ref[...]
    pair = kv_ref[...].astype(F32)
    for n in range(2):
        aw_out[:, 256 + 128 * n : 384 + 128 * n] = pair[:, n, :].astype(BF16)
    aw_out[:, 512:] = ow_ref[...].astype(F32).T.astype(BF16)

    def inner(rows):
        both = iw_ref[rows, :, :].astype(F32)
        for c in range(3):
            for n in range(2):
                fw_out[c, rows, cols * n : cols * (n + 1)] = both[:, n, cols * c : cols * (c + 1)].astype(BF16)

    by_rows(iw_ref.shape[0], 32, inner)
    for c in range(3):
        fw_out[c, :, 2 * cols :] = dw_ref[cols * c : cols * (c + 1), :].astype(F32).T.astype(BF16)
    for source, target in ((qg_ref, gq_out), (kg_ref, gk_out)):
        target[...] = jnp.concatenate([source[...], source[...]], axis=1)


def fused_begin(lengths, inputs, cotangent, weights, query_gain, key_gain, n_c):
    size, seqs, width = inputs.shape
    shard = weights[0].shape[0]
    hidden = weights[3].shape[2]
    return pl.pallas_call(
        begin_kernel,
        out_shape=(
            shape((size, seqs * width), BF16),
            shape((seqs, size, width), BF16),
            shape((shard, 768), BF16),
            shape((n_c, shard, 3 * hidden // n_c), BF16),
            shape((1, LANES), F32),
            shape((1, LANES), F32),
        ),
        in_specs=[SMEM] + [VMEM] * 9,
        out_specs=(VMEM,) * 6,
        compiler_params=pltpu.CompilerParams(vmem_limit_bytes=VMEM_LIMIT),
        name="begin",
    )(lengths, inputs, cotangent, *weights, query_gain[None, :], key_gain[None, :])


def finish_kernel(
    lengths, ig_ref, blk_ref, awg_ref, ffg_ref,
    block_out, input_out, query_out, pair_out, output_out, inner_out, down_out,
):
    size, seqs, width = input_out.shape
    hidden = down_out.shape[0]
    cols = hidden // 3
    start = lax.axis_index("tensor") * size

    def step(rows):
        place = start + rows.start + iota((32, width), 0)
        parts = []
        for s in range(seqs):
            lanes = slice(width * s, width * (s + 1))
            input_out[rows, s, :] = ig_ref[rows, lanes]
            parts.append(jnp.where(place < lengths[s], blk_ref[s, rows, :].astype(F32), 0.0))
        block_out[rows, :, :] = jnp.stack(parts, axis=1).astype(BF16)

    by_rows(size, 32, step)
    query_out[...] = awg_ref[:, :256]
    for n in range(2):
        pair_out[:, n, :] = awg_ref[:, 256 + 128 * n : 384 + 128 * n]
    output_out[...] = awg_ref[:, 512:].T
    for c in range(3):
        base = 3 * cols * c
        for n in range(2):
            inner_out[:, n, cols * c : cols * (c + 1)] = ffg_ref[:, base + cols * n : base + cols * (n + 1)]
        down_out[cols * c : cols * (c + 1), :] = ffg_ref[:, base + 2 * cols : base + 3 * cols].T


def fused_finish(lengths, ig, blk, awg, ffg):
    seqs, size, width = blk.shape
    shard, wide = ffg.shape
    hidden = wide // 3
    return pl.pallas_call(
        finish_kernel,
        out_shape=(
            shape((size, seqs, width), BF16),
            shape((size, seqs, width), F32),
            shape((shard, 256), F32),
            shape((shard, 2, 128), F32),
            shape((256, shard), F32),
            shape((shard, 2, hidden), F32),
            shape((hidden, shard), F32),
        ),
        in_specs=[SMEM] + [VMEM] * 4,
        out_specs=(VMEM,) * 7,
        compiler_params=pltpu.CompilerParams(vmem_limit_bytes=VMEM_LIMIT),
        name="finish",
    )(lengths, ig, blk, awg, ffg)


def swap(values, axis, bits):
    return lax.ppermute(values, axis, [(i, i ^ bits) for i in range(lax.axis_size(axis))])


def gather_tokens(block):
    far = swap(block, "tensor", 2)
    return [block, swap(block, "tensor", 1), far, swap(far, "tensor", 1)]


def scatter_tokens(keep, send):
    near = swap(send, "tensor", 1)
    middle = (keep[1].astype(F32) + near[1].astype(F32)).astype(BF16)
    far = swap(middle, "tensor", 2)
    return keep[0].astype(F32) + near[0].astype(F32) + far.astype(F32)


def gather_shards(shard):
    if lax.axis_size("dp") != 8 or shard.shape[0] % LANES:
        return [lax.all_gather(shard, "dp", axis=0, tiled=True)]
    slots = [shard, swap(shard, "dp", 1)]
    for bits in (2, 4, 6):
        there = swap(shard, "dp", bits)
        slots += [there, swap(there, "dp", 1)]
    return slots


def scatter_shards(grads):
    if len(grads) == 1:
        return lax.psum_scatter(grads[0].astype(F32), "dp", scatter_dimension=0, tiled=True)
    keep, send = grads
    near = swap(send, "dp", 1)
    both = keep.astype(F32) + near.astype(F32)
    total = both[0]
    for slot in (1, 2, 3):
        total = total + swap(both[slot].astype(BF16), "dp", 2 * slot).astype(F32)
    return total


def sum_everywhere(values):
    for axis in ("tensor", "dp"):
        bits = 1
        while bits < lax.axis_size(axis):
            values = values + swap(values, axis, bits)
            bits *= 2
    return values


def norm_rows(values, gain):
    factor = lax.rsqrt(jnp.mean(values * values, axis=-1, keepdims=True) + EPS)
    return (values * factor * gain, factor)


def norm_back(values, factor, gain, upstream):
    weighted = upstream * gain
    inner = jnp.mean(values * weighted, axis=-1, keepdims=True)
    return factor * weighted - values * factor * factor * factor * inner


def tables(full, head_width):
    half = head_width // 2
    freqs = THETA ** (-jnp.arange(half, dtype=F32) * 2.0 / head_width)
    angles = jnp.arange(full, dtype=F32)[:, None] * freqs[None, :]
    cosines, sines = jnp.cos(angles), jnp.sin(angles)
    return (jnp.tile(cosines, (1, 4)), jnp.tile(jnp.concatenate([-sines, sines], axis=1), (1, 2)))


def local_plain(
    inputs,
    lengths,
    query_weight,
    key_value_weight,
    output_weight,
    inner_weight,
    down_weight,
    mixer_gain,
    query_gain,
    key_gain,
    dense_gain,
    cotangent,
):
    size, seqs, width = inputs.shape
    parts = lax.axis_size("tensor")
    full = size * parts
    head = query_gain.shape[0]
    query_cols = query_weight.shape[1]
    pair_cols = key_value_weight.shape[2]
    hidden = inner_weight.shape[2]
    shard = query_weight.shape[0]
    me_t, me_d = lax.axis_index("tensor"), lax.axis_index("dp")
    n_c = 3
    cols = hidden // n_c
    cosines, sines = tables(full, head)
    gq = jnp.tile(query_gain, 2)[None, :]
    gk = jnp.tile(key_gain, 2)[None, :]

    down_turned = down_weight.T
    attn_shard = jnp.concatenate(
        [query_weight, key_value_weight.reshape(shard, 2 * pair_cols), output_weight.T], axis=1
    )
    attn_w = gather_shards(attn_shard)
    positions = me_t * size + jnp.arange(size, dtype=jnp.int32)
    scals = [
        jnp.stack([me_t.astype(jnp.int32), me_d.astype(jnp.int32), lengths[s], jnp.int32(0)])
        for s in range(seqs)
    ]
    tokens = [inputs[:, s].astype(F32) for s in range(seqs)]
    valid = [(positions < lengths[s])[:, None] for s in range(seqs)]
    firsts = [norm_rows(tokens[s], mixer_gain) for s in range(seqs)]
    normed = [gather_tokens(firsts[s][0].astype(BF16)) for s in range(seqs)]
    ff_w = []
    for c in range(n_c):
        part = slice(c * cols, (c + 1) * cols)
        ff_w.append(
            gather_shards(
                jnp.concatenate(
                    [inner_weight[:, 0, part], inner_weight[:, 1, part], down_turned[:, part]], axis=1
                )
            )
        )
    upstream = [jnp.where(valid[s], cotangent[:, s].astype(F32), 0.0) for s in range(seqs)]
    up_parts = [gather_tokens(upstream[s].astype(BF16)) for s in range(seqs)]

    saved, residual, seconds, dense = [], [], [], []
    for s in range(seqs):
        outs = attn_fwd(scals[s], cosines, sines, gq, gk, normed[s], attn_w)
        saved.append(outs[:6])
        residual.append(tokens[s] + scatter_tokens(outs[6], outs[7]))
        dense_in, factor = norm_rows(residual[s], dense_gain)
        seconds.append(factor)
        dense.append(gather_tokens(dense_in.astype(BF16)))

    x_parts = [part for s in range(seqs) for part in dense[s]]
    u_parts = [part for s in range(seqs) for part in up_parts[s]]
    hids, ggus, ff_grads = [], [], []
    for c in range(n_c):
        hid, ggu, grads = feed_forward(scals[0], x_parts, u_parts, ff_w[c])
        hids.append(hid)
        ggus.append(ggu)
        ff_grads.append(scatter_shards(grads))

    block_out, input_gradient, attn_grads = [], [], []
    mixer_part = dense_part = gain_part = 0.0
    for s in range(seqs):
        ykeep, ysend, gkeep, gsend = ff_out(s, scals[s], parts, size, hids, ggus, ff_w)
        grad_dense = scatter_tokens(gkeep, gsend)
        dense_part = dense_part + jnp.sum(grad_dense * residual[s] * seconds[s], axis=0)
        grad_residual = upstream[s] + norm_back(residual[s], seconds[s], dense_gain, grad_dense)
        r_parts = gather_tokens(grad_residual.astype(BF16))
        nkeep, nsend, gains, grads = attn_bwd(
            scals[s], cosines, sines, gq, gk, saved[s], normed[s], r_parts, attn_w
        )
        attn_grads.append(grads)
        gain_part = gain_part + gains
        grad_normed = scatter_tokens(nkeep, nsend)
        factor = firsts[s][1]
        mixer_part = mixer_part + jnp.sum(grad_normed * tokens[s] * factor, axis=0)
        input_gradient.append(grad_residual + norm_back(tokens[s], factor, mixer_gain, grad_normed))
        out_sum = scatter_tokens(ykeep, ysend)
        block_out.append(jnp.where(valid[s], residual[s] + out_sum, 0.0).astype(BF16))

    summed = [
        sum(part.astype(F32) for part in parts_of).astype(BF16) for parts_of in zip(*attn_grads)
    ]
    attn_grad = scatter_shards(summed)
    early = sum_everywhere(jnp.concatenate([dense_part.reshape(-1, LANES), gain_part], axis=0))
    mixer = sum_everywhere(mixer_part.reshape(-1, LANES)).reshape(-1)
    dense_rows = width // LANES
    folded = early[dense_rows:, :head] + early[dense_rows:, head:]
    inner_gradient = jnp.stack(
        [
            jnp.concatenate([grad[:, p * cols : (p + 1) * cols] for grad in ff_grads], axis=1)
            for p in range(2)
        ],
        axis=1,
    )
    down_gradient = jnp.concatenate([grad[:, 2 * cols :] for grad in ff_grads], axis=1).T
    return (
        jnp.stack(block_out, axis=1),
        jnp.stack(input_gradient, axis=1),
        attn_grad[:, :query_cols],
        attn_grad[:, query_cols : query_cols + 2 * pair_cols].reshape(shard, 2, pair_cols),
        attn_grad[:, query_cols + 2 * pair_cols :].T,
        inner_gradient,
        down_gradient,
        mixer,
        folded[0],
        folded[1],
        early[:dense_rows].reshape(-1),
    )


def local(*args):
    inputs, shard = args[0], args[2].shape[0]
    if lax.axis_size("dp") == 8 and lax.axis_size("tensor") == 4 and shard % LANES == 0 and inputs.shape[1] == 2:
        return local_fused(*args)
    return local_plain(*args)


def rope_tables(full, head):
    half = head // 2
    freqs = np.float32(THETA) ** (-np.arange(half, dtype=np.float32) * np.float32(2.0) / np.float32(head))
    angles = np.arange(full, dtype=np.float32)[:, None] * freqs[None, :].astype(np.float32)
    cosines, sines = np.cos(angles), np.sin(angles)
    return (
        jnp.asarray(np.tile(cosines, (1, 4)), F32),
        jnp.asarray(np.tile(np.concatenate([-sines, sines], axis=1), (1, 2)), F32),
    )


def local_fused(
    inputs,
    lengths,
    query_weight,
    key_value_weight,
    output_weight,
    inner_weight,
    down_weight,
    mixer_gain,
    query_gain,
    key_gain,
    dense_gain,
    cotangent,
):
    size, seqs, width = inputs.shape
    parts = lax.axis_size("tensor")
    full = size * parts
    head = query_gain.shape[0]
    tabs = rope_tables(full, head)
    weights = (query_weight, key_value_weight, output_weight, inner_weight, down_weight)
    x, upstream, attn_shard, ff_shard, gq, gk = fused_begin(
        lengths, inputs, cotangent, weights, query_gain, key_gain, 3
    )
    gains = (gq, gk, mixer_gain[None, :], dense_gain[None, :])
    *_, blk, input_gradient, attn_grad, ff_grad, sums = fused_block(
        lengths, x, attn_shard, upstream, ff_shard, tabs, gains
    )
    finished = fused_finish(lengths, input_gradient, blk, attn_grad, ff_grad)
    folded = sums[16:, :head] + sums[16:, head:]
    return tuple(finished) + (
        sums[:8].reshape(-1),
        folded[0],
        folded[1],
        sums[8:16].reshape(-1),
    )


def solution(mesh):
    return jax.shard_map(
        local,
        mesh=mesh,
        in_specs=(
            P("tensor", "dp", None),
            P("dp"),
            P("dp", "tensor"),
            P("dp", None, "tensor"),
            P("tensor", "dp"),
            P("dp", None, "tensor"),
            P("tensor", "dp"),
            P(),
            P(),
            P(),
            P(),
            P("tensor", "dp", None),
        ),
        out_specs=(
            P("tensor", "dp", None),
            P("tensor", "dp", None),
            P("dp", "tensor"),
            P("dp", None, "tensor"),
            P("tensor", "dp"),
            P("dp", None, "tensor"),
            P("tensor", "dp"),
            P(),
            P(),
            P(),
            P(),
        ),
        check_vma=False,
    )
```

```python
import functools

import jax
import jax.numpy as jnp
import numpy as np
from jax import lax
from jax.experimental import pallas as pl
from jax.experimental.pallas import tpu as pltpu
from jax.sharding import PartitionSpec as P

EPS = 1e-05
THETA = 1000000.0
LOG2E = 1.4426950408889634
F32 = jnp.float32
BF16 = jnp.bfloat16
HIGH = lax.Precision.HIGHEST
LANES = 128
VMEM_LIMIT = 56 * 1024 * 1024
BLOCK_LIMIT = 62 * 1024 * 1024
ANY = pl.BlockSpec(memory_space=pl.ANY)
VMEM = pl.BlockSpec(memory_space=pltpu.VMEM)
SMEM = pl.BlockSpec(memory_space=pltpu.SMEM)


def dot(a, b, **kw):
    return lax.dot_general(
        a, b, (((1,), (0,)), ((), ())), preferred_element_type=F32, **kw
    )


def dot_nt(a, b, **kw):
    return lax.dot_general(
        a, b, (((1,), (1,)), ((), ())), preferred_element_type=F32, **kw
    )


def dot_tn(a, b, **kw):
    return lax.dot_general(
        a, b, (((0,), (0,)), ((), ())), preferred_element_type=F32, **kw
    )


def iota(shape, axis):
    return lax.broadcasted_iota(jnp.int32, shape, axis)


def low_half(shape):
    return iota(shape, 1) % LANES < LANES // 2


def head_blocks(scale):
    shape = (LANES, LANES)
    return jnp.where(iota(shape, 0) // 64 == iota(shape, 1) // 64, scale, 0.0).astype(F32)


def head_rows(scale):
    return jnp.where(iota((8, 256), 0) == iota((8, 256), 1) // 64, scale, 0.0).astype(F32)


def partner(values):
    first = iota(values.shape, 1) % 64 < 32
    return jnp.where(first, pltpu.roll(values, LANES - 32, 1), pltpu.roll(values, 32, 1))


def rows_of(index, size):
    return pl.ds(pl.multiple_of(index * size, size), size)


def load_all(sources, targets, sems, first):
    copies = []
    for number, (source, target) in enumerate(zip(sources, targets)):
        copy = pltpu.make_async_copy(source, target, sems.at[first + number])
        copy.start()
        copies.append(copy)
    return copies


def shard_targets(w_refs, ws, me):
    size = w_refs[0].shape[0]
    if len(w_refs) == 1:
        return [ws]
    return [ws.at[rows_of(me ^ slot, size)] for slot in range(len(w_refs))]


def store_slots(whole, out_refs, me):
    if len(out_refs) == 1:
        out_refs[0][...] = whole[...]
        return
    keep_ref, send_ref = out_refs
    size = keep_ref.shape[1]
    for slot in range(2 * keep_ref.shape[0]):
        (send_ref if slot % 2 else keep_ref)[slot // 2] = whole[rows_of(me ^ slot, size), :]


def padded_heads(first, second, low, g, e):
    here = low if e == 0 else jnp.logical_not(low)
    return jnp.where(here, first if g == e else second, 0.0).astype(BF16)


def project_rows(r, size, length, xs, ws, tabs, gains, raw_ref, q_ref, k_ref, v_ref, kp, vp):
    rows = rows_of(r, size)
    cos_ref, sin_ref = tabs
    gq_ref, gk_ref = gains
    mean_of = head_blocks(1.0 / 64)
    low = low_half((size, LANES))
    projected = dot(xs[rows, :], ws[:, :512])
    raw_ref[rows, :] = projected[:, :384]
    cosines, sines = cos_ref[rows, :], sin_ref[rows, :]

    def turned(values, gain):
        mean = dot(values * values, mean_of, precision=HIGH)
        normed = values * lax.rsqrt(mean + EPS) * gain
        return normed * cosines + partner(normed) * sines

    for g in range(2):
        lanes = slice(LANES * g, LANES * (g + 1))
        q_ref[rows, lanes] = turned(projected[:, lanes], gq_ref[...]).astype(BF16)
    keys = turned(projected[:, 256:384], gk_ref[...])
    values = projected[:, 384:512]
    k_ref[rows, :] = keys.astype(BF16)
    v_ref[rows, :] = values.astype(BF16)
    live = r * size + iota((size, LANES), 0) < length
    ones = jnp.where(live, 1.0, 0.0)
    values = jnp.where(live, values, 0.0)
    keys_swap, values_swap = pltpu.roll(keys, 64, 1), pltpu.roll(values, 64, 1)
    for g in range(2):
        for e in range(2):
            kp[2 * g + e, rows, :] = padded_heads(keys, keys_swap, low, g, e)
            vp[2 * g + e, rows, :LANES] = padded_heads(values, values_swap, low, g, e)
            vp[2 * g + e, rows, LANES:] = padded_heads(ones, ones, low, g, e)


def attend_rows(i, size, q_ref, kp, vp, acc, att_ref, lse_ref):
    rows = rows_of(i, size)
    factor = LOG2E / 8.0
    causal = iota((size, size), 1) <= iota((size, size), 0)
    queries = [q_ref[rows, LANES * g : LANES * (g + 1)] for g in range(2)]

    def block(kb, masked):
        cols = rows_of(kb, size)
        sums = []
        for g in range(2):
            total = None
            for e in range(2):
                weights = jnp.exp2(dot_nt(queries[g], kp[2 * g + e, cols, :]) * factor)
                if masked:
                    weights = jnp.where(causal, weights, 0.0)
                part = dot(weights.astype(BF16), vp[2 * g + e, cols, :])
                total = part if total is None else total + part
            sums.append(total)
        return sums

    for g, total in enumerate(block(i, True)):
        acc[g] = total

    def more(kb, carry):
        for g, total in enumerate(block(kb, False)):
            acc[g] += total
        return carry

    lax.fori_loop(i - i, i, more, None)
    logs = []
    for g in range(2):
        lanes = slice(LANES * g, LANES * (g + 1))
        summed = acc[g, :, LANES:]
        att_ref[rows, lanes] = (acc[g, :, :LANES] / summed).astype(BF16)
        logs.append(jnp.log2(summed))
    lse_ref[:, rows] = dot_nt(head_rows(1.0 / 64), jnp.concatenate(logs, axis=1), precision=HIGH)


def attn_fwd_kernel(parts, n_w, scal, cos_ref, sin_ref, gq_ref, gk_ref, *refs):
    x_refs, refs = refs[:parts], refs[parts:]
    w_refs, refs = refs[:n_w], refs[n_w:]
    (raw_ref, q_ref, k_ref, v_ref, att_ref, lse_ref, keep_ref, send_ref, xs, ws, kp, vp, acc, sems) = refs
    size = x_refs[0].shape[0]
    me_t, me_d, length = scal[0], scal[1], scal[2]
    copies = load_all(w_refs, shard_targets(w_refs, ws, me_d), sems, 0)
    copies += load_all(x_refs, [xs.at[rows_of(me_t ^ j, size)] for j in range(parts)], sems, n_w)
    for copy in copies:
        copy.wait()

    def project(r, carry):
        project_rows(
            r, size, length, xs, ws, (cos_ref, sin_ref), (gq_ref, gk_ref), raw_ref, q_ref, k_ref, v_ref, kp, vp
        )
        return carry

    def attend(i, carry):
        attend_rows(i, size, q_ref, kp, vp, acc, att_ref, lse_ref)
        return carry

    lax.fori_loop(0, parts, project, 0)
    lax.fori_loop(0, parts, attend, 0)
    for j in range(parts):
        out = dot_nt(att_ref[rows_of(me_t ^ j, size), :], ws[:, 512:])
        (send_ref if j % 2 else keep_ref)[j // 2] = out.astype(BF16)


def attn_fwd(scal, cosines, sines, gq, gk, x_parts, w_parts):
    parts, n_w = len(x_parts), len(w_parts)
    size, width = x_parts[0].shape
    full = parts * size
    cols = w_parts[0].shape[1]
    pair = jax.ShapeDtypeStruct((parts // 2, size, width), BF16)
    return pl.pallas_call(
        functools.partial(attn_fwd_kernel, parts, n_w),
        out_shape=(
            jax.ShapeDtypeStruct((full, 384), F32),
            jax.ShapeDtypeStruct((full, 256), BF16),
            jax.ShapeDtypeStruct((full, 128), BF16),
            jax.ShapeDtypeStruct((full, 128), BF16),
            jax.ShapeDtypeStruct((full, 256), BF16),
            jax.ShapeDtypeStruct((8, full), F32),
            pair,
            pair,
        ),
        in_specs=[SMEM] + [VMEM] * 4 + [ANY] * (parts + n_w),
        out_specs=(VMEM,) * 8,
        scratch_shapes=[
            pltpu.VMEM((full, width), BF16),
            pltpu.VMEM((width, cols), BF16),
            pltpu.VMEM((4, full, LANES), BF16),
            pltpu.VMEM((4, full, 2 * LANES), BF16),
            pltpu.VMEM((2, size, 2 * LANES), F32),
            pltpu.SemaphoreType.DMA((n_w + parts,)),
        ],
        compiler_params=pltpu.CompilerParams(vmem_limit_bytes=VMEM_LIMIT),
        cost_estimate=pl.CostEstimate(flops=8_000_000_000, bytes_accessed=12_000_000, transcendentals=3_000_000),
        name="attention_forward",
    )(scal, cosines, sines, gq, gk, *x_parts, *w_parts)


def prepare_rows(r, size, length, gs, ws, k_ref, v_ref, att_ref, ga, drow, kp, kt, vp):
    rows = rows_of(r, size)
    low = low_half((size, LANES))
    grad = dot(gs[rows, :], ws[:, 512:]).astype(BF16)
    ga[rows, :] = grad
    drow[:, rows] = dot_nt(head_rows(1.0), grad.astype(F32) * att_ref[rows, :].astype(F32), precision=HIGH)
    live = r * size + iota((size, LANES), 0) < length
    keys = jnp.where(live, k_ref[rows, :].astype(F32), 0.0)
    values = jnp.where(live, v_ref[rows, :].astype(F32), 0.0)
    keys_swap, values_swap = pltpu.roll(keys, 64, 1), pltpu.roll(values, 64, 1)
    for g in range(2):
        for e in range(2):
            here = low if e == 0 else jnp.logical_not(low)
            padded = jnp.where(here, keys if g == e else keys_swap, 0.0)
            kp[2 * g + e, rows, :] = padded.astype(BF16)
            kt[2 * g + e, :, rows] = padded.T.astype(BF16)
            vp[2 * g + e, rows, :] = padded_heads(values, values_swap, low, g, e)


def sweep_rows(i, size, q_ref, ga, kp, kt, vp, drow, lrow, acc, dq, dk, dv):
    rows = rows_of(i, size)
    factor = LOG2E / 8.0
    causal = iota((size, size), 0) <= iota((size, size), 1)
    low2 = iota((2 * size, LANES), 0) // size == iota((2 * size, LANES), 1) // 64
    queries, grads, queries2, grads2 = [], [], [], []
    for g in range(2):
        lanes = slice(LANES * g, LANES * (g + 1))
        queries.append(q_ref[rows, lanes])
        grads.append(ga[rows, lanes])
        for source, target in ((queries, queries2), (grads, grads2)):
            both = jnp.concatenate([source[g], source[g]], axis=0)
            target.append(jnp.where(low2, both, jnp.zeros_like(both)))

    def block(kb, masked):
        cols = rows_of(kb, size)
        parts_t = []
        for g in range(2):
            weights2, scores2, turned = [], [], None
            for e in range(2):
                h = 2 * g + e
                weights = jnp.exp2(dot_nt(kp[h, cols, :], queries[g]) * factor - lrow[h : h + 1, rows])
                if masked:
                    weights = jnp.where(causal, weights, 0.0)
                grad_weights = dot_nt(vp[h, cols, :], grads[g])
                grad_scores = (weights * (grad_weights - drow[h : h + 1, rows])).astype(BF16)
                weights2.append(weights.astype(BF16))
                scores2.append(grad_scores)
                part = dot(kt[h, :, cols], grad_scores)
                turned = part if turned is None else turned + part
            dv[g, cols, :] += dot(jnp.concatenate(weights2, axis=1), grads2[g])
            dk[g, cols, :] += dot(jnp.concatenate(scores2, axis=1), queries2[g])
            parts_t.append(turned)
        return parts_t

    for g, total in enumerate(block(i, True)):
        acc[g] = total

    def more(kb, carry):
        for g, total in enumerate(block(kb, False)):
            acc[g] += total
        return carry

    lax.fori_loop(i - i, i, more, None)
    for g in range(2):
        dq[rows, LANES * g : LANES * (g + 1)] = acc[g].T


def unproject_head(rows, grad, tabs, gain_ref, raw_ref, lanes, gp, gains_ref, row):
    cosines, sines = tabs[0][rows, :], tabs[1][rows, :]
    mean_of = head_blocks(1.0 / 64)
    raw = raw_ref[rows, lanes]
    rms = lax.rsqrt(dot(raw * raw, mean_of, precision=HIGH) + EPS)
    turned = grad * cosines - partner(grad) * sines
    gains_ref[row : row + 1, :] += jnp.sum(turned * raw * rms, axis=0, keepdims=True)
    weighted = turned * gain_ref[...]
    inner = dot(raw * weighted, mean_of, precision=HIGH)
    gp[rows, lanes] = (rms * weighted - raw * (rms * rms * rms) * inner).astype(BF16)


def unproject_queries(r, size, tabs, gain_ref, raw_ref, dq, gp, gains_ref):
    rows = rows_of(r, size)
    for g in range(2):
        lanes = slice(LANES * g, LANES * (g + 1))
        unproject_head(rows, dq[rows, lanes] * 0.125, tabs, gain_ref, raw_ref, lanes, gp, gains_ref, 0)


def unproject_pairs(r, size, length, tabs, gain_ref, raw_ref, dk, dv, gp, gains_ref):
    rows = rows_of(r, size)
    low = low_half((size, LANES))
    live = r * size + iota((size, LANES), 0) < length

    def folded(ref):
        first, second = ref[0, rows, :], ref[1, rows, :]
        both = jnp.where(low, first + pltpu.roll(first, 64, 1), second + pltpu.roll(second, 64, 1))
        return jnp.where(live, both, 0.0)

    unproject_head(rows, folded(dk) * 0.125, tabs, gain_ref, raw_ref, slice(256, 384), gp, gains_ref, 1)
    gp[rows, 384:512] = folded(dv).astype(BF16)


def attn_bwd_kernel(parts, n_w, scal, cos_ref, sin_ref, gq_ref, gk_ref, raw_ref, q_ref, k_ref, v_ref, att_ref, lse_ref, *refs):
    x_refs, refs = refs[:parts], refs[parts:]
    r_refs, refs = refs[:parts], refs[parts:]
    w_refs, refs = refs[:n_w], refs[n_w:]
    n_g = 1 if n_w == 1 else 2
    keep_ref, send_ref, gains_ref = refs[:3]
    g_refs, refs = refs[3 : 3 + n_g], refs[3 + n_g :]
    xs, gs, ws, kp, vp, kt, ga, dq, dk, dv, gp, whole, drow, acc, sems = refs
    size = x_refs[0].shape[0]
    me_t, me_d, length = scal[0], scal[1], scal[2]
    copies = load_all(w_refs, shard_targets(w_refs, ws, me_d), sems, 0)
    copies += load_all(r_refs, [gs.at[rows_of(me_t ^ j, size)] for j in range(parts)], sems, n_w)
    copies += load_all(x_refs, [xs.at[rows_of(me_t ^ j, size)] for j in range(parts)], sems, n_w + parts)
    for copy in copies:
        copy.wait()

    def prepare(r, carry):
        prepare_rows(r, size, length, gs, ws, k_ref, v_ref, att_ref, ga, drow, kp, kt, vp)
        return carry

    def sweep(i, carry):
        sweep_rows(i, size, q_ref, ga, kp, kt, vp, drow, lse_ref, acc, dq, dk, dv)
        return carry

    def unproject(r, carry):
        unproject_queries(r, size, (cos_ref, sin_ref), gq_ref, raw_ref, dq, gp, gains_ref)
        unproject_pairs(r, size, length, (cos_ref, sin_ref), gk_ref, raw_ref, dk, dv, gp, gains_ref)
        return carry

    lax.fori_loop(0, parts, prepare, 0)
    dk[...] = jnp.zeros_like(dk)
    dv[...] = jnp.zeros_like(dv)
    lax.fori_loop(0, parts, sweep, 0)
    gains_ref[...] = jnp.zeros_like(gains_ref)
    lax.fori_loop(0, parts, unproject, 0)
    for j in range(parts):
        out = dot_nt(gp[rows_of(me_t ^ j, size), :], ws[:, :512])
        (send_ref if j % 2 else keep_ref)[j // 2] = out.astype(BF16)

    def weigh(b, carry):
        rows = rows_of(b, 256)
        whole[rows, :512] = dot_tn(xs[:, rows], gp[...]).astype(BF16)
        whole[rows, 512:] = dot_tn(gs[:, rows], att_ref[...]).astype(BF16)
        return carry

    lax.fori_loop(0, whole.shape[0] // 256, weigh, 0)
    store_slots(whole, g_refs, me_d)


def slot_shapes(n_w, width, cols):
    if n_w == 1:
        return (jax.ShapeDtypeStruct((width, cols), BF16),)
    return (jax.ShapeDtypeStruct((n_w // 2, width // n_w, cols), BF16),) * 2


def attn_bwd(scal, cosines, sines, gq, gk, saved, x_parts, r_parts, w_parts):
    parts, n_w = len(x_parts), len(w_parts)
    size, width = x_parts[0].shape
    full = parts * size
    cols = w_parts[0].shape[1]
    pair = jax.ShapeDtypeStruct((parts // 2, size, width), BF16)
    g_shapes = slot_shapes(n_w, width, cols)
    outs = pl.pallas_call(
        functools.partial(attn_bwd_kernel, parts, n_w),
        out_shape=(pair, pair, jax.ShapeDtypeStruct((8, LANES), F32)) + g_shapes,
        in_specs=[SMEM] + [VMEM] * 10 + [ANY] * (2 * parts + n_w),
        out_specs=(VMEM,) * (3 + len(g_shapes)),
        scratch_shapes=[
            pltpu.VMEM((full, width), BF16),
            pltpu.VMEM((full, width), BF16),
            pltpu.VMEM((width, cols), BF16),
            pltpu.VMEM((4, full, LANES), BF16),
            pltpu.VMEM((4, full, LANES), BF16),
            pltpu.VMEM((4, LANES, full), BF16),
            pltpu.VMEM((full, 256), BF16),
            pltpu.VMEM((full, 256), F32),
            pltpu.VMEM((2, full, LANES), F32),
            pltpu.VMEM((2, full, LANES), F32),
            pltpu.VMEM((full, 512), BF16),
            pltpu.VMEM((width, cols), BF16),
            pltpu.VMEM((8, full), F32),
            pltpu.VMEM((2, LANES, size), F32),
            pltpu.SemaphoreType.DMA((n_w + 2 * parts,)),
        ],
        compiler_params=pltpu.CompilerParams(vmem_limit_bytes=VMEM_LIMIT),
        cost_estimate=pl.CostEstimate(flops=14_000_000_000, bytes_accessed=15_000_000, transcendentals=3_000_000),
        name="attention_backward",
    )(scal, cosines, sines, gq, gk, *saved, *x_parts, *r_parts, *w_parts)
    return outs[0], outs[1], outs[2], outs[3:]


def ff_kernel(n_x, n_w, scal, *refs):
    x_refs, refs = refs[:n_x], refs[n_x:]
    u_refs, refs = refs[:n_x], refs[n_x:]
    w_refs, refs = refs[:n_w], refs[n_w:]
    n_g = 1 if n_w == 1 else 2
    hid_ref, ggu_ref = refs[:2]
    g_refs, refs = refs[2 : 2 + n_g], refs[2 + n_g :]
    xs, us, ws, whole, sems = refs
    size = x_refs[0].shape[0]
    me_d = scal[1]
    cols = ws.shape[1] // 3
    copies = load_all(w_refs, shard_targets(w_refs, ws, me_d), sems, 0)
    x_copies = load_all(x_refs, [xs.at[pl.ds(j * size, size)] for j in range(n_x)], sems, n_w)
    u_copies = load_all(u_refs, [us.at[pl.ds(j * size, size)] for j in range(n_x)], sems, n_w + n_x)
    for copy in copies + x_copies + u_copies:
        copy.wait()

    def tokens(r, carry):
        rows = rows_of(r, size)
        gate_up = dot(xs[rows, :], ws[:, : 2 * cols])
        grad = dot(us[rows, :], ws[:, 2 * cols :])
        gate, up = gate_up[:, :cols], gate_up[:, cols:]
        sig = 1.0 / (1.0 + jnp.exp2(gate * -LOG2E))
        silu = gate * sig
        hid_ref[rows, :] = (silu * up).astype(BF16)
        ggu_ref[rows, :cols] = (grad * up * (sig + silu * (1.0 - sig))).astype(BF16)
        ggu_ref[rows, cols:] = (grad * silu).astype(BF16)
        return carry

    lax.fori_loop(0, n_x, tokens, 0)

    def weigh(b, carry):
        rows = rows_of(b, 256)
        whole[rows, : 2 * cols] = dot_tn(xs[:, rows], ggu_ref[...]).astype(BF16)
        whole[rows, 2 * cols :] = dot_tn(us[:, rows], hid_ref[...]).astype(BF16)
        return carry

    lax.fori_loop(0, whole.shape[0] // 256, weigh, 0)
    store_slots(whole, g_refs, me_d)


def feed_forward(scal, x_parts, u_parts, w_parts):
    n_x, n_w = len(x_parts), len(w_parts)
    size, width = x_parts[0].shape
    full = n_x * size
    wide = w_parts[0].shape[1]
    cols = wide // 3
    g_shapes = slot_shapes(n_w, width, wide)
    outs = pl.pallas_call(
        functools.partial(ff_kernel, n_x, n_w),
        out_shape=(
            jax.ShapeDtypeStruct((full, cols), BF16),
            jax.ShapeDtypeStruct((full, 2 * cols), BF16),
        )
        + g_shapes,
        in_specs=[SMEM] + [ANY] * (2 * n_x + n_w),
        out_specs=(VMEM,) * (2 + len(g_shapes)),
        scratch_shapes=[
            pltpu.VMEM((full, width), BF16),
            pltpu.VMEM((full, width), BF16),
            pltpu.VMEM((width, wide), BF16),
            pltpu.VMEM((width, wide), BF16),
            pltpu.SemaphoreType.DMA((n_w + 2 * n_x,)),
        ],
        compiler_params=pltpu.CompilerParams(vmem_limit_bytes=VMEM_LIMIT),
        cost_estimate=pl.CostEstimate(flops=4 * full * width * wide, bytes_accessed=20_000_000, transcendentals=full * cols),
        name="feed_forward",
    )(scal, *x_parts, *u_parts, *w_parts)
    return outs[0], outs[1], outs[2:]


def ff_out_kernel(parts, n_c, n_w, seq, scal, *refs):
    hid_refs, refs = refs[:n_c], refs[n_c:]
    ggu_refs, refs = refs[:n_c], refs[n_c:]
    w_refs, refs = refs[: n_c * n_w], refs[n_c * n_w :]
    ykeep_ref, ysend_ref, gkeep_ref, gsend_ref, hs, gs, ws, sems = refs
    size = ykeep_ref.shape[1]
    full = parts * size
    me_d = scal[1]
    wide = ws.shape[2]
    cols = wide // 3
    copies = []
    first = 0
    for c in range(n_c):
        targets = shard_targets(w_refs[c * n_w : (c + 1) * n_w], ws.at[c], me_d)
        copies += load_all(w_refs[c * n_w : (c + 1) * n_w], targets, sems, first)
        first += n_w
    mine = pl.ds(seq * full, full)
    copies += load_all([ref.at[mine] for ref in ggu_refs], [gs.at[c] for c in range(n_c)], sems, first)
    copies += load_all([ref.at[mine] for ref in hid_refs], [hs.at[c] for c in range(n_c)], sems, first + n_c)
    for copy in copies:
        copy.wait()
    for j in range(parts):
        rows = pl.ds(j * size, size)
        grad = sum(dot_nt(gs[c, rows, :], ws[c, :, : 2 * cols]) for c in range(n_c))
        (gsend_ref if j % 2 else gkeep_ref)[j // 2] = grad.astype(BF16)
        out = sum(dot_nt(hs[c, rows, :], ws[c, :, 2 * cols :]) for c in range(n_c))
        (ysend_ref if j % 2 else ykeep_ref)[j // 2] = out.astype(BF16)


def ff_out(seq, scal, parts, size, hids, ggus, w_chunks):
    n_c, n_w = len(w_chunks), len(w_chunks[0])
    wide = w_chunks[0][0].shape[1]
    width = w_chunks[0][0].shape[0] * n_w
    full = parts * size
    cols = wide // 3
    pair = jax.ShapeDtypeStruct((parts // 2, size, width), BF16)
    return pl.pallas_call(
        functools.partial(ff_out_kernel, parts, n_c, n_w, seq),
        out_shape=(pair,) * 4,
        in_specs=[SMEM] + [ANY] * (2 * n_c + n_c * n_w),
        out_specs=(VMEM,) * 4,
        scratch_shapes=[
            pltpu.VMEM((n_c, full, cols), BF16),
            pltpu.VMEM((n_c, full, 2 * cols), BF16),
            pltpu.VMEM((n_c, width, wide), BF16),
            pltpu.SemaphoreType.DMA((n_c * n_w + 2 * n_c,)),
        ],
        compiler_params=pltpu.CompilerParams(vmem_limit_bytes=VMEM_LIMIT),
        cost_estimate=pl.CostEstimate(flops=2 * full * width * wide * n_c, bytes_accessed=22_000_000, transcendentals=0),
        name="feed_forward_out",
    )(scal, *hids, *ggus, *[shard for chunk in w_chunks for shard in chunk])


def flip(index, bits):
    for bit in (1, 2, 4):
        if bits & bit:
            index = index + bit - 2 * bit * lax.rem(lax.div(index, bit), 2)
    return index


class Spot:
    def __init__(self, index, choices):
        self.index = index
        self.flips = {0: index}
        for bits in choices:
            self.flips[bits] = flip(index, bits)


def spots():
    me_t = Spot(lax.axis_index("tensor"), (1, 2, 3))
    me_d = Spot(lax.axis_index("dp"), (1, 2, 3, 4, 5, 6, 7))
    me_d.x = lax.rem(me_d.index, 2)
    me_d.beside = 1 - me_d.x
    me_d.z = Spot(lax.div(me_d.index, 2), (1, 2, 3))
    return me_t, me_d


def greet(barrier, me_d, me_t, along_d, along_t):
    devices = [{"dp": me_d.flips[bits]} for bits in along_d]
    devices += [{"tensor": me_t.flips[bits]} for bits in along_t]
    for device in devices:
        pl.semaphore_signal(barrier, inc=1, device_id=device, device_id_type=pl.DeviceIdType.MESH)
    return lambda: pl.semaphore_wait(barrier, len(devices))


def remote(source, target, sems, number, device):
    return pltpu.make_async_remote_copy(
        src_ref=source,
        dst_ref=target,
        send_sem=sems.at[0, number],
        recv_sem=sems.at[1, number],
        device_id=device,
        device_id_type=pl.DeviceIdType.MESH,
    )


class Remote:
    LIMIT = 128

    def __init__(self, sems):
        self.sems, self.used = sems, 0

    def __call__(self, source, target, device):
        assert self.used < self.LIMIT
        self.used += 1
        return remote(source, target, self.sems, self.used - 1, device)


class Local:
    LIMIT = 64

    def __init__(self, sems):
        self.sems, self.used = sems, 0

    def make(self, source, target):
        assert self.used < self.LIMIT
        self.used += 1
        return pltpu.make_async_copy(source, target, self.sems.at[self.used - 1])

    def __call__(self, source, target):
        copy = self.make(source, target)
        copy.start()
        return copy


COPY_SEMS = [
    pltpu.SemaphoreType.DMA((2, Remote.LIMIT)),
    pltpu.SemaphoreType.DMA((Local.LIMIT,)),
]


class ShardGather:
    def __init__(self, shard, place, send, me_d, direct=False):
        def pass_on(bits, target):
            there = place(me_d.flips[bits])
            return send(there, there, {"dp": me_d.flips[target]})

        mine = place(me_d.index)
        self.beside, self.next, self.across = [send(shard, mine, {"dp": me_d.flips[bits]}) for bits in (1, 2, 4)]
        self.direct = direct
        self.on = send(shard, mine, {"dp": me_d.flips[6]}) if direct else pass_on(4, 2)
        self.passed = [pass_on(bits, 1) for bits in (4, 2, 6)]

    def start_x(self):
        self.beside.start()

    def start_z(self):
        self.next.start()
        self.across.start()
        if self.direct:
            self.on.start()

    def forward(self):
        self.next.wait_recv()
        self.passed[1].start()
        self.across.wait_recv()
        if not self.direct:
            self.on.start()
        self.passed[0].start()

    def forward_last(self):
        self.on.wait_recv()
        self.passed[2].start()

    def arrive(self):
        self.beside.wait_recv()
        for copy in self.passed:
            copy.wait_recv()

    def drain(self):
        for copy in [self.beside, self.next, self.across, self.on] + self.passed:
            copy.wait_send()


class TokenGather:
    def __init__(self, block, whole, send, me_t):
        size = block.shape[0]
        mine = whole.at[rows_of(me_t.index, size)]
        there = whole.at[rows_of(me_t.flips[2], size)]
        near = {"tensor": me_t.flips[1]}
        self.near = send(block, mine, near)
        self.far = send(block, mine, {"tensor": me_t.flips[2]})
        self.passed = send(there, there, near)

    def start(self):
        self.far.start()
        self.near.start()

    def forward(self):
        self.far.wait_recv()
        self.passed.start()

    def arrive(self):
        self.near.wait_recv()
        self.passed.wait_recv()

    def drain(self):
        for copy in (self.near, self.far, self.passed):
            copy.wait_send()


class TokenReduce:
    def __init__(self, blocks, near, far, send, me_t, mine=None):
        device = {"tensor": me_t.flips[1]}
        self.blocks, self.near_ref, self.far_ref, self.mine = blocks, near, far, mine
        self.places = (me_t.index, me_t.flips[2])
        self.size = far.shape[0]
        self.near = [
            send(blocks.at[rows_of(me_t.flips[1 + 2 * n], self.size)], near.at[n], device) for n in range(2)
        ]
        self.far = send(near.at[1], far, {"tensor": me_t.flips[2]})

    def load(self, here):
        return [here(self.blocks.at[rows_of(place, self.size)], self.mine.at[n]) for n, place in enumerate(self.places)]

    def start(self, *which):
        for n in which or (1, 0):
            self.near[n].start()

    def part(self, n, rows):
        if self.mine is not None:
            return self.mine[n, rows, :].astype(F32)
        start = pl.multiple_of(self.places[n] * self.size + rows.start, 32)
        return self.blocks[pl.ds(start, rows.size), :].astype(F32)

    def middle(self):
        self.near[1].wait_recv()

        def step(rows):
            total = self.part(1, rows) + self.near_ref[1, rows, :].astype(F32)
            self.near_ref[1, rows, :] = total.astype(BF16)

        by_rows(self.size, 32, step)
        self.far.start()

    def arrive(self):
        self.near[0].wait_recv()
        self.far.wait_recv()

    def rows(self, rows):
        total = self.part(0, rows) + self.near_ref[0, rows, :].astype(F32)
        return total + self.far_ref[rows, :].astype(F32)

    def drain(self):
        for copy in self.near + [self.far]:
            copy.wait_send()


class ShardNear:
    def __init__(self, whole, near, out, send, me_d, mine=None):
        self.whole, self.near_ref, self.out, self.mine = whole, near, out, mine
        self.z, self.x = me_d.z, me_d.x
        self.size = near.shape[1]
        self.near = send(whole.at[:, me_d.beside], near, {"dp": me_d.flips[1]})

    def load(self, here):
        return [here(self.whole.at[:, self.x], self.mine)]

    def start(self):
        self.near.start()

    def part(self, there, rows):
        if self.mine is not None:
            return self.mine[there, rows, :].astype(F32)
        return self.whole[there, self.x, rows, :].astype(F32)

    def middle(self, far=None):
        self.near.wait_recv()
        for k in (1, 3, 2, 0):
            there = self.z.flips[k]

            def step(rows):
                total = self.part(there, rows) + self.near_ref[there, rows, :].astype(F32)
                if k:
                    self.near_ref[there, rows, :] = total.astype(BF16)
                else:
                    self.out[rows, :] = total

            by_rows(self.size, 32, step)
            if k and far is not None:
                far.ready(k)

    def drain(self):
        self.near.wait_send()


class ShardFar:
    def __init__(self, near, far, out, send, me_d):
        self.far_ref, self.out = far, out
        self.size = far.shape[1]
        self.far = [send(near.at[me_d.z.flips[k]], far.at[k - 1], {"dp": me_d.flips[2 * k]}) for k in (1, 2, 3)]
        self.last = self.far
        self.terms = (0, 1, 2)

    def ready(self, k):
        self.far[k - 1].start()

    def finish(self):
        for copy in self.last:
            copy.wait_recv()

        def step(rows):
            total = self.out[rows, :]
            for k in self.terms:
                total = total + self.far_ref[k, rows, :].astype(F32)
            self.out[rows, :] = total

        by_rows(self.size, 32, step)

    def drain(self):
        for copy in self.far:
            copy.wait_send()


class ShardHalves(ShardFar):
    def __init__(self, near, far, out, send, me_d):
        self.near_ref, self.far_ref, self.out = near, far, out
        self.size = far.shape[1]
        z = me_d.z.flips
        self.across = z[2]
        self.far = [
            send(near.at[z[1]], far.at[0], {"dp": me_d.flips[2]}),
            send(near.at[z[3]], far.at[1], {"dp": me_d.flips[2]}),
            send(near.at[z[2]], far.at[2], {"dp": me_d.flips[4]}),
        ]
        self.last = (self.far[0], self.far[2])
        self.terms = (0, 2)

    def ready(self, k):
        if k != 2:
            self.far[k // 2].start()

    def middle(self):
        self.far[1].wait_recv()

        def step(rows):
            total = self.near_ref[self.across, rows, :].astype(F32) + self.far_ref[1, rows, :].astype(F32)
            self.near_ref[self.across, rows, :] = total.astype(BF16)

        by_rows(self.size, 32, step)
        self.far[2].start()


def by_rows(count, step, body):
    def run(b, carry):
        body(rows_of(b, step))
        return carry

    lax.fori_loop(0, count // step, run, None)


def loop(start, stop, body):
    def run(i, carry):
        body(i)
        return carry

    lax.fori_loop(start, stop, run, None)


def rms_factor(values):
    return lax.rsqrt(jnp.mean(values * values, axis=-1, keepdims=True) + EPS)


def shape(dims, kind):
    return jax.ShapeDtypeStruct(dims, kind)


def block_kernel(
    lengths, in_ref, cot_ref, qw_ref, kv_ref, ow_ref, iw_ref, dw_ref, cos_ref, sin_ref, qg_ref, kg_ref, mg_ref, dg_ref,
    normed_out, raw_out, q_out, k_out, v_out, att_out, lse_out, r_out, blk_out,
    ig_ref, awg_ref, ffg_ref, sums_ref,
    x_ref, gq_ref, gk_ref, xs, ws, dn, us, outp, onear, ofar, resid, wnear, wfar, whole, dgain, put, got_t, got_d, free,
    sems, local_sems,
):
    seqs, full, width = xs.shape
    size = resid.shape[1]
    parts = full // size
    n_c = 3
    shard = qw_ref.shape[0]
    cols = iw_ref.shape[2] // n_c
    wide = 3 * cols
    me_t, me_d = spots()
    send, here = Remote(sems), Local(local_sems)
    mine_t, mine_d = rows_of(me_t.index, size), rows_of(me_d.index, shard)
    halves = [pl.ds(s * full, full) for s in range(seqs)]
    own_rows = [rows_of(s * parts + me_t.index, size) for s in range(seqs)]
    every_row = pl.ds(0, seqs * full)
    lanes_of = [slice(width * s, width * (s + 1)) for s in range(seqs)]

    def wait(copies):
        for copy in copies:
            copy.wait()

    pro_w = [
        ShardGather(ws.at[mine_d, lanes], lambda i, lanes=lanes: ws.at[rows_of(i, shard), lanes], send, me_d)
        for lanes in (slice(0, 256), slice(256, 512))
    ]
    out_w = ShardGather(ws.at[mine_d, 512:], lambda i: ws.at[rows_of(i, shard), 512:], send, me_d, True)
    normed = [TokenGather(xs.at[s, mine_t], xs.at[s], send, me_t) for s in range(seqs)]
    ups = [TokenGather(us.at[own_rows[s]], us.at[halves[s]], send, me_t) for s in range(seqs)]
    denses = [TokenGather(dn.at[own_rows[s]], dn.at[halves[s]], send, me_t) for s in range(seqs)]
    out_places = (outp, xs.at[0])
    back_places = (outp, xs.at[1])
    norm_places = (outp, dn.at[halves[0]])
    outs, backs, norms = [
        [TokenReduce(places[s], onear.at[s], ofar.at[s], send, me_t) for s in range(seqs)]
        for places in (out_places, back_places, norm_places)
    ]
    lows = [xs.at[0, pl.ds(s * size, size)] for s in range(seqs)]
    resids = [TokenGather(lows[s], r_out.at[s], send, me_t) for s in range(seqs)]
    ff_sums = [ffg_ref.at[:, wide * c : wide * (c + 1)] for c in range(n_c)]
    near = [ShardNear(whole.at[c], wnear.at[c], ff_sums[c], send, me_d) for c in range(2)]
    far = [ShardHalves(wnear.at[c], wfar.at[c], ff_sums[c], send, me_d) for c in range(2)]
    steps = [
        [send(put.at[0], got_t.at[me_t.index], {"tensor": me_t.flips[bits]}) for bits in (1, 2, 3)],
        [send(put.at[1], got_d.at[me_d.index], {"dp": me_d.flips[bits]}) for bits in (1, 2, 3, 4, 5, 6, 7)],
    ]
    load_own = [here.make(us.at[own_rows[s]], xs.at[0, pl.ds((seqs + s) * size, size)]) for s in range(seqs)]
    keeps = [here.make(xs.at[s], normed_out.at[s]) for s in range(seqs)]
    backup = [here.make(normed_out.at[s], xs.at[s]) for s in range(seqs)]
    low_keeps = [here.make(lows[s], r_out.at[s, mine_t]) for s in range(seqs)]

    def after_out(s):
        outs[s].arrive()
        outs[s].drain()

        def norm(rows):
            values = x_ref[rows, lanes_of[s]].astype(F32) + outs[s].rows(rows)
            resid[s, rows, :] = values
            target = pl.ds(pl.multiple_of((s * parts + me_t.index) * size + rows.start, 32), 32)
            dn[target, :] = (values * rms_factor(values) * dg_ref[...]).astype(BF16)

        by_rows(size, 32, norm)
        denses[s].start()
        if s:
            for copy in load_own:
                copy.start()

    def after_back(s):
        backs[s].arrive()
        backs[s].drain()

        def step(rows):
            grad = backs[s].rows(rows)
            values = resid[s, rows, :]
            factor = rms_factor(values)
            product = grad * values * factor
            dgain[...] += jnp.sum(product.reshape(-1, 8, width), axis=0)
            weighted = grad * dg_ref[...]
            inner = jnp.mean(values * weighted, axis=-1, keepdims=True)
            place = pl.ds(pl.multiple_of((seqs + s) * size + rows.start, 32), 32)
            total = xs[0, place, :].astype(F32) + factor * weighted - values * (factor * factor * factor) * inner
            ig_ref[rows, lanes_of[s]] = total
            lows[s][rows, :] = total.astype(BF16)

        by_rows(size, 32, step)
        resids[s].start()
        low_keeps[s].start()

    def after_norm(s):
        norms[s].arrive()

        def step(rows):
            values = x_ref[rows, lanes_of[s]].astype(F32)
            factor = rms_factor(values)
            weighted = norms[s].rows(rows) * mg_ref[...]
            inner = jnp.mean(values * weighted, axis=-1, keepdims=True)
            ig_ref[rows, lanes_of[s]] += factor * weighted - values * (factor * factor * factor) * inner

        by_rows(size, 32, step)

    def until_backward(wf):
        ff_w = [ShardGather(wf.at[c, mine_d], lambda i, c=c: wf.at[c, rows_of(i, shard)], send, me_d) for c in range(n_c)]

        def attention(kp, vp, acc, raw, q, k, v, att, lse, inb, cotb, kvb, owb, iwb, dwb):
            kept = ((raw, raw_out), (q, q_out), (k, k_out), (v, v_out), (att, att_out), (lse, lse_out))
            flushes = []

            def project(s):
                loop(0, parts, lambda r: project_rows(
                    r, size, lengths[s], xs.at[s], ws, (cos_ref, sin_ref), (gq_ref, gk_ref),
                    raw.at[s], q.at[s], k.at[s], v.at[s], kp, vp,
                ))

            def attend(s, start, stop):
                loop(start, stop, lambda i: attend_rows(i, size, q.at[s], kp, vp, acc, att.at[s], lse.at[s]))

            def out(s):
                for n, bits in enumerate((3, 1, 2, 0)):
                    rows = rows_of(me_t.flips[bits], size)
                    out_places[s][rows, :] = dot_nt(att[s, rows, :], ws[:, 512:]).astype(BF16)
                    if n < 2:
                        outs[s].start(1 - n)

            def first_rows(rows):
                values = inb[rows, :, :].astype(F32)
                target = pl.ds(pl.multiple_of(me_t.index * size + rows.start, 32), 32)
                for s in range(seqs):
                    mine = values[:, s, :]
                    x_ref[rows, lanes_of[s]] = mine.astype(BF16)
                    xs[s, target, :] = (mine * rms_factor(mine) * mg_ref[...]).astype(BF16)

            def upstream_rows(rows):
                grads = cotb[rows, :, :].astype(F32)
                place = me_t.index * size + rows.start + iota((32, width), 0)
                for s in range(seqs):
                    target = pl.ds(pl.multiple_of((s * parts + me_t.index) * size + rows.start, 32), 32)
                    us[target, :] = jnp.where(place < lengths[s], grads[:, s, :], 0.0).astype(BF16)

            def inner_rows(rows):
                both = iwb[rows, :, :].astype(F32)
                target = pl.ds(pl.multiple_of(me_d.index * shard + rows.start, 32), 32)
                for c in range(n_c):
                    for n in range(2):
                        part = both[:, n, cols * c : cols * (c + 1)]
                        wf[c, target, cols * n : cols * (n + 1)] = part.astype(BF16)

            entered = greet(
                pltpu.get_barrier_semaphore(), me_d, me_t, (1, 2, 3, 4, 5, 6, 7), (1, 2, 3)
            )
            load_x = here(in_ref, inb)
            load_a = [here(qw_ref, ws.at[mine_d, :256]), here(kv_ref, kvb), here(ow_ref, owb)]
            load_f = [here(iw_ref, iwb), here(dw_ref, dwb)]
            load_u = here(cot_ref, cotb)
            for source, target in ((qg_ref, gq_ref), (kg_ref, gk_ref)):
                target[...] = jnp.concatenate([source[...], source[...]], axis=1)
            wait(load_a)
            pair = kvb[...].astype(F32)
            for n in range(2):
                ws[mine_d, 256 + 128 * n : 384 + 128 * n] = pair[:, n, :].astype(BF16)
            ws[mine_d, 512:] = owb[...].astype(F32).T.astype(BF16)
            load_x.wait()
            by_rows(size, 32, first_rows)
            entered()
            normed[0].start()
            for exchange in pro_w:
                exchange.start_z()
                exchange.start_x()
            wait(load_f)
            for c in range(n_c):
                wf[c, mine_d, 2 * cols :] = dwb[cols * c : cols * (c + 1), :].astype(F32).T.astype(BF16)
            by_rows(shard, 32, inner_rows)
            for exchange in pro_w:
                exchange.forward()
            for exchange in pro_w:
                exchange.forward_last()
            out_w.start_z()
            out_w.start_x()
            normed[0].forward()
            normed[1].start()
            normed[0].arrive()
            ff_w[0].start_z()
            load_u.wait()
            by_rows(size, 32, upstream_rows)
            for exchange in pro_w:
                exchange.arrive()
            ff_w[0].start_x()
            project(0)
            keeps[0].start()
            out_w.forward()
            out_w.forward_last()
            attend(0, 0, 3)
            normed[1].forward()
            ups[0].start()
            attend(0, 3, parts)
            ff_w[0].forward()
            out_w.arrive()
            out(0)
            outs[0].middle()
            for source, target in kept:
                flushes.append(here(source.at[0], target.at[0]))
            normed[1].arrive()
            project(1)
            keeps[1].start()
            ff_w[0].forward_last()
            ff_w[1].start_z()
            ff_w[1].start_x()
            attend(1, 0, 3)
            ups[0].forward()
            attend(1, 3, parts)
            normed[0].drain()
            keeps[0].wait()
            out(1)
            for source, target in kept:
                flushes.append(here(source.at[1], target.at[1]))
            after_out(0)
            outs[1].middle()
            ff_w[1].forward()
            ff_w[2].start_z()
            ff_w[2].start_x()
            wait(flushes)

        pl.run_scoped(
            attention,
            pltpu.VMEM((4, full, LANES), BF16),
            pltpu.VMEM((4, full, 2 * LANES), BF16),
            pltpu.VMEM((2, size, 2 * LANES), F32),
            pltpu.VMEM((seqs, full, 384), F32),
            pltpu.VMEM((seqs, full, 256), BF16),
            pltpu.VMEM((seqs, full, 128), BF16),
            pltpu.VMEM((seqs, full, 128), BF16),
            pltpu.VMEM((seqs, full, 256), BF16),
            pltpu.VMEM((seqs, 8, full), F32),
            pltpu.VMEM(in_ref.shape, BF16),
            pltpu.VMEM(cot_ref.shape, BF16),
            pltpu.VMEM(kv_ref.shape, BF16),
            pltpu.VMEM(ow_ref.shape, BF16),
            pltpu.VMEM(iw_ref.shape, BF16),
            pltpu.VMEM(dw_ref.shape, BF16),
        )

        def feed_forward(hid, ggu):
            def tokens(c, s):
                def run(r):
                    rows = rows_of(r, size)
                    gate_up = dot(dn[rows, :], wf[c, :, : 2 * cols])
                    grad = dot(us[rows, :], wf[c, :, 2 * cols :])
                    gate, up = gate_up[:, :cols], gate_up[:, cols:]
                    sig = 1.0 / (1.0 + jnp.exp2(gate * -LOG2E))
                    silu = gate * sig
                    hid[c, rows, :] = (silu * up).astype(BF16)
                    ggu[c, rows, :cols] = (grad * up * (sig + silu * (1.0 - sig))).astype(BF16)
                    ggu[c, rows, cols:] = (grad * silu).astype(BF16)

                loop(s * parts, (s + 1) * parts, run)

            def weigh(c, tokens, more=False):
                def run(b):
                    rows = rows_of(b, 256)
                    dims = whole.shape[2:4]
                    inner = dot_tn(dn[tokens, rows], ggu[c, tokens, :]).reshape(dims + (2 * cols,))
                    down = dot_tn(us[tokens, rows], hid[c, tokens, :]).reshape(dims + (cols,))
                    if more:
                        inner = inner + whole[c % 2, b, :, :, : 2 * cols].astype(F32)
                        down = down + whole[c % 2, b, :, :, 2 * cols :].astype(F32)
                    whole[c % 2, b, :, :, : 2 * cols] = inner.astype(BF16)
                    whole[c % 2, b, :, :, 2 * cols :] = down.astype(BF16)

                loop(0, whole.shape[1], run)

            def grad_blocks(s, between=None):
                for n, bits in enumerate((3, 1, 2, 0)):
                    if n == 2 and between is not None:
                        between()
                    rows = rows_of(s * parts + me_t.flips[bits], size)
                    left = jnp.concatenate([ggu[c, rows, :] for c in range(n_c)], axis=1)
                    right = jnp.concatenate([wf[c, :, : 2 * cols] for c in range(n_c)], axis=1)
                    total = dot_nt(left, right)
                    back_places[s][rows_of(me_t.flips[bits], size), :] = total.astype(BF16)
                    if n < 2:
                        backs[s].start(1 - n)

            def down_block(r):
                rows = rows_of(r, size)
                left = jnp.concatenate([hid[c, rows, :] for c in range(n_c)], axis=1)
                right = jnp.concatenate([wf[c, :, 2 * cols :] for c in range(n_c)], axis=1)
                total = dot_nt(left, right)
                us[rows, :] = total.astype(BF16)

            denses[0].forward()
            ups[1].start()
            ff_w[1].forward_last()
            ups[0].arrive()
            ff_w[0].arrive()
            denses[0].arrive()
            tokens(0, 0)
            ff_w[2].forward()
            weigh(0, halves[0])
            after_out(1)
            ff_w[1].arrive()
            tokens(1, 0)
            ff_w[2].forward_last()
            weigh(1, halves[0])
            ups[1].forward()
            denses[1].forward()
            ups[1].arrive()
            denses[1].arrive()
            tokens(0, 1)
            weigh(0, halves[1], True)
            near[0].start()
            ff_w[2].arrive()
            tokens(2, 0)
            grad_blocks(0)
            backs[0].middle()
            tokens(1, 1)
            weigh(1, halves[1], True)
            tokens(2, 1)
            normed[1].drain()
            keeps[1].wait()
            dgain[...] = jnp.zeros_like(dgain)
            wait(load_own)
            after_back(0)

            def next_chunk():
                near[0].middle(far[0])
                near[1].start()
                near[0].drain()

            grad_blocks(1, next_chunk)
            backs[1].middle()
            weigh(2, every_row)
            ups[0].drain()
            ups[1].drain()
            loop(0, parts, down_block)
            resids[0].forward()
            loop(parts, seqs * parts, down_block)
            far[0].middle()
            for exchange in ff_w + denses:
                exchange.drain()

        pl.run_scoped(
            feed_forward,
            pltpu.VMEM((n_c, seqs * full, cols), BF16),
            pltpu.VMEM((n_c, seqs * full, 2 * cols), BF16),
        )

    pl.run_scoped(until_backward, pltpu.VMEM((n_c, 8 * shard, wide), BF16))

    def backward(
        kp, vp, kt, ga, dq, dk, dv, gp, drow, acc, gains, mixer, raw, q, k, v, att, lse,
        wo, wq, wk, lnear, lfar, pnear, pfar, ynear, yfar,
    ):
        entered = greet(free, me_d, me_t, (1, 2, 4, 6), (1, 2))
        downs = [TokenReduce(us.at[halves[s]], ynear.at[s], yfar.at[s], send, me_t) for s in range(seqs)]
        late_near, late_far = [], []
        for n in range(2):
            half = pl.ds(n * shard // 2, shard // 2)
            refs = lnear.at[:, half], ff_sums[2].at[half]
            late_near.append(ShardNear(whole.at[0, :, :, half], refs[0], refs[1], send, me_d))
            late_far.append(ShardHalves(refs[0], lfar.at[:, half], refs[1], send, me_d))
        pieces = ((wo, slice(512, 768)), (wq, slice(0, 256)), (wk, slice(256, 512)))
        pro_near = [ShardNear(part, pnear.at[n], awg_ref.at[:, lanes], send, me_d) for n, (part, lanes) in enumerate(pieces)]
        pro_far = [
            (ShardHalves if n else ShardFar)(pnear.at[n], pfar.at[n], awg_ref.at[:, lanes], send, me_d)
            for n, (part, lanes) in enumerate(pieces)
        ]
        kept = ((k_out, k), (v_out, v), (att_out, att), (lse_out, lse), (q_out, q))
        load_s = [[here(source.at[s], target.at[s]) for source, target in kept] for s in range(seqs)]
        load_raw = [here(raw_out.at[0], raw)]
        gains[...] = jnp.zeros_like(gains)
        mixer[...] = jnp.zeros_like(mixer)

        def load_grad(s):
            resids[s].arrive()
            low_keeps[s].wait()
            here(r_out.at[s], dn.at[halves[s]]).wait()

        def prepare(s):
            loop(0, parts, lambda r: prepare_rows(
                r, size, lengths[s], dn.at[halves[s]], ws, k.at[s], v.at[s], att.at[s], ga, drow, kp, kt, vp
            ))
            dk[...] = jnp.zeros_like(dk)
            dv[...] = jnp.zeros_like(dv)

        def sweep(s, start, stop):
            loop(start, stop, lambda i: sweep_rows(i, size, q.at[s], ga, kp, kt, vp, drow, lse.at[s], acc, dq, dk, dv))

        def unproject_q(s):
            loop(0, parts, lambda r: unproject_queries(r, size, (cos_ref, sin_ref), gq_ref, raw, dq, gp.at[s], gains))

        def unproject_kv(s):
            loop(0, parts, lambda r: unproject_pairs(
                r, size, lengths[s], (cos_ref, sin_ref), gk_ref, raw, dk, dv, gp.at[s], gains
            ))

        def norm_blocks(s):
            for n, bits in enumerate((3, 1, 2, 0)):
                rows = rows_of(me_t.flips[bits], size)
                norm_places[s][rows, :] = dot_nt(gp[s, rows, :], ws[:, :512]).astype(BF16)
                if n < 2:
                    norms[s].start(1 - n)

        def weigh_out():
            def run(b):
                rows = rows_of(b, 256)
                total = sum(dot_tn(dn[halves[s], rows], att[s]) for s in range(seqs))
                wo[b] = total.astype(BF16).reshape(wo.shape[1:])

            loop(0, wo.shape[0], run)

        def weigh(target, lanes):
            def run(b):
                rows = rows_of(b, 256)
                total = sum(dot_tn(xs[s, :, rows], gp[s, :, lanes]) for s in range(seqs))
                target[b] = total.astype(BF16).reshape(target.shape[1:])
                product = total * ws[rows, lanes].astype(F32)
                high = product.astype(BF16)
                rest = (product - high.astype(F32)).astype(BF16)
                ones = jnp.ones((8, product.shape[1]), BF16)
                mixer[:, rows] += dot_nt(ones, high) + dot_nt(ones, rest)

            loop(0, target.shape[0], run)

        def after_down(s):
            downs[s].arrive()

            def step(rows):
                target = pl.ds(pl.multiple_of(s * size + rows.start, 32), 32)
                outp[target, :] = (resid[s, rows, :] + downs[s].rows(rows)).astype(BF16)

            by_rows(size, 32, step)
            return here(outp.at[pl.ds(s * size, size)], blk_out.at[s])

        def total_of(n, got, index):
            got[index] = put[n]
            for copy in steps[n]:
                copy.wait_recv()
            total = got[0]
            for place in range(1, got.shape[0]):
                total = total + got[place]
            return total

        wait(load_s[0])
        load_grad(0)
        prepare(0)
        entered()
        after_back(1)
        late_near[0].start()
        for exchange in downs:
            exchange.start()
        sweep(0, 0, 2)
        near[1].middle(far[1])
        sweep(0, 2, 3)
        downs[0].middle()
        sweep(0, 3, parts)
        wait(load_raw)
        unproject_q(0)
        unproject_kv(0)
        resids[1].forward()
        load_raw = [here(raw_out.at[1], raw)]
        late_near[0].middle(late_far[0])
        late_near[1].start()
        norm_blocks(0)
        norms[0].middle()
        far[1].middle()
        load_grad(1)
        for exchange in resids:
            exchange.drain()
        for copy in backup:
            copy.start()
        wait(load_s[1])
        prepare(1)
        far[0].finish()
        weigh_out()
        pro_near[0].start()
        late_near[1].middle(late_far[1])
        sweep(1, 0, 2)
        late_far[0].middle()
        downs[1].middle()
        sweep(1, 2, 3)
        pro_near[0].middle(pro_far[0])
        sweep(1, 3, parts)
        late_far[1].middle()
        wait(load_raw)
        unproject_kv(1)
        wait(backup)
        weigh(wk, pieces[2][1])
        pro_near[2].start()
        unproject_q(1)
        weigh(wq, pieces[1][1])
        pro_near[1].start()
        for row, vector in ((0, mixer[0:1, :] / mg_ref[...]), (8, jnp.sum(dgain[...], axis=0, keepdims=True))):
            for i in range(8):
                put[0, row + i : row + i + 1, :] = vector[:, LANES * i : LANES * (i + 1)]
        put[0, 16:, :] = gains[...]
        for copy in steps[0]:
            copy.start()
        norm_blocks(1)
        pro_near[2].middle(pro_far[2])
        norms[1].middle()
        put[1] = total_of(0, got_t, me_t.index)
        for copy in steps[1]:
            copy.start()
        after_norm(0)
        norms[0].drain()
        stays = [after_down(0)]
        pro_near[1].middle(pro_far[1])
        pro_far[2].middle()
        stays.append(after_down(1))
        far[1].finish()
        pro_far[0].finish()
        for exchange in late_far:
            exchange.finish()
        pro_far[1].middle()
        sums_ref[...] = total_of(1, got_d, me_d.index)
        after_norm(1)
        pro_far[2].finish()
        pro_far[1].finish()
        wait(stays)
        for copy in steps[0] + steps[1]:
            copy.wait_send()
        for exchange in downs + late_near + late_far + pro_near + pro_far:
            exchange.drain()

    pl.run_scoped(
        backward,
        pltpu.VMEM((4, full, LANES), BF16),
        pltpu.VMEM((4, full, LANES), BF16),
        pltpu.VMEM((4, LANES, full), BF16),
        pltpu.VMEM((full, 256), BF16),
        pltpu.VMEM((full, 256), F32),
        pltpu.VMEM((2, full, LANES), F32),
        pltpu.VMEM((2, full, LANES), F32),
        pltpu.VMEM((seqs, full, 512), BF16),
        pltpu.VMEM((8, full), F32),
        pltpu.VMEM((2, LANES, size), F32),
        pltpu.VMEM((8, LANES), F32),
        pltpu.VMEM((8, width), F32),
        pltpu.VMEM((full, 384), F32),
        pltpu.VMEM((seqs, full, 256), BF16),
        pltpu.VMEM((seqs, full, 128), BF16),
        pltpu.VMEM((seqs, full, 128), BF16),
        pltpu.VMEM((seqs, full, 256), BF16),
        pltpu.VMEM((seqs, 8, full), F32),
        pltpu.VMEM((4, 2, shard, 256), BF16),
        pltpu.VMEM((4, 2, shard, 256), BF16),
        pltpu.VMEM((4, 2, shard, 256), BF16),
        pltpu.VMEM((4, shard, wide), BF16),
        pltpu.VMEM((3, shard, wide), BF16),
        pltpu.VMEM((3, 4, shard, 256), BF16),
        pltpu.VMEM((3, 3, shard, 256), BF16),
        pltpu.VMEM((seqs, 2, size, width), BF16),
        pltpu.VMEM((seqs, size, width), BF16),
    )
    for exchange in pro_w + [out_w, near[1]] + far + norms[1:]:
        exchange.drain()


def fused_block(lengths, inputs, cotangent, weights, tabs, gains):
    size, seqs, width = inputs.shape
    full = 4 * size
    shard = weights[0].shape[0]
    cols = 768
    n_c = 3
    wide = 3 * weights[3].shape[2] // n_c
    dp = 8
    return pl.pallas_call(
        block_kernel,
        out_shape=(
            shape((seqs, full, width), BF16),
            shape((seqs, full, 384), F32),
            shape((seqs, full, 256), BF16),
            shape((seqs, full, 128), BF16),
            shape((seqs, full, 128), BF16),
            shape((seqs, full, 256), BF16),
            shape((seqs, 8, full), F32),
            shape((seqs, full, width), BF16),
            shape((seqs, size, width), BF16),
            shape((size, seqs * width), F32),
            shape((shard, cols), F32),
            shape((shard, n_c * wide), F32),
            shape((24, LANES), F32),
        ),
        in_specs=[SMEM] + [ANY] * 7 + [VMEM] * 6,
        out_specs=(ANY,) * 9 + (VMEM,) * 4,
        scratch_shapes=[
            pltpu.VMEM((size, seqs * width), BF16),
            pltpu.VMEM((1, LANES), F32),
            pltpu.VMEM((1, LANES), F32),
            pltpu.VMEM((seqs, full, width), BF16),
            pltpu.VMEM((dp * shard, cols), BF16),
            pltpu.VMEM((seqs * full, width), BF16),
            pltpu.VMEM((seqs * full, width), BF16),
            pltpu.VMEM((full, width), BF16),
            pltpu.VMEM((seqs, 2, size, width), BF16),
            pltpu.VMEM((seqs, size, width), BF16),
            pltpu.VMEM((seqs, size, width), F32),
            pltpu.VMEM((2, 4, shard, wide), BF16),
            pltpu.VMEM((2, 3, shard, wide), BF16),
            pltpu.VMEM((2, 4, 2, shard, wide), BF16),
            pltpu.VMEM((8, width), F32),
            pltpu.VMEM((2, 24, LANES), F32),
            pltpu.VMEM((4, 24, LANES), F32),
            pltpu.VMEM((8, 24, LANES), F32),
            pltpu.SemaphoreType.REGULAR,
        ]
        + COPY_SEMS,
        compiler_params=pltpu.CompilerParams(
            vmem_limit_bytes=BLOCK_LIMIT, collective_id=0, has_side_effects=True
        ),
        cost_estimate=pl.CostEstimate(flops=90_000_000_000, bytes_accessed=60_000_000, transcendentals=14_000_000),
        name="block",
    )(lengths, inputs, cotangent, *weights, *tabs, *gains)


def finish_kernel(
    lengths, ig_ref, blk_ref, awg_ref, ffg_ref,
    block_out, input_out, query_out, pair_out, output_out, inner_out, down_out,
):
    size, seqs, width = input_out.shape
    hidden = down_out.shape[0]
    cols = hidden // 3
    start = lax.axis_index("tensor") * size

    def step(rows):
        place = start + rows.start + iota((32, width), 0)
        parts = []
        for s in range(seqs):
            lanes = slice(width * s, width * (s + 1))
            input_out[rows, s, :] = ig_ref[rows, lanes]
            parts.append(jnp.where(place < lengths[s], blk_ref[s, rows, :].astype(F32), 0.0))
        block_out[rows, :, :] = jnp.stack(parts, axis=1).astype(BF16)

    by_rows(size, 32, step)
    query_out[...] = awg_ref[:, :256]
    for n in range(2):
        pair_out[:, n, :] = awg_ref[:, 256 + 128 * n : 384 + 128 * n]
    output_out[...] = awg_ref[:, 512:].T
    for c in range(3):
        base = 3 * cols * c
        for n in range(2):
            inner_out[:, n, cols * c : cols * (c + 1)] = ffg_ref[:, base + cols * n : base + cols * (n + 1)]
        down_out[cols * c : cols * (c + 1), :] = ffg_ref[:, base + 2 * cols : base + 3 * cols].T


def fused_finish(lengths, ig, blk, awg, ffg):
    seqs, size, width = blk.shape
    shard, wide = ffg.shape
    hidden = wide // 3
    return pl.pallas_call(
        finish_kernel,
        out_shape=(
            shape((size, seqs, width), BF16),
            shape((size, seqs, width), F32),
            shape((shard, 256), F32),
            shape((shard, 2, 128), F32),
            shape((256, shard), F32),
            shape((shard, 2, hidden), F32),
            shape((hidden, shard), F32),
        ),
        in_specs=[SMEM] + [VMEM] * 4,
        out_specs=(VMEM,) * 7,
        compiler_params=pltpu.CompilerParams(vmem_limit_bytes=VMEM_LIMIT),
        name="finish",
    )(lengths, ig, blk, awg, ffg)


def swap(values, axis, bits):
    return lax.ppermute(values, axis, [(i, i ^ bits) for i in range(lax.axis_size(axis))])


def gather_tokens(block):
    far = swap(block, "tensor", 2)
    return [block, swap(block, "tensor", 1), far, swap(far, "tensor", 1)]


def scatter_tokens(keep, send):
    near = swap(send, "tensor", 1)
    middle = (keep[1].astype(F32) + near[1].astype(F32)).astype(BF16)
    far = swap(middle, "tensor", 2)
    return keep[0].astype(F32) + near[0].astype(F32) + far.astype(F32)


def gather_shards(shard):
    if lax.axis_size("dp") != 8 or shard.shape[0] % LANES:
        return [lax.all_gather(shard, "dp", axis=0, tiled=True)]
    slots = [shard, swap(shard, "dp", 1)]
    for bits in (2, 4, 6):
        there = swap(shard, "dp", bits)
        slots += [there, swap(there, "dp", 1)]
    return slots


def scatter_shards(grads):
    if len(grads) == 1:
        return lax.psum_scatter(grads[0].astype(F32), "dp", scatter_dimension=0, tiled=True)
    keep, send = grads
    near = swap(send, "dp", 1)
    both = keep.astype(F32) + near.astype(F32)
    total = both[0]
    for slot in (1, 2, 3):
        total = total + swap(both[slot].astype(BF16), "dp", 2 * slot).astype(F32)
    return total


def sum_everywhere(values):
    for axis in ("tensor", "dp"):
        bits = 1
        while bits < lax.axis_size(axis):
            values = values + swap(values, axis, bits)
            bits *= 2
    return values


def norm_rows(values, gain):
    factor = lax.rsqrt(jnp.mean(values * values, axis=-1, keepdims=True) + EPS)
    return (values * factor * gain, factor)


def norm_back(values, factor, gain, upstream):
    weighted = upstream * gain
    inner = jnp.mean(values * weighted, axis=-1, keepdims=True)
    return factor * weighted - values * factor * factor * factor * inner


def tables(full, head_width):
    half = head_width // 2
    freqs = THETA ** (-jnp.arange(half, dtype=F32) * 2.0 / head_width)
    angles = jnp.arange(full, dtype=F32)[:, None] * freqs[None, :]
    cosines, sines = jnp.cos(angles), jnp.sin(angles)
    return (jnp.tile(cosines, (1, 4)), jnp.tile(jnp.concatenate([-sines, sines], axis=1), (1, 2)))


def local_plain(
    inputs,
    lengths,
    query_weight,
    key_value_weight,
    output_weight,
    inner_weight,
    down_weight,
    mixer_gain,
    query_gain,
    key_gain,
    dense_gain,
    cotangent,
):
    size, seqs, width = inputs.shape
    parts = lax.axis_size("tensor")
    full = size * parts
    head = query_gain.shape[0]
    query_cols = query_weight.shape[1]
    pair_cols = key_value_weight.shape[2]
    hidden = inner_weight.shape[2]
    shard = query_weight.shape[0]
    me_t, me_d = lax.axis_index("tensor"), lax.axis_index("dp")
    n_c = 3
    cols = hidden // n_c
    cosines, sines = tables(full, head)
    gq = jnp.tile(query_gain, 2)[None, :]
    gk = jnp.tile(key_gain, 2)[None, :]

    down_turned = down_weight.T
    attn_shard = jnp.concatenate(
        [query_weight, key_value_weight.reshape(shard, 2 * pair_cols), output_weight.T], axis=1
    )
    attn_w = gather_shards(attn_shard)
    positions = me_t * size + jnp.arange(size, dtype=jnp.int32)
    scals = [
        jnp.stack([me_t.astype(jnp.int32), me_d.astype(jnp.int32), lengths[s], jnp.int32(0)])
        for s in range(seqs)
    ]
    tokens = [inputs[:, s].astype(F32) for s in range(seqs)]
    valid = [(positions < lengths[s])[:, None] for s in range(seqs)]
    firsts = [norm_rows(tokens[s], mixer_gain) for s in range(seqs)]
    normed = [gather_tokens(firsts[s][0].astype(BF16)) for s in range(seqs)]
    ff_w = []
    for c in range(n_c):
        part = slice(c * cols, (c + 1) * cols)
        ff_w.append(
            gather_shards(
                jnp.concatenate(
                    [inner_weight[:, 0, part], inner_weight[:, 1, part], down_turned[:, part]], axis=1
                )
            )
        )
    upstream = [jnp.where(valid[s], cotangent[:, s].astype(F32), 0.0) for s in range(seqs)]
    up_parts = [gather_tokens(upstream[s].astype(BF16)) for s in range(seqs)]

    saved, residual, seconds, dense = [], [], [], []
    for s in range(seqs):
        outs = attn_fwd(scals[s], cosines, sines, gq, gk, normed[s], attn_w)
        saved.append(outs[:6])
        residual.append(tokens[s] + scatter_tokens(outs[6], outs[7]))
        dense_in, factor = norm_rows(residual[s], dense_gain)
        seconds.append(factor)
        dense.append(gather_tokens(dense_in.astype(BF16)))

    x_parts = [part for s in range(seqs) for part in dense[s]]
    u_parts = [part for s in range(seqs) for part in up_parts[s]]
    hids, ggus, ff_grads = [], [], []
    for c in range(n_c):
        hid, ggu, grads = feed_forward(scals[0], x_parts, u_parts, ff_w[c])
        hids.append(hid)
        ggus.append(ggu)
        ff_grads.append(scatter_shards(grads))

    block_out, input_gradient, attn_grads = [], [], []
    mixer_part = dense_part = gain_part = 0.0
    for s in range(seqs):
        ykeep, ysend, gkeep, gsend = ff_out(s, scals[s], parts, size, hids, ggus, ff_w)
        grad_dense = scatter_tokens(gkeep, gsend)
        dense_part = dense_part + jnp.sum(grad_dense * residual[s] * seconds[s], axis=0)
        grad_residual = upstream[s] + norm_back(residual[s], seconds[s], dense_gain, grad_dense)
        r_parts = gather_tokens(grad_residual.astype(BF16))
        nkeep, nsend, gains, grads = attn_bwd(
            scals[s], cosines, sines, gq, gk, saved[s], normed[s], r_parts, attn_w
        )
        attn_grads.append(grads)
        gain_part = gain_part + gains
        grad_normed = scatter_tokens(nkeep, nsend)
        factor = firsts[s][1]
        mixer_part = mixer_part + jnp.sum(grad_normed * tokens[s] * factor, axis=0)
        input_gradient.append(grad_residual + norm_back(tokens[s], factor, mixer_gain, grad_normed))
        out_sum = scatter_tokens(ykeep, ysend)
        block_out.append(jnp.where(valid[s], residual[s] + out_sum, 0.0).astype(BF16))

    summed = [
        sum(part.astype(F32) for part in parts_of).astype(BF16) for parts_of in zip(*attn_grads)
    ]
    attn_grad = scatter_shards(summed)
    early = sum_everywhere(jnp.concatenate([dense_part.reshape(-1, LANES), gain_part], axis=0))
    mixer = sum_everywhere(mixer_part.reshape(-1, LANES)).reshape(-1)
    dense_rows = width // LANES
    folded = early[dense_rows:, :head] + early[dense_rows:, head:]
    inner_gradient = jnp.stack(
        [
            jnp.concatenate([grad[:, p * cols : (p + 1) * cols] for grad in ff_grads], axis=1)
            for p in range(2)
        ],
        axis=1,
    )
    down_gradient = jnp.concatenate([grad[:, 2 * cols :] for grad in ff_grads], axis=1).T
    return (
        jnp.stack(block_out, axis=1),
        jnp.stack(input_gradient, axis=1),
        attn_grad[:, :query_cols],
        attn_grad[:, query_cols : query_cols + 2 * pair_cols].reshape(shard, 2, pair_cols),
        attn_grad[:, query_cols + 2 * pair_cols :].T,
        inner_gradient,
        down_gradient,
        mixer,
        folded[0],
        folded[1],
        early[:dense_rows].reshape(-1),
    )


def local(*args):
    inputs, shard = args[0], args[2].shape[0]
    if lax.axis_size("dp") == 8 and lax.axis_size("tensor") == 4 and shard % LANES == 0 and inputs.shape[1] == 2:
        return local_fused(*args)
    return local_plain(*args)


def rope_tables(full, head):
    half = head // 2
    freqs = np.float32(THETA) ** (-np.arange(half, dtype=np.float32) * np.float32(2.0) / np.float32(head))
    angles = np.arange(full, dtype=np.float32)[:, None] * freqs[None, :].astype(np.float32)
    cosines, sines = np.cos(angles), np.sin(angles)
    return (
        jnp.asarray(np.tile(cosines, (1, 4)), F32),
        jnp.asarray(np.tile(np.concatenate([-sines, sines], axis=1), (1, 2)), F32),
    )


def local_fused(
    inputs,
    lengths,
    query_weight,
    key_value_weight,
    output_weight,
    inner_weight,
    down_weight,
    mixer_gain,
    query_gain,
    key_gain,
    dense_gain,
    cotangent,
):
    size, seqs, width = inputs.shape
    parts = lax.axis_size("tensor")
    full = size * parts
    head = query_gain.shape[0]
    tabs = rope_tables(full, head)
    weights = (query_weight, key_value_weight, output_weight, inner_weight, down_weight)
    gains = (query_gain[None, :], key_gain[None, :], mixer_gain[None, :], dense_gain[None, :])
    *_, blk, input_gradient, attn_grad, ff_grad, sums = fused_block(
        lengths, inputs, cotangent, weights, tabs, gains
    )
    finished = fused_finish(lengths, input_gradient, blk, attn_grad, ff_grad)
    folded = sums[16:, :head] + sums[16:, head:]
    return tuple(finished) + (
        sums[:8].reshape(-1),
        folded[0],
        folded[1],
        sums[8:16].reshape(-1),
    )


def solution(mesh):
    return jax.shard_map(
        local,
        mesh=mesh,
        in_specs=(
            P("tensor", "dp", None),
            P("dp"),
            P("dp", "tensor"),
            P("dp", None, "tensor"),
            P("tensor", "dp"),
            P("dp", None, "tensor"),
            P("tensor", "dp"),
            P(),
            P(),
            P(),
            P(),
            P("tensor", "dp", None),
        ),
        out_specs=(
            P("tensor", "dp", None),
            P("tensor", "dp", None),
            P("dp", "tensor"),
            P("dp", None, "tensor"),
            P("tensor", "dp"),
            P("dp", None, "tensor"),
            P("tensor", "dp"),
            P(),
            P(),
            P(),
            P(),
        ),
        check_vma=False,
    )
```

```python
import functools

import jax
import jax.numpy as jnp
import numpy as np
from jax import lax
from jax.experimental import pallas as pl
from jax.experimental.pallas import tpu as pltpu
from jax.sharding import PartitionSpec as P

EPS = 1e-05
THETA = 1000000.0
LOG2E = 1.4426950408889634
F32 = jnp.float32
BF16 = jnp.bfloat16
HIGH = lax.Precision.HIGHEST
LANES = 128
VMEM_LIMIT = 56 * 1024 * 1024
BLOCK_LIMIT = 62 * 1024 * 1024
ANY = pl.BlockSpec(memory_space=pl.ANY)
VMEM = pl.BlockSpec(memory_space=pltpu.VMEM)
SMEM = pl.BlockSpec(memory_space=pltpu.SMEM)


def dot(a, b, **kw):
    return lax.dot_general(
        a, b, (((1,), (0,)), ((), ())), preferred_element_type=F32, **kw
    )


def dot_nt(a, b, **kw):
    return lax.dot_general(
        a, b, (((1,), (1,)), ((), ())), preferred_element_type=F32, **kw
    )


def dot_tn(a, b, **kw):
    return lax.dot_general(
        a, b, (((0,), (0,)), ((), ())), preferred_element_type=F32, **kw
    )


def iota(shape, axis):
    return lax.broadcasted_iota(jnp.int32, shape, axis)


def low_half(shape):
    return iota(shape, 1) % LANES < LANES // 2


def head_blocks(scale):
    shape = (LANES, LANES)
    return jnp.where(iota(shape, 0) // 64 == iota(shape, 1) // 64, scale, 0.0).astype(F32)


def head_rows(scale):
    return jnp.where(iota((8, 256), 0) == iota((8, 256), 1) // 64, scale, 0.0).astype(F32)


def partner(values):
    first = iota(values.shape, 1) % 64 < 32
    return jnp.where(first, pltpu.roll(values, LANES - 32, 1), pltpu.roll(values, 32, 1))


def rows_of(index, size):
    if isinstance(index, int):
        return pl.ds(index * size, size)
    return pl.ds(pl.multiple_of(index * size, size), size)


def load_all(sources, targets, sems, first):
    copies = []
    for number, (source, target) in enumerate(zip(sources, targets)):
        copy = pltpu.make_async_copy(source, target, sems.at[first + number])
        copy.start()
        copies.append(copy)
    return copies


def shard_targets(w_refs, ws, me):
    size = w_refs[0].shape[0]
    if len(w_refs) == 1:
        return [ws]
    return [ws.at[rows_of(me ^ slot, size)] for slot in range(len(w_refs))]


def store_slots(whole, out_refs, me):
    if len(out_refs) == 1:
        out_refs[0][...] = whole[...]
        return
    keep_ref, send_ref = out_refs
    size = keep_ref.shape[1]
    for slot in range(2 * keep_ref.shape[0]):
        (send_ref if slot % 2 else keep_ref)[slot // 2] = whole[rows_of(me ^ slot, size), :]


def padded_heads(first, second, low, g, e):
    here = low if e == 0 else jnp.logical_not(low)
    return jnp.where(here, first if g == e else second, 0.0).astype(BF16)


def project_rows(r, size, length, xs, ws, tabs, gains, raw_ref, q_ref, k_ref, v_ref, kp, vp):
    rows = rows_of(r, size)
    cos_ref, sin_ref = tabs
    gq_ref, gk_ref = gains
    mean_of = head_blocks(1.0 / 64)
    low = low_half((size, LANES))
    projected = dot(xs[rows, :], ws[:, :512])
    raw_ref[rows, :] = projected[:, :384]
    cosines, sines = cos_ref[rows, :], sin_ref[rows, :]

    def turned(values, gain):
        mean = dot(values * values, mean_of, precision=HIGH)
        normed = values * lax.rsqrt(mean + EPS) * gain
        return normed * cosines + partner(normed) * sines

    for g in range(2):
        lanes = slice(LANES * g, LANES * (g + 1))
        q_ref[rows, lanes] = turned(projected[:, lanes], gq_ref[...]).astype(BF16)
    keys = turned(projected[:, 256:384], gk_ref[...])
    values = projected[:, 384:512]
    k_ref[rows, :] = keys.astype(BF16)
    v_ref[rows, :] = values.astype(BF16)
    live = r * size + iota((size, LANES), 0) < length
    ones = jnp.where(live, 1.0, 0.0)
    values = jnp.where(live, values, 0.0)
    keys_swap, values_swap = pltpu.roll(keys, 64, 1), pltpu.roll(values, 64, 1)
    for g in range(2):
        for e in range(2):
            kp[2 * g + e, rows, :] = padded_heads(keys, keys_swap, low, g, e)
            vp[2 * g + e, rows, :LANES] = padded_heads(values, values_swap, low, g, e)
            vp[2 * g + e, rows, LANES:] = padded_heads(ones, ones, low, g, e)


def attend_rows(i, size, q_ref, kp, vp, acc, att_ref, lse_ref):
    rows = rows_of(i, size)
    factor = LOG2E / 8.0
    causal = iota((size, size), 1) <= iota((size, size), 0)
    queries = [q_ref[rows, LANES * g : LANES * (g + 1)] for g in range(2)]

    def block(kb, masked):
        cols = rows_of(kb, size)
        sums = []
        for g in range(2):
            total = None
            for e in range(2):
                weights = jnp.exp2(dot_nt(queries[g], kp[2 * g + e, cols, :]) * factor)
                if masked:
                    weights = jnp.where(causal, weights, 0.0)
                part = dot(weights.astype(BF16), vp[2 * g + e, cols, :])
                total = part if total is None else total + part
            sums.append(total)
        return sums

    totals = block(i, True)
    if isinstance(i, int):
        for kb in range(i):
            totals = [total + part for total, part in zip(totals, block(kb, False))]
    else:
        for g, total in enumerate(totals):
            acc[g] = total

        def more(kb, carry):
            for g, total in enumerate(block(kb, False)):
                acc[g] += total
            return carry

        lax.fori_loop(i - i, i, more, None)
        totals = [acc[g] for g in range(2)]
    logs = []
    for g in range(2):
        lanes = slice(LANES * g, LANES * (g + 1))
        summed = totals[g][:, LANES:]
        att_ref[rows, lanes] = (totals[g][:, :LANES] / summed).astype(BF16)
        logs.append(jnp.log2(summed))
    lse_ref[:, rows] = dot_nt(head_rows(1.0 / 64), jnp.concatenate(logs, axis=1), precision=HIGH)


def attn_fwd_kernel(parts, n_w, scal, cos_ref, sin_ref, gq_ref, gk_ref, *refs):
    x_refs, refs = refs[:parts], refs[parts:]
    w_refs, refs = refs[:n_w], refs[n_w:]
    (raw_ref, q_ref, k_ref, v_ref, att_ref, lse_ref, keep_ref, send_ref, xs, ws, kp, vp, acc, sems) = refs
    size = x_refs[0].shape[0]
    me_t, me_d, length = scal[0], scal[1], scal[2]
    copies = load_all(w_refs, shard_targets(w_refs, ws, me_d), sems, 0)
    copies += load_all(x_refs, [xs.at[rows_of(me_t ^ j, size)] for j in range(parts)], sems, n_w)
    for copy in copies:
        copy.wait()

    def project(r, carry):
        project_rows(
            r, size, length, xs, ws, (cos_ref, sin_ref), (gq_ref, gk_ref), raw_ref, q_ref, k_ref, v_ref, kp, vp
        )
        return carry

    def attend(i, carry):
        attend_rows(i, size, q_ref, kp, vp, acc, att_ref, lse_ref)
        return carry

    lax.fori_loop(0, parts, project, 0)
    lax.fori_loop(0, parts, attend, 0)
    for j in range(parts):
        out = dot_nt(att_ref[rows_of(me_t ^ j, size), :], ws[:, 512:])
        (send_ref if j % 2 else keep_ref)[j // 2] = out.astype(BF16)


def attn_fwd(scal, cosines, sines, gq, gk, x_parts, w_parts):
    parts, n_w = len(x_parts), len(w_parts)
    size, width = x_parts[0].shape
    full = parts * size
    cols = w_parts[0].shape[1]
    pair = jax.ShapeDtypeStruct((parts // 2, size, width), BF16)
    return pl.pallas_call(
        functools.partial(attn_fwd_kernel, parts, n_w),
        out_shape=(
            jax.ShapeDtypeStruct((full, 384), F32),
            jax.ShapeDtypeStruct((full, 256), BF16),
            jax.ShapeDtypeStruct((full, 128), BF16),
            jax.ShapeDtypeStruct((full, 128), BF16),
            jax.ShapeDtypeStruct((full, 256), BF16),
            jax.ShapeDtypeStruct((8, full), F32),
            pair,
            pair,
        ),
        in_specs=[SMEM] + [VMEM] * 4 + [ANY] * (parts + n_w),
        out_specs=(VMEM,) * 8,
        scratch_shapes=[
            pltpu.VMEM((full, width), BF16),
            pltpu.VMEM((width, cols), BF16),
            pltpu.VMEM((4, full, LANES), BF16),
            pltpu.VMEM((4, full, 2 * LANES), BF16),
            pltpu.VMEM((2, size, 2 * LANES), F32),
            pltpu.SemaphoreType.DMA((n_w + parts,)),
        ],
        compiler_params=pltpu.CompilerParams(vmem_limit_bytes=VMEM_LIMIT),
        cost_estimate=pl.CostEstimate(flops=8_000_000_000, bytes_accessed=12_000_000, transcendentals=3_000_000),
        name="attention_forward",
    )(scal, cosines, sines, gq, gk, *x_parts, *w_parts)


def prepare_rows(r, size, length, gs, ws, k_ref, v_ref, att_ref, ga, drow, kp, kt, vp):
    rows = rows_of(r, size)
    low = low_half((size, LANES))
    grad = dot(gs[rows, :], ws[:, 512:]).astype(BF16)
    ga[rows, :] = grad
    drow[:, rows] = dot_nt(head_rows(1.0), grad.astype(F32) * att_ref[rows, :].astype(F32), precision=HIGH)
    live = r * size + iota((size, LANES), 0) < length
    keys = jnp.where(live, k_ref[rows, :].astype(F32), 0.0)
    values = jnp.where(live, v_ref[rows, :].astype(F32), 0.0)
    keys_swap, values_swap = pltpu.roll(keys, 64, 1), pltpu.roll(values, 64, 1)
    for g in range(2):
        for e in range(2):
            here = low if e == 0 else jnp.logical_not(low)
            padded = jnp.where(here, keys if g == e else keys_swap, 0.0)
            kp[2 * g + e, rows, :] = padded.astype(BF16)
            kt[2 * g + e, :, rows] = padded.T.astype(BF16)
            vp[2 * g + e, rows, :] = padded_heads(values, values_swap, low, g, e)


def sweep_rows(i, size, q_ref, ga, kp, kt, vp, drow, lrow, acc, dq, dk, dv):
    rows = rows_of(i, size)
    factor = LOG2E / 8.0
    causal = iota((size, size), 0) <= iota((size, size), 1)
    low2 = iota((2 * size, LANES), 0) // size == iota((2 * size, LANES), 1) // 64
    queries, grads, queries2, grads2 = [], [], [], []
    for g in range(2):
        lanes = slice(LANES * g, LANES * (g + 1))
        queries.append(q_ref[rows, lanes])
        grads.append(ga[rows, lanes])
        for source, target in ((queries, queries2), (grads, grads2)):
            both = jnp.concatenate([source[g], source[g]], axis=0)
            target.append(jnp.where(low2, both, jnp.zeros_like(both)))

    def block(kb, masked):
        cols = rows_of(kb, size)
        parts_t = []
        for g in range(2):
            weights2, scores2, turned = [], [], None
            for e in range(2):
                h = 2 * g + e
                weights = jnp.exp2(dot_nt(kp[h, cols, :], queries[g]) * factor - lrow[h : h + 1, rows])
                if masked:
                    weights = jnp.where(causal, weights, 0.0)
                grad_weights = dot_nt(vp[h, cols, :], grads[g])
                grad_scores = (weights * (grad_weights - drow[h : h + 1, rows])).astype(BF16)
                weights2.append(weights.astype(BF16))
                scores2.append(grad_scores)
                part = dot(kt[h, :, cols], grad_scores)
                turned = part if turned is None else turned + part
            dv[g, cols, :] += dot(jnp.concatenate(weights2, axis=1), grads2[g])
            dk[g, cols, :] += dot(jnp.concatenate(scores2, axis=1), queries2[g])
            parts_t.append(turned)
        return parts_t

    if isinstance(i, int):
        totals = block(i, True)
        for kb in range(i):
            totals = [total + part for total, part in zip(totals, block(kb, False))]
        for g in range(2):
            dq[rows, LANES * g : LANES * (g + 1)] = totals[g].T
        return
    for g, total in enumerate(block(i, True)):
        acc[g] = total

    def more(kb, carry):
        for g, total in enumerate(block(kb, False)):
            acc[g] += total
        return carry

    lax.fori_loop(i - i, i, more, None)
    for g in range(2):
        dq[rows, LANES * g : LANES * (g + 1)] = acc[g].T


def unproject_head(rows, grad, tabs, gain_ref, raw_ref, lanes, gp, gains_ref, row):
    cosines, sines = tabs[0][rows, :], tabs[1][rows, :]
    mean_of = head_blocks(1.0 / 64)
    raw = raw_ref[rows, lanes]
    rms = lax.rsqrt(dot(raw * raw, mean_of, precision=HIGH) + EPS)
    turned = grad * cosines - partner(grad) * sines
    gains_ref[row : row + 1, :] += jnp.sum(turned * raw * rms, axis=0, keepdims=True)
    weighted = turned * gain_ref[...]
    inner = dot(raw * weighted, mean_of, precision=HIGH)
    gp[rows, lanes] = (rms * weighted - raw * (rms * rms * rms) * inner).astype(BF16)


def unproject_queries(r, size, tabs, gain_ref, raw_ref, dq, gp, gains_ref):
    rows = rows_of(r, size)
    for g in range(2):
        lanes = slice(LANES * g, LANES * (g + 1))
        unproject_head(rows, dq[rows, lanes] * 0.125, tabs, gain_ref, raw_ref, lanes, gp, gains_ref, 0)


def unproject_pairs(r, size, length, tabs, gain_ref, raw_ref, dk, dv, gp, gains_ref):
    rows = rows_of(r, size)
    low = low_half((size, LANES))
    live = r * size + iota((size, LANES), 0) < length

    def folded(ref):
        first, second = ref[0, rows, :], ref[1, rows, :]
        both = jnp.where(low, first + pltpu.roll(first, 64, 1), second + pltpu.roll(second, 64, 1))
        return jnp.where(live, both, 0.0)

    unproject_head(rows, folded(dk) * 0.125, tabs, gain_ref, raw_ref, slice(256, 384), gp, gains_ref, 1)
    gp[rows, 384:512] = folded(dv).astype(BF16)


def attn_bwd_kernel(parts, n_w, scal, cos_ref, sin_ref, gq_ref, gk_ref, raw_ref, q_ref, k_ref, v_ref, att_ref, lse_ref, *refs):
    x_refs, refs = refs[:parts], refs[parts:]
    r_refs, refs = refs[:parts], refs[parts:]
    w_refs, refs = refs[:n_w], refs[n_w:]
    n_g = 1 if n_w == 1 else 2
    keep_ref, send_ref, gains_ref = refs[:3]
    g_refs, refs = refs[3 : 3 + n_g], refs[3 + n_g :]
    xs, gs, ws, kp, vp, kt, ga, dq, dk, dv, gp, whole, drow, acc, sems = refs
    size = x_refs[0].shape[0]
    me_t, me_d, length = scal[0], scal[1], scal[2]
    copies = load_all(w_refs, shard_targets(w_refs, ws, me_d), sems, 0)
    copies += load_all(r_refs, [gs.at[rows_of(me_t ^ j, size)] for j in range(parts)], sems, n_w)
    copies += load_all(x_refs, [xs.at[rows_of(me_t ^ j, size)] for j in range(parts)], sems, n_w + parts)
    for copy in copies:
        copy.wait()

    def prepare(r, carry):
        prepare_rows(r, size, length, gs, ws, k_ref, v_ref, att_ref, ga, drow, kp, kt, vp)
        return carry

    def sweep(i, carry):
        sweep_rows(i, size, q_ref, ga, kp, kt, vp, drow, lse_ref, acc, dq, dk, dv)
        return carry

    def unproject(r, carry):
        unproject_queries(r, size, (cos_ref, sin_ref), gq_ref, raw_ref, dq, gp, gains_ref)
        unproject_pairs(r, size, length, (cos_ref, sin_ref), gk_ref, raw_ref, dk, dv, gp, gains_ref)
        return carry

    lax.fori_loop(0, parts, prepare, 0)
    dk[...] = jnp.zeros_like(dk)
    dv[...] = jnp.zeros_like(dv)
    lax.fori_loop(0, parts, sweep, 0)
    gains_ref[...] = jnp.zeros_like(gains_ref)
    lax.fori_loop(0, parts, unproject, 0)
    for j in range(parts):
        out = dot_nt(gp[rows_of(me_t ^ j, size), :], ws[:, :512])
        (send_ref if j % 2 else keep_ref)[j // 2] = out.astype(BF16)

    def weigh(b, carry):
        rows = rows_of(b, 256)
        whole[rows, :512] = dot_tn(xs[:, rows], gp[...]).astype(BF16)
        whole[rows, 512:] = dot_tn(gs[:, rows], att_ref[...]).astype(BF16)
        return carry

    lax.fori_loop(0, whole.shape[0] // 256, weigh, 0)
    store_slots(whole, g_refs, me_d)


def slot_shapes(n_w, width, cols):
    if n_w == 1:
        return (jax.ShapeDtypeStruct((width, cols), BF16),)
    return (jax.ShapeDtypeStruct((n_w // 2, width // n_w, cols), BF16),) * 2


def attn_bwd(scal, cosines, sines, gq, gk, saved, x_parts, r_parts, w_parts):
    parts, n_w = len(x_parts), len(w_parts)
    size, width = x_parts[0].shape
    full = parts * size
    cols = w_parts[0].shape[1]
    pair = jax.ShapeDtypeStruct((parts // 2, size, width), BF16)
    g_shapes = slot_shapes(n_w, width, cols)
    outs = pl.pallas_call(
        functools.partial(attn_bwd_kernel, parts, n_w),
        out_shape=(pair, pair, jax.ShapeDtypeStruct((8, LANES), F32)) + g_shapes,
        in_specs=[SMEM] + [VMEM] * 10 + [ANY] * (2 * parts + n_w),
        out_specs=(VMEM,) * (3 + len(g_shapes)),
        scratch_shapes=[
            pltpu.VMEM((full, width), BF16),
            pltpu.VMEM((full, width), BF16),
            pltpu.VMEM((width, cols), BF16),
            pltpu.VMEM((4, full, LANES), BF16),
            pltpu.VMEM((4, full, LANES), BF16),
            pltpu.VMEM((4, LANES, full), BF16),
            pltpu.VMEM((full, 256), BF16),
            pltpu.VMEM((full, 256), F32),
            pltpu.VMEM((2, full, LANES), F32),
            pltpu.VMEM((2, full, LANES), F32),
            pltpu.VMEM((full, 512), BF16),
            pltpu.VMEM((width, cols), BF16),
            pltpu.VMEM((8, full), F32),
            pltpu.VMEM((2, LANES, size), F32),
            pltpu.SemaphoreType.DMA((n_w + 2 * parts,)),
        ],
        compiler_params=pltpu.CompilerParams(vmem_limit_bytes=VMEM_LIMIT),
        cost_estimate=pl.CostEstimate(flops=14_000_000_000, bytes_accessed=15_000_000, transcendentals=3_000_000),
        name="attention_backward",
    )(scal, cosines, sines, gq, gk, *saved, *x_parts, *r_parts, *w_parts)
    return outs[0], outs[1], outs[2], outs[3:]


def ff_kernel(n_x, n_w, scal, *refs):
    x_refs, refs = refs[:n_x], refs[n_x:]
    u_refs, refs = refs[:n_x], refs[n_x:]
    w_refs, refs = refs[:n_w], refs[n_w:]
    n_g = 1 if n_w == 1 else 2
    hid_ref, ggu_ref = refs[:2]
    g_refs, refs = refs[2 : 2 + n_g], refs[2 + n_g :]
    xs, us, ws, whole, sems = refs
    size = x_refs[0].shape[0]
    me_d = scal[1]
    cols = ws.shape[1] // 3
    copies = load_all(w_refs, shard_targets(w_refs, ws, me_d), sems, 0)
    x_copies = load_all(x_refs, [xs.at[pl.ds(j * size, size)] for j in range(n_x)], sems, n_w)
    u_copies = load_all(u_refs, [us.at[pl.ds(j * size, size)] for j in range(n_x)], sems, n_w + n_x)
    for copy in copies + x_copies + u_copies:
        copy.wait()

    def tokens(r, carry):
        rows = rows_of(r, size)
        gate_up = dot(xs[rows, :], ws[:, : 2 * cols])
        grad = dot(us[rows, :], ws[:, 2 * cols :])
        gate, up = gate_up[:, :cols], gate_up[:, cols:]
        sig = 1.0 / (1.0 + jnp.exp2(gate * -LOG2E))
        silu = gate * sig
        hid_ref[rows, :] = (silu * up).astype(BF16)
        ggu_ref[rows, :cols] = (grad * up * (sig + silu * (1.0 - sig))).astype(BF16)
        ggu_ref[rows, cols:] = (grad * silu).astype(BF16)
        return carry

    lax.fori_loop(0, n_x, tokens, 0)

    def weigh(b, carry):
        rows = rows_of(b, 256)
        whole[rows, : 2 * cols] = dot_tn(xs[:, rows], ggu_ref[...]).astype(BF16)
        whole[rows, 2 * cols :] = dot_tn(us[:, rows], hid_ref[...]).astype(BF16)
        return carry

    lax.fori_loop(0, whole.shape[0] // 256, weigh, 0)
    store_slots(whole, g_refs, me_d)


def feed_forward(scal, x_parts, u_parts, w_parts):
    n_x, n_w = len(x_parts), len(w_parts)
    size, width = x_parts[0].shape
    full = n_x * size
    wide = w_parts[0].shape[1]
    cols = wide // 3
    g_shapes = slot_shapes(n_w, width, wide)
    outs = pl.pallas_call(
        functools.partial(ff_kernel, n_x, n_w),
        out_shape=(
            jax.ShapeDtypeStruct((full, cols), BF16),
            jax.ShapeDtypeStruct((full, 2 * cols), BF16),
        )
        + g_shapes,
        in_specs=[SMEM] + [ANY] * (2 * n_x + n_w),
        out_specs=(VMEM,) * (2 + len(g_shapes)),
        scratch_shapes=[
            pltpu.VMEM((full, width), BF16),
            pltpu.VMEM((full, width), BF16),
            pltpu.VMEM((width, wide), BF16),
            pltpu.VMEM((width, wide), BF16),
            pltpu.SemaphoreType.DMA((n_w + 2 * n_x,)),
        ],
        compiler_params=pltpu.CompilerParams(vmem_limit_bytes=VMEM_LIMIT),
        cost_estimate=pl.CostEstimate(flops=4 * full * width * wide, bytes_accessed=20_000_000, transcendentals=full * cols),
        name="feed_forward",
    )(scal, *x_parts, *u_parts, *w_parts)
    return outs[0], outs[1], outs[2:]


def ff_out_kernel(parts, n_c, n_w, seq, scal, *refs):
    hid_refs, refs = refs[:n_c], refs[n_c:]
    ggu_refs, refs = refs[:n_c], refs[n_c:]
    w_refs, refs = refs[: n_c * n_w], refs[n_c * n_w :]
    ykeep_ref, ysend_ref, gkeep_ref, gsend_ref, hs, gs, ws, sems = refs
    size = ykeep_ref.shape[1]
    full = parts * size
    me_d = scal[1]
    wide = ws.shape[2]
    cols = wide // 3
    copies = []
    first = 0
    for c in range(n_c):
        targets = shard_targets(w_refs[c * n_w : (c + 1) * n_w], ws.at[c], me_d)
        copies += load_all(w_refs[c * n_w : (c + 1) * n_w], targets, sems, first)
        first += n_w
    mine = pl.ds(seq * full, full)
    copies += load_all([ref.at[mine] for ref in ggu_refs], [gs.at[c] for c in range(n_c)], sems, first)
    copies += load_all([ref.at[mine] for ref in hid_refs], [hs.at[c] for c in range(n_c)], sems, first + n_c)
    for copy in copies:
        copy.wait()
    for j in range(parts):
        rows = pl.ds(j * size, size)
        grad = sum(dot_nt(gs[c, rows, :], ws[c, :, : 2 * cols]) for c in range(n_c))
        (gsend_ref if j % 2 else gkeep_ref)[j // 2] = grad.astype(BF16)
        out = sum(dot_nt(hs[c, rows, :], ws[c, :, 2 * cols :]) for c in range(n_c))
        (ysend_ref if j % 2 else ykeep_ref)[j // 2] = out.astype(BF16)


def ff_out(seq, scal, parts, size, hids, ggus, w_chunks):
    n_c, n_w = len(w_chunks), len(w_chunks[0])
    wide = w_chunks[0][0].shape[1]
    width = w_chunks[0][0].shape[0] * n_w
    full = parts * size
    cols = wide // 3
    pair = jax.ShapeDtypeStruct((parts // 2, size, width), BF16)
    return pl.pallas_call(
        functools.partial(ff_out_kernel, parts, n_c, n_w, seq),
        out_shape=(pair,) * 4,
        in_specs=[SMEM] + [ANY] * (2 * n_c + n_c * n_w),
        out_specs=(VMEM,) * 4,
        scratch_shapes=[
            pltpu.VMEM((n_c, full, cols), BF16),
            pltpu.VMEM((n_c, full, 2 * cols), BF16),
            pltpu.VMEM((n_c, width, wide), BF16),
            pltpu.SemaphoreType.DMA((n_c * n_w + 2 * n_c,)),
        ],
        compiler_params=pltpu.CompilerParams(vmem_limit_bytes=VMEM_LIMIT),
        cost_estimate=pl.CostEstimate(flops=2 * full * width * wide * n_c, bytes_accessed=22_000_000, transcendentals=0),
        name="feed_forward_out",
    )(scal, *hids, *ggus, *[shard for chunk in w_chunks for shard in chunk])


def flip(index, bits):
    for bit in (1, 2, 4):
        if bits & bit:
            index = index + bit - 2 * bit * lax.rem(lax.div(index, bit), 2)
    return index


class Spot:
    def __init__(self, index, choices):
        self.index = index
        self.flips = {0: index}
        for bits in choices:
            self.flips[bits] = flip(index, bits)


def spots():
    me_t = Spot(lax.axis_index("tensor"), (1, 2, 3))
    me_d = Spot(lax.axis_index("dp"), (1, 2, 3, 4, 5, 6, 7))
    me_d.x = lax.rem(me_d.index, 2)
    me_d.beside = 1 - me_d.x
    me_d.z = Spot(lax.div(me_d.index, 2), (1, 2, 3))
    return me_t, me_d


def greet(barrier, me_d, me_t, along_d, along_t):
    devices = [{"dp": me_d.flips[bits]} for bits in along_d]
    devices += [{"tensor": me_t.flips[bits]} for bits in along_t]
    for device in devices:
        pl.semaphore_signal(barrier, inc=1, device_id=device, device_id_type=pl.DeviceIdType.MESH)
    return lambda: pl.semaphore_wait(barrier, len(devices))


def remote(source, target, sems, number, device):
    return pltpu.make_async_remote_copy(
        src_ref=source,
        dst_ref=target,
        send_sem=sems.at[0, number],
        recv_sem=sems.at[1, number],
        device_id=device,
        device_id_type=pl.DeviceIdType.MESH,
    )


class Remote:
    LIMIT = 128

    def __init__(self, sems):
        self.sems, self.used = sems, 0

    def __call__(self, source, target, device):
        assert self.used < self.LIMIT
        self.used += 1
        return remote(source, target, self.sems, self.used - 1, device)


class Local:
    LIMIT = 64

    def __init__(self, sems):
        self.sems, self.used = sems, 0

    def make(self, source, target):
        assert self.used < self.LIMIT
        self.used += 1
        return pltpu.make_async_copy(source, target, self.sems.at[self.used - 1])

    def __call__(self, source, target):
        copy = self.make(source, target)
        copy.start()
        return copy


COPY_SEMS = [
    pltpu.SemaphoreType.DMA((2, Remote.LIMIT)),
    pltpu.SemaphoreType.DMA((Local.LIMIT,)),
]


class ShardGather:
    def __init__(self, shard, place, send, me_d, direct=False):
        def pass_on(bits, target):
            there = place(me_d.flips[bits])
            return send(there, there, {"dp": me_d.flips[target]})

        mine = place(me_d.index)
        self.beside, self.next, self.across = [send(shard, mine, {"dp": me_d.flips[bits]}) for bits in (1, 2, 4)]
        self.direct = direct
        self.on = send(shard, mine, {"dp": me_d.flips[6]}) if direct else pass_on(4, 2)
        self.passed = [pass_on(bits, 1) for bits in (4, 2, 6)]

    def start_x(self):
        self.beside.start()

    def start_z(self):
        self.next.start()
        self.across.start()
        if self.direct:
            self.on.start()

    def forward(self):
        self.next.wait_recv()
        self.passed[1].start()
        self.across.wait_recv()
        if not self.direct:
            self.on.start()
        self.passed[0].start()

    def forward_last(self):
        self.on.wait_recv()
        self.passed[2].start()

    def arrive(self):
        self.beside.wait_recv()
        for copy in self.passed:
            copy.wait_recv()

    def drain(self):
        for copy in [self.beside, self.next, self.across, self.on] + self.passed:
            copy.wait_send()


class TokenGather:
    def __init__(self, block, whole, send, me_t):
        size = block.shape[0]
        mine = whole.at[rows_of(me_t.index, size)]
        there = whole.at[rows_of(me_t.flips[2], size)]
        near = {"tensor": me_t.flips[1]}
        self.near = send(block, mine, near)
        self.far = send(block, mine, {"tensor": me_t.flips[2]})
        self.passed = send(there, there, near)

    def start(self):
        self.far.start()
        self.near.start()

    def forward(self):
        self.far.wait_recv()
        self.passed.start()

    def arrive(self):
        self.near.wait_recv()
        self.passed.wait_recv()

    def drain(self):
        for copy in (self.near, self.far, self.passed):
            copy.wait_send()


class TokenReduce:
    def __init__(self, blocks, near, far, send, me_t, mine=None):
        device = {"tensor": me_t.flips[1]}
        self.blocks, self.near_ref, self.far_ref, self.mine = blocks, near, far, mine
        self.places = (me_t.index, me_t.flips[2])
        self.size = far.shape[0]
        self.near = [
            send(blocks.at[rows_of(me_t.flips[1 + 2 * n], self.size)], near.at[n], device) for n in range(2)
        ]
        self.far = send(near.at[1], far, {"tensor": me_t.flips[2]})

    def load(self, here):
        return [here(self.blocks.at[rows_of(place, self.size)], self.mine.at[n]) for n, place in enumerate(self.places)]

    def start(self, *which):
        for n in which or (1, 0):
            self.near[n].start()

    def part(self, n, rows):
        if self.mine is not None:
            return self.mine[n, rows, :].astype(F32)
        start = pl.multiple_of(self.places[n] * self.size + rows.start, 32)
        return self.blocks[pl.ds(start, rows.size), :].astype(F32)

    def middle(self):
        self.near[1].wait_recv()

        def step(rows):
            total = self.part(1, rows) + self.near_ref[1, rows, :].astype(F32)
            self.near_ref[1, rows, :] = total.astype(BF16)

        by_rows(self.size, 32, step)
        self.far.start()

    def arrive(self):
        self.near[0].wait_recv()
        self.far.wait_recv()

    def rows(self, rows):
        total = self.part(0, rows) + self.near_ref[0, rows, :].astype(F32)
        return total + self.far_ref[rows, :].astype(F32)

    def drain(self):
        for copy in self.near + [self.far]:
            copy.wait_send()


class ShardNear:
    def __init__(self, whole, near, out, send, me_d, mine=None):
        self.whole, self.near_ref, self.out, self.mine = whole, near, out, mine
        self.z, self.x = me_d.z, me_d.x
        self.size = near.shape[1]
        self.near = send(whole.at[:, me_d.beside], near, {"dp": me_d.flips[1]})

    def load(self, here):
        return [here(self.whole.at[:, self.x], self.mine)]

    def start(self):
        self.near.start()

    def part(self, there, rows):
        if self.mine is not None:
            return self.mine[there, rows, :].astype(F32)
        return self.whole[there, self.x, rows, :].astype(F32)

    def middle(self, far=None):
        self.near.wait_recv()
        for k in (1, 3, 2, 0):
            there = self.z.flips[k]

            def step(rows):
                total = self.part(there, rows) + self.near_ref[there, rows, :].astype(F32)
                if k:
                    self.near_ref[there, rows, :] = total.astype(BF16)
                else:
                    self.out[rows, :] = total

            by_rows(self.size, 32, step)
            if k and far is not None:
                far.ready(k)

    def drain(self):
        self.near.wait_send()


class ShardFar:
    def __init__(self, near, far, out, send, me_d):
        self.far_ref, self.out = far, out
        self.size = far.shape[1]
        self.far = [send(near.at[me_d.z.flips[k]], far.at[k - 1], {"dp": me_d.flips[2 * k]}) for k in (1, 2, 3)]
        self.last = self.far
        self.terms = (0, 1, 2)

    def ready(self, k):
        self.far[k - 1].start()

    def finish(self):
        for copy in self.last:
            copy.wait_recv()

        def step(rows):
            total = self.out[rows, :]
            for k in self.terms:
                total = total + self.far_ref[k, rows, :].astype(F32)
            self.out[rows, :] = total

        by_rows(self.size, 32, step)

    def drain(self):
        for copy in self.far:
            copy.wait_send()


class ShardHalves(ShardFar):
    def __init__(self, near, far, out, send, me_d):
        self.near_ref, self.far_ref, self.out = near, far, out
        self.size = far.shape[1]
        z = me_d.z.flips
        self.across = z[2]
        self.far = [
            send(near.at[z[1]], far.at[0], {"dp": me_d.flips[2]}),
            send(near.at[z[3]], far.at[1], {"dp": me_d.flips[2]}),
            send(near.at[z[2]], far.at[2], {"dp": me_d.flips[4]}),
        ]
        self.last = (self.far[0], self.far[2])
        self.terms = (0, 2)

    def ready(self, k):
        if k != 2:
            self.far[k // 2].start()

    def middle(self):
        self.far[1].wait_recv()

        def step(rows):
            total = self.near_ref[self.across, rows, :].astype(F32) + self.far_ref[1, rows, :].astype(F32)
            self.near_ref[self.across, rows, :] = total.astype(BF16)

        by_rows(self.size, 32, step)
        self.far[2].start()


def by_rows(count, step, body):
    def run(b, carry):
        body(rows_of(b, step))
        return carry

    lax.fori_loop(0, count // step, run, None)


def loop(start, stop, body, unroll=False):
    def run(i, carry):
        body(i)
        return carry

    lax.fori_loop(start, stop, run, None, unroll=unroll)


def rms_factor(values):
    return lax.rsqrt(jnp.mean(values * values, axis=-1, keepdims=True) + EPS)


def shape(dims, kind):
    return jax.ShapeDtypeStruct(dims, kind)


def block_kernel(
    lengths, in_ref, cot_ref, qw_ref, kv_ref, ow_ref, iw_ref, dw_ref, cos_ref, sin_ref, qg_ref, kg_ref, mg_ref, dg_ref,
    normed_out, raw_out, q_out, k_out, v_out, att_out, lse_out, r_out, blk_out,
    ig_ref, awg_ref, ffg_ref, sums_ref,
    x_ref, gq_ref, gk_ref, xs, ws, dn, us, outp, onear, ofar, resid, wnear, wfar, whole, dgain, put, got_t, got_d, free,
    sems, local_sems,
):
    seqs, full, width = xs.shape
    size = resid.shape[1]
    parts = full // size
    n_c = 3
    shard = qw_ref.shape[0]
    cols = iw_ref.shape[2] // n_c
    wide = 3 * cols
    me_t, me_d = spots()
    send, here = Remote(sems), Local(local_sems)
    mine_t, mine_d = rows_of(me_t.index, size), rows_of(me_d.index, shard)
    halves = [pl.ds(s * full, full) for s in range(seqs)]
    own_rows = [rows_of(s * parts + me_t.index, size) for s in range(seqs)]
    every_row = pl.ds(0, seqs * full)
    lanes_of = [slice(width * s, width * (s + 1)) for s in range(seqs)]

    def wait(copies):
        for copy in copies:
            copy.wait()

    pro_w = [
        ShardGather(ws.at[mine_d, lanes], lambda i, lanes=lanes: ws.at[rows_of(i, shard), lanes], send, me_d)
        for lanes in (slice(0, 256), slice(256, 512))
    ]
    out_w = ShardGather(ws.at[mine_d, 512:], lambda i: ws.at[rows_of(i, shard), 512:], send, me_d, True)
    normed = [TokenGather(xs.at[s, mine_t], xs.at[s], send, me_t) for s in range(seqs)]
    ups = [TokenGather(us.at[own_rows[s]], us.at[halves[s]], send, me_t) for s in range(seqs)]
    denses = [TokenGather(dn.at[own_rows[s]], dn.at[halves[s]], send, me_t) for s in range(seqs)]
    out_places = (outp, xs.at[0])
    back_places = (outp, xs.at[1])
    norm_places = (outp, dn.at[halves[0]])
    outs, backs, norms = [
        [TokenReduce(places[s], onear.at[s], ofar.at[s], send, me_t) for s in range(seqs)]
        for places in (out_places, back_places, norm_places)
    ]
    lows = [xs.at[0, pl.ds(s * size, size)] for s in range(seqs)]
    resids = [TokenGather(lows[s], r_out.at[s], send, me_t) for s in range(seqs)]
    ff_sums = [ffg_ref.at[:, wide * c : wide * (c + 1)] for c in range(n_c)]
    near = [ShardNear(whole.at[c], wnear.at[c], ff_sums[c], send, me_d) for c in range(2)]
    far = [ShardHalves(wnear.at[c], wfar.at[c], ff_sums[c], send, me_d) for c in range(2)]
    steps = [
        [send(put.at[0], got_t.at[me_t.index], {"tensor": me_t.flips[bits]}) for bits in (1, 2, 3)],
        [send(put.at[1], got_d.at[me_d.index], {"dp": me_d.flips[bits]}) for bits in (1, 2, 3, 4, 5, 6, 7)],
    ]
    load_own = [here.make(us.at[own_rows[s]], xs.at[0, pl.ds((seqs + s) * size, size)]) for s in range(seqs)]
    keeps = [here.make(xs.at[s], normed_out.at[s]) for s in range(seqs)]
    backup = [here.make(normed_out.at[s], xs.at[s]) for s in range(seqs)]
    low_keeps = [here.make(lows[s], r_out.at[s, mine_t]) for s in range(seqs)]

    def after_out(s):
        outs[s].arrive()
        outs[s].drain()

        def norm(rows):
            values = x_ref[rows, lanes_of[s]].astype(F32) + outs[s].rows(rows)
            resid[s, rows, :] = values
            target = pl.ds(pl.multiple_of((s * parts + me_t.index) * size + rows.start, 32), 32)
            dn[target, :] = (values * rms_factor(values) * dg_ref[...]).astype(BF16)

        by_rows(size, 32, norm)
        denses[s].start()
        if s:
            for copy in load_own:
                copy.start()

    def after_back(s):
        backs[s].arrive()
        backs[s].drain()

        def step(rows):
            grad = backs[s].rows(rows)
            values = resid[s, rows, :]
            factor = rms_factor(values)
            product = grad * values * factor
            dgain[...] += jnp.sum(product.reshape(-1, 8, width), axis=0)
            weighted = grad * dg_ref[...]
            inner = jnp.mean(values * weighted, axis=-1, keepdims=True)
            place = pl.ds(pl.multiple_of((seqs + s) * size + rows.start, 32), 32)
            total = xs[0, place, :].astype(F32) + factor * weighted - values * (factor * factor * factor) * inner
            ig_ref[rows, lanes_of[s]] = total
            lows[s][rows, :] = total.astype(BF16)

        by_rows(size, 32, step)
        resids[s].start()
        low_keeps[s].start()

    def after_norm(s):
        norms[s].arrive()

        def step(rows):
            values = x_ref[rows, lanes_of[s]].astype(F32)
            factor = rms_factor(values)
            weighted = norms[s].rows(rows) * mg_ref[...]
            inner = jnp.mean(values * weighted, axis=-1, keepdims=True)
            ig_ref[rows, lanes_of[s]] += factor * weighted - values * (factor * factor * factor) * inner

        by_rows(size, 32, step)

    def until_backward(wf):
        ff_w = [ShardGather(wf.at[c, mine_d], lambda i, c=c: wf.at[c, rows_of(i, shard)], send, me_d) for c in range(n_c)]

        def attention(kp, vp, acc, raw, q, k, v, att, lse, inb, cotb, kvb, owb, iwb, dwb):
            kept = ((raw, raw_out), (q, q_out), (k, k_out), (v, v_out), (att, att_out), (lse, lse_out))
            flushes = []

            def project(s):
                loop(0, parts, lambda r: project_rows(
                    r, size, lengths[s], xs.at[s], ws, (cos_ref, sin_ref), (gq_ref, gk_ref),
                    raw.at[s], q.at[s], k.at[s], v.at[s], kp, vp,
                ), True)

            def attend(s, start, stop):
                for i in range(start, stop):
                    attend_rows(i, size, q.at[s], kp, vp, acc, att.at[s], lse.at[s])

            def out(s):
                for n, bits in enumerate((3, 1, 2, 0)):
                    rows = rows_of(me_t.flips[bits], size)
                    out_places[s][rows, :] = dot_nt(att[s, rows, :], ws[:, 512:]).astype(BF16)
                    if n < 2:
                        outs[s].start(1 - n)

            def first_rows(rows):
                values = inb[rows, :, :].astype(F32)
                target = pl.ds(pl.multiple_of(me_t.index * size + rows.start, 32), 32)
                for s in range(seqs):
                    mine = values[:, s, :]
                    x_ref[rows, lanes_of[s]] = mine.astype(BF16)
                    xs[s, target, :] = (mine * rms_factor(mine) * mg_ref[...]).astype(BF16)

            def upstream_rows(rows):
                grads = cotb[rows, :, :].astype(F32)
                place = me_t.index * size + rows.start + iota((32, width), 0)
                for s in range(seqs):
                    target = pl.ds(pl.multiple_of((s * parts + me_t.index) * size + rows.start, 32), 32)
                    us[target, :] = jnp.where(place < lengths[s], grads[:, s, :], 0.0).astype(BF16)

            def inner_rows(rows):
                both = iwb[rows, :, :].astype(F32)
                target = pl.ds(pl.multiple_of(me_d.index * shard + rows.start, 32), 32)
                for c in range(n_c):
                    for n in range(2):
                        part = both[:, n, cols * c : cols * (c + 1)]
                        wf[c, target, cols * n : cols * (n + 1)] = part.astype(BF16)

            entered = greet(
                pltpu.get_barrier_semaphore(), me_d, me_t, (1, 2, 3, 4, 5, 6, 7), (1, 2, 3)
            )
            load_x = here(in_ref, inb)
            load_a = [here(qw_ref, ws.at[mine_d, :256]), here(kv_ref, kvb), here(ow_ref, owb)]
            load_f = [here(iw_ref, iwb), here(dw_ref, dwb)]
            load_u = here(cot_ref, cotb)
            for source, target in ((qg_ref, gq_ref), (kg_ref, gk_ref)):
                target[...] = jnp.concatenate([source[...], source[...]], axis=1)
            wait(load_a)
            pair = kvb[...].astype(F32)
            for n in range(2):
                ws[mine_d, 256 + 128 * n : 384 + 128 * n] = pair[:, n, :].astype(BF16)
            ws[mine_d, 512:] = owb[...].astype(F32).T.astype(BF16)
            load_x.wait()
            by_rows(size, 32, first_rows)
            entered()
            normed[0].start()
            for exchange in pro_w:
                exchange.start_z()
                exchange.start_x()
            wait(load_f)
            for c in range(n_c):
                wf[c, mine_d, 2 * cols :] = dwb[cols * c : cols * (c + 1), :].astype(F32).T.astype(BF16)
            by_rows(shard, 32, inner_rows)
            for exchange in pro_w:
                exchange.forward()
            for exchange in pro_w:
                exchange.forward_last()
            out_w.start_z()
            out_w.start_x()
            normed[0].forward()
            normed[1].start()
            normed[0].arrive()
            ff_w[0].start_z()
            load_u.wait()
            by_rows(size, 32, upstream_rows)
            for exchange in pro_w:
                exchange.arrive()
            ff_w[0].start_x()
            project(0)
            keeps[0].start()
            out_w.forward()
            out_w.forward_last()
            attend(0, 0, 3)
            normed[1].forward()
            ups[0].start()
            attend(0, 3, parts)
            ff_w[0].forward()
            out_w.arrive()
            out(0)
            outs[0].middle()
            for source, target in kept:
                flushes.append(here(source.at[0], target.at[0]))
            normed[1].arrive()
            project(1)
            keeps[1].start()
            ff_w[0].forward_last()
            ff_w[1].start_z()
            ff_w[1].start_x()
            attend(1, 0, 3)
            ups[0].forward()
            attend(1, 3, parts)
            normed[0].drain()
            keeps[0].wait()
            out(1)
            for source, target in kept:
                flushes.append(here(source.at[1], target.at[1]))
            after_out(0)
            outs[1].middle()
            ff_w[1].forward()
            ff_w[2].start_z()
            ff_w[2].start_x()
            wait(flushes)

        pl.run_scoped(
            attention,
            pltpu.VMEM((4, full, LANES), BF16),
            pltpu.VMEM((4, full, 2 * LANES), BF16),
            pltpu.VMEM((2, size, 2 * LANES), F32),
            pltpu.VMEM((seqs, full, 384), F32),
            pltpu.VMEM((seqs, full, 256), BF16),
            pltpu.VMEM((seqs, full, 128), BF16),
            pltpu.VMEM((seqs, full, 128), BF16),
            pltpu.VMEM((seqs, full, 256), BF16),
            pltpu.VMEM((seqs, 8, full), F32),
            pltpu.VMEM(in_ref.shape, BF16),
            pltpu.VMEM(cot_ref.shape, BF16),
            pltpu.VMEM(kv_ref.shape, BF16),
            pltpu.VMEM(ow_ref.shape, BF16),
            pltpu.VMEM(iw_ref.shape, BF16),
            pltpu.VMEM(dw_ref.shape, BF16),
        )

        def feed_forward(hid, ggu):
            def tokens(c, s):
                def run(r):
                    rows = rows_of(r, size)
                    gate_up = dot(dn[rows, :], wf[c, :, : 2 * cols])
                    grad = dot(us[rows, :], wf[c, :, 2 * cols :])
                    gate, up = gate_up[:, :cols], gate_up[:, cols:]
                    sig = 1.0 / (1.0 + jnp.exp2(gate * -LOG2E))
                    silu = gate * sig
                    hid[c, rows, :] = (silu * up).astype(BF16)
                    ggu[c, rows, :cols] = (grad * up * (sig + silu * (1.0 - sig))).astype(BF16)
                    ggu[c, rows, cols:] = (grad * silu).astype(BF16)

                loop(s * parts, (s + 1) * parts, run, True)

            def weigh(c, tokens, more=False):
                def run(b):
                    rows = rows_of(b, 256)
                    dims = whole.shape[2:4]
                    inner = dot_tn(dn[tokens, rows], ggu[c, tokens, :]).reshape(dims + (2 * cols,))
                    down = dot_tn(us[tokens, rows], hid[c, tokens, :]).reshape(dims + (cols,))
                    if more:
                        inner = inner + whole[c % 2, b, :, :, : 2 * cols].astype(F32)
                        down = down + whole[c % 2, b, :, :, 2 * cols :].astype(F32)
                    whole[c % 2, b, :, :, : 2 * cols] = inner.astype(BF16)
                    whole[c % 2, b, :, :, 2 * cols :] = down.astype(BF16)

                loop(0, whole.shape[1], run)

            def grad_blocks(s):
                for n, bits in enumerate((3, 1, 2, 0)):
                    rows = rows_of(s * parts + me_t.flips[bits], size)
                    left = jnp.concatenate([ggu[c, rows, :] for c in range(n_c)], axis=1)
                    right = jnp.concatenate([wf[c, :, : 2 * cols] for c in range(n_c)], axis=1)
                    total = dot_nt(left, right)
                    back_places[s][rows_of(me_t.flips[bits], size), :] = total.astype(BF16)
                    if n < 2:
                        backs[s].start(1 - n)

            def down_block(r):
                rows = rows_of(r, size)
                left = jnp.concatenate([hid[c, rows, :] for c in range(n_c)], axis=1)
                right = jnp.concatenate([wf[c, :, 2 * cols :] for c in range(n_c)], axis=1)
                total = dot_nt(left, right)
                us[rows, :] = total.astype(BF16)

            denses[0].forward()
            ups[1].start()
            ff_w[1].forward_last()
            ups[0].arrive()
            ff_w[0].arrive()
            denses[0].arrive()
            tokens(0, 0)
            ff_w[2].forward()
            weigh(0, halves[0])
            after_out(1)
            ff_w[1].arrive()
            tokens(1, 0)
            ff_w[2].forward_last()
            weigh(1, halves[0])
            ups[1].forward()
            denses[1].forward()
            ups[1].arrive()
            denses[1].arrive()
            tokens(0, 1)
            weigh(0, halves[1], True)
            near[0].start()
            ff_w[2].arrive()
            tokens(2, 0)
            grad_blocks(0)
            backs[0].middle()
            tokens(1, 1)
            weigh(1, halves[1], True)
            tokens(2, 1)
            normed[1].drain()
            keeps[1].wait()
            dgain[...] = jnp.zeros_like(dgain)
            wait(load_own)
            grad_blocks(1)
            after_back(0)
            near[0].middle(far[0])
            near[1].start()
            near[0].drain()
            backs[1].middle()
            weigh(2, every_row)
            ups[0].drain()
            ups[1].drain()
            loop(0, parts, down_block, True)
            loop(parts, seqs * parts, down_block, True)
            resids[0].forward()
            far[0].middle()
            for exchange in ff_w + denses:
                exchange.drain()

        pl.run_scoped(
            feed_forward,
            pltpu.VMEM((n_c, seqs * full, cols), BF16),
            pltpu.VMEM((n_c, seqs * full, 2 * cols), BF16),
        )

    pl.run_scoped(until_backward, pltpu.VMEM((n_c, 8 * shard, wide), BF16))

    def backward(
        kp, vp, kt, ga, dq, dk, dv, gp, drow, acc, gains, mixer, raw, q, k, v, att, lse,
        wo, wq, wk, lnear, lfar, pnear, pfar, ynear, yfar,
    ):
        entered = greet(free, me_d, me_t, (1, 2, 4, 6), (1, 2))
        downs = [TokenReduce(us.at[halves[s]], ynear.at[s], yfar.at[s], send, me_t) for s in range(seqs)]
        late_near, late_far = [], []
        for n in range(2):
            half = pl.ds(n * shard // 2, shard // 2)
            refs = lnear.at[:, half], ff_sums[2].at[half]
            late_near.append(ShardNear(whole.at[0, :, :, half], refs[0], refs[1], send, me_d))
            late_far.append(ShardHalves(refs[0], lfar.at[:, half], refs[1], send, me_d))
        pieces = ((wo, slice(512, 768)), (wq, slice(0, 256)), (wk, slice(256, 512)))
        pro_near = [ShardNear(part, pnear.at[n], awg_ref.at[:, lanes], send, me_d) for n, (part, lanes) in enumerate(pieces)]
        pro_far = [
            (ShardHalves if n else ShardFar)(pnear.at[n], pfar.at[n], awg_ref.at[:, lanes], send, me_d)
            for n, (part, lanes) in enumerate(pieces)
        ]
        kept = ((k_out, k), (v_out, v), (att_out, att), (lse_out, lse), (q_out, q))
        load_s = [[here(source.at[s], target.at[s]) for source, target in kept] for s in range(seqs)]
        load_raw = [here(raw_out.at[0], raw)]
        gains[...] = jnp.zeros_like(gains)
        mixer[...] = jnp.zeros_like(mixer)

        def load_grad(s):
            resids[s].arrive()
            low_keeps[s].wait()
            here(r_out.at[s], dn.at[halves[s]]).wait()

        def prepare(s):
            loop(0, parts, lambda r: prepare_rows(
                r, size, lengths[s], dn.at[halves[s]], ws, k.at[s], v.at[s], att.at[s], ga, drow, kp, kt, vp
            ), True)
            dk[...] = jnp.zeros_like(dk)
            dv[...] = jnp.zeros_like(dv)

        def sweep(s, start, stop):
            for i in range(start, stop):
                sweep_rows(i, size, q.at[s], ga, kp, kt, vp, drow, lse.at[s], acc, dq, dk, dv)

        def unproject_q(s):
            loop(0, parts, lambda r: unproject_queries(r, size, (cos_ref, sin_ref), gq_ref, raw, dq, gp.at[s], gains), True)

        def unproject_kv(s):
            loop(0, parts, lambda r: unproject_pairs(
                r, size, lengths[s], (cos_ref, sin_ref), gk_ref, raw, dk, dv, gp.at[s], gains
            ), True)

        def norm_blocks(s):
            for n, bits in enumerate((3, 1, 2, 0)):
                rows = rows_of(me_t.flips[bits], size)
                norm_places[s][rows, :] = dot_nt(gp[s, rows, :], ws[:, :512]).astype(BF16)
                if n < 2:
                    norms[s].start(1 - n)

        def weigh_out():
            def run(b):
                rows = rows_of(b, 256)
                total = sum(dot_tn(dn[halves[s], rows], att[s]) for s in range(seqs))
                wo[b] = total.astype(BF16).reshape(wo.shape[1:])

            loop(0, wo.shape[0], run)

        def weigh(target, lanes):
            def run(b):
                rows = rows_of(b, 256)
                total = sum(dot_tn(xs[s, :, rows], gp[s, :, lanes]) for s in range(seqs))
                target[b] = total.astype(BF16).reshape(target.shape[1:])
                product = total * ws[rows, lanes].astype(F32)
                high = product.astype(BF16)
                rest = (product - high.astype(F32)).astype(BF16)
                ones = jnp.ones((8, product.shape[1]), BF16)
                mixer[:, rows] += dot_nt(ones, high) + dot_nt(ones, rest)

            loop(0, target.shape[0], run)

        def after_down(s):
            downs[s].arrive()

            def step(rows):
                target = pl.ds(pl.multiple_of(s * size + rows.start, 32), 32)
                outp[target, :] = (resid[s, rows, :] + downs[s].rows(rows)).astype(BF16)

            by_rows(size, 32, step)
            return here(outp.at[pl.ds(s * size, size)], blk_out.at[s])

        def total_of(n, got, index):
            got[index] = put[n]
            for copy in steps[n]:
                copy.wait_recv()
            total = got[0]
            for place in range(1, got.shape[0]):
                total = total + got[place]
            return total

        wait(load_s[0])
        load_grad(0)
        prepare(0)
        entered()
        late_near[0].start()
        for exchange in downs:
            exchange.start()
        sweep(0, 0, 2)
        after_back(1)
        sweep(0, 2, 3)
        near[1].middle(far[1])
        sweep(0, 3, parts)
        wait(load_raw)
        unproject_q(0)
        unproject_kv(0)
        load_raw = [here(raw_out.at[1], raw)]
        norm_blocks(0)
        resids[1].forward()
        norms[0].middle()
        late_near[0].middle(late_far[0])
        late_near[1].start()
        downs[0].middle()
        load_grad(1)
        for exchange in resids:
            exchange.drain()
        for copy in backup:
            copy.start()
        wait(load_s[1])
        prepare(1)
        far[1].middle()
        far[0].finish()
        weigh_out()
        pro_near[0].start()
        sweep(1, 0, 2)
        downs[1].middle()
        sweep(1, 2, 3)
        late_near[1].middle(late_far[1])
        late_far[0].middle()
        sweep(1, 3, parts)
        pro_near[0].middle(pro_far[0])
        wait(load_raw)
        unproject_kv(1)
        wait(backup)
        weigh(wk, pieces[2][1])
        pro_near[2].start()
        unproject_q(1)
        weigh(wq, pieces[1][1])
        pro_near[1].start()
        for row, vector in ((0, mixer[0:1, :] / mg_ref[...]), (8, jnp.sum(dgain[...], axis=0, keepdims=True))):
            for i in range(8):
                put[0, row + i : row + i + 1, :] = vector[:, LANES * i : LANES * (i + 1)]
        put[0, 16:, :] = gains[...]
        for copy in steps[0]:
            copy.start()
        norm_blocks(1)
        pro_near[2].middle(pro_far[2])
        norms[1].middle()
        late_far[1].middle()
        put[1] = total_of(0, got_t, me_t.index)
        for copy in steps[1]:
            copy.start()
        after_norm(0)
        norms[0].drain()
        stays = [after_down(0)]
        pro_near[1].middle(pro_far[1])
        pro_far[2].middle()
        stays.append(after_down(1))
        far[1].finish()
        pro_far[0].finish()
        for exchange in late_far:
            exchange.finish()
        pro_far[1].middle()
        sums_ref[...] = total_of(1, got_d, me_d.index)
        after_norm(1)
        pro_far[2].finish()
        pro_far[1].finish()
        wait(stays)
        for copy in steps[0] + steps[1]:
            copy.wait_send()
        for exchange in downs + late_near + late_far + pro_near + pro_far:
            exchange.drain()

    pl.run_scoped(
        backward,
        pltpu.VMEM((4, full, LANES), BF16),
        pltpu.VMEM((4, full, LANES), BF16),
        pltpu.VMEM((4, LANES, full), BF16),
        pltpu.VMEM((full, 256), BF16),
        pltpu.VMEM((full, 256), F32),
        pltpu.VMEM((2, full, LANES), F32),
        pltpu.VMEM((2, full, LANES), F32),
        pltpu.VMEM((seqs, full, 512), BF16),
        pltpu.VMEM((8, full), F32),
        pltpu.VMEM((2, LANES, size), F32),
        pltpu.VMEM((8, LANES), F32),
        pltpu.VMEM((8, width), F32),
        pltpu.VMEM((full, 384), F32),
        pltpu.VMEM((seqs, full, 256), BF16),
        pltpu.VMEM((seqs, full, 128), BF16),
        pltpu.VMEM((seqs, full, 128), BF16),
        pltpu.VMEM((seqs, full, 256), BF16),
        pltpu.VMEM((seqs, 8, full), F32),
        pltpu.VMEM((4, 2, shard, 256), BF16),
        pltpu.VMEM((4, 2, shard, 256), BF16),
        pltpu.VMEM((4, 2, shard, 256), BF16),
        pltpu.VMEM((4, shard, wide), BF16),
        pltpu.VMEM((3, shard, wide), BF16),
        pltpu.VMEM((3, 4, shard, 256), BF16),
        pltpu.VMEM((3, 3, shard, 256), BF16),
        pltpu.VMEM((seqs, 2, size, width), BF16),
        pltpu.VMEM((seqs, size, width), BF16),
    )
    for exchange in pro_w + [out_w, near[1]] + far + norms[1:]:
        exchange.drain()


def fused_block(lengths, inputs, cotangent, weights, tabs, gains):
    size, seqs, width = inputs.shape
    full = 4 * size
    shard = weights[0].shape[0]
    cols = 768
    n_c = 3
    wide = 3 * weights[3].shape[2] // n_c
    dp = 8
    return pl.pallas_call(
        block_kernel,
        out_shape=(
            shape((seqs, full, width), BF16),
            shape((seqs, full, 384), F32),
            shape((seqs, full, 256), BF16),
            shape((seqs, full, 128), BF16),
            shape((seqs, full, 128), BF16),
            shape((seqs, full, 256), BF16),
            shape((seqs, 8, full), F32),
            shape((seqs, full, width), BF16),
            shape((seqs, size, width), BF16),
            shape((size, seqs * width), F32),
            shape((shard, cols), F32),
            shape((shard, n_c * wide), F32),
            shape((24, LANES), F32),
        ),
        in_specs=[SMEM] + [ANY] * 7 + [VMEM] * 6,
        out_specs=(ANY,) * 9 + (VMEM,) * 4,
        scratch_shapes=[
            pltpu.VMEM((size, seqs * width), BF16),
            pltpu.VMEM((1, LANES), F32),
            pltpu.VMEM((1, LANES), F32),
            pltpu.VMEM((seqs, full, width), BF16),
            pltpu.VMEM((dp * shard, cols), BF16),
            pltpu.VMEM((seqs * full, width), BF16),
            pltpu.VMEM((seqs * full, width), BF16),
            pltpu.VMEM((full, width), BF16),
            pltpu.VMEM((seqs, 2, size, width), BF16),
            pltpu.VMEM((seqs, size, width), BF16),
            pltpu.VMEM((seqs, size, width), F32),
            pltpu.VMEM((2, 4, shard, wide), BF16),
            pltpu.VMEM((2, 3, shard, wide), BF16),
            pltpu.VMEM((2, 4, 2, shard, wide), BF16),
            pltpu.VMEM((8, width), F32),
            pltpu.VMEM((2, 24, LANES), F32),
            pltpu.VMEM((4, 24, LANES), F32),
            pltpu.VMEM((8, 24, LANES), F32),
            pltpu.SemaphoreType.REGULAR,
        ]
        + COPY_SEMS,
        compiler_params=pltpu.CompilerParams(
            vmem_limit_bytes=BLOCK_LIMIT, collective_id=0, has_side_effects=True
        ),
        cost_estimate=pl.CostEstimate(flops=90_000_000_000, bytes_accessed=60_000_000, transcendentals=14_000_000),
        name="block",
    )(lengths, inputs, cotangent, *weights, *tabs, *gains)


def finish_kernel(
    lengths, ig_ref, blk_ref, awg_ref, ffg_ref,
    block_out, input_out, query_out, pair_out, output_out, inner_out, down_out,
):
    size, seqs, width = input_out.shape
    hidden = down_out.shape[0]
    cols = hidden // 3
    start = lax.axis_index("tensor") * size

    def step(rows):
        place = start + rows.start + iota((32, width), 0)
        parts = []
        for s in range(seqs):
            lanes = slice(width * s, width * (s + 1))
            input_out[rows, s, :] = ig_ref[rows, lanes]
            parts.append(jnp.where(place < lengths[s], blk_ref[s, rows, :].astype(F32), 0.0))
        block_out[rows, :, :] = jnp.stack(parts, axis=1).astype(BF16)

    by_rows(size, 32, step)
    query_out[...] = awg_ref[:, :256]
    for n in range(2):
        pair_out[:, n, :] = awg_ref[:, 256 + 128 * n : 384 + 128 * n]
    output_out[...] = awg_ref[:, 512:].T
    for c in range(3):
        base = 3 * cols * c
        for n in range(2):
            inner_out[:, n, cols * c : cols * (c + 1)] = ffg_ref[:, base + cols * n : base + cols * (n + 1)]
        down_out[cols * c : cols * (c + 1), :] = ffg_ref[:, base + 2 * cols : base + 3 * cols].T


def fused_finish(lengths, ig, blk, awg, ffg):
    seqs, size, width = blk.shape
    shard, wide = ffg.shape
    hidden = wide // 3
    return pl.pallas_call(
        finish_kernel,
        out_shape=(
            shape((size, seqs, width), BF16),
            shape((size, seqs, width), F32),
            shape((shard, 256), F32),
            shape((shard, 2, 128), F32),
            shape((256, shard), F32),
            shape((shard, 2, hidden), F32),
            shape((hidden, shard), F32),
        ),
        in_specs=[SMEM] + [VMEM] * 4,
        out_specs=(VMEM,) * 7,
        compiler_params=pltpu.CompilerParams(vmem_limit_bytes=VMEM_LIMIT),
        name="finish",
    )(lengths, ig, blk, awg, ffg)


def swap(values, axis, bits):
    return lax.ppermute(values, axis, [(i, i ^ bits) for i in range(lax.axis_size(axis))])


def gather_tokens(block):
    far = swap(block, "tensor", 2)
    return [block, swap(block, "tensor", 1), far, swap(far, "tensor", 1)]


def scatter_tokens(keep, send):
    near = swap(send, "tensor", 1)
    middle = (keep[1].astype(F32) + near[1].astype(F32)).astype(BF16)
    far = swap(middle, "tensor", 2)
    return keep[0].astype(F32) + near[0].astype(F32) + far.astype(F32)


def gather_shards(shard):
    if lax.axis_size("dp") != 8 or shard.shape[0] % LANES:
        return [lax.all_gather(shard, "dp", axis=0, tiled=True)]
    slots = [shard, swap(shard, "dp", 1)]
    for bits in (2, 4, 6):
        there = swap(shard, "dp", bits)
        slots += [there, swap(there, "dp", 1)]
    return slots


def scatter_shards(grads):
    if len(grads) == 1:
        return lax.psum_scatter(grads[0].astype(F32), "dp", scatter_dimension=0, tiled=True)
    keep, send = grads
    near = swap(send, "dp", 1)
    both = keep.astype(F32) + near.astype(F32)
    total = both[0]
    for slot in (1, 2, 3):
        total = total + swap(both[slot].astype(BF16), "dp", 2 * slot).astype(F32)
    return total


def sum_everywhere(values):
    for axis in ("tensor", "dp"):
        bits = 1
        while bits < lax.axis_size(axis):
            values = values + swap(values, axis, bits)
            bits *= 2
    return values


def norm_rows(values, gain):
    factor = lax.rsqrt(jnp.mean(values * values, axis=-1, keepdims=True) + EPS)
    return (values * factor * gain, factor)


def norm_back(values, factor, gain, upstream):
    weighted = upstream * gain
    inner = jnp.mean(values * weighted, axis=-1, keepdims=True)
    return factor * weighted - values * factor * factor * factor * inner


def tables(full, head_width):
    half = head_width // 2
    freqs = THETA ** (-jnp.arange(half, dtype=F32) * 2.0 / head_width)
    angles = jnp.arange(full, dtype=F32)[:, None] * freqs[None, :]
    cosines, sines = jnp.cos(angles), jnp.sin(angles)
    return (jnp.tile(cosines, (1, 4)), jnp.tile(jnp.concatenate([-sines, sines], axis=1), (1, 2)))


def local_plain(
    inputs,
    lengths,
    query_weight,
    key_value_weight,
    output_weight,
    inner_weight,
    down_weight,
    mixer_gain,
    query_gain,
    key_gain,
    dense_gain,
    cotangent,
):
    size, seqs, width = inputs.shape
    parts = lax.axis_size("tensor")
    full = size * parts
    head = query_gain.shape[0]
    query_cols = query_weight.shape[1]
    pair_cols = key_value_weight.shape[2]
    hidden = inner_weight.shape[2]
    shard = query_weight.shape[0]
    me_t, me_d = lax.axis_index("tensor"), lax.axis_index("dp")
    n_c = 3
    cols = hidden // n_c
    cosines, sines = tables(full, head)
    gq = jnp.tile(query_gain, 2)[None, :]
    gk = jnp.tile(key_gain, 2)[None, :]

    down_turned = down_weight.T
    attn_shard = jnp.concatenate(
        [query_weight, key_value_weight.reshape(shard, 2 * pair_cols), output_weight.T], axis=1
    )
    attn_w = gather_shards(attn_shard)
    positions = me_t * size + jnp.arange(size, dtype=jnp.int32)
    scals = [
        jnp.stack([me_t.astype(jnp.int32), me_d.astype(jnp.int32), lengths[s], jnp.int32(0)])
        for s in range(seqs)
    ]
    tokens = [inputs[:, s].astype(F32) for s in range(seqs)]
    valid = [(positions < lengths[s])[:, None] for s in range(seqs)]
    firsts = [norm_rows(tokens[s], mixer_gain) for s in range(seqs)]
    normed = [gather_tokens(firsts[s][0].astype(BF16)) for s in range(seqs)]
    ff_w = []
    for c in range(n_c):
        part = slice(c * cols, (c + 1) * cols)
        ff_w.append(
            gather_shards(
                jnp.concatenate(
                    [inner_weight[:, 0, part], inner_weight[:, 1, part], down_turned[:, part]], axis=1
                )
            )
        )
    upstream = [jnp.where(valid[s], cotangent[:, s].astype(F32), 0.0) for s in range(seqs)]
    up_parts = [gather_tokens(upstream[s].astype(BF16)) for s in range(seqs)]

    saved, residual, seconds, dense = [], [], [], []
    for s in range(seqs):
        outs = attn_fwd(scals[s], cosines, sines, gq, gk, normed[s], attn_w)
        saved.append(outs[:6])
        residual.append(tokens[s] + scatter_tokens(outs[6], outs[7]))
        dense_in, factor = norm_rows(residual[s], dense_gain)
        seconds.append(factor)
        dense.append(gather_tokens(dense_in.astype(BF16)))

    x_parts = [part for s in range(seqs) for part in dense[s]]
    u_parts = [part for s in range(seqs) for part in up_parts[s]]
    hids, ggus, ff_grads = [], [], []
    for c in range(n_c):
        hid, ggu, grads = feed_forward(scals[0], x_parts, u_parts, ff_w[c])
        hids.append(hid)
        ggus.append(ggu)
        ff_grads.append(scatter_shards(grads))

    block_out, input_gradient, attn_grads = [], [], []
    mixer_part = dense_part = gain_part = 0.0
    for s in range(seqs):
        ykeep, ysend, gkeep, gsend = ff_out(s, scals[s], parts, size, hids, ggus, ff_w)
        grad_dense = scatter_tokens(gkeep, gsend)
        dense_part = dense_part + jnp.sum(grad_dense * residual[s] * seconds[s], axis=0)
        grad_residual = upstream[s] + norm_back(residual[s], seconds[s], dense_gain, grad_dense)
        r_parts = gather_tokens(grad_residual.astype(BF16))
        nkeep, nsend, gains, grads = attn_bwd(
            scals[s], cosines, sines, gq, gk, saved[s], normed[s], r_parts, attn_w
        )
        attn_grads.append(grads)
        gain_part = gain_part + gains
        grad_normed = scatter_tokens(nkeep, nsend)
        factor = firsts[s][1]
        mixer_part = mixer_part + jnp.sum(grad_normed * tokens[s] * factor, axis=0)
        input_gradient.append(grad_residual + norm_back(tokens[s], factor, mixer_gain, grad_normed))
        out_sum = scatter_tokens(ykeep, ysend)
        block_out.append(jnp.where(valid[s], residual[s] + out_sum, 0.0).astype(BF16))

    summed = [
        sum(part.astype(F32) for part in parts_of).astype(BF16) for parts_of in zip(*attn_grads)
    ]
    attn_grad = scatter_shards(summed)
    early = sum_everywhere(jnp.concatenate([dense_part.reshape(-1, LANES), gain_part], axis=0))
    mixer = sum_everywhere(mixer_part.reshape(-1, LANES)).reshape(-1)
    dense_rows = width // LANES
    folded = early[dense_rows:, :head] + early[dense_rows:, head:]
    inner_gradient = jnp.stack(
        [
            jnp.concatenate([grad[:, p * cols : (p + 1) * cols] for grad in ff_grads], axis=1)
            for p in range(2)
        ],
        axis=1,
    )
    down_gradient = jnp.concatenate([grad[:, 2 * cols :] for grad in ff_grads], axis=1).T
    return (
        jnp.stack(block_out, axis=1),
        jnp.stack(input_gradient, axis=1),
        attn_grad[:, :query_cols],
        attn_grad[:, query_cols : query_cols + 2 * pair_cols].reshape(shard, 2, pair_cols),
        attn_grad[:, query_cols + 2 * pair_cols :].T,
        inner_gradient,
        down_gradient,
        mixer,
        folded[0],
        folded[1],
        early[:dense_rows].reshape(-1),
    )


def local(*args):
    inputs, shard = args[0], args[2].shape[0]
    if lax.axis_size("dp") == 8 and lax.axis_size("tensor") == 4 and shard % LANES == 0 and inputs.shape[1] == 2:
        return local_fused(*args)
    return local_plain(*args)


def rope_tables(full, head):
    half = head // 2
    freqs = np.float32(THETA) ** (-np.arange(half, dtype=np.float32) * np.float32(2.0) / np.float32(head))
    angles = np.arange(full, dtype=np.float32)[:, None] * freqs[None, :].astype(np.float32)
    cosines, sines = np.cos(angles), np.sin(angles)
    return (
        jnp.asarray(np.tile(cosines, (1, 4)), F32),
        jnp.asarray(np.tile(np.concatenate([-sines, sines], axis=1), (1, 2)), F32),
    )


def local_fused(
    inputs,
    lengths,
    query_weight,
    key_value_weight,
    output_weight,
    inner_weight,
    down_weight,
    mixer_gain,
    query_gain,
    key_gain,
    dense_gain,
    cotangent,
):
    size, seqs, width = inputs.shape
    parts = lax.axis_size("tensor")
    full = size * parts
    head = query_gain.shape[0]
    tabs = rope_tables(full, head)
    weights = (query_weight, key_value_weight, output_weight, inner_weight, down_weight)
    gains = (query_gain[None, :], key_gain[None, :], mixer_gain[None, :], dense_gain[None, :])
    *_, blk, input_gradient, attn_grad, ff_grad, sums = fused_block(
        lengths, inputs, cotangent, weights, tabs, gains
    )
    finished = fused_finish(lengths, input_gradient, blk, attn_grad, ff_grad)
    folded = sums[16:, :head] + sums[16:, head:]
    return tuple(finished) + (
        sums[:8].reshape(-1),
        folded[0],
        folded[1],
        sums[8:16].reshape(-1),
    )


def solution(mesh):
    return jax.shard_map(
        local,
        mesh=mesh,
        in_specs=(
            P("tensor", "dp", None),
            P("dp"),
            P("dp", "tensor"),
            P("dp", None, "tensor"),
            P("tensor", "dp"),
            P("dp", None, "tensor"),
            P("tensor", "dp"),
            P(),
            P(),
            P(),
            P(),
            P("tensor", "dp", None),
        ),
        out_specs=(
            P("tensor", "dp", None),
            P("tensor", "dp", None),
            P("dp", "tensor"),
            P("dp", None, "tensor"),
            P("tensor", "dp"),
            P("dp", None, "tensor"),
            P("tensor", "dp"),
            P(),
            P(),
            P(),
            P(),
        ),
        check_vma=False,
    )
```

```python
import functools

import jax
import jax.numpy as jnp
import numpy as np
from jax import lax
from jax.experimental import pallas as pl
from jax.experimental.pallas import tpu as pltpu
from jax.sharding import PartitionSpec as P

EPS = 1e-05
THETA = 1000000.0
LOG2E = 1.4426950408889634
F32 = jnp.float32
BF16 = jnp.bfloat16
HIGH = lax.Precision.HIGHEST
LANES = 128
VMEM_LIMIT = 56 * 1024 * 1024
BLOCK_LIMIT = 62 * 1024 * 1024
ANY = pl.BlockSpec(memory_space=pl.ANY)
VMEM = pl.BlockSpec(memory_space=pltpu.VMEM)
SMEM = pl.BlockSpec(memory_space=pltpu.SMEM)


def dot(a, b, **kw):
    return lax.dot_general(
        a, b, (((1,), (0,)), ((), ())), preferred_element_type=F32, **kw
    )


def dot_nt(a, b, **kw):
    return lax.dot_general(
        a, b, (((1,), (1,)), ((), ())), preferred_element_type=F32, **kw
    )


def dot_tn(a, b, **kw):
    return lax.dot_general(
        a, b, (((0,), (0,)), ((), ())), preferred_element_type=F32, **kw
    )


def iota(shape, axis):
    return lax.broadcasted_iota(jnp.int32, shape, axis)


def low_half(shape):
    return iota(shape, 1) % LANES < LANES // 2


def head_blocks(scale):
    shape = (LANES, LANES)
    return jnp.where(iota(shape, 0) // 64 == iota(shape, 1) // 64, scale, 0.0).astype(F32)


def head_rows(scale):
    return jnp.where(iota((8, 256), 0) == iota((8, 256), 1) // 64, scale, 0.0).astype(F32)


def partner(values):
    first = iota(values.shape, 1) % 64 < 32
    return jnp.where(first, pltpu.roll(values, LANES - 32, 1), pltpu.roll(values, 32, 1))


def rows_of(index, size):
    if isinstance(index, int):
        return pl.ds(index * size, size)
    return pl.ds(pl.multiple_of(index * size, size), size)


def load_all(sources, targets, sems, first):
    copies = []
    for number, (source, target) in enumerate(zip(sources, targets)):
        copy = pltpu.make_async_copy(source, target, sems.at[first + number])
        copy.start()
        copies.append(copy)
    return copies


def shard_targets(w_refs, ws, me):
    size = w_refs[0].shape[0]
    if len(w_refs) == 1:
        return [ws]
    return [ws.at[rows_of(me ^ slot, size)] for slot in range(len(w_refs))]


def store_slots(whole, out_refs, me):
    if len(out_refs) == 1:
        out_refs[0][...] = whole[...]
        return
    keep_ref, send_ref = out_refs
    size = keep_ref.shape[1]
    for slot in range(2 * keep_ref.shape[0]):
        (send_ref if slot % 2 else keep_ref)[slot // 2] = whole[rows_of(me ^ slot, size), :]


def padded_heads(first, second, low, g, e):
    here = low if e == 0 else jnp.logical_not(low)
    return jnp.where(here, first if g == e else second, 0.0).astype(BF16)


def project_rows(r, size, length, xs, ws, tabs, gains, raw_ref, q_ref, k_ref, v_ref, kp, vp):
    rows = rows_of(r, size)
    cos_ref, sin_ref = tabs
    gq_ref, gk_ref = gains
    mean_of = head_blocks(1.0 / 64)
    low = low_half((size, LANES))
    projected = dot(xs[rows, :], ws[:, :512])
    raw_ref[rows, :] = projected[:, :384]
    cosines, sines = cos_ref[rows, :], sin_ref[rows, :]

    def turned(values, gain):
        mean = dot(values * values, mean_of, precision=HIGH)
        normed = values * lax.rsqrt(mean + EPS) * gain
        return normed * cosines + partner(normed) * sines

    for g in range(2):
        lanes = slice(LANES * g, LANES * (g + 1))
        q_ref[rows, lanes] = turned(projected[:, lanes], gq_ref[...]).astype(BF16)
    keys = turned(projected[:, 256:384], gk_ref[...])
    values = projected[:, 384:512]
    k_ref[rows, :] = keys.astype(BF16)
    v_ref[rows, :] = values.astype(BF16)
    live = r * size + iota((size, LANES), 0) < length
    ones = jnp.where(live, 1.0, 0.0)
    values = jnp.where(live, values, 0.0)
    keys_swap, values_swap = pltpu.roll(keys, 64, 1), pltpu.roll(values, 64, 1)
    for g in range(2):
        for e in range(2):
            kp[2 * g + e, rows, :] = padded_heads(keys, keys_swap, low, g, e)
            vp[2 * g + e, rows, :LANES] = padded_heads(values, values_swap, low, g, e)
            vp[2 * g + e, rows, LANES:] = padded_heads(ones, ones, low, g, e)


def attend_rows(i, size, q_ref, kp, vp, acc, att_ref, lse_ref):
    rows = rows_of(i, size)
    factor = LOG2E / 8.0
    causal = iota((size, size), 1) <= iota((size, size), 0)
    queries = [q_ref[rows, LANES * g : LANES * (g + 1)] for g in range(2)]

    def block(kb, masked):
        cols = rows_of(kb, size)
        sums = []
        for g in range(2):
            total = None
            for e in range(2):
                weights = jnp.exp2(dot_nt(queries[g], kp[2 * g + e, cols, :]) * factor)
                if masked:
                    weights = jnp.where(causal, weights, 0.0)
                part = dot(weights.astype(BF16), vp[2 * g + e, cols, :])
                total = part if total is None else total + part
            sums.append(total)
        return sums

    totals = block(i, True)
    if isinstance(i, int):
        for kb in range(i):
            totals = [total + part for total, part in zip(totals, block(kb, False))]
    else:
        for g, total in enumerate(totals):
            acc[g] = total

        def more(kb, carry):
            for g, total in enumerate(block(kb, False)):
                acc[g] += total
            return carry

        lax.fori_loop(i - i, i, more, None)
        totals = [acc[g] for g in range(2)]
    logs = []
    for g in range(2):
        lanes = slice(LANES * g, LANES * (g + 1))
        summed = totals[g][:, LANES:]
        att_ref[rows, lanes] = (totals[g][:, :LANES] / summed).astype(BF16)
        logs.append(jnp.log2(summed))
    lse_ref[:, rows] = dot_nt(head_rows(1.0 / 64), jnp.concatenate(logs, axis=1), precision=HIGH)


def attn_fwd_kernel(parts, n_w, scal, cos_ref, sin_ref, gq_ref, gk_ref, *refs):
    x_refs, refs = refs[:parts], refs[parts:]
    w_refs, refs = refs[:n_w], refs[n_w:]
    (raw_ref, q_ref, k_ref, v_ref, att_ref, lse_ref, keep_ref, send_ref, xs, ws, kp, vp, acc, sems) = refs
    size = x_refs[0].shape[0]
    me_t, me_d, length = scal[0], scal[1], scal[2]
    copies = load_all(w_refs, shard_targets(w_refs, ws, me_d), sems, 0)
    copies += load_all(x_refs, [xs.at[rows_of(me_t ^ j, size)] for j in range(parts)], sems, n_w)
    for copy in copies:
        copy.wait()

    def project(r, carry):
        project_rows(
            r, size, length, xs, ws, (cos_ref, sin_ref), (gq_ref, gk_ref), raw_ref, q_ref, k_ref, v_ref, kp, vp
        )
        return carry

    def attend(i, carry):
        attend_rows(i, size, q_ref, kp, vp, acc, att_ref, lse_ref)
        return carry

    lax.fori_loop(0, parts, project, 0)
    lax.fori_loop(0, parts, attend, 0)
    for j in range(parts):
        out = dot_nt(att_ref[rows_of(me_t ^ j, size), :], ws[:, 512:])
        (send_ref if j % 2 else keep_ref)[j // 2] = out.astype(BF16)


def attn_fwd(scal, cosines, sines, gq, gk, x_parts, w_parts):
    parts, n_w = len(x_parts), len(w_parts)
    size, width = x_parts[0].shape
    full = parts * size
    cols = w_parts[0].shape[1]
    pair = jax.ShapeDtypeStruct((parts // 2, size, width), BF16)
    return pl.pallas_call(
        functools.partial(attn_fwd_kernel, parts, n_w),
        out_shape=(
            jax.ShapeDtypeStruct((full, 384), F32),
            jax.ShapeDtypeStruct((full, 256), BF16),
            jax.ShapeDtypeStruct((full, 128), BF16),
            jax.ShapeDtypeStruct((full, 128), BF16),
            jax.ShapeDtypeStruct((full, 256), BF16),
            jax.ShapeDtypeStruct((8, full), F32),
            pair,
            pair,
        ),
        in_specs=[SMEM] + [VMEM] * 4 + [ANY] * (parts + n_w),
        out_specs=(VMEM,) * 8,
        scratch_shapes=[
            pltpu.VMEM((full, width), BF16),
            pltpu.VMEM((width, cols), BF16),
            pltpu.VMEM((4, full, LANES), BF16),
            pltpu.VMEM((4, full, 2 * LANES), BF16),
            pltpu.VMEM((2, size, 2 * LANES), F32),
            pltpu.SemaphoreType.DMA((n_w + parts,)),
        ],
        compiler_params=pltpu.CompilerParams(vmem_limit_bytes=VMEM_LIMIT),
        cost_estimate=pl.CostEstimate(flops=8_000_000_000, bytes_accessed=12_000_000, transcendentals=3_000_000),
        name="attention_forward",
    )(scal, cosines, sines, gq, gk, *x_parts, *w_parts)


def prepare_rows(r, size, length, gs, ws, k_ref, v_ref, att_ref, ga, drow, kp, kt, vp):
    rows = rows_of(r, size)
    low = low_half((size, LANES))
    grad = dot(gs[rows, :], ws[:, 512:]).astype(BF16)
    ga[rows, :] = grad
    drow[:, rows] = dot_nt(head_rows(1.0), grad.astype(F32) * att_ref[rows, :].astype(F32), precision=HIGH)
    live = r * size + iota((size, LANES), 0) < length
    keys = jnp.where(live, k_ref[rows, :].astype(F32), 0.0)
    values = jnp.where(live, v_ref[rows, :].astype(F32), 0.0)
    keys_swap, values_swap = pltpu.roll(keys, 64, 1), pltpu.roll(values, 64, 1)
    for g in range(2):
        for e in range(2):
            here = low if e == 0 else jnp.logical_not(low)
            padded = jnp.where(here, keys if g == e else keys_swap, 0.0)
            kp[2 * g + e, rows, :] = padded.astype(BF16)
            kt[2 * g + e, :, rows] = padded.T.astype(BF16)
            vp[2 * g + e, rows, :] = padded_heads(values, values_swap, low, g, e)


def sweep_rows(i, size, q_ref, ga, kp, kt, vp, drow, lrow, acc, dq, dk, dv):
    rows = rows_of(i, size)
    factor = LOG2E / 8.0
    causal = iota((size, size), 0) <= iota((size, size), 1)
    low2 = iota((2 * size, LANES), 0) // size == iota((2 * size, LANES), 1) // 64
    queries, grads, queries2, grads2 = [], [], [], []
    for g in range(2):
        lanes = slice(LANES * g, LANES * (g + 1))
        queries.append(q_ref[rows, lanes])
        grads.append(ga[rows, lanes])
        for source, target in ((queries, queries2), (grads, grads2)):
            both = jnp.concatenate([source[g], source[g]], axis=0)
            target.append(jnp.where(low2, both, jnp.zeros_like(both)))

    def block(kb, masked):
        cols = rows_of(kb, size)
        parts_t = []
        for g in range(2):
            weights2, scores2, turned = [], [], None
            for e in range(2):
                h = 2 * g + e
                weights = jnp.exp2(dot_nt(kp[h, cols, :], queries[g]) * factor - lrow[h : h + 1, rows])
                if masked:
                    weights = jnp.where(causal, weights, 0.0)
                grad_weights = dot_nt(vp[h, cols, :], grads[g])
                grad_scores = (weights * (grad_weights - drow[h : h + 1, rows])).astype(BF16)
                weights2.append(weights.astype(BF16))
                scores2.append(grad_scores)
                part = dot(kt[h, :, cols], grad_scores)
                turned = part if turned is None else turned + part
            dv[g, cols, :] += dot(jnp.concatenate(weights2, axis=1), grads2[g])
            dk[g, cols, :] += dot(jnp.concatenate(scores2, axis=1), queries2[g])
            parts_t.append(turned)
        return parts_t

    if isinstance(i, int):
        totals = block(i, True)
        for kb in range(i):
            totals = [total + part for total, part in zip(totals, block(kb, False))]
        for g in range(2):
            dq[rows, LANES * g : LANES * (g + 1)] = totals[g].T
        return
    for g, total in enumerate(block(i, True)):
        acc[g] = total

    def more(kb, carry):
        for g, total in enumerate(block(kb, False)):
            acc[g] += total
        return carry

    lax.fori_loop(i - i, i, more, None)
    for g in range(2):
        dq[rows, LANES * g : LANES * (g + 1)] = acc[g].T


def unproject_head(rows, grad, tabs, gain_ref, raw_ref, lanes, gp, gains_ref, row):
    cosines, sines = tabs[0][rows, :], tabs[1][rows, :]
    mean_of = head_blocks(1.0 / 64)
    raw = raw_ref[rows, lanes]
    rms = lax.rsqrt(dot(raw * raw, mean_of, precision=HIGH) + EPS)
    turned = grad * cosines - partner(grad) * sines
    gains_ref[row : row + 1, :] += jnp.sum(turned * raw * rms, axis=0, keepdims=True)
    weighted = turned * gain_ref[...]
    inner = dot(raw * weighted, mean_of, precision=HIGH)
    gp[rows, lanes] = (rms * weighted - raw * (rms * rms * rms) * inner).astype(BF16)


def unproject_queries(r, size, tabs, gain_ref, raw_ref, dq, gp, gains_ref):
    rows = rows_of(r, size)
    for g in range(2):
        lanes = slice(LANES * g, LANES * (g + 1))
        unproject_head(rows, dq[rows, lanes] * 0.125, tabs, gain_ref, raw_ref, lanes, gp, gains_ref, 0)


def unproject_pairs(r, size, length, tabs, gain_ref, raw_ref, dk, dv, gp, gains_ref):
    rows = rows_of(r, size)
    low = low_half((size, LANES))
    live = r * size + iota((size, LANES), 0) < length

    def folded(ref):
        first, second = ref[0, rows, :], ref[1, rows, :]
        both = jnp.where(low, first + pltpu.roll(first, 64, 1), second + pltpu.roll(second, 64, 1))
        return jnp.where(live, both, 0.0)

    unproject_head(rows, folded(dk) * 0.125, tabs, gain_ref, raw_ref, slice(256, 384), gp, gains_ref, 1)
    gp[rows, 384:512] = folded(dv).astype(BF16)


def attn_bwd_kernel(parts, n_w, scal, cos_ref, sin_ref, gq_ref, gk_ref, raw_ref, q_ref, k_ref, v_ref, att_ref, lse_ref, *refs):
    x_refs, refs = refs[:parts], refs[parts:]
    r_refs, refs = refs[:parts], refs[parts:]
    w_refs, refs = refs[:n_w], refs[n_w:]
    n_g = 1 if n_w == 1 else 2
    keep_ref, send_ref, gains_ref = refs[:3]
    g_refs, refs = refs[3 : 3 + n_g], refs[3 + n_g :]
    xs, gs, ws, kp, vp, kt, ga, dq, dk, dv, gp, whole, drow, acc, sems = refs
    size = x_refs[0].shape[0]
    me_t, me_d, length = scal[0], scal[1], scal[2]
    copies = load_all(w_refs, shard_targets(w_refs, ws, me_d), sems, 0)
    copies += load_all(r_refs, [gs.at[rows_of(me_t ^ j, size)] for j in range(parts)], sems, n_w)
    copies += load_all(x_refs, [xs.at[rows_of(me_t ^ j, size)] for j in range(parts)], sems, n_w + parts)
    for copy in copies:
        copy.wait()

    def prepare(r, carry):
        prepare_rows(r, size, length, gs, ws, k_ref, v_ref, att_ref, ga, drow, kp, kt, vp)
        return carry

    def sweep(i, carry):
        sweep_rows(i, size, q_ref, ga, kp, kt, vp, drow, lse_ref, acc, dq, dk, dv)
        return carry

    def unproject(r, carry):
        unproject_queries(r, size, (cos_ref, sin_ref), gq_ref, raw_ref, dq, gp, gains_ref)
        unproject_pairs(r, size, length, (cos_ref, sin_ref), gk_ref, raw_ref, dk, dv, gp, gains_ref)
        return carry

    lax.fori_loop(0, parts, prepare, 0)
    dk[...] = jnp.zeros_like(dk)
    dv[...] = jnp.zeros_like(dv)
    lax.fori_loop(0, parts, sweep, 0)
    gains_ref[...] = jnp.zeros_like(gains_ref)
    lax.fori_loop(0, parts, unproject, 0)
    for j in range(parts):
        out = dot_nt(gp[rows_of(me_t ^ j, size), :], ws[:, :512])
        (send_ref if j % 2 else keep_ref)[j // 2] = out.astype(BF16)

    def weigh(b, carry):
        rows = rows_of(b, 256)
        whole[rows, :512] = dot_tn(xs[:, rows], gp[...]).astype(BF16)
        whole[rows, 512:] = dot_tn(gs[:, rows], att_ref[...]).astype(BF16)
        return carry

    lax.fori_loop(0, whole.shape[0] // 256, weigh, 0)
    store_slots(whole, g_refs, me_d)


def slot_shapes(n_w, width, cols):
    if n_w == 1:
        return (jax.ShapeDtypeStruct((width, cols), BF16),)
    return (jax.ShapeDtypeStruct((n_w // 2, width // n_w, cols), BF16),) * 2


def attn_bwd(scal, cosines, sines, gq, gk, saved, x_parts, r_parts, w_parts):
    parts, n_w = len(x_parts), len(w_parts)
    size, width = x_parts[0].shape
    full = parts * size
    cols = w_parts[0].shape[1]
    pair = jax.ShapeDtypeStruct((parts // 2, size, width), BF16)
    g_shapes = slot_shapes(n_w, width, cols)
    outs = pl.pallas_call(
        functools.partial(attn_bwd_kernel, parts, n_w),
        out_shape=(pair, pair, jax.ShapeDtypeStruct((8, LANES), F32)) + g_shapes,
        in_specs=[SMEM] + [VMEM] * 10 + [ANY] * (2 * parts + n_w),
        out_specs=(VMEM,) * (3 + len(g_shapes)),
        scratch_shapes=[
            pltpu.VMEM((full, width), BF16),
            pltpu.VMEM((full, width), BF16),
            pltpu.VMEM((width, cols), BF16),
            pltpu.VMEM((4, full, LANES), BF16),
            pltpu.VMEM((4, full, LANES), BF16),
            pltpu.VMEM((4, LANES, full), BF16),
            pltpu.VMEM((full, 256), BF16),
            pltpu.VMEM((full, 256), F32),
            pltpu.VMEM((2, full, LANES), F32),
            pltpu.VMEM((2, full, LANES), F32),
            pltpu.VMEM((full, 512), BF16),
            pltpu.VMEM((width, cols), BF16),
            pltpu.VMEM((8, full), F32),
            pltpu.VMEM((2, LANES, size), F32),
            pltpu.SemaphoreType.DMA((n_w + 2 * parts,)),
        ],
        compiler_params=pltpu.CompilerParams(vmem_limit_bytes=VMEM_LIMIT),
        cost_estimate=pl.CostEstimate(flops=14_000_000_000, bytes_accessed=15_000_000, transcendentals=3_000_000),
        name="attention_backward",
    )(scal, cosines, sines, gq, gk, *saved, *x_parts, *r_parts, *w_parts)
    return outs[0], outs[1], outs[2], outs[3:]


def ff_kernel(n_x, n_w, scal, *refs):
    x_refs, refs = refs[:n_x], refs[n_x:]
    u_refs, refs = refs[:n_x], refs[n_x:]
    w_refs, refs = refs[:n_w], refs[n_w:]
    n_g = 1 if n_w == 1 else 2
    hid_ref, ggu_ref = refs[:2]
    g_refs, refs = refs[2 : 2 + n_g], refs[2 + n_g :]
    xs, us, ws, whole, sems = refs
    size = x_refs[0].shape[0]
    me_d = scal[1]
    cols = ws.shape[1] // 3
    copies = load_all(w_refs, shard_targets(w_refs, ws, me_d), sems, 0)
    x_copies = load_all(x_refs, [xs.at[pl.ds(j * size, size)] for j in range(n_x)], sems, n_w)
    u_copies = load_all(u_refs, [us.at[pl.ds(j * size, size)] for j in range(n_x)], sems, n_w + n_x)
    for copy in copies + x_copies + u_copies:
        copy.wait()

    def tokens(r, carry):
        rows = rows_of(r, size)
        gate_up = dot(xs[rows, :], ws[:, : 2 * cols])
        grad = dot(us[rows, :], ws[:, 2 * cols :])
        gate, up = gate_up[:, :cols], gate_up[:, cols:]
        sig = 1.0 / (1.0 + jnp.exp2(gate * -LOG2E))
        silu = gate * sig
        hid_ref[rows, :] = (silu * up).astype(BF16)
        ggu_ref[rows, :cols] = (grad * up * (sig + silu * (1.0 - sig))).astype(BF16)
        ggu_ref[rows, cols:] = (grad * silu).astype(BF16)
        return carry

    lax.fori_loop(0, n_x, tokens, 0)

    def weigh(b, carry):
        rows = rows_of(b, 256)
        whole[rows, : 2 * cols] = dot_tn(xs[:, rows], ggu_ref[...]).astype(BF16)
        whole[rows, 2 * cols :] = dot_tn(us[:, rows], hid_ref[...]).astype(BF16)
        return carry

    lax.fori_loop(0, whole.shape[0] // 256, weigh, 0)
    store_slots(whole, g_refs, me_d)


def feed_forward(scal, x_parts, u_parts, w_parts):
    n_x, n_w = len(x_parts), len(w_parts)
    size, width = x_parts[0].shape
    full = n_x * size
    wide = w_parts[0].shape[1]
    cols = wide // 3
    g_shapes = slot_shapes(n_w, width, wide)
    outs = pl.pallas_call(
        functools.partial(ff_kernel, n_x, n_w),
        out_shape=(
            jax.ShapeDtypeStruct((full, cols), BF16),
            jax.ShapeDtypeStruct((full, 2 * cols), BF16),
        )
        + g_shapes,
        in_specs=[SMEM] + [ANY] * (2 * n_x + n_w),
        out_specs=(VMEM,) * (2 + len(g_shapes)),
        scratch_shapes=[
            pltpu.VMEM((full, width), BF16),
            pltpu.VMEM((full, width), BF16),
            pltpu.VMEM((width, wide), BF16),
            pltpu.VMEM((width, wide), BF16),
            pltpu.SemaphoreType.DMA((n_w + 2 * n_x,)),
        ],
        compiler_params=pltpu.CompilerParams(vmem_limit_bytes=VMEM_LIMIT),
        cost_estimate=pl.CostEstimate(flops=4 * full * width * wide, bytes_accessed=20_000_000, transcendentals=full * cols),
        name="feed_forward",
    )(scal, *x_parts, *u_parts, *w_parts)
    return outs[0], outs[1], outs[2:]


def ff_out_kernel(parts, n_c, n_w, seq, scal, *refs):
    hid_refs, refs = refs[:n_c], refs[n_c:]
    ggu_refs, refs = refs[:n_c], refs[n_c:]
    w_refs, refs = refs[: n_c * n_w], refs[n_c * n_w :]
    ykeep_ref, ysend_ref, gkeep_ref, gsend_ref, hs, gs, ws, sems = refs
    size = ykeep_ref.shape[1]
    full = parts * size
    me_d = scal[1]
    wide = ws.shape[2]
    cols = wide // 3
    copies = []
    first = 0
    for c in range(n_c):
        targets = shard_targets(w_refs[c * n_w : (c + 1) * n_w], ws.at[c], me_d)
        copies += load_all(w_refs[c * n_w : (c + 1) * n_w], targets, sems, first)
        first += n_w
    mine = pl.ds(seq * full, full)
    copies += load_all([ref.at[mine] for ref in ggu_refs], [gs.at[c] for c in range(n_c)], sems, first)
    copies += load_all([ref.at[mine] for ref in hid_refs], [hs.at[c] for c in range(n_c)], sems, first + n_c)
    for copy in copies:
        copy.wait()
    for j in range(parts):
        rows = pl.ds(j * size, size)
        grad = sum(dot_nt(gs[c, rows, :], ws[c, :, : 2 * cols]) for c in range(n_c))
        (gsend_ref if j % 2 else gkeep_ref)[j // 2] = grad.astype(BF16)
        out = sum(dot_nt(hs[c, rows, :], ws[c, :, 2 * cols :]) for c in range(n_c))
        (ysend_ref if j % 2 else ykeep_ref)[j // 2] = out.astype(BF16)


def ff_out(seq, scal, parts, size, hids, ggus, w_chunks):
    n_c, n_w = len(w_chunks), len(w_chunks[0])
    wide = w_chunks[0][0].shape[1]
    width = w_chunks[0][0].shape[0] * n_w
    full = parts * size
    cols = wide // 3
    pair = jax.ShapeDtypeStruct((parts // 2, size, width), BF16)
    return pl.pallas_call(
        functools.partial(ff_out_kernel, parts, n_c, n_w, seq),
        out_shape=(pair,) * 4,
        in_specs=[SMEM] + [ANY] * (2 * n_c + n_c * n_w),
        out_specs=(VMEM,) * 4,
        scratch_shapes=[
            pltpu.VMEM((n_c, full, cols), BF16),
            pltpu.VMEM((n_c, full, 2 * cols), BF16),
            pltpu.VMEM((n_c, width, wide), BF16),
            pltpu.SemaphoreType.DMA((n_c * n_w + 2 * n_c,)),
        ],
        compiler_params=pltpu.CompilerParams(vmem_limit_bytes=VMEM_LIMIT),
        cost_estimate=pl.CostEstimate(flops=2 * full * width * wide * n_c, bytes_accessed=22_000_000, transcendentals=0),
        name="feed_forward_out",
    )(scal, *hids, *ggus, *[shard for chunk in w_chunks for shard in chunk])


def flip(index, bits):
    for bit in (1, 2, 4):
        if bits & bit:
            index = index + bit - 2 * bit * lax.rem(lax.div(index, bit), 2)
    return index


class Spot:
    def __init__(self, index, choices):
        self.index = index
        self.flips = {0: index}
        for bits in choices:
            self.flips[bits] = flip(index, bits)


def spots():
    me_t = Spot(lax.axis_index("tensor"), (1, 2, 3))
    me_d = Spot(lax.axis_index("dp"), (1, 2, 3, 4, 5, 6, 7))
    me_d.x = lax.rem(me_d.index, 2)
    me_d.beside = 1 - me_d.x
    me_d.z = Spot(lax.div(me_d.index, 2), (1, 2, 3))
    return me_t, me_d


def greet(barrier, me_d, me_t, along_d, along_t):
    devices = [{"dp": me_d.flips[bits]} for bits in along_d]
    devices += [{"tensor": me_t.flips[bits]} for bits in along_t]
    for device in devices:
        pl.semaphore_signal(barrier, inc=1, device_id=device, device_id_type=pl.DeviceIdType.MESH)
    return lambda: pl.semaphore_wait(barrier, len(devices))


def remote(source, target, sems, number, device):
    return pltpu.make_async_remote_copy(
        src_ref=source,
        dst_ref=target,
        send_sem=sems.at[0, number],
        recv_sem=sems.at[1, number],
        device_id=device,
        device_id_type=pl.DeviceIdType.MESH,
    )


class Remote:
    LIMIT = 128

    def __init__(self, sems):
        self.sems, self.used = sems, 0

    def __call__(self, source, target, device):
        assert self.used < self.LIMIT
        self.used += 1
        return remote(source, target, self.sems, self.used - 1, device)


class Local:
    LIMIT = 64

    def __init__(self, sems):
        self.sems, self.used = sems, 0

    def make(self, source, target):
        assert self.used < self.LIMIT
        self.used += 1
        return pltpu.make_async_copy(source, target, self.sems.at[self.used - 1])

    def __call__(self, source, target):
        copy = self.make(source, target)
        copy.start()
        return copy


COPY_SEMS = [
    pltpu.SemaphoreType.DMA((2, Remote.LIMIT)),
    pltpu.SemaphoreType.DMA((Local.LIMIT,)),
]


class ShardGather:
    def __init__(self, shard, place, send, me_d, direct=False):
        def pass_on(bits, target):
            there = place(me_d.flips[bits])
            return send(there, there, {"dp": me_d.flips[target]})

        mine = place(me_d.index)
        self.beside, self.next, self.across = [send(shard, mine, {"dp": me_d.flips[bits]}) for bits in (1, 2, 4)]
        self.direct = direct
        self.on = send(shard, mine, {"dp": me_d.flips[6]}) if direct else pass_on(4, 2)
        self.passed = [pass_on(bits, 1) for bits in (4, 2, 6)]

    def start_x(self):
        self.beside.start()

    def start_z(self):
        self.next.start()
        self.across.start()
        if self.direct:
            self.on.start()

    def forward(self):
        self.next.wait_recv()
        self.passed[1].start()
        self.across.wait_recv()
        if not self.direct:
            self.on.start()
        self.passed[0].start()

    def forward_last(self):
        self.on.wait_recv()
        self.passed[2].start()

    def arrive(self):
        self.beside.wait_recv()
        for copy in self.passed:
            copy.wait_recv()

    def drain(self):
        for copy in [self.beside, self.next, self.across, self.on] + self.passed:
            copy.wait_send()


class TokenGather:
    def __init__(self, block, whole, send, me_t):
        size = block.shape[0]
        mine = whole.at[rows_of(me_t.index, size)]
        there = whole.at[rows_of(me_t.flips[2], size)]
        near = {"tensor": me_t.flips[1]}
        self.near = send(block, mine, near)
        self.far = send(block, mine, {"tensor": me_t.flips[2]})
        self.passed = send(there, there, near)

    def start(self):
        self.far.start()
        self.near.start()

    def forward(self):
        self.far.wait_recv()
        self.passed.start()

    def arrive(self):
        self.near.wait_recv()
        self.passed.wait_recv()

    def drain(self):
        for copy in (self.near, self.far, self.passed):
            copy.wait_send()


class TokenReduce:
    def __init__(self, blocks, near, far, send, me_t, mine=None):
        device = {"tensor": me_t.flips[1]}
        self.blocks, self.near_ref, self.far_ref, self.mine = blocks, near, far, mine
        self.places = (me_t.index, me_t.flips[2])
        self.size = far.shape[0]
        self.near = [
            send(blocks.at[rows_of(me_t.flips[1 + 2 * n], self.size)], near.at[n], device) for n in range(2)
        ]
        self.far = send(near.at[1], far, {"tensor": me_t.flips[2]})

    def load(self, here):
        return [here(self.blocks.at[rows_of(place, self.size)], self.mine.at[n]) for n, place in enumerate(self.places)]

    def start(self, *which):
        for n in which or (1, 0):
            self.near[n].start()

    def part(self, n, rows):
        if self.mine is not None:
            return self.mine[n, rows, :].astype(F32)
        start = pl.multiple_of(self.places[n] * self.size + rows.start, 32)
        return self.blocks[pl.ds(start, rows.size), :].astype(F32)

    def middle(self):
        self.near[1].wait_recv()

        def step(rows):
            total = self.part(1, rows) + self.near_ref[1, rows, :].astype(F32)
            self.near_ref[1, rows, :] = total.astype(BF16)

        by_rows(self.size, 32, step)
        self.far.start()

    def arrive(self):
        self.near[0].wait_recv()
        self.far.wait_recv()

    def rows(self, rows):
        total = self.part(0, rows) + self.near_ref[0, rows, :].astype(F32)
        return total + self.far_ref[rows, :].astype(F32)

    def drain(self):
        for copy in self.near + [self.far]:
            copy.wait_send()


class ShardNear:
    def __init__(self, whole, near, out, send, me_d, mine=None):
        self.whole, self.near_ref, self.out, self.mine = whole, near, out, mine
        self.z, self.x = me_d.z, me_d.x
        self.size = near.shape[1]
        self.near = send(whole.at[:, me_d.beside], near, {"dp": me_d.flips[1]})

    def load(self, here):
        return [here(self.whole.at[:, self.x], self.mine)]

    def start(self):
        self.near.start()

    def part(self, there, rows):
        if self.mine is not None:
            return self.mine[there, rows, :].astype(F32)
        return self.whole[there, self.x, rows, :].astype(F32)

    def middle(self, far=None):
        self.near.wait_recv()
        for k in (1, 3, 2, 0):
            there = self.z.flips[k]

            def step(rows):
                total = self.part(there, rows) + self.near_ref[there, rows, :].astype(F32)
                if k:
                    self.near_ref[there, rows, :] = total.astype(BF16)
                else:
                    self.out[rows, :] = total

            by_rows(self.size, 32, step)
            if k and far is not None:
                far.ready(k)

    def drain(self):
        self.near.wait_send()


class ShardFar:
    def __init__(self, near, far, out, send, me_d):
        self.far_ref, self.out = far, out
        self.size = far.shape[1]
        self.far = [send(near.at[me_d.z.flips[k]], far.at[k - 1], {"dp": me_d.flips[2 * k]}) for k in (1, 2, 3)]
        self.last = self.far
        self.terms = (0, 1, 2)

    def ready(self, k):
        self.far[k - 1].start()

    def finish(self):
        for copy in self.last:
            copy.wait_recv()

        def step(rows):
            total = self.out[rows, :]
            for k in self.terms:
                total = total + self.far_ref[k, rows, :].astype(F32)
            self.out[rows, :] = total

        by_rows(self.size, 32, step)

    def drain(self):
        for copy in self.far:
            copy.wait_send()


class ShardHalves(ShardFar):
    def __init__(self, near, far, out, send, me_d):
        self.near_ref, self.far_ref, self.out = near, far, out
        self.size = far.shape[1]
        z = me_d.z.flips
        self.across = z[2]
        self.far = [
            send(near.at[z[1]], far.at[0], {"dp": me_d.flips[2]}),
            send(near.at[z[3]], far.at[1], {"dp": me_d.flips[2]}),
            send(near.at[z[2]], far.at[2], {"dp": me_d.flips[4]}),
        ]
        self.last = (self.far[0], self.far[2])
        self.terms = (0, 2)

    def ready(self, k):
        if k != 2:
            self.far[k // 2].start()

    def middle(self):
        self.far[1].wait_recv()

        def step(rows):
            total = self.near_ref[self.across, rows, :].astype(F32) + self.far_ref[1, rows, :].astype(F32)
            self.near_ref[self.across, rows, :] = total.astype(BF16)

        by_rows(self.size, 32, step)
        self.far[2].start()


def by_rows(count, step, body):
    def run(b, carry):
        body(rows_of(b, step))
        return carry

    lax.fori_loop(0, count // step, run, None)


def loop(start, stop, body, unroll=False):
    def run(i, carry):
        body(i)
        return carry

    lax.fori_loop(start, stop, run, None, unroll=unroll)


def rms_factor(values):
    return lax.rsqrt(jnp.mean(values * values, axis=-1, keepdims=True) + EPS)


def shape(dims, kind):
    return jax.ShapeDtypeStruct(dims, kind)


def block_kernel(
    lengths, in_ref, cot_ref, qw_ref, kv_ref, ow_ref, iw_ref, dw_ref, cos_ref, sin_ref, qg_ref, kg_ref, mg_ref, dg_ref,
    normed_out, raw_out, q_out, k_out, v_out, att_out, lse_out, r_out, blk_out,
    ig_ref, awg_ref, ffg_ref, sums_ref,
    x_ref, gq_ref, gk_ref, xs, ws, dn, us, outp, onear, ofar, resid, wnear, wfar, whole, dgain, put, got_t, got_d, free,
    sems, local_sems,
):
    seqs, full, width = xs.shape
    size = resid.shape[1]
    parts = full // size
    n_c = 3
    shard = qw_ref.shape[0]
    cols = iw_ref.shape[2] // n_c
    wide = 3 * cols
    me_t, me_d = spots()
    send, here = Remote(sems), Local(local_sems)
    mine_t, mine_d = rows_of(me_t.index, size), rows_of(me_d.index, shard)
    halves = [pl.ds(s * full, full) for s in range(seqs)]
    own_rows = [rows_of(s * parts + me_t.index, size) for s in range(seqs)]
    every_row = pl.ds(0, seqs * full)
    lanes_of = [slice(width * s, width * (s + 1)) for s in range(seqs)]

    def wait(copies):
        for copy in copies:
            copy.wait()

    pro_w = [
        ShardGather(ws.at[mine_d, lanes], lambda i, lanes=lanes: ws.at[rows_of(i, shard), lanes], send, me_d)
        for lanes in (slice(0, 256), slice(256, 512))
    ]
    out_w = ShardGather(ws.at[mine_d, 512:], lambda i: ws.at[rows_of(i, shard), 512:], send, me_d, True)
    normed = [TokenGather(xs.at[s, mine_t], xs.at[s], send, me_t) for s in range(seqs)]
    ups = [TokenGather(us.at[own_rows[s]], us.at[halves[s]], send, me_t) for s in range(seqs)]
    denses = [TokenGather(dn.at[own_rows[s]], dn.at[halves[s]], send, me_t) for s in range(seqs)]
    out_places = (outp, xs.at[0])
    back_places = (outp, xs.at[1])
    norm_places = (outp, dn.at[halves[0]])
    outs, backs, norms = [
        [TokenReduce(places[s], onear.at[s], ofar.at[s], send, me_t) for s in range(seqs)]
        for places in (out_places, back_places, norm_places)
    ]
    lows = [xs.at[0, pl.ds(s * size, size)] for s in range(seqs)]
    resids = [TokenGather(lows[s], r_out.at[s], send, me_t) for s in range(seqs)]
    ff_sums = [ffg_ref.at[:, wide * c : wide * (c + 1)] for c in range(n_c)]
    near = [ShardNear(whole.at[c], wnear.at[c], ff_sums[c], send, me_d) for c in range(2)]
    far = [ShardHalves(wnear.at[c], wfar.at[c], ff_sums[c], send, me_d) for c in range(2)]
    steps = [
        [send(put.at[0], got_t.at[me_t.index], {"tensor": me_t.flips[bits]}) for bits in (1, 2, 3)],
        [send(put.at[1], got_d.at[me_d.index], {"dp": me_d.flips[bits]}) for bits in (1, 2, 3, 4, 5, 6, 7)],
    ]
    load_own = [here.make(us.at[own_rows[s]], xs.at[0, pl.ds((seqs + s) * size, size)]) for s in range(seqs)]
    keeps = [here.make(xs.at[s], normed_out.at[s]) for s in range(seqs)]
    backup = [here.make(normed_out.at[s], xs.at[s]) for s in range(seqs)]
    low_keeps = [here.make(lows[s], r_out.at[s, mine_t]) for s in range(seqs)]

    def after_out(s):
        outs[s].arrive()
        outs[s].drain()

        def norm(rows):
            values = x_ref[rows, lanes_of[s]].astype(F32) + outs[s].rows(rows)
            resid[s, rows, :] = values
            target = pl.ds(pl.multiple_of((s * parts + me_t.index) * size + rows.start, 32), 32)
            dn[target, :] = (values * rms_factor(values) * dg_ref[...]).astype(BF16)

        by_rows(size, 32, norm)
        denses[s].start()
        if s:
            for copy in load_own:
                copy.start()

    def after_back(s):
        backs[s].arrive()
        backs[s].drain()

        def step(rows):
            grad = backs[s].rows(rows)
            values = resid[s, rows, :]
            factor = rms_factor(values)
            product = grad * values * factor
            dgain[...] += jnp.sum(product.reshape(-1, 8, width), axis=0)
            weighted = grad * dg_ref[...]
            inner = jnp.mean(values * weighted, axis=-1, keepdims=True)
            place = pl.ds(pl.multiple_of((seqs + s) * size + rows.start, 32), 32)
            total = xs[0, place, :].astype(F32) + factor * weighted - values * (factor * factor * factor) * inner
            ig_ref[rows, lanes_of[s]] = total
            lows[s][rows, :] = total.astype(BF16)

        by_rows(size, 32, step)
        resids[s].start()
        low_keeps[s].start()

    def after_norm(s):
        norms[s].arrive()

        def step(rows):
            values = x_ref[rows, lanes_of[s]].astype(F32)
            factor = rms_factor(values)
            weighted = norms[s].rows(rows) * mg_ref[...]
            inner = jnp.mean(values * weighted, axis=-1, keepdims=True)
            ig_ref[rows, lanes_of[s]] += factor * weighted - values * (factor * factor * factor) * inner

        by_rows(size, 32, step)

    def until_backward(wf):
        ff_w = [ShardGather(wf.at[c, mine_d], lambda i, c=c: wf.at[c, rows_of(i, shard)], send, me_d) for c in range(n_c)]

        def attention(kp, vp, acc, raw, q, k, v, att, lse, inb, cotb, kvb, owb, iwb, dwb):
            kept = ((raw, raw_out), (q, q_out), (k, k_out), (v, v_out), (att, att_out), (lse, lse_out))
            flushes = []

            def project(s):
                loop(0, parts, lambda r: project_rows(
                    r, size, lengths[s], xs.at[s], ws, (cos_ref, sin_ref), (gq_ref, gk_ref),
                    raw.at[s], q.at[s], k.at[s], v.at[s], kp, vp,
                ), True)

            def attend(s, start, stop):
                for i in range(start, stop):
                    attend_rows(i, size, q.at[s], kp, vp, acc, att.at[s], lse.at[s])

            def out(s):
                for n, bits in enumerate((3, 1, 2, 0)):
                    rows = rows_of(me_t.flips[bits], size)
                    out_places[s][rows, :] = dot_nt(att[s, rows, :], ws[:, 512:]).astype(BF16)
                    if n < 2:
                        outs[s].start(1 - n)

            def first_rows(s):
                def step(rows):
                    mine = inb[rows, :, :].astype(F32)[:, s, :]
                    target = pl.ds(pl.multiple_of(me_t.index * size + rows.start, 32), 32)
                    x_ref[rows, lanes_of[s]] = mine.astype(BF16)
                    xs[s, target, :] = (mine * rms_factor(mine) * mg_ref[...]).astype(BF16)

                by_rows(size, 32, step)

            def upstream_rows(rows):
                grads = cotb[rows, :, :].astype(F32)
                place = me_t.index * size + rows.start + iota((32, width), 0)
                for s in range(seqs):
                    target = pl.ds(pl.multiple_of((s * parts + me_t.index) * size + rows.start, 32), 32)
                    us[target, :] = jnp.where(place < lengths[s], grads[:, s, :], 0.0).astype(BF16)

            def inner_rows(rows):
                both = iwb[rows, :, :].astype(F32)
                target = pl.ds(pl.multiple_of(me_d.index * shard + rows.start, 32), 32)
                for c in range(n_c):
                    for n in range(2):
                        part = both[:, n, cols * c : cols * (c + 1)]
                        wf[c, target, cols * n : cols * (n + 1)] = part.astype(BF16)

            entered = greet(
                pltpu.get_barrier_semaphore(), me_d, me_t, (1, 2, 3, 4, 5, 6, 7), (1, 2, 3)
            )
            load_a = [here(qw_ref, ws.at[mine_d, :256]), here(kv_ref, kvb)]
            load_x = here(in_ref, inb)
            load_o = here(ow_ref, owb)
            load_f = [here(iw_ref, iwb), here(dw_ref, dwb)]
            load_u = here(cot_ref, cotb)
            wait(load_a)
            pair = kvb[...].astype(F32)
            for n in range(2):
                ws[mine_d, 256 + 128 * n : 384 + 128 * n] = pair[:, n, :].astype(BF16)
            load_x.wait()
            first_rows(0)
            entered()
            for exchange in pro_w:
                exchange.start_z()
                exchange.start_x()
            normed[0].start()
            for source, target in ((qg_ref, gq_ref), (kg_ref, gk_ref)):
                target[...] = jnp.concatenate([source[...], source[...]], axis=1)
            first_rows(1)
            for exchange in pro_w:
                exchange.forward()
            load_o.wait()
            ws[mine_d, 512:] = owb[...].astype(F32).T.astype(BF16)
            wait(load_f)
            for c in range(n_c):
                wf[c, mine_d, 2 * cols :] = dwb[cols * c : cols * (c + 1), :].astype(F32).T.astype(BF16)
            by_rows(shard, 32, inner_rows)
            for exchange in pro_w:
                exchange.forward_last()
            out_w.start_z()
            out_w.start_x()
            normed[0].forward()
            normed[1].start()
            normed[0].arrive()
            ff_w[0].start_z()
            load_u.wait()
            by_rows(size, 32, upstream_rows)
            for exchange in pro_w:
                exchange.arrive()
            ff_w[0].start_x()
            project(0)
            keeps[0].start()
            out_w.forward()
            out_w.forward_last()
            attend(0, 0, 3)
            normed[1].forward()
            ups[0].start()
            attend(0, 3, parts)
            ff_w[0].forward()
            out_w.arrive()
            out(0)
            outs[0].middle()
            for source, target in kept:
                flushes.append(here(source.at[0], target.at[0]))
            normed[1].arrive()
            project(1)
            keeps[1].start()
            ff_w[0].forward_last()
            ff_w[1].start_z()
            ff_w[1].start_x()
            attend(1, 0, 3)
            ups[0].forward()
            attend(1, 3, parts)
            normed[0].drain()
            keeps[0].wait()
            out(1)
            for source, target in kept:
                flushes.append(here(source.at[1], target.at[1]))
            after_out(0)
            outs[1].middle()
            ff_w[1].forward()
            ff_w[2].start_z()
            ff_w[2].start_x()
            wait(flushes)

        pl.run_scoped(
            attention,
            pltpu.VMEM((4, full, LANES), BF16),
            pltpu.VMEM((4, full, 2 * LANES), BF16),
            pltpu.VMEM((2, size, 2 * LANES), F32),
            pltpu.VMEM((seqs, full, 384), F32),
            pltpu.VMEM((seqs, full, 256), BF16),
            pltpu.VMEM((seqs, full, 128), BF16),
            pltpu.VMEM((seqs, full, 128), BF16),
            pltpu.VMEM((seqs, full, 256), BF16),
            pltpu.VMEM((seqs, 8, full), F32),
            pltpu.VMEM(in_ref.shape, BF16),
            pltpu.VMEM(cot_ref.shape, BF16),
            pltpu.VMEM(kv_ref.shape, BF16),
            pltpu.VMEM(ow_ref.shape, BF16),
            pltpu.VMEM(iw_ref.shape, BF16),
            pltpu.VMEM(dw_ref.shape, BF16),
        )

        def feed_forward(hid, ggu):
            def tokens(c, s):
                def run(r):
                    rows = rows_of(r, size)
                    gate_up = dot(dn[rows, :], wf[c, :, : 2 * cols])
                    grad = dot(us[rows, :], wf[c, :, 2 * cols :])
                    gate, up = gate_up[:, :cols], gate_up[:, cols:]
                    sig = 1.0 / (1.0 + jnp.exp2(gate * -LOG2E))
                    silu = gate * sig
                    hid[c, rows, :] = (silu * up).astype(BF16)
                    ggu[c, rows, :cols] = (grad * up * (sig + silu * (1.0 - sig))).astype(BF16)
                    ggu[c, rows, cols:] = (grad * silu).astype(BF16)

                loop(s * parts, (s + 1) * parts, run, True)

            def weigh(c, tokens, more=False):
                def run(b):
                    rows = rows_of(b, 256)
                    dims = whole.shape[2:4]
                    inner = dot_tn(dn[tokens, rows], ggu[c, tokens, :]).reshape(dims + (2 * cols,))
                    down = dot_tn(us[tokens, rows], hid[c, tokens, :]).reshape(dims + (cols,))
                    if more:
                        inner = inner + whole[c % 2, b, :, :, : 2 * cols].astype(F32)
                        down = down + whole[c % 2, b, :, :, 2 * cols :].astype(F32)
                    whole[c % 2, b, :, :, : 2 * cols] = inner.astype(BF16)
                    whole[c % 2, b, :, :, 2 * cols :] = down.astype(BF16)

                loop(0, whole.shape[1], run)

            def grad_blocks(s):
                for n, bits in enumerate((3, 1, 2, 0)):
                    rows = rows_of(s * parts + me_t.flips[bits], size)
                    left = jnp.concatenate([ggu[c, rows, :] for c in range(n_c)], axis=1)
                    right = jnp.concatenate([wf[c, :, : 2 * cols] for c in range(n_c)], axis=1)
                    total = dot_nt(left, right)
                    back_places[s][rows_of(me_t.flips[bits], size), :] = total.astype(BF16)
                    if n < 2:
                        backs[s].start(1 - n)

            def down_block(r):
                rows = rows_of(r, size)
                left = jnp.concatenate([hid[c, rows, :] for c in range(n_c)], axis=1)
                right = jnp.concatenate([wf[c, :, 2 * cols :] for c in range(n_c)], axis=1)
                total = dot_nt(left, right)
                us[rows, :] = total.astype(BF16)

            denses[0].forward()
            ups[1].start()
            ff_w[1].forward_last()
            ups[0].arrive()
            ff_w[0].arrive()
            denses[0].arrive()
            tokens(0, 0)
            ff_w[2].forward()
            weigh(0, halves[0])
            after_out(1)
            ff_w[1].arrive()
            tokens(1, 0)
            ff_w[2].forward_last()
            weigh(1, halves[0])
            ups[1].forward()
            denses[1].forward()
            ups[1].arrive()
            denses[1].arrive()
            tokens(0, 1)
            weigh(0, halves[1], True)
            near[0].start()
            ff_w[2].arrive()
            tokens(2, 0)
            grad_blocks(0)
            backs[0].middle()
            tokens(1, 1)
            weigh(1, halves[1], True)
            tokens(2, 1)
            normed[1].drain()
            keeps[1].wait()
            dgain[...] = jnp.zeros_like(dgain)
            wait(load_own)
            grad_blocks(1)
            after_back(0)
            near[0].middle(far[0])
            near[1].start()
            near[0].drain()
            backs[1].middle()
            weigh(2, every_row)
            ups[0].drain()
            ups[1].drain()
            loop(0, parts, down_block, True)
            loop(parts, seqs * parts, down_block, True)
            resids[0].forward()
            far[0].middle()
            for exchange in ff_w + denses:
                exchange.drain()

        pl.run_scoped(
            feed_forward,
            pltpu.VMEM((n_c, seqs * full, cols), BF16),
            pltpu.VMEM((n_c, seqs * full, 2 * cols), BF16),
        )

    pl.run_scoped(until_backward, pltpu.VMEM((n_c, 8 * shard, wide), BF16))

    def backward(
        kp, vp, kt, ga, dq, dk, dv, gp, drow, acc, gains, mixer, raw, q, k, v, att, lse,
        wo, wq, wk, lnear, lfar, pnear, pfar, ynear, yfar,
    ):
        entered = greet(free, me_d, me_t, (1, 2, 4, 6), (1, 2))
        downs = [TokenReduce(us.at[halves[s]], ynear.at[s], yfar.at[s], send, me_t) for s in range(seqs)]
        late_near, late_far = [], []
        for n in range(2):
            half = pl.ds(n * shard // 2, shard // 2)
            refs = lnear.at[:, half], ff_sums[2].at[half]
            late_near.append(ShardNear(whole.at[0, :, :, half], refs[0], refs[1], send, me_d))
            late_far.append(ShardHalves(refs[0], lfar.at[:, half], refs[1], send, me_d))
        pieces = ((wo, slice(512, 768)), (wq, slice(0, 256)), (wk, slice(256, 512)))
        pro_near = [ShardNear(part, pnear.at[n], awg_ref.at[:, lanes], send, me_d) for n, (part, lanes) in enumerate(pieces)]
        pro_far = [
            (ShardHalves if n else ShardFar)(pnear.at[n], pfar.at[n], awg_ref.at[:, lanes], send, me_d)
            for n, (part, lanes) in enumerate(pieces)
        ]
        kept = ((k_out, k), (v_out, v), (att_out, att), (lse_out, lse), (q_out, q))
        load_s = [[here(source.at[s], target.at[s]) for source, target in kept] for s in range(seqs)]
        load_raw = [here(raw_out.at[0], raw)]
        gains[...] = jnp.zeros_like(gains)
        mixer[...] = jnp.zeros_like(mixer)

        def load_grad(s):
            resids[s].arrive()
            low_keeps[s].wait()
            here(r_out.at[s], dn.at[halves[s]]).wait()

        def prepare(s):
            loop(0, parts, lambda r: prepare_rows(
                r, size, lengths[s], dn.at[halves[s]], ws, k.at[s], v.at[s], att.at[s], ga, drow, kp, kt, vp
            ), True)
            dk[...] = jnp.zeros_like(dk)
            dv[...] = jnp.zeros_like(dv)

        def sweep(s, start, stop):
            for i in range(start, stop):
                sweep_rows(i, size, q.at[s], ga, kp, kt, vp, drow, lse.at[s], acc, dq, dk, dv)

        def unproject_q(s):
            loop(0, parts, lambda r: unproject_queries(r, size, (cos_ref, sin_ref), gq_ref, raw, dq, gp.at[s], gains), True)

        def unproject_kv(s):
            loop(0, parts, lambda r: unproject_pairs(
                r, size, lengths[s], (cos_ref, sin_ref), gk_ref, raw, dk, dv, gp.at[s], gains
            ), True)

        def norm_blocks(s):
            for n, bits in enumerate((3, 1, 2, 0)):
                rows = rows_of(me_t.flips[bits], size)
                norm_places[s][rows, :] = dot_nt(gp[s, rows, :], ws[:, :512]).astype(BF16)
                if n < 2:
                    norms[s].start(1 - n)

        def weigh_out():
            def run(b):
                rows = rows_of(b, 256)
                total = sum(dot_tn(dn[halves[s], rows], att[s]) for s in range(seqs))
                wo[b] = total.astype(BF16).reshape(wo.shape[1:])

            loop(0, wo.shape[0], run)

        def weigh(target, lanes):
            def run(b):
                rows = rows_of(b, 256)
                total = sum(dot_tn(xs[s, :, rows], gp[s, :, lanes]) for s in range(seqs))
                target[b] = total.astype(BF16).reshape(target.shape[1:])
                product = total * ws[rows, lanes].astype(F32)
                high = product.astype(BF16)
                rest = (product - high.astype(F32)).astype(BF16)
                ones = jnp.ones((8, product.shape[1]), BF16)
                mixer[:, rows] += dot_nt(ones, high) + dot_nt(ones, rest)

            loop(0, target.shape[0], run)

        def after_down(s):
            downs[s].arrive()

            def step(rows):
                target = pl.ds(pl.multiple_of(s * size + rows.start, 32), 32)
                outp[target, :] = (resid[s, rows, :] + downs[s].rows(rows)).astype(BF16)

            by_rows(size, 32, step)
            return here(outp.at[pl.ds(s * size, size)], blk_out.at[s])

        def total_of(n, got, index):
            got[index] = put[n]
            for copy in steps[n]:
                copy.wait_recv()
            total = got[0]
            for place in range(1, got.shape[0]):
                total = total + got[place]
            return total

        wait(load_s[0])
        load_grad(0)
        prepare(0)
        entered()
        late_near[0].start()
        for exchange in downs:
            exchange.start()
        sweep(0, 0, 2)
        after_back(1)
        sweep(0, 2, 3)
        near[1].middle(far[1])
        sweep(0, 3, parts)
        wait(load_raw)
        unproject_q(0)
        unproject_kv(0)
        load_raw = [here(raw_out.at[1], raw)]
        norm_blocks(0)
        resids[1].forward()
        norms[0].middle()
        late_near[0].middle(late_far[0])
        late_near[1].start()
        downs[0].middle()
        load_grad(1)
        for exchange in resids:
            exchange.drain()
        for copy in backup:
            copy.start()
        wait(load_s[1])
        prepare(1)
        far[1].middle()
        far[0].finish()
        weigh_out()
        pro_near[0].start()
        sweep(1, 0, 2)
        downs[1].middle()
        sweep(1, 2, 3)
        late_near[1].middle(late_far[1])
        late_far[0].middle()
        sweep(1, 3, parts)
        pro_near[0].middle(pro_far[0])
        wait(load_raw)
        unproject_kv(1)
        wait(backup)
        weigh(wk, pieces[2][1])
        pro_near[2].start()
        unproject_q(1)
        weigh(wq, pieces[1][1])
        pro_near[1].start()
        for row, vector in ((0, mixer[0:1, :] / mg_ref[...]), (8, jnp.sum(dgain[...], axis=0, keepdims=True))):
            for i in range(8):
                put[0, row + i : row + i + 1, :] = vector[:, LANES * i : LANES * (i + 1)]
        put[0, 16:, :] = gains[...]
        for copy in steps[0]:
            copy.start()
        norm_blocks(1)
        norms[1].middle()
        late_far[1].middle()
        pro_near[2].middle(pro_far[2])
        put[1] = total_of(0, got_t, me_t.index)
        for copy in steps[1]:
            copy.start()
        after_norm(0)
        norms[0].drain()
        stays = [after_down(0)]
        pro_near[1].middle(pro_far[1])
        pro_far[2].middle()
        stays.append(after_down(1))
        far[1].finish()
        pro_far[0].finish()
        for exchange in late_far:
            exchange.finish()
        pro_far[1].middle()
        sums_ref[...] = total_of(1, got_d, me_d.index)
        after_norm(1)
        pro_far[2].finish()
        pro_far[1].finish()
        wait(stays)
        for copy in steps[0] + steps[1]:
            copy.wait_send()
        for exchange in downs + late_near + late_far + pro_near + pro_far:
            exchange.drain()

    pl.run_scoped(
        backward,
        pltpu.VMEM((4, full, LANES), BF16),
        pltpu.VMEM((4, full, LANES), BF16),
        pltpu.VMEM((4, LANES, full), BF16),
        pltpu.VMEM((full, 256), BF16),
        pltpu.VMEM((full, 256), F32),
        pltpu.VMEM((2, full, LANES), F32),
        pltpu.VMEM((2, full, LANES), F32),
        pltpu.VMEM((seqs, full, 512), BF16),
        pltpu.VMEM((8, full), F32),
        pltpu.VMEM((2, LANES, size), F32),
        pltpu.VMEM((8, LANES), F32),
        pltpu.VMEM((8, width), F32),
        pltpu.VMEM((full, 384), F32),
        pltpu.VMEM((seqs, full, 256), BF16),
        pltpu.VMEM((seqs, full, 128), BF16),
        pltpu.VMEM((seqs, full, 128), BF16),
        pltpu.VMEM((seqs, full, 256), BF16),
        pltpu.VMEM((seqs, 8, full), F32),
        pltpu.VMEM((4, 2, shard, 256), BF16),
        pltpu.VMEM((4, 2, shard, 256), BF16),
        pltpu.VMEM((4, 2, shard, 256), BF16),
        pltpu.VMEM((4, shard, wide), BF16),
        pltpu.VMEM((3, shard, wide), BF16),
        pltpu.VMEM((3, 4, shard, 256), BF16),
        pltpu.VMEM((3, 3, shard, 256), BF16),
        pltpu.VMEM((seqs, 2, size, width), BF16),
        pltpu.VMEM((seqs, size, width), BF16),
    )
    for exchange in pro_w + [out_w, near[1]] + far + norms[1:]:
        exchange.drain()


def fused_block(lengths, inputs, cotangent, weights, tabs, gains):
    size, seqs, width = inputs.shape
    full = 4 * size
    shard = weights[0].shape[0]
    cols = 768
    n_c = 3
    wide = 3 * weights[3].shape[2] // n_c
    dp = 8
    return pl.pallas_call(
        block_kernel,
        out_shape=(
            shape((seqs, full, width), BF16),
            shape((seqs, full, 384), F32),
            shape((seqs, full, 256), BF16),
            shape((seqs, full, 128), BF16),
            shape((seqs, full, 128), BF16),
            shape((seqs, full, 256), BF16),
            shape((seqs, 8, full), F32),
            shape((seqs, full, width), BF16),
            shape((seqs, size, width), BF16),
            shape((size, seqs * width), F32),
            shape((shard, cols), F32),
            shape((shard, n_c * wide), F32),
            shape((24, LANES), F32),
        ),
        in_specs=[SMEM] + [ANY] * 7 + [VMEM] * 6,
        out_specs=(ANY,) * 9 + (VMEM,) * 4,
        scratch_shapes=[
            pltpu.VMEM((size, seqs * width), BF16),
            pltpu.VMEM((1, LANES), F32),
            pltpu.VMEM((1, LANES), F32),
            pltpu.VMEM((seqs, full, width), BF16),
            pltpu.VMEM((dp * shard, cols), BF16),
            pltpu.VMEM((seqs * full, width), BF16),
            pltpu.VMEM((seqs * full, width), BF16),
            pltpu.VMEM((full, width), BF16),
            pltpu.VMEM((seqs, 2, size, width), BF16),
            pltpu.VMEM((seqs, size, width), BF16),
            pltpu.VMEM((seqs, size, width), F32),
            pltpu.VMEM((2, 4, shard, wide), BF16),
            pltpu.VMEM((2, 3, shard, wide), BF16),
            pltpu.VMEM((2, 4, 2, shard, wide), BF16),
            pltpu.VMEM((8, width), F32),
            pltpu.VMEM((2, 24, LANES), F32),
            pltpu.VMEM((4, 24, LANES), F32),
            pltpu.VMEM((8, 24, LANES), F32),
            pltpu.SemaphoreType.REGULAR,
        ]
        + COPY_SEMS,
        compiler_params=pltpu.CompilerParams(
            vmem_limit_bytes=BLOCK_LIMIT, collective_id=0, has_side_effects=True
        ),
        cost_estimate=pl.CostEstimate(flops=90_000_000_000, bytes_accessed=60_000_000, transcendentals=14_000_000),
        name="block",
    )(lengths, inputs, cotangent, *weights, *tabs, *gains)


def finish_kernel(
    lengths, ig_ref, blk_ref, awg_ref, ffg_ref,
    block_out, input_out, query_out, pair_out, output_out, inner_out, down_out,
):
    size, seqs, width = input_out.shape
    hidden = down_out.shape[0]
    cols = hidden // 3
    start = lax.axis_index("tensor") * size

    def step(rows):
        place = start + rows.start + iota((32, width), 0)
        parts = []
        for s in range(seqs):
            lanes = slice(width * s, width * (s + 1))
            input_out[rows, s, :] = ig_ref[rows, lanes]
            parts.append(jnp.where(place < lengths[s], blk_ref[s, rows, :].astype(F32), 0.0))
        block_out[rows, :, :] = jnp.stack(parts, axis=1).astype(BF16)

    by_rows(size, 32, step)
    query_out[...] = awg_ref[:, :256]
    for n in range(2):
        pair_out[:, n, :] = awg_ref[:, 256 + 128 * n : 384 + 128 * n]
    output_out[...] = awg_ref[:, 512:].T
    for c in range(3):
        base = 3 * cols * c
        for n in range(2):
            inner_out[:, n, cols * c : cols * (c + 1)] = ffg_ref[:, base + cols * n : base + cols * (n + 1)]
        down_out[cols * c : cols * (c + 1), :] = ffg_ref[:, base + 2 * cols : base + 3 * cols].T


def fused_finish(lengths, ig, blk, awg, ffg):
    seqs, size, width = blk.shape
    shard, wide = ffg.shape
    hidden = wide // 3
    return pl.pallas_call(
        finish_kernel,
        out_shape=(
            shape((size, seqs, width), BF16),
            shape((size, seqs, width), F32),
            shape((shard, 256), F32),
            shape((shard, 2, 128), F32),
            shape((256, shard), F32),
            shape((shard, 2, hidden), F32),
            shape((hidden, shard), F32),
        ),
        in_specs=[SMEM] + [VMEM] * 4,
        out_specs=(VMEM,) * 7,
        compiler_params=pltpu.CompilerParams(vmem_limit_bytes=VMEM_LIMIT),
        name="finish",
    )(lengths, ig, blk, awg, ffg)


def swap(values, axis, bits):
    return lax.ppermute(values, axis, [(i, i ^ bits) for i in range(lax.axis_size(axis))])


def gather_tokens(block):
    far = swap(block, "tensor", 2)
    return [block, swap(block, "tensor", 1), far, swap(far, "tensor", 1)]


def scatter_tokens(keep, send):
    near = swap(send, "tensor", 1)
    middle = (keep[1].astype(F32) + near[1].astype(F32)).astype(BF16)
    far = swap(middle, "tensor", 2)
    return keep[0].astype(F32) + near[0].astype(F32) + far.astype(F32)


def gather_shards(shard):
    if lax.axis_size("dp") != 8 or shard.shape[0] % LANES:
        return [lax.all_gather(shard, "dp", axis=0, tiled=True)]
    slots = [shard, swap(shard, "dp", 1)]
    for bits in (2, 4, 6):
        there = swap(shard, "dp", bits)
        slots += [there, swap(there, "dp", 1)]
    return slots


def scatter_shards(grads):
    if len(grads) == 1:
        return lax.psum_scatter(grads[0].astype(F32), "dp", scatter_dimension=0, tiled=True)
    keep, send = grads
    near = swap(send, "dp", 1)
    both = keep.astype(F32) + near.astype(F32)
    total = both[0]
    for slot in (1, 2, 3):
        total = total + swap(both[slot].astype(BF16), "dp", 2 * slot).astype(F32)
    return total


def sum_everywhere(values):
    for axis in ("tensor", "dp"):
        bits = 1
        while bits < lax.axis_size(axis):
            values = values + swap(values, axis, bits)
            bits *= 2
    return values


def norm_rows(values, gain):
    factor = lax.rsqrt(jnp.mean(values * values, axis=-1, keepdims=True) + EPS)
    return (values * factor * gain, factor)


def norm_back(values, factor, gain, upstream):
    weighted = upstream * gain
    inner = jnp.mean(values * weighted, axis=-1, keepdims=True)
    return factor * weighted - values * factor * factor * factor * inner


def tables(full, head_width):
    half = head_width // 2
    freqs = THETA ** (-jnp.arange(half, dtype=F32) * 2.0 / head_width)
    angles = jnp.arange(full, dtype=F32)[:, None] * freqs[None, :]
    cosines, sines = jnp.cos(angles), jnp.sin(angles)
    return (jnp.tile(cosines, (1, 4)), jnp.tile(jnp.concatenate([-sines, sines], axis=1), (1, 2)))


def local_plain(
    inputs,
    lengths,
    query_weight,
    key_value_weight,
    output_weight,
    inner_weight,
    down_weight,
    mixer_gain,
    query_gain,
    key_gain,
    dense_gain,
    cotangent,
):
    size, seqs, width = inputs.shape
    parts = lax.axis_size("tensor")
    full = size * parts
    head = query_gain.shape[0]
    query_cols = query_weight.shape[1]
    pair_cols = key_value_weight.shape[2]
    hidden = inner_weight.shape[2]
    shard = query_weight.shape[0]
    me_t, me_d = lax.axis_index("tensor"), lax.axis_index("dp")
    n_c = 3
    cols = hidden // n_c
    cosines, sines = tables(full, head)
    gq = jnp.tile(query_gain, 2)[None, :]
    gk = jnp.tile(key_gain, 2)[None, :]

    down_turned = down_weight.T
    attn_shard = jnp.concatenate(
        [query_weight, key_value_weight.reshape(shard, 2 * pair_cols), output_weight.T], axis=1
    )
    attn_w = gather_shards(attn_shard)
    positions = me_t * size + jnp.arange(size, dtype=jnp.int32)
    scals = [
        jnp.stack([me_t.astype(jnp.int32), me_d.astype(jnp.int32), lengths[s], jnp.int32(0)])
        for s in range(seqs)
    ]
    tokens = [inputs[:, s].astype(F32) for s in range(seqs)]
    valid = [(positions < lengths[s])[:, None] for s in range(seqs)]
    firsts = [norm_rows(tokens[s], mixer_gain) for s in range(seqs)]
    normed = [gather_tokens(firsts[s][0].astype(BF16)) for s in range(seqs)]
    ff_w = []
    for c in range(n_c):
        part = slice(c * cols, (c + 1) * cols)
        ff_w.append(
            gather_shards(
                jnp.concatenate(
                    [inner_weight[:, 0, part], inner_weight[:, 1, part], down_turned[:, part]], axis=1
                )
            )
        )
    upstream = [jnp.where(valid[s], cotangent[:, s].astype(F32), 0.0) for s in range(seqs)]
    up_parts = [gather_tokens(upstream[s].astype(BF16)) for s in range(seqs)]

    saved, residual, seconds, dense = [], [], [], []
    for s in range(seqs):
        outs = attn_fwd(scals[s], cosines, sines, gq, gk, normed[s], attn_w)
        saved.append(outs[:6])
        residual.append(tokens[s] + scatter_tokens(outs[6], outs[7]))
        dense_in, factor = norm_rows(residual[s], dense_gain)
        seconds.append(factor)
        dense.append(gather_tokens(dense_in.astype(BF16)))

    x_parts = [part for s in range(seqs) for part in dense[s]]
    u_parts = [part for s in range(seqs) for part in up_parts[s]]
    hids, ggus, ff_grads = [], [], []
    for c in range(n_c):
        hid, ggu, grads = feed_forward(scals[0], x_parts, u_parts, ff_w[c])
        hids.append(hid)
        ggus.append(ggu)
        ff_grads.append(scatter_shards(grads))

    block_out, input_gradient, attn_grads = [], [], []
    mixer_part = dense_part = gain_part = 0.0
    for s in range(seqs):
        ykeep, ysend, gkeep, gsend = ff_out(s, scals[s], parts, size, hids, ggus, ff_w)
        grad_dense = scatter_tokens(gkeep, gsend)
        dense_part = dense_part + jnp.sum(grad_dense * residual[s] * seconds[s], axis=0)
        grad_residual = upstream[s] + norm_back(residual[s], seconds[s], dense_gain, grad_dense)
        r_parts = gather_tokens(grad_residual.astype(BF16))
        nkeep, nsend, gains, grads = attn_bwd(
            scals[s], cosines, sines, gq, gk, saved[s], normed[s], r_parts, attn_w
        )
        attn_grads.append(grads)
        gain_part = gain_part + gains
        grad_normed = scatter_tokens(nkeep, nsend)
        factor = firsts[s][1]
        mixer_part = mixer_part + jnp.sum(grad_normed * tokens[s] * factor, axis=0)
        input_gradient.append(grad_residual + norm_back(tokens[s], factor, mixer_gain, grad_normed))
        out_sum = scatter_tokens(ykeep, ysend)
        block_out.append(jnp.where(valid[s], residual[s] + out_sum, 0.0).astype(BF16))

    summed = [
        sum(part.astype(F32) for part in parts_of).astype(BF16) for parts_of in zip(*attn_grads)
    ]
    attn_grad = scatter_shards(summed)
    early = sum_everywhere(jnp.concatenate([dense_part.reshape(-1, LANES), gain_part], axis=0))
    mixer = sum_everywhere(mixer_part.reshape(-1, LANES)).reshape(-1)
    dense_rows = width // LANES
    folded = early[dense_rows:, :head] + early[dense_rows:, head:]
    inner_gradient = jnp.stack(
        [
            jnp.concatenate([grad[:, p * cols : (p + 1) * cols] for grad in ff_grads], axis=1)
            for p in range(2)
        ],
        axis=1,
    )
    down_gradient = jnp.concatenate([grad[:, 2 * cols :] for grad in ff_grads], axis=1).T
    return (
        jnp.stack(block_out, axis=1),
        jnp.stack(input_gradient, axis=1),
        attn_grad[:, :query_cols],
        attn_grad[:, query_cols : query_cols + 2 * pair_cols].reshape(shard, 2, pair_cols),
        attn_grad[:, query_cols + 2 * pair_cols :].T,
        inner_gradient,
        down_gradient,
        mixer,
        folded[0],
        folded[1],
        early[:dense_rows].reshape(-1),
    )


def local(*args):
    inputs, shard = args[0], args[2].shape[0]
    if lax.axis_size("dp") == 8 and lax.axis_size("tensor") == 4 and shard % LANES == 0 and inputs.shape[1] == 2:
        return local_fused(*args)
    return local_plain(*args)


def rope_tables(full, head):
    half = head // 2
    freqs = np.float32(THETA) ** (-np.arange(half, dtype=np.float32) * np.float32(2.0) / np.float32(head))
    angles = np.arange(full, dtype=np.float32)[:, None] * freqs[None, :].astype(np.float32)
    cosines, sines = np.cos(angles), np.sin(angles)
    return (
        jnp.asarray(np.tile(cosines, (1, 4)), F32),
        jnp.asarray(np.tile(np.concatenate([-sines, sines], axis=1), (1, 2)), F32),
    )


def local_fused(
    inputs,
    lengths,
    query_weight,
    key_value_weight,
    output_weight,
    inner_weight,
    down_weight,
    mixer_gain,
    query_gain,
    key_gain,
    dense_gain,
    cotangent,
):
    size, seqs, width = inputs.shape
    parts = lax.axis_size("tensor")
    full = size * parts
    head = query_gain.shape[0]
    tabs = rope_tables(full, head)
    weights = (query_weight, key_value_weight, output_weight, inner_weight, down_weight)
    gains = (query_gain[None, :], key_gain[None, :], mixer_gain[None, :], dense_gain[None, :])
    *_, blk, input_gradient, attn_grad, ff_grad, sums = fused_block(
        lengths, inputs, cotangent, weights, tabs, gains
    )
    finished = fused_finish(lengths, input_gradient, blk, attn_grad, ff_grad)
    folded = sums[16:, :head] + sums[16:, head:]
    return tuple(finished) + (
        sums[:8].reshape(-1),
        folded[0],
        folded[1],
        sums[8:16].reshape(-1),
    )


def solution(mesh):
    return jax.shard_map(
        local,
        mesh=mesh,
        in_specs=(
            P("tensor", "dp", None),
            P("dp"),
            P("dp", "tensor"),
            P("dp", None, "tensor"),
            P("tensor", "dp"),
            P("dp", None, "tensor"),
            P("tensor", "dp"),
            P(),
            P(),
            P(),
            P(),
            P("tensor", "dp", None),
        ),
        out_specs=(
            P("tensor", "dp", None),
            P("tensor", "dp", None),
            P("dp", "tensor"),
            P("dp", None, "tensor"),
            P("tensor", "dp"),
            P("dp", None, "tensor"),
            P("tensor", "dp"),
            P(),
            P(),
            P(),
            P(),
        ),
        check_vma=False,
    )
```

```python
import functools

import jax
import jax.numpy as jnp
import numpy as np
from jax import lax
from jax.experimental import pallas as pl
from jax.experimental.pallas import tpu as pltpu
from jax.sharding import PartitionSpec as P

EPS = 1e-05
THETA = 1000000.0
LOG2E = 1.4426950408889634
F32 = jnp.float32
BF16 = jnp.bfloat16
HIGH = lax.Precision.HIGHEST
LANES = 128
VMEM_LIMIT = 56 * 1024 * 1024
BLOCK_LIMIT = 62 * 1024 * 1024
ANY = pl.BlockSpec(memory_space=pl.ANY)
VMEM = pl.BlockSpec(memory_space=pltpu.VMEM)
SMEM = pl.BlockSpec(memory_space=pltpu.SMEM)


def dot(a, b, **kw):
    return lax.dot_general(
        a, b, (((1,), (0,)), ((), ())), preferred_element_type=F32, **kw
    )


def dot_nt(a, b, **kw):
    return lax.dot_general(
        a, b, (((1,), (1,)), ((), ())), preferred_element_type=F32, **kw
    )


def dot_tn(a, b, **kw):
    return lax.dot_general(
        a, b, (((0,), (0,)), ((), ())), preferred_element_type=F32, **kw
    )


def iota(shape, axis):
    return lax.broadcasted_iota(jnp.int32, shape, axis)


def low_half(shape):
    return iota(shape, 1) % LANES < LANES // 2


def head_blocks(scale):
    shape = (LANES, LANES)
    return jnp.where(iota(shape, 0) // 64 == iota(shape, 1) // 64, scale, 0.0).astype(F32)


def head_rows(scale):
    return jnp.where(iota((8, 256), 0) == iota((8, 256), 1) // 64, scale, 0.0).astype(F32)


def partner(values):
    first = iota(values.shape, 1) % 64 < 32
    return jnp.where(first, pltpu.roll(values, LANES - 32, 1), pltpu.roll(values, 32, 1))


def rows_of(index, size):
    if isinstance(index, int):
        return pl.ds(index * size, size)
    return pl.ds(pl.multiple_of(index * size, size), size)


def load_all(sources, targets, sems, first):
    copies = []
    for number, (source, target) in enumerate(zip(sources, targets)):
        copy = pltpu.make_async_copy(source, target, sems.at[first + number])
        copy.start()
        copies.append(copy)
    return copies


def shard_targets(w_refs, ws, me):
    size = w_refs[0].shape[0]
    if len(w_refs) == 1:
        return [ws]
    return [ws.at[rows_of(me ^ slot, size)] for slot in range(len(w_refs))]


def store_slots(whole, out_refs, me):
    if len(out_refs) == 1:
        out_refs[0][...] = whole[...]
        return
    keep_ref, send_ref = out_refs
    size = keep_ref.shape[1]
    for slot in range(2 * keep_ref.shape[0]):
        (send_ref if slot % 2 else keep_ref)[slot // 2] = whole[rows_of(me ^ slot, size), :]


def padded_heads(first, second, low, g, e):
    here = low if e == 0 else jnp.logical_not(low)
    return jnp.where(here, first if g == e else second, 0.0).astype(BF16)


def project_rows(r, size, length, xs, ws, tabs, gains, raw_ref, q_ref, k_ref, v_ref, kp, vp):
    rows = rows_of(r, size)
    cos_ref, sin_ref = tabs
    gq_ref, gk_ref = gains
    mean_of = head_blocks(1.0 / 64)
    low = low_half((size, LANES))
    projected = dot(xs[rows, :], ws[:, :512])
    raw_ref[rows, :] = projected[:, :384]
    cosines, sines = cos_ref[rows, :], sin_ref[rows, :]

    def turned(values, gain):
        mean = dot(values * values, mean_of, precision=HIGH)
        normed = values * lax.rsqrt(mean + EPS) * gain
        return normed * cosines + partner(normed) * sines

    for g in range(2):
        lanes = slice(LANES * g, LANES * (g + 1))
        q_ref[rows, lanes] = turned(projected[:, lanes], gq_ref[...]).astype(BF16)
    keys = turned(projected[:, 256:384], gk_ref[...])
    values = projected[:, 384:512]
    k_ref[rows, :] = keys.astype(BF16)
    v_ref[rows, :] = values.astype(BF16)
    live = r * size + iota((size, LANES), 0) < length
    ones = jnp.where(live, 1.0, 0.0)
    values = jnp.where(live, values, 0.0)
    keys_swap, values_swap = pltpu.roll(keys, 64, 1), pltpu.roll(values, 64, 1)
    for g in range(2):
        for e in range(2):
            kp[2 * g + e, rows, :] = padded_heads(keys, keys_swap, low, g, e)
            vp[2 * g + e, rows, :LANES] = padded_heads(values, values_swap, low, g, e)
            vp[2 * g + e, rows, LANES:] = padded_heads(ones, ones, low, g, e)


def attend_rows(i, size, q_ref, kp, vp, acc, att_ref, lse_ref):
    rows = rows_of(i, size)
    factor = LOG2E / 8.0
    causal = iota((size, size), 1) <= iota((size, size), 0)
    queries = [q_ref[rows, LANES * g : LANES * (g + 1)] for g in range(2)]

    def block(kb, masked):
        cols = rows_of(kb, size)
        sums = []
        for g in range(2):
            total = None
            for e in range(2):
                weights = jnp.exp2(dot_nt(queries[g], kp[2 * g + e, cols, :]) * factor)
                if masked:
                    weights = jnp.where(causal, weights, 0.0)
                part = dot(weights.astype(BF16), vp[2 * g + e, cols, :])
                total = part if total is None else total + part
            sums.append(total)
        return sums

    totals = block(i, True)
    if isinstance(i, int):
        for kb in range(i):
            totals = [total + part for total, part in zip(totals, block(kb, False))]
    else:
        for g, total in enumerate(totals):
            acc[g] = total

        def more(kb, carry):
            for g, total in enumerate(block(kb, False)):
                acc[g] += total
            return carry

        lax.fori_loop(i - i, i, more, None)
        totals = [acc[g] for g in range(2)]
    logs = []
    for g in range(2):
        lanes = slice(LANES * g, LANES * (g + 1))
        summed = totals[g][:, LANES:]
        att_ref[rows, lanes] = (totals[g][:, :LANES] / summed).astype(BF16)
        logs.append(jnp.log2(summed))
    lse_ref[:, rows] = dot_nt(head_rows(1.0 / 64), jnp.concatenate(logs, axis=1), precision=HIGH)


def attn_fwd_kernel(parts, n_w, scal, cos_ref, sin_ref, gq_ref, gk_ref, *refs):
    x_refs, refs = refs[:parts], refs[parts:]
    w_refs, refs = refs[:n_w], refs[n_w:]
    (raw_ref, q_ref, k_ref, v_ref, att_ref, lse_ref, keep_ref, send_ref, xs, ws, kp, vp, acc, sems) = refs
    size = x_refs[0].shape[0]
    me_t, me_d, length = scal[0], scal[1], scal[2]
    copies = load_all(w_refs, shard_targets(w_refs, ws, me_d), sems, 0)
    copies += load_all(x_refs, [xs.at[rows_of(me_t ^ j, size)] for j in range(parts)], sems, n_w)
    for copy in copies:
        copy.wait()

    def project(r, carry):
        project_rows(
            r, size, length, xs, ws, (cos_ref, sin_ref), (gq_ref, gk_ref), raw_ref, q_ref, k_ref, v_ref, kp, vp
        )
        return carry

    def attend(i, carry):
        attend_rows(i, size, q_ref, kp, vp, acc, att_ref, lse_ref)
        return carry

    lax.fori_loop(0, parts, project, 0)
    lax.fori_loop(0, parts, attend, 0)
    for j in range(parts):
        out = dot_nt(att_ref[rows_of(me_t ^ j, size), :], ws[:, 512:])
        (send_ref if j % 2 else keep_ref)[j // 2] = out.astype(BF16)


def attn_fwd(scal, cosines, sines, gq, gk, x_parts, w_parts):
    parts, n_w = len(x_parts), len(w_parts)
    size, width = x_parts[0].shape
    full = parts * size
    cols = w_parts[0].shape[1]
    pair = jax.ShapeDtypeStruct((parts // 2, size, width), BF16)
    return pl.pallas_call(
        functools.partial(attn_fwd_kernel, parts, n_w),
        out_shape=(
            jax.ShapeDtypeStruct((full, 384), F32),
            jax.ShapeDtypeStruct((full, 256), BF16),
            jax.ShapeDtypeStruct((full, 128), BF16),
            jax.ShapeDtypeStruct((full, 128), BF16),
            jax.ShapeDtypeStruct((full, 256), BF16),
            jax.ShapeDtypeStruct((8, full), F32),
            pair,
            pair,
        ),
        in_specs=[SMEM] + [VMEM] * 4 + [ANY] * (parts + n_w),
        out_specs=(VMEM,) * 8,
        scratch_shapes=[
            pltpu.VMEM((full, width), BF16),
            pltpu.VMEM((width, cols), BF16),
            pltpu.VMEM((4, full, LANES), BF16),
            pltpu.VMEM((4, full, 2 * LANES), BF16),
            pltpu.VMEM((2, size, 2 * LANES), F32),
            pltpu.SemaphoreType.DMA((n_w + parts,)),
        ],
        compiler_params=pltpu.CompilerParams(vmem_limit_bytes=VMEM_LIMIT),
        cost_estimate=pl.CostEstimate(flops=8_000_000_000, bytes_accessed=12_000_000, transcendentals=3_000_000),
        name="attention_forward",
    )(scal, cosines, sines, gq, gk, *x_parts, *w_parts)


def prepare_rows(r, size, length, gs, ws, k_ref, v_ref, att_ref, ga, drow, kp, kt, vp):
    rows = rows_of(r, size)
    low = low_half((size, LANES))
    grad = dot(gs[rows, :], ws[:, 512:]).astype(BF16)
    ga[rows, :] = grad
    drow[:, rows] = dot_nt(head_rows(1.0), grad.astype(F32) * att_ref[rows, :].astype(F32), precision=HIGH)
    live = r * size + iota((size, LANES), 0) < length
    keys = jnp.where(live, k_ref[rows, :].astype(F32), 0.0)
    values = jnp.where(live, v_ref[rows, :].astype(F32), 0.0)
    keys_swap, values_swap = pltpu.roll(keys, 64, 1), pltpu.roll(values, 64, 1)
    for g in range(2):
        for e in range(2):
            here = low if e == 0 else jnp.logical_not(low)
            padded = jnp.where(here, keys if g == e else keys_swap, 0.0)
            kp[2 * g + e, rows, :] = padded.astype(BF16)
            kt[2 * g + e, :, rows] = padded.T.astype(BF16)
            vp[2 * g + e, rows, :] = padded_heads(values, values_swap, low, g, e)


def sweep_rows(i, size, q_ref, ga, kp, kt, vp, drow, lrow, acc, dq, dk, dv):
    rows = rows_of(i, size)
    factor = LOG2E / 8.0
    causal = iota((size, size), 0) <= iota((size, size), 1)
    low2 = iota((2 * size, LANES), 0) // size == iota((2 * size, LANES), 1) // 64
    queries, grads, queries2, grads2 = [], [], [], []
    for g in range(2):
        lanes = slice(LANES * g, LANES * (g + 1))
        queries.append(q_ref[rows, lanes])
        grads.append(ga[rows, lanes])
        for source, target in ((queries, queries2), (grads, grads2)):
            both = jnp.concatenate([source[g], source[g]], axis=0)
            target.append(jnp.where(low2, both, jnp.zeros_like(both)))

    def block(kb, masked):
        cols = rows_of(kb, size)
        parts_t = []
        for g in range(2):
            weights2, scores2, turned = [], [], None
            for e in range(2):
                h = 2 * g + e
                weights = jnp.exp2(dot_nt(kp[h, cols, :], queries[g]) * factor - lrow[h : h + 1, rows])
                if masked:
                    weights = jnp.where(causal, weights, 0.0)
                grad_weights = dot_nt(vp[h, cols, :], grads[g])
                grad_scores = (weights * (grad_weights - drow[h : h + 1, rows])).astype(BF16)
                weights2.append(weights.astype(BF16))
                scores2.append(grad_scores)
                part = dot(kt[h, :, cols], grad_scores)
                turned = part if turned is None else turned + part
            dv[g, cols, :] += dot(jnp.concatenate(weights2, axis=1), grads2[g])
            dk[g, cols, :] += dot(jnp.concatenate(scores2, axis=1), queries2[g])
            parts_t.append(turned)
        return parts_t

    if isinstance(i, int):
        totals = block(i, True)
        for kb in range(i):
            totals = [total + part for total, part in zip(totals, block(kb, False))]
        for g in range(2):
            dq[rows, LANES * g : LANES * (g + 1)] = totals[g].T
        return
    for g, total in enumerate(block(i, True)):
        acc[g] = total

    def more(kb, carry):
        for g, total in enumerate(block(kb, False)):
            acc[g] += total
        return carry

    lax.fori_loop(i - i, i, more, None)
    for g in range(2):
        dq[rows, LANES * g : LANES * (g + 1)] = acc[g].T


def unproject_head(rows, grad, tabs, gain_ref, raw_ref, lanes, gp, gains_ref, row):
    cosines, sines = tabs[0][rows, :], tabs[1][rows, :]
    mean_of = head_blocks(1.0 / 64)
    raw = raw_ref[rows, lanes]
    rms = lax.rsqrt(dot(raw * raw, mean_of, precision=HIGH) + EPS)
    turned = grad * cosines - partner(grad) * sines
    gains_ref[row : row + 1, :] += jnp.sum(turned * raw * rms, axis=0, keepdims=True)
    weighted = turned * gain_ref[...]
    inner = dot(raw * weighted, mean_of, precision=HIGH)
    gp[rows, lanes] = (rms * weighted - raw * (rms * rms * rms) * inner).astype(BF16)


def unproject_queries(r, size, tabs, gain_ref, raw_ref, dq, gp, gains_ref):
    rows = rows_of(r, size)
    for g in range(2):
        lanes = slice(LANES * g, LANES * (g + 1))
        unproject_head(rows, dq[rows, lanes] * 0.125, tabs, gain_ref, raw_ref, lanes, gp, gains_ref, 0)


def unproject_pairs(r, size, length, tabs, gain_ref, raw_ref, dk, dv, gp, gains_ref):
    rows = rows_of(r, size)
    low = low_half((size, LANES))
    live = r * size + iota((size, LANES), 0) < length

    def folded(ref):
        first, second = ref[0, rows, :], ref[1, rows, :]
        both = jnp.where(low, first + pltpu.roll(first, 64, 1), second + pltpu.roll(second, 64, 1))
        return jnp.where(live, both, 0.0)

    unproject_head(rows, folded(dk) * 0.125, tabs, gain_ref, raw_ref, slice(256, 384), gp, gains_ref, 1)
    gp[rows, 384:512] = folded(dv).astype(BF16)


def attn_bwd_kernel(parts, n_w, scal, cos_ref, sin_ref, gq_ref, gk_ref, raw_ref, q_ref, k_ref, v_ref, att_ref, lse_ref, *refs):
    x_refs, refs = refs[:parts], refs[parts:]
    r_refs, refs = refs[:parts], refs[parts:]
    w_refs, refs = refs[:n_w], refs[n_w:]
    n_g = 1 if n_w == 1 else 2
    keep_ref, send_ref, gains_ref = refs[:3]
    g_refs, refs = refs[3 : 3 + n_g], refs[3 + n_g :]
    xs, gs, ws, kp, vp, kt, ga, dq, dk, dv, gp, whole, drow, acc, sems = refs
    size = x_refs[0].shape[0]
    me_t, me_d, length = scal[0], scal[1], scal[2]
    copies = load_all(w_refs, shard_targets(w_refs, ws, me_d), sems, 0)
    copies += load_all(r_refs, [gs.at[rows_of(me_t ^ j, size)] for j in range(parts)], sems, n_w)
    copies += load_all(x_refs, [xs.at[rows_of(me_t ^ j, size)] for j in range(parts)], sems, n_w + parts)
    for copy in copies:
        copy.wait()

    def prepare(r, carry):
        prepare_rows(r, size, length, gs, ws, k_ref, v_ref, att_ref, ga, drow, kp, kt, vp)
        return carry

    def sweep(i, carry):
        sweep_rows(i, size, q_ref, ga, kp, kt, vp, drow, lse_ref, acc, dq, dk, dv)
        return carry

    def unproject(r, carry):
        unproject_queries(r, size, (cos_ref, sin_ref), gq_ref, raw_ref, dq, gp, gains_ref)
        unproject_pairs(r, size, length, (cos_ref, sin_ref), gk_ref, raw_ref, dk, dv, gp, gains_ref)
        return carry

    lax.fori_loop(0, parts, prepare, 0)
    dk[...] = jnp.zeros_like(dk)
    dv[...] = jnp.zeros_like(dv)
    lax.fori_loop(0, parts, sweep, 0)
    gains_ref[...] = jnp.zeros_like(gains_ref)
    lax.fori_loop(0, parts, unproject, 0)
    for j in range(parts):
        out = dot_nt(gp[rows_of(me_t ^ j, size), :], ws[:, :512])
        (send_ref if j % 2 else keep_ref)[j // 2] = out.astype(BF16)

    def weigh(b, carry):
        rows = rows_of(b, 256)
        whole[rows, :512] = dot_tn(xs[:, rows], gp[...]).astype(BF16)
        whole[rows, 512:] = dot_tn(gs[:, rows], att_ref[...]).astype(BF16)
        return carry

    lax.fori_loop(0, whole.shape[0] // 256, weigh, 0)
    store_slots(whole, g_refs, me_d)


def slot_shapes(n_w, width, cols):
    if n_w == 1:
        return (jax.ShapeDtypeStruct((width, cols), BF16),)
    return (jax.ShapeDtypeStruct((n_w // 2, width // n_w, cols), BF16),) * 2


def attn_bwd(scal, cosines, sines, gq, gk, saved, x_parts, r_parts, w_parts):
    parts, n_w = len(x_parts), len(w_parts)
    size, width = x_parts[0].shape
    full = parts * size
    cols = w_parts[0].shape[1]
    pair = jax.ShapeDtypeStruct((parts // 2, size, width), BF16)
    g_shapes = slot_shapes(n_w, width, cols)
    outs = pl.pallas_call(
        functools.partial(attn_bwd_kernel, parts, n_w),
        out_shape=(pair, pair, jax.ShapeDtypeStruct((8, LANES), F32)) + g_shapes,
        in_specs=[SMEM] + [VMEM] * 10 + [ANY] * (2 * parts + n_w),
        out_specs=(VMEM,) * (3 + len(g_shapes)),
        scratch_shapes=[
            pltpu.VMEM((full, width), BF16),
            pltpu.VMEM((full, width), BF16),
            pltpu.VMEM((width, cols), BF16),
            pltpu.VMEM((4, full, LANES), BF16),
            pltpu.VMEM((4, full, LANES), BF16),
            pltpu.VMEM((4, LANES, full), BF16),
            pltpu.VMEM((full, 256), BF16),
            pltpu.VMEM((full, 256), F32),
            pltpu.VMEM((2, full, LANES), F32),
            pltpu.VMEM((2, full, LANES), F32),
            pltpu.VMEM((full, 512), BF16),
            pltpu.VMEM((width, cols), BF16),
            pltpu.VMEM((8, full), F32),
            pltpu.VMEM((2, LANES, size), F32),
            pltpu.SemaphoreType.DMA((n_w + 2 * parts,)),
        ],
        compiler_params=pltpu.CompilerParams(vmem_limit_bytes=VMEM_LIMIT),
        cost_estimate=pl.CostEstimate(flops=14_000_000_000, bytes_accessed=15_000_000, transcendentals=3_000_000),
        name="attention_backward",
    )(scal, cosines, sines, gq, gk, *saved, *x_parts, *r_parts, *w_parts)
    return outs[0], outs[1], outs[2], outs[3:]


def ff_kernel(n_x, n_w, scal, *refs):
    x_refs, refs = refs[:n_x], refs[n_x:]
    u_refs, refs = refs[:n_x], refs[n_x:]
    w_refs, refs = refs[:n_w], refs[n_w:]
    n_g = 1 if n_w == 1 else 2
    hid_ref, ggu_ref = refs[:2]
    g_refs, refs = refs[2 : 2 + n_g], refs[2 + n_g :]
    xs, us, ws, whole, sems = refs
    size = x_refs[0].shape[0]
    me_d = scal[1]
    cols = ws.shape[1] // 3
    copies = load_all(w_refs, shard_targets(w_refs, ws, me_d), sems, 0)
    x_copies = load_all(x_refs, [xs.at[pl.ds(j * size, size)] for j in range(n_x)], sems, n_w)
    u_copies = load_all(u_refs, [us.at[pl.ds(j * size, size)] for j in range(n_x)], sems, n_w + n_x)
    for copy in copies + x_copies + u_copies:
        copy.wait()

    def tokens(r, carry):
        rows = rows_of(r, size)
        gate_up = dot(xs[rows, :], ws[:, : 2 * cols])
        grad = dot(us[rows, :], ws[:, 2 * cols :])
        gate, up = gate_up[:, :cols], gate_up[:, cols:]
        sig = 1.0 / (1.0 + jnp.exp2(gate * -LOG2E))
        silu = gate * sig
        hid_ref[rows, :] = (silu * up).astype(BF16)
        ggu_ref[rows, :cols] = (grad * up * (sig + silu * (1.0 - sig))).astype(BF16)
        ggu_ref[rows, cols:] = (grad * silu).astype(BF16)
        return carry

    lax.fori_loop(0, n_x, tokens, 0)

    def weigh(b, carry):
        rows = rows_of(b, 256)
        whole[rows, : 2 * cols] = dot_tn(xs[:, rows], ggu_ref[...]).astype(BF16)
        whole[rows, 2 * cols :] = dot_tn(us[:, rows], hid_ref[...]).astype(BF16)
        return carry

    lax.fori_loop(0, whole.shape[0] // 256, weigh, 0)
    store_slots(whole, g_refs, me_d)


def feed_forward(scal, x_parts, u_parts, w_parts):
    n_x, n_w = len(x_parts), len(w_parts)
    size, width = x_parts[0].shape
    full = n_x * size
    wide = w_parts[0].shape[1]
    cols = wide // 3
    g_shapes = slot_shapes(n_w, width, wide)
    outs = pl.pallas_call(
        functools.partial(ff_kernel, n_x, n_w),
        out_shape=(
            jax.ShapeDtypeStruct((full, cols), BF16),
            jax.ShapeDtypeStruct((full, 2 * cols), BF16),
        )
        + g_shapes,
        in_specs=[SMEM] + [ANY] * (2 * n_x + n_w),
        out_specs=(VMEM,) * (2 + len(g_shapes)),
        scratch_shapes=[
            pltpu.VMEM((full, width), BF16),
            pltpu.VMEM((full, width), BF16),
            pltpu.VMEM((width, wide), BF16),
            pltpu.VMEM((width, wide), BF16),
            pltpu.SemaphoreType.DMA((n_w + 2 * n_x,)),
        ],
        compiler_params=pltpu.CompilerParams(vmem_limit_bytes=VMEM_LIMIT),
        cost_estimate=pl.CostEstimate(flops=4 * full * width * wide, bytes_accessed=20_000_000, transcendentals=full * cols),
        name="feed_forward",
    )(scal, *x_parts, *u_parts, *w_parts)
    return outs[0], outs[1], outs[2:]


def ff_out_kernel(parts, n_c, n_w, seq, scal, *refs):
    hid_refs, refs = refs[:n_c], refs[n_c:]
    ggu_refs, refs = refs[:n_c], refs[n_c:]
    w_refs, refs = refs[: n_c * n_w], refs[n_c * n_w :]
    ykeep_ref, ysend_ref, gkeep_ref, gsend_ref, hs, gs, ws, sems = refs
    size = ykeep_ref.shape[1]
    full = parts * size
    me_d = scal[1]
    wide = ws.shape[2]
    cols = wide // 3
    copies = []
    first = 0
    for c in range(n_c):
        targets = shard_targets(w_refs[c * n_w : (c + 1) * n_w], ws.at[c], me_d)
        copies += load_all(w_refs[c * n_w : (c + 1) * n_w], targets, sems, first)
        first += n_w
    mine = pl.ds(seq * full, full)
    copies += load_all([ref.at[mine] for ref in ggu_refs], [gs.at[c] for c in range(n_c)], sems, first)
    copies += load_all([ref.at[mine] for ref in hid_refs], [hs.at[c] for c in range(n_c)], sems, first + n_c)
    for copy in copies:
        copy.wait()
    for j in range(parts):
        rows = pl.ds(j * size, size)
        grad = sum(dot_nt(gs[c, rows, :], ws[c, :, : 2 * cols]) for c in range(n_c))
        (gsend_ref if j % 2 else gkeep_ref)[j // 2] = grad.astype(BF16)
        out = sum(dot_nt(hs[c, rows, :], ws[c, :, 2 * cols :]) for c in range(n_c))
        (ysend_ref if j % 2 else ykeep_ref)[j // 2] = out.astype(BF16)


def ff_out(seq, scal, parts, size, hids, ggus, w_chunks):
    n_c, n_w = len(w_chunks), len(w_chunks[0])
    wide = w_chunks[0][0].shape[1]
    width = w_chunks[0][0].shape[0] * n_w
    full = parts * size
    cols = wide // 3
    pair = jax.ShapeDtypeStruct((parts // 2, size, width), BF16)
    return pl.pallas_call(
        functools.partial(ff_out_kernel, parts, n_c, n_w, seq),
        out_shape=(pair,) * 4,
        in_specs=[SMEM] + [ANY] * (2 * n_c + n_c * n_w),
        out_specs=(VMEM,) * 4,
        scratch_shapes=[
            pltpu.VMEM((n_c, full, cols), BF16),
            pltpu.VMEM((n_c, full, 2 * cols), BF16),
            pltpu.VMEM((n_c, width, wide), BF16),
            pltpu.SemaphoreType.DMA((n_c * n_w + 2 * n_c,)),
        ],
        compiler_params=pltpu.CompilerParams(vmem_limit_bytes=VMEM_LIMIT),
        cost_estimate=pl.CostEstimate(flops=2 * full * width * wide * n_c, bytes_accessed=22_000_000, transcendentals=0),
        name="feed_forward_out",
    )(scal, *hids, *ggus, *[shard for chunk in w_chunks for shard in chunk])


def flip(index, bits):
    for bit in (1, 2, 4):
        if bits & bit:
            index = index + bit - 2 * bit * lax.rem(lax.div(index, bit), 2)
    return index


class Spot:
    def __init__(self, index, choices):
        self.index = index
        self.flips = {0: index}
        for bits in choices:
            self.flips[bits] = flip(index, bits)


def spots():
    me_t = Spot(lax.axis_index("tensor"), (1, 2, 3))
    me_d = Spot(lax.axis_index("dp"), (1, 2, 3, 4, 5, 6, 7))
    me_d.x = lax.rem(me_d.index, 2)
    me_d.beside = 1 - me_d.x
    me_d.z = Spot(lax.div(me_d.index, 2), (1, 2, 3))
    return me_t, me_d


def greet(barrier, me_d, me_t, along_d, along_t):
    devices = [{"dp": me_d.flips[bits]} for bits in along_d]
    devices += [{"tensor": me_t.flips[bits]} for bits in along_t]
    for device in devices:
        pl.semaphore_signal(barrier, inc=1, device_id=device, device_id_type=pl.DeviceIdType.MESH)
    return lambda: pl.semaphore_wait(barrier, len(devices))


def remote(source, target, sems, number, device):
    return pltpu.make_async_remote_copy(
        src_ref=source,
        dst_ref=target,
        send_sem=sems.at[0, number],
        recv_sem=sems.at[1, number],
        device_id=device,
        device_id_type=pl.DeviceIdType.MESH,
    )


class Remote:
    LIMIT = 128

    def __init__(self, sems):
        self.sems, self.used = sems, 0

    def __call__(self, source, target, device):
        assert self.used < self.LIMIT
        self.used += 1
        return remote(source, target, self.sems, self.used - 1, device)


class Local:
    LIMIT = 64

    def __init__(self, sems):
        self.sems, self.used = sems, 0

    def make(self, source, target):
        assert self.used < self.LIMIT
        self.used += 1
        return pltpu.make_async_copy(source, target, self.sems.at[self.used - 1])

    def __call__(self, source, target):
        copy = self.make(source, target)
        copy.start()
        return copy


COPY_SEMS = [
    pltpu.SemaphoreType.DMA((2, Remote.LIMIT)),
    pltpu.SemaphoreType.DMA((Local.LIMIT,)),
]


class ShardGather:
    def __init__(self, shard, place, send, me_d, direct=False):
        def pass_on(bits, target):
            there = place(me_d.flips[bits])
            return send(there, there, {"dp": me_d.flips[target]})

        mine = place(me_d.index)
        self.beside, self.next, self.across = [send(shard, mine, {"dp": me_d.flips[bits]}) for bits in (1, 2, 4)]
        self.direct = direct
        self.on = send(shard, mine, {"dp": me_d.flips[6]}) if direct else pass_on(4, 2)
        self.passed = [pass_on(bits, 1) for bits in (4, 2, 6)]

    def start_x(self):
        self.beside.start()

    def start_z(self):
        self.next.start()
        self.across.start()
        if self.direct:
            self.on.start()

    def forward(self):
        self.next.wait_recv()
        self.passed[1].start()
        self.across.wait_recv()
        if not self.direct:
            self.on.start()
        self.passed[0].start()

    def forward_last(self):
        self.on.wait_recv()
        self.passed[2].start()

    def arrive(self):
        self.beside.wait_recv()
        for copy in self.passed:
            copy.wait_recv()

    def drain(self):
        for copy in [self.beside, self.next, self.across, self.on] + self.passed:
            copy.wait_send()


class TokenGather:
    def __init__(self, block, whole, send, me_t):
        size = block.shape[0]
        mine = whole.at[rows_of(me_t.index, size)]
        there = whole.at[rows_of(me_t.flips[2], size)]
        near = {"tensor": me_t.flips[1]}
        self.near = send(block, mine, near)
        self.far = send(block, mine, {"tensor": me_t.flips[2]})
        self.passed = send(there, there, near)

    def start(self):
        self.far.start()
        self.near.start()

    def forward(self):
        self.far.wait_recv()
        self.passed.start()

    def arrive(self):
        self.near.wait_recv()
        self.passed.wait_recv()

    def drain(self):
        for copy in (self.near, self.far, self.passed):
            copy.wait_send()


class TokenReduce:
    def __init__(self, blocks, near, far, send, me_t, mine=None):
        device = {"tensor": me_t.flips[1]}
        self.blocks, self.near_ref, self.far_ref, self.mine = blocks, near, far, mine
        self.places = (me_t.index, me_t.flips[2])
        self.size = far.shape[0]
        self.near = [
            send(blocks.at[rows_of(me_t.flips[1 + 2 * n], self.size)], near.at[n], device) for n in range(2)
        ]
        self.far = send(near.at[1], far, {"tensor": me_t.flips[2]})

    def load(self, here):
        return [here(self.blocks.at[rows_of(place, self.size)], self.mine.at[n]) for n, place in enumerate(self.places)]

    def start(self, *which):
        for n in which or (1, 0):
            self.near[n].start()

    def part(self, n, rows):
        if self.mine is not None:
            return self.mine[n, rows, :].astype(F32)
        start = pl.multiple_of(self.places[n] * self.size + rows.start, 32)
        return self.blocks[pl.ds(start, rows.size), :].astype(F32)

    def middle(self):
        self.near[1].wait_recv()

        def step(rows):
            total = self.part(1, rows) + self.near_ref[1, rows, :].astype(F32)
            self.near_ref[1, rows, :] = total.astype(BF16)

        by_rows(self.size, 32, step)
        self.far.start()

    def arrive(self):
        self.near[0].wait_recv()
        self.far.wait_recv()

    def rows(self, rows):
        total = self.part(0, rows) + self.near_ref[0, rows, :].astype(F32)
        return total + self.far_ref[rows, :].astype(F32)

    def drain(self):
        for copy in self.near + [self.far]:
            copy.wait_send()


class ShardNear:
    def __init__(self, whole, near, out, send, me_d, mine=None):
        self.whole, self.near_ref, self.out, self.mine = whole, near, out, mine
        self.z, self.x = me_d.z, me_d.x
        self.size = near.shape[1]
        self.near = send(whole.at[:, me_d.beside], near, {"dp": me_d.flips[1]})

    def load(self, here):
        return [here(self.whole.at[:, self.x], self.mine)]

    def start(self):
        self.near.start()

    def part(self, there, rows):
        if self.mine is not None:
            return self.mine[there, rows, :].astype(F32)
        return self.whole[there, self.x, rows, :].astype(F32)

    def middle(self, far=None):
        self.near.wait_recv()
        for k in (1, 3, 2, 0):
            there = self.z.flips[k]

            def step(rows):
                total = self.part(there, rows) + self.near_ref[there, rows, :].astype(F32)
                if k:
                    self.near_ref[there, rows, :] = total.astype(BF16)
                else:
                    self.out[rows, :] = total

            by_rows(self.size, 32, step)
            if k and far is not None:
                far.ready(k)

    def drain(self):
        self.near.wait_send()


class ShardFar:
    def __init__(self, near, far, out, send, me_d):
        self.far_ref, self.out = far, out
        self.size = far.shape[1]
        self.far = [send(near.at[me_d.z.flips[k]], far.at[k - 1], {"dp": me_d.flips[2 * k]}) for k in (1, 2, 3)]
        self.last = self.far
        self.terms = (0, 1, 2)

    def ready(self, k):
        self.far[k - 1].start()

    def finish(self):
        for copy in self.last:
            copy.wait_recv()

        def step(rows):
            total = self.out[rows, :]
            for k in self.terms:
                total = total + self.far_ref[k, rows, :].astype(F32)
            self.out[rows, :] = total

        by_rows(self.size, 32, step)

    def drain(self):
        for copy in self.far:
            copy.wait_send()


class ShardHalves(ShardFar):
    def __init__(self, near, far, out, send, me_d):
        self.near_ref, self.far_ref, self.out = near, far, out
        self.size = far.shape[1]
        z = me_d.z.flips
        self.across = z[2]
        self.far = [
            send(near.at[z[1]], far.at[0], {"dp": me_d.flips[2]}),
            send(near.at[z[3]], far.at[1], {"dp": me_d.flips[2]}),
            send(near.at[z[2]], far.at[2], {"dp": me_d.flips[4]}),
        ]
        self.last = (self.far[0], self.far[2])
        self.terms = (0, 2)

    def ready(self, k):
        if k != 2:
            self.far[k // 2].start()

    def middle(self):
        self.far[1].wait_recv()

        def step(rows):
            total = self.near_ref[self.across, rows, :].astype(F32) + self.far_ref[1, rows, :].astype(F32)
            self.near_ref[self.across, rows, :] = total.astype(BF16)

        by_rows(self.size, 32, step)
        self.far[2].start()


def by_rows(count, step, body):
    def run(b, carry):
        body(rows_of(b, step))
        return carry

    lax.fori_loop(0, count // step, run, None)


def loop(start, stop, body, unroll=False):
    def run(i, carry):
        body(i)
        return carry

    lax.fori_loop(start, stop, run, None, unroll=unroll)


def rms_factor(values):
    return lax.rsqrt(jnp.mean(values * values, axis=-1, keepdims=True) + EPS)


def shape(dims, kind):
    return jax.ShapeDtypeStruct(dims, kind)


def block_kernel(
    lengths, in_ref, cot_ref, qw_ref, kv_ref, ow_ref, iw_ref, dw_ref, cos_ref, sin_ref, qg_ref, kg_ref, mg_ref, dg_ref,
    normed_out, raw_out, q_out, k_out, v_out, att_out, lse_out, r_out, blk_out,
    ig_ref, awg_ref, ffg_ref, sums_ref,
    x_ref, gq_ref, gk_ref, xs, ws, dn, us, outp, onear, ofar, resid, wnear, wfar, whole, dgain, put, got_t, got_d, free,
    sems, local_sems,
):
    seqs, full, width = xs.shape
    size = resid.shape[1]
    parts = full // size
    n_c = 3
    shard = qw_ref.shape[0]
    cols = iw_ref.shape[2] // n_c
    wide = 3 * cols
    me_t, me_d = spots()
    send, here = Remote(sems), Local(local_sems)
    mine_t, mine_d = rows_of(me_t.index, size), rows_of(me_d.index, shard)
    halves = [pl.ds(s * full, full) for s in range(seqs)]
    own_rows = [rows_of(s * parts + me_t.index, size) for s in range(seqs)]
    every_row = pl.ds(0, seqs * full)
    lanes_of = [slice(width * s, width * (s + 1)) for s in range(seqs)]

    def wait(copies):
        for copy in copies:
            copy.wait()

    pro_w = [
        ShardGather(ws.at[mine_d, lanes], lambda i, lanes=lanes: ws.at[rows_of(i, shard), lanes], send, me_d)
        for lanes in (slice(0, 256), slice(256, 512))
    ]
    out_w = ShardGather(ws.at[mine_d, 512:], lambda i: ws.at[rows_of(i, shard), 512:], send, me_d, True)
    normed = [TokenGather(xs.at[s, mine_t], xs.at[s], send, me_t) for s in range(seqs)]
    ups = [TokenGather(us.at[own_rows[s]], us.at[halves[s]], send, me_t) for s in range(seqs)]
    denses = [TokenGather(dn.at[own_rows[s]], dn.at[halves[s]], send, me_t) for s in range(seqs)]
    out_places = (outp, xs.at[0])
    back_places = (outp, xs.at[1])
    norm_places = (outp, dn.at[halves[0]])
    outs, backs, norms = [
        [TokenReduce(places[s], onear.at[s], ofar.at[s], send, me_t) for s in range(seqs)]
        for places in (out_places, back_places, norm_places)
    ]
    lows = [xs.at[0, pl.ds(s * size, size)] for s in range(seqs)]
    resids = [TokenGather(lows[s], r_out.at[s], send, me_t) for s in range(seqs)]
    ff_sums = [ffg_ref.at[:, wide * c : wide * (c + 1)] for c in range(n_c)]
    near = [ShardNear(whole.at[c], wnear.at[c], ff_sums[c], send, me_d) for c in range(2)]
    far = [ShardHalves(wnear.at[c], wfar.at[c], ff_sums[c], send, me_d) for c in range(2)]
    steps = [
        [send(put.at[0], got_t.at[me_t.index], {"tensor": me_t.flips[bits]}) for bits in (1, 2, 3)],
        [send(put.at[1], got_d.at[me_d.index], {"dp": me_d.flips[bits]}) for bits in (1, 2, 3, 4, 5, 6, 7)],
    ]
    load_own = [here.make(us.at[own_rows[s]], xs.at[0, pl.ds((seqs + s) * size, size)]) for s in range(seqs)]
    keeps = [here.make(xs.at[s], normed_out.at[s]) for s in range(seqs)]
    backup = [here.make(normed_out.at[s], xs.at[s]) for s in range(seqs)]
    low_keeps = [here.make(lows[s], r_out.at[s, mine_t]) for s in range(seqs)]

    def after_out(s):
        outs[s].arrive()
        outs[s].drain()

        def norm(rows):
            values = x_ref[rows, lanes_of[s]].astype(F32) + outs[s].rows(rows)
            resid[s, rows, :] = values
            target = pl.ds(pl.multiple_of((s * parts + me_t.index) * size + rows.start, 32), 32)
            dn[target, :] = (values * rms_factor(values) * dg_ref[...]).astype(BF16)

        by_rows(size, 32, norm)
        denses[s].start()
        if s:
            for copy in load_own:
                copy.start()

    def after_back(s):
        backs[s].arrive()
        backs[s].drain()

        def step(rows):
            grad = backs[s].rows(rows)
            values = resid[s, rows, :]
            factor = rms_factor(values)
            product = grad * values * factor
            dgain[...] += jnp.sum(product.reshape(-1, 8, width), axis=0)
            weighted = grad * dg_ref[...]
            inner = jnp.mean(values * weighted, axis=-1, keepdims=True)
            place = pl.ds(pl.multiple_of((seqs + s) * size + rows.start, 32), 32)
            total = xs[0, place, :].astype(F32) + factor * weighted - values * (factor * factor * factor) * inner
            ig_ref[rows, lanes_of[s]] = total
            lows[s][rows, :] = total.astype(BF16)

        by_rows(size, 32, step)
        resids[s].start()
        low_keeps[s].start()

    def after_norm(s):
        norms[s].arrive()

        def step(rows):
            values = x_ref[rows, lanes_of[s]].astype(F32)
            factor = rms_factor(values)
            weighted = norms[s].rows(rows) * mg_ref[...]
            inner = jnp.mean(values * weighted, axis=-1, keepdims=True)
            ig_ref[rows, lanes_of[s]] += factor * weighted - values * (factor * factor * factor) * inner

        by_rows(size, 32, step)

    def until_backward(wf):
        ff_w = [ShardGather(wf.at[c, mine_d], lambda i, c=c: wf.at[c, rows_of(i, shard)], send, me_d) for c in range(n_c)]

        def attention(kp, vp, acc, raw, q, k, v, att, lse, inb, cotb, kvb, owb, iwb, dwb):
            kept = ((raw, raw_out), (q, q_out), (k, k_out), (v, v_out), (att, att_out), (lse, lse_out))
            flushes = []

            def project(s):
                loop(0, parts, lambda r: project_rows(
                    r, size, lengths[s], xs.at[s], ws, (cos_ref, sin_ref), (gq_ref, gk_ref),
                    raw.at[s], q.at[s], k.at[s], v.at[s], kp, vp,
                ), True)

            def attend(s, start, stop):
                for i in range(start, stop):
                    attend_rows(i, size, q.at[s], kp, vp, acc, att.at[s], lse.at[s])

            def out(s):
                for n, bits in enumerate((3, 1, 2, 0)):
                    rows = rows_of(me_t.flips[bits], size)
                    out_places[s][rows, :] = dot_nt(att[s, rows, :], ws[:, 512:]).astype(BF16)
                    if n < 2:
                        outs[s].start(1 - n)

            def first_rows(s):
                def step(rows):
                    mine = inb[rows, :, :].astype(F32)[:, s, :]
                    target = pl.ds(pl.multiple_of(me_t.index * size + rows.start, 32), 32)
                    x_ref[rows, lanes_of[s]] = mine.astype(BF16)
                    xs[s, target, :] = (mine * rms_factor(mine) * mg_ref[...]).astype(BF16)

                by_rows(size, 32, step)

            def upstream_rows(rows):
                grads = cotb[rows, :, :].astype(F32)
                place = me_t.index * size + rows.start + iota((32, width), 0)
                for s in range(seqs):
                    target = pl.ds(pl.multiple_of((s * parts + me_t.index) * size + rows.start, 32), 32)
                    us[target, :] = jnp.where(place < lengths[s], grads[:, s, :], 0.0).astype(BF16)

            def inner_rows(rows):
                both = iwb[rows, :, :].astype(F32)
                target = pl.ds(pl.multiple_of(me_d.index * shard + rows.start, 32), 32)
                for c in range(n_c):
                    for n in range(2):
                        part = both[:, n, cols * c : cols * (c + 1)]
                        wf[c, target, cols * n : cols * (n + 1)] = part.astype(BF16)

            entered = greet(
                pltpu.get_barrier_semaphore(), me_d, me_t, (1, 2, 3, 4, 5, 6, 7), (1, 2, 3)
            )
            load_a = [here(qw_ref, ws.at[mine_d, :256]), here(kv_ref, kvb)]
            load_x = here(in_ref, inb)
            load_o = here(ow_ref, owb)
            load_f = [here(iw_ref, iwb), here(dw_ref, dwb)]
            load_u = here(cot_ref, cotb)
            wait(load_a)
            pair = kvb[...].astype(F32)
            for n in range(2):
                ws[mine_d, 256 + 128 * n : 384 + 128 * n] = pair[:, n, :].astype(BF16)
            load_x.wait()
            first_rows(0)
            entered()
            for exchange in pro_w:
                exchange.start_z()
                exchange.start_x()
            normed[0].start()
            for source, target in ((qg_ref, gq_ref), (kg_ref, gk_ref)):
                target[...] = jnp.concatenate([source[...], source[...]], axis=1)
            first_rows(1)
            for exchange in pro_w:
                exchange.forward()
            load_o.wait()
            ws[mine_d, 512:] = owb[...].astype(F32).T.astype(BF16)
            wait(load_f)
            for c in range(n_c):
                wf[c, mine_d, 2 * cols :] = dwb[cols * c : cols * (c + 1), :].astype(F32).T.astype(BF16)
            by_rows(shard, 32, inner_rows)
            for exchange in pro_w:
                exchange.forward_last()
            out_w.start_z()
            out_w.start_x()
            normed[0].forward()
            normed[1].start()
            normed[0].arrive()
            ff_w[0].start_z()
            load_u.wait()
            by_rows(size, 32, upstream_rows)
            for exchange in pro_w:
                exchange.arrive()
            ff_w[0].start_x()
            project(0)
            keeps[0].start()
            out_w.forward()
            out_w.forward_last()
            attend(0, 0, 3)
            normed[1].forward()
            ups[0].start()
            attend(0, 3, parts)
            ff_w[0].forward()
            out_w.arrive()
            out(0)
            outs[0].middle()
            for source, target in kept:
                flushes.append(here(source.at[0], target.at[0]))
            normed[1].arrive()
            project(1)
            keeps[1].start()
            ff_w[0].forward_last()
            ff_w[1].start_z()
            ff_w[1].start_x()
            attend(1, 0, 3)
            ups[0].forward()
            attend(1, 3, parts)
            normed[0].drain()
            keeps[0].wait()
            out(1)
            for source, target in kept:
                flushes.append(here(source.at[1], target.at[1]))
            after_out(0)
            outs[1].middle()
            ff_w[1].forward()
            ff_w[2].start_z()
            ff_w[2].start_x()
            wait(flushes)

        pl.run_scoped(
            attention,
            pltpu.VMEM((4, full, LANES), BF16),
            pltpu.VMEM((4, full, 2 * LANES), BF16),
            pltpu.VMEM((2, size, 2 * LANES), F32),
            pltpu.VMEM((seqs, full, 384), F32),
            pltpu.VMEM((seqs, full, 256), BF16),
            pltpu.VMEM((seqs, full, 128), BF16),
            pltpu.VMEM((seqs, full, 128), BF16),
            pltpu.VMEM((seqs, full, 256), BF16),
            pltpu.VMEM((seqs, 8, full), F32),
            pltpu.VMEM(in_ref.shape, BF16),
            pltpu.VMEM(cot_ref.shape, BF16),
            pltpu.VMEM(kv_ref.shape, BF16),
            pltpu.VMEM(ow_ref.shape, BF16),
            pltpu.VMEM(iw_ref.shape, BF16),
            pltpu.VMEM(dw_ref.shape, BF16),
        )

        def feed_forward(hid, ggu):
            def tokens(c, s):
                def run(r):
                    rows = rows_of(r, size)
                    gate_up = dot(dn[rows, :], wf[c, :, : 2 * cols])
                    grad = dot(us[rows, :], wf[c, :, 2 * cols :])
                    gate, up = gate_up[:, :cols], gate_up[:, cols:]
                    sig = 1.0 / (1.0 + jnp.exp2(gate * -LOG2E))
                    silu = gate * sig
                    hid[c, rows, :] = (silu * up).astype(BF16)
                    ggu[c, rows, :cols] = (grad * up * (sig + silu * (1.0 - sig))).astype(BF16)
                    ggu[c, rows, cols:] = (grad * silu).astype(BF16)

                loop(s * parts, (s + 1) * parts, run, True)

            def weigh(c, tokens, more=False):
                def run(b):
                    rows = rows_of(b, 256)
                    dims = whole.shape[2:4]
                    inner = dot_tn(dn[tokens, rows], ggu[c, tokens, :]).reshape(dims + (2 * cols,))
                    down = dot_tn(us[tokens, rows], hid[c, tokens, :]).reshape(dims + (cols,))
                    if more:
                        inner = inner + whole[c % 2, b, :, :, : 2 * cols].astype(F32)
                        down = down + whole[c % 2, b, :, :, 2 * cols :].astype(F32)
                    whole[c % 2, b, :, :, : 2 * cols] = inner.astype(BF16)
                    whole[c % 2, b, :, :, 2 * cols :] = down.astype(BF16)

                loop(0, whole.shape[1], run)

            def grad_sum(rows, chunks):
                left = jnp.concatenate([ggu[c, rows, :] for c in chunks], axis=1)
                right = jnp.concatenate([wf[c, :, : 2 * cols] for c in chunks], axis=1)
                return dot_nt(left, right)

            def first_grads(r):
                rows = rows_of(r, size)
                outp[rows, :] = grad_sum(rows, range(n_c - 1)).astype(BF16)

            def grad_blocks(s):
                for n, bits in enumerate((3, 1, 2, 0)):
                    rows = rows_of(s * parts + me_t.flips[bits], size)
                    place = rows_of(me_t.flips[bits], size)
                    if s:
                        total = grad_sum(rows, range(n_c))
                    else:
                        total = grad_sum(rows, (n_c - 1,)) + outp[place, :].astype(F32)
                    back_places[s][place, :] = total.astype(BF16)
                    if n < 2:
                        backs[s].start(1 - n)

            def down_block(r):
                rows = rows_of(r, size)
                left = jnp.concatenate([hid[c, rows, :] for c in range(n_c)], axis=1)
                right = jnp.concatenate([wf[c, :, 2 * cols :] for c in range(n_c)], axis=1)
                total = dot_nt(left, right)
                us[rows, :] = total.astype(BF16)

            denses[0].forward()
            ups[1].start()
            ff_w[1].forward_last()
            ups[0].arrive()
            ff_w[0].arrive()
            denses[0].arrive()
            tokens(0, 0)
            ff_w[2].forward()
            weigh(0, halves[0])
            after_out(1)
            ff_w[1].arrive()
            tokens(1, 0)
            ff_w[2].forward_last()
            weigh(1, halves[0])
            loop(0, parts, first_grads, True)
            ups[1].forward()
            denses[1].forward()
            ups[1].arrive()
            denses[1].arrive()
            tokens(0, 1)
            weigh(0, halves[1], True)
            near[0].start()
            ff_w[2].arrive()
            tokens(2, 0)
            grad_blocks(0)
            backs[0].middle()
            tokens(1, 1)
            weigh(1, halves[1], True)
            tokens(2, 1)
            normed[1].drain()
            keeps[1].wait()
            dgain[...] = jnp.zeros_like(dgain)
            wait(load_own)
            grad_blocks(1)
            after_back(0)
            near[0].middle(far[0])
            near[1].start()
            near[0].drain()
            backs[1].middle()
            weigh(2, every_row)
            ups[0].drain()
            ups[1].drain()
            loop(0, parts, down_block, True)
            loop(parts, seqs * parts, down_block, True)
            resids[0].forward()
            far[0].middle()
            for exchange in ff_w + denses:
                exchange.drain()

        pl.run_scoped(
            feed_forward,
            pltpu.VMEM((n_c, seqs * full, cols), BF16),
            pltpu.VMEM((n_c, seqs * full, 2 * cols), BF16),
        )

    pl.run_scoped(until_backward, pltpu.VMEM((n_c, 8 * shard, wide), BF16))

    def backward(
        kp, vp, kt, ga, dq, dk, dv, gp, drow, acc, gains, mixer, raw, q, k, v, att, lse,
        wo, wq, wk, lnear, lfar, pnear, pfar, ynear, yfar,
    ):
        entered = greet(free, me_d, me_t, (1, 2, 4, 6), (1, 2))
        downs = [TokenReduce(us.at[halves[s]], ynear.at[s], yfar.at[s], send, me_t) for s in range(seqs)]
        late_near, late_far = [], []
        for n in range(2):
            half = pl.ds(n * shard // 2, shard // 2)
            refs = lnear.at[:, half], ff_sums[2].at[half]
            late_near.append(ShardNear(whole.at[0, :, :, half], refs[0], refs[1], send, me_d))
            late_far.append(ShardHalves(refs[0], lfar.at[:, half], refs[1], send, me_d))
        pieces = ((wo, slice(512, 768)), (wq, slice(0, 256)), (wk, slice(256, 512)))
        pro_near = [ShardNear(part, pnear.at[n], awg_ref.at[:, lanes], send, me_d) for n, (part, lanes) in enumerate(pieces)]
        pro_far = [
            (ShardHalves if n else ShardFar)(pnear.at[n], pfar.at[n], awg_ref.at[:, lanes], send, me_d)
            for n, (part, lanes) in enumerate(pieces)
        ]
        kept = ((k_out, k), (v_out, v), (att_out, att), (lse_out, lse), (q_out, q))
        load_s = [[here(source.at[s], target.at[s]) for source, target in kept] for s in range(seqs)]
        load_raw = [here(raw_out.at[0], raw)]
        gains[...] = jnp.zeros_like(gains)
        mixer[...] = jnp.zeros_like(mixer)

        def load_grad(s):
            resids[s].arrive()
            low_keeps[s].wait()
            here(r_out.at[s], dn.at[halves[s]]).wait()

        def prepare(s):
            loop(0, parts, lambda r: prepare_rows(
                r, size, lengths[s], dn.at[halves[s]], ws, k.at[s], v.at[s], att.at[s], ga, drow, kp, kt, vp
            ), True)
            dk[...] = jnp.zeros_like(dk)
            dv[...] = jnp.zeros_like(dv)

        def sweep(s, start, stop):
            for i in range(start, stop):
                sweep_rows(i, size, q.at[s], ga, kp, kt, vp, drow, lse.at[s], acc, dq, dk, dv)

        def unproject_q(s):
            loop(0, parts, lambda r: unproject_queries(r, size, (cos_ref, sin_ref), gq_ref, raw, dq, gp.at[s], gains), True)

        def unproject_kv(s):
            loop(0, parts, lambda r: unproject_pairs(
                r, size, lengths[s], (cos_ref, sin_ref), gk_ref, raw, dk, dv, gp.at[s], gains
            ), True)

        def norm_blocks(s):
            for n, bits in enumerate((3, 1, 2, 0)):
                rows = rows_of(me_t.flips[bits], size)
                norm_places[s][rows, :] = dot_nt(gp[s, rows, :], ws[:, :512]).astype(BF16)
                if n < 2:
                    norms[s].start(1 - n)

        def weigh_out():
            def run(b):
                rows = rows_of(b, 256)
                total = sum(dot_tn(dn[halves[s], rows], att[s]) for s in range(seqs))
                wo[b] = total.astype(BF16).reshape(wo.shape[1:])

            loop(0, wo.shape[0], run)

        def weigh(target, lanes):
            def run(b):
                rows = rows_of(b, 256)
                total = sum(dot_tn(xs[s, :, rows], gp[s, :, lanes]) for s in range(seqs))
                target[b] = total.astype(BF16).reshape(target.shape[1:])
                product = total * ws[rows, lanes].astype(F32)
                high = product.astype(BF16)
                rest = (product - high.astype(F32)).astype(BF16)
                ones = jnp.ones((8, product.shape[1]), BF16)
                mixer[:, rows] += dot_nt(ones, high) + dot_nt(ones, rest)

            loop(0, target.shape[0], run)

        def after_down(s):
            downs[s].arrive()

            def step(rows):
                target = pl.ds(pl.multiple_of(s * size + rows.start, 32), 32)
                outp[target, :] = (resid[s, rows, :] + downs[s].rows(rows)).astype(BF16)

            by_rows(size, 32, step)
            return here(outp.at[pl.ds(s * size, size)], blk_out.at[s])

        def total_of(n, got, index):
            got[index] = put[n]
            for copy in steps[n]:
                copy.wait_recv()
            total = got[0]
            for place in range(1, got.shape[0]):
                total = total + got[place]
            return total

        wait(load_s[0])
        load_grad(0)
        prepare(0)
        entered()
        late_near[0].start()
        for exchange in downs:
            exchange.start()
        sweep(0, 0, 2)
        after_back(1)
        sweep(0, 2, 3)
        near[1].middle(far[1])
        sweep(0, 3, parts)
        wait(load_raw)
        unproject_q(0)
        unproject_kv(0)
        load_raw = [here(raw_out.at[1], raw)]
        norm_blocks(0)
        resids[1].forward()
        norms[0].middle()
        late_near[0].middle(late_far[0])
        late_near[1].start()
        downs[0].middle()
        load_grad(1)
        for exchange in resids:
            exchange.drain()
        for copy in backup:
            copy.start()
        wait(load_s[1])
        prepare(1)
        far[1].middle()
        far[0].finish()
        weigh_out()
        pro_near[0].start()
        sweep(1, 0, 2)
        downs[1].middle()
        sweep(1, 2, 3)
        late_near[1].middle(late_far[1])
        late_far[0].middle()
        sweep(1, 3, parts)
        pro_near[0].middle(pro_far[0])
        wait(load_raw)
        unproject_kv(1)
        wait(backup)
        weigh(wk, pieces[2][1])
        pro_near[2].start()
        unproject_q(1)
        weigh(wq, pieces[1][1])
        pro_near[1].start()
        for row, vector in ((0, mixer[0:1, :] / mg_ref[...]), (8, jnp.sum(dgain[...], axis=0, keepdims=True))):
            for i in range(8):
                put[0, row + i : row + i + 1, :] = vector[:, LANES * i : LANES * (i + 1)]
        put[0, 16:, :] = gains[...]
        for copy in steps[0]:
            copy.start()
        norm_blocks(1)
        norms[1].middle()
        late_far[1].middle()
        pro_near[2].middle(pro_far[2])
        put[1] = total_of(0, got_t, me_t.index)
        for copy in steps[1]:
            copy.start()
        after_norm(0)
        norms[0].drain()
        stays = [after_down(0)]
        pro_near[1].middle(pro_far[1])
        pro_far[2].middle()
        stays.append(after_down(1))
        far[1].finish()
        pro_far[0].finish()
        for exchange in late_far:
            exchange.finish()
        pro_far[1].middle()
        sums_ref[...] = total_of(1, got_d, me_d.index)
        after_norm(1)
        pro_far[2].finish()
        pro_far[1].finish()
        wait(stays)
        for copy in steps[0] + steps[1]:
            copy.wait_send()
        for exchange in downs + late_near + late_far + pro_near + pro_far:
            exchange.drain()

    pl.run_scoped(
        backward,
        pltpu.VMEM((4, full, LANES), BF16),
        pltpu.VMEM((4, full, LANES), BF16),
        pltpu.VMEM((4, LANES, full), BF16),
        pltpu.VMEM((full, 256), BF16),
        pltpu.VMEM((full, 256), F32),
        pltpu.VMEM((2, full, LANES), F32),
        pltpu.VMEM((2, full, LANES), F32),
        pltpu.VMEM((seqs, full, 512), BF16),
        pltpu.VMEM((8, full), F32),
        pltpu.VMEM((2, LANES, size), F32),
        pltpu.VMEM((8, LANES), F32),
        pltpu.VMEM((8, width), F32),
        pltpu.VMEM((full, 384), F32),
        pltpu.VMEM((seqs, full, 256), BF16),
        pltpu.VMEM((seqs, full, 128), BF16),
        pltpu.VMEM((seqs, full, 128), BF16),
        pltpu.VMEM((seqs, full, 256), BF16),
        pltpu.VMEM((seqs, 8, full), F32),
        pltpu.VMEM((4, 2, shard, 256), BF16),
        pltpu.VMEM((4, 2, shard, 256), BF16),
        pltpu.VMEM((4, 2, shard, 256), BF16),
        pltpu.VMEM((4, shard, wide), BF16),
        pltpu.VMEM((3, shard, wide), BF16),
        pltpu.VMEM((3, 4, shard, 256), BF16),
        pltpu.VMEM((3, 3, shard, 256), BF16),
        pltpu.VMEM((seqs, 2, size, width), BF16),
        pltpu.VMEM((seqs, size, width), BF16),
    )
    for exchange in pro_w + [out_w, near[1]] + far + norms[1:]:
        exchange.drain()


def fused_block(lengths, inputs, cotangent, weights, tabs, gains):
    size, seqs, width = inputs.shape
    full = 4 * size
    shard = weights[0].shape[0]
    cols = 768
    n_c = 3
    wide = 3 * weights[3].shape[2] // n_c
    dp = 8
    return pl.pallas_call(
        block_kernel,
        out_shape=(
            shape((seqs, full, width), BF16),
            shape((seqs, full, 384), F32),
            shape((seqs, full, 256), BF16),
            shape((seqs, full, 128), BF16),
            shape((seqs, full, 128), BF16),
            shape((seqs, full, 256), BF16),
            shape((seqs, 8, full), F32),
            shape((seqs, full, width), BF16),
            shape((seqs, size, width), BF16),
            shape((size, seqs * width), F32),
            shape((shard, cols), F32),
            shape((shard, n_c * wide), F32),
            shape((24, LANES), F32),
        ),
        in_specs=[SMEM] + [ANY] * 7 + [VMEM] * 6,
        out_specs=(ANY,) * 9 + (VMEM,) * 4,
        scratch_shapes=[
            pltpu.VMEM((size, seqs * width), BF16),
            pltpu.VMEM((1, LANES), F32),
            pltpu.VMEM((1, LANES), F32),
            pltpu.VMEM((seqs, full, width), BF16),
            pltpu.VMEM((dp * shard, cols), BF16),
            pltpu.VMEM((seqs * full, width), BF16),
            pltpu.VMEM((seqs * full, width), BF16),
            pltpu.VMEM((full, width), BF16),
            pltpu.VMEM((seqs, 2, size, width), BF16),
            pltpu.VMEM((seqs, size, width), BF16),
            pltpu.VMEM((seqs, size, width), F32),
            pltpu.VMEM((2, 4, shard, wide), BF16),
            pltpu.VMEM((2, 3, shard, wide), BF16),
            pltpu.VMEM((2, 4, 2, shard, wide), BF16),
            pltpu.VMEM((8, width), F32),
            pltpu.VMEM((2, 24, LANES), F32),
            pltpu.VMEM((4, 24, LANES), F32),
            pltpu.VMEM((8, 24, LANES), F32),
            pltpu.SemaphoreType.REGULAR,
        ]
        + COPY_SEMS,
        compiler_params=pltpu.CompilerParams(
            vmem_limit_bytes=BLOCK_LIMIT, collective_id=0, has_side_effects=True
        ),
        cost_estimate=pl.CostEstimate(flops=90_000_000_000, bytes_accessed=60_000_000, transcendentals=14_000_000),
        name="block",
    )(lengths, inputs, cotangent, *weights, *tabs, *gains)


def finish_kernel(
    lengths, ig_ref, blk_ref, awg_ref, ffg_ref,
    block_out, input_out, query_out, pair_out, output_out, inner_out, down_out,
):
    size, seqs, width = input_out.shape
    hidden = down_out.shape[0]
    cols = hidden // 3
    start = lax.axis_index("tensor") * size

    def step(rows):
        place = start + rows.start + iota((32, width), 0)
        parts = []
        for s in range(seqs):
            lanes = slice(width * s, width * (s + 1))
            input_out[rows, s, :] = ig_ref[rows, lanes]
            parts.append(jnp.where(place < lengths[s], blk_ref[s, rows, :].astype(F32), 0.0))
        block_out[rows, :, :] = jnp.stack(parts, axis=1).astype(BF16)

    by_rows(size, 32, step)
    query_out[...] = awg_ref[:, :256]
    for n in range(2):
        pair_out[:, n, :] = awg_ref[:, 256 + 128 * n : 384 + 128 * n]
    output_out[...] = awg_ref[:, 512:].T
    for c in range(3):
        base = 3 * cols * c
        for n in range(2):
            inner_out[:, n, cols * c : cols * (c + 1)] = ffg_ref[:, base + cols * n : base + cols * (n + 1)]
        down_out[cols * c : cols * (c + 1), :] = ffg_ref[:, base + 2 * cols : base + 3 * cols].T


def fused_finish(lengths, ig, blk, awg, ffg):
    seqs, size, width = blk.shape
    shard, wide = ffg.shape
    hidden = wide // 3
    return pl.pallas_call(
        finish_kernel,
        out_shape=(
            shape((size, seqs, width), BF16),
            shape((size, seqs, width), F32),
            shape((shard, 256), F32),
            shape((shard, 2, 128), F32),
            shape((256, shard), F32),
            shape((shard, 2, hidden), F32),
            shape((hidden, shard), F32),
        ),
        in_specs=[SMEM] + [VMEM] * 4,
        out_specs=(VMEM,) * 7,
        compiler_params=pltpu.CompilerParams(vmem_limit_bytes=VMEM_LIMIT),
        name="finish",
    )(lengths, ig, blk, awg, ffg)


def swap(values, axis, bits):
    return lax.ppermute(values, axis, [(i, i ^ bits) for i in range(lax.axis_size(axis))])


def gather_tokens(block):
    far = swap(block, "tensor", 2)
    return [block, swap(block, "tensor", 1), far, swap(far, "tensor", 1)]


def scatter_tokens(keep, send):
    near = swap(send, "tensor", 1)
    middle = (keep[1].astype(F32) + near[1].astype(F32)).astype(BF16)
    far = swap(middle, "tensor", 2)
    return keep[0].astype(F32) + near[0].astype(F32) + far.astype(F32)


def gather_shards(shard):
    if lax.axis_size("dp") != 8 or shard.shape[0] % LANES:
        return [lax.all_gather(shard, "dp", axis=0, tiled=True)]
    slots = [shard, swap(shard, "dp", 1)]
    for bits in (2, 4, 6):
        there = swap(shard, "dp", bits)
        slots += [there, swap(there, "dp", 1)]
    return slots


def scatter_shards(grads):
    if len(grads) == 1:
        return lax.psum_scatter(grads[0].astype(F32), "dp", scatter_dimension=0, tiled=True)
    keep, send = grads
    near = swap(send, "dp", 1)
    both = keep.astype(F32) + near.astype(F32)
    total = both[0]
    for slot in (1, 2, 3):
        total = total + swap(both[slot].astype(BF16), "dp", 2 * slot).astype(F32)
    return total


def sum_everywhere(values):
    for axis in ("tensor", "dp"):
        bits = 1
        while bits < lax.axis_size(axis):
            values = values + swap(values, axis, bits)
            bits *= 2
    return values


def norm_rows(values, gain):
    factor = lax.rsqrt(jnp.mean(values * values, axis=-1, keepdims=True) + EPS)
    return (values * factor * gain, factor)


def norm_back(values, factor, gain, upstream):
    weighted = upstream * gain
    inner = jnp.mean(values * weighted, axis=-1, keepdims=True)
    return factor * weighted - values * factor * factor * factor * inner


def tables(full, head_width):
    half = head_width // 2
    freqs = THETA ** (-jnp.arange(half, dtype=F32) * 2.0 / head_width)
    angles = jnp.arange(full, dtype=F32)[:, None] * freqs[None, :]
    cosines, sines = jnp.cos(angles), jnp.sin(angles)
    return (jnp.tile(cosines, (1, 4)), jnp.tile(jnp.concatenate([-sines, sines], axis=1), (1, 2)))


def local_plain(
    inputs,
    lengths,
    query_weight,
    key_value_weight,
    output_weight,
    inner_weight,
    down_weight,
    mixer_gain,
    query_gain,
    key_gain,
    dense_gain,
    cotangent,
):
    size, seqs, width = inputs.shape
    parts = lax.axis_size("tensor")
    full = size * parts
    head = query_gain.shape[0]
    query_cols = query_weight.shape[1]
    pair_cols = key_value_weight.shape[2]
    hidden = inner_weight.shape[2]
    shard = query_weight.shape[0]
    me_t, me_d = lax.axis_index("tensor"), lax.axis_index("dp")
    n_c = 3
    cols = hidden // n_c
    cosines, sines = tables(full, head)
    gq = jnp.tile(query_gain, 2)[None, :]
    gk = jnp.tile(key_gain, 2)[None, :]

    down_turned = down_weight.T
    attn_shard = jnp.concatenate(
        [query_weight, key_value_weight.reshape(shard, 2 * pair_cols), output_weight.T], axis=1
    )
    attn_w = gather_shards(attn_shard)
    positions = me_t * size + jnp.arange(size, dtype=jnp.int32)
    scals = [
        jnp.stack([me_t.astype(jnp.int32), me_d.astype(jnp.int32), lengths[s], jnp.int32(0)])
        for s in range(seqs)
    ]
    tokens = [inputs[:, s].astype(F32) for s in range(seqs)]
    valid = [(positions < lengths[s])[:, None] for s in range(seqs)]
    firsts = [norm_rows(tokens[s], mixer_gain) for s in range(seqs)]
    normed = [gather_tokens(firsts[s][0].astype(BF16)) for s in range(seqs)]
    ff_w = []
    for c in range(n_c):
        part = slice(c * cols, (c + 1) * cols)
        ff_w.append(
            gather_shards(
                jnp.concatenate(
                    [inner_weight[:, 0, part], inner_weight[:, 1, part], down_turned[:, part]], axis=1
                )
            )
        )
    upstream = [jnp.where(valid[s], cotangent[:, s].astype(F32), 0.0) for s in range(seqs)]
    up_parts = [gather_tokens(upstream[s].astype(BF16)) for s in range(seqs)]

    saved, residual, seconds, dense = [], [], [], []
    for s in range(seqs):
        outs = attn_fwd(scals[s], cosines, sines, gq, gk, normed[s], attn_w)
        saved.append(outs[:6])
        residual.append(tokens[s] + scatter_tokens(outs[6], outs[7]))
        dense_in, factor = norm_rows(residual[s], dense_gain)
        seconds.append(factor)
        dense.append(gather_tokens(dense_in.astype(BF16)))

    x_parts = [part for s in range(seqs) for part in dense[s]]
    u_parts = [part for s in range(seqs) for part in up_parts[s]]
    hids, ggus, ff_grads = [], [], []
    for c in range(n_c):
        hid, ggu, grads = feed_forward(scals[0], x_parts, u_parts, ff_w[c])
        hids.append(hid)
        ggus.append(ggu)
        ff_grads.append(scatter_shards(grads))

    block_out, input_gradient, attn_grads = [], [], []
    mixer_part = dense_part = gain_part = 0.0
    for s in range(seqs):
        ykeep, ysend, gkeep, gsend = ff_out(s, scals[s], parts, size, hids, ggus, ff_w)
        grad_dense = scatter_tokens(gkeep, gsend)
        dense_part = dense_part + jnp.sum(grad_dense * residual[s] * seconds[s], axis=0)
        grad_residual = upstream[s] + norm_back(residual[s], seconds[s], dense_gain, grad_dense)
        r_parts = gather_tokens(grad_residual.astype(BF16))
        nkeep, nsend, gains, grads = attn_bwd(
            scals[s], cosines, sines, gq, gk, saved[s], normed[s], r_parts, attn_w
        )
        attn_grads.append(grads)
        gain_part = gain_part + gains
        grad_normed = scatter_tokens(nkeep, nsend)
        factor = firsts[s][1]
        mixer_part = mixer_part + jnp.sum(grad_normed * tokens[s] * factor, axis=0)
        input_gradient.append(grad_residual + norm_back(tokens[s], factor, mixer_gain, grad_normed))
        out_sum = scatter_tokens(ykeep, ysend)
        block_out.append(jnp.where(valid[s], residual[s] + out_sum, 0.0).astype(BF16))

    summed = [
        sum(part.astype(F32) for part in parts_of).astype(BF16) for parts_of in zip(*attn_grads)
    ]
    attn_grad = scatter_shards(summed)
    early = sum_everywhere(jnp.concatenate([dense_part.reshape(-1, LANES), gain_part], axis=0))
    mixer = sum_everywhere(mixer_part.reshape(-1, LANES)).reshape(-1)
    dense_rows = width // LANES
    folded = early[dense_rows:, :head] + early[dense_rows:, head:]
    inner_gradient = jnp.stack(
        [
            jnp.concatenate([grad[:, p * cols : (p + 1) * cols] for grad in ff_grads], axis=1)
            for p in range(2)
        ],
        axis=1,
    )
    down_gradient = jnp.concatenate([grad[:, 2 * cols :] for grad in ff_grads], axis=1).T
    return (
        jnp.stack(block_out, axis=1),
        jnp.stack(input_gradient, axis=1),
        attn_grad[:, :query_cols],
        attn_grad[:, query_cols : query_cols + 2 * pair_cols].reshape(shard, 2, pair_cols),
        attn_grad[:, query_cols + 2 * pair_cols :].T,
        inner_gradient,
        down_gradient,
        mixer,
        folded[0],
        folded[1],
        early[:dense_rows].reshape(-1),
    )


def local(*args):
    inputs, shard = args[0], args[2].shape[0]
    if lax.axis_size("dp") == 8 and lax.axis_size("tensor") == 4 and shard % LANES == 0 and inputs.shape[1] == 2:
        return local_fused(*args)
    return local_plain(*args)


def rope_tables(full, head):
    half = head // 2
    freqs = np.float32(THETA) ** (-np.arange(half, dtype=np.float32) * np.float32(2.0) / np.float32(head))
    angles = np.arange(full, dtype=np.float32)[:, None] * freqs[None, :].astype(np.float32)
    cosines, sines = np.cos(angles), np.sin(angles)
    return (
        jnp.asarray(np.tile(cosines, (1, 4)), F32),
        jnp.asarray(np.tile(np.concatenate([-sines, sines], axis=1), (1, 2)), F32),
    )


def local_fused(
    inputs,
    lengths,
    query_weight,
    key_value_weight,
    output_weight,
    inner_weight,
    down_weight,
    mixer_gain,
    query_gain,
    key_gain,
    dense_gain,
    cotangent,
):
    size, seqs, width = inputs.shape
    parts = lax.axis_size("tensor")
    full = size * parts
    head = query_gain.shape[0]
    tabs = rope_tables(full, head)
    weights = (query_weight, key_value_weight, output_weight, inner_weight, down_weight)
    gains = (query_gain[None, :], key_gain[None, :], mixer_gain[None, :], dense_gain[None, :])
    *_, blk, input_gradient, attn_grad, ff_grad, sums = fused_block(
        lengths, inputs, cotangent, weights, tabs, gains
    )
    finished = fused_finish(lengths, input_gradient, blk, attn_grad, ff_grad)
    folded = sums[16:, :head] + sums[16:, head:]
    return tuple(finished) + (
        sums[:8].reshape(-1),
        folded[0],
        folded[1],
        sums[8:16].reshape(-1),
    )


def solution(mesh):
    return jax.shard_map(
        local,
        mesh=mesh,
        in_specs=(
            P("tensor", "dp", None),
            P("dp"),
            P("dp", "tensor"),
            P("dp", None, "tensor"),
            P("tensor", "dp"),
            P("dp", None, "tensor"),
            P("tensor", "dp"),
            P(),
            P(),
            P(),
            P(),
            P("tensor", "dp", None),
        ),
        out_specs=(
            P("tensor", "dp", None),
            P("tensor", "dp", None),
            P("dp", "tensor"),
            P("dp", None, "tensor"),
            P("tensor", "dp"),
            P("dp", None, "tensor"),
            P("tensor", "dp"),
            P(),
            P(),
            P(),
            P(),
        ),
        check_vma=False,
    )
```
